32 devices in a mesh: dp: 8 (over z, x), mp: 4 (over y, core).
Axes of the slice: x: 2, y: 2, z: 4, core: 2. Of those that a mesh axis runs over, the one named last changes fastest.
Arguments:
- char_input: bfloat16 [8192, 4096], P(('dp', 'mp')), may hold values from -6 to 6
- char_counts: int32 [8192], P(('dp', 'mp')), may hold values from 1 to 16, as said below
- word_source: int32 [8192], P(('dp', 'mp')), may hold values from 0 to 8191, as said below
- segment_ids: int32 [8192], P(('dp', 'mp')), may hold values from 0 to 4, as said below
- cotangent: bfloat16 [8192, 512], P(('dp', 'mp')), may hold values from -6 to 6
- char_norm_gains: bfloat16 [2, 256], replicated, may hold values from 0.099609375 to 1.8984375
- char_qkv: bfloat16 [256, 768], replicated, may hold values from -0.375 to 0.375
- char_out: bfloat16 [256, 256], replicated, may hold values from -0.75 to 0.75
- char_up: bfloat16 [256, 1024], replicated, may hold values from -0.375 to 0.375
- char_down: bfloat16 [1024, 256], replicated, may hold values from -0.1875 to 0.1875
- pool_vector: bfloat16 [256], replicated, may hold values from -0.375 to 0.375
- char_proj: bfloat16 [256, 512], replicated, may hold values from -0.375 to 0.375
- word_norm_gains: bfloat16 [2, 512], replicated, may hold values from 0.099609375 to 1.8984375
- word_qkv: bfloat16 [3, 512, 512], P(None, None, 'mp'), may hold values from -0.25 to 0.25
- word_out: bfloat16 [512, 512], P('mp'), may hold values from -3 to 3
- word_up: bfloat16 [512, 2048], P(None, 'mp'), may hold values from -0.25 to 0.25
- word_down: bfloat16 [2048, 512], P('mp'), may hold values from -0.125 to 0.125
Outputs:
- word_output: bfloat16 [8192, 512], P(('dp', 'mp'))
- char_input_grad: float32 [8192, 4096], P(('dp', 'mp'))
- grad_char_qkv: float32 [256, 768], P('dp', 'mp')
- grad_char_out: float32 [256, 256], P('dp', 'mp')
- grad_char_up: float32 [256, 1024], P('dp', 'mp')
- grad_char_down: float32 [1024, 256], P('dp', 'mp')
- grad_char_proj: float32 [256, 512], P('dp', 'mp')
- grad_word_qkv: float32 [3, 512, 512], P(None, 'dp', 'mp')
- grad_word_out: float32 [512, 512], P('mp', 'dp')
- grad_word_up: float32 [512, 2048], P('dp', 'mp')
- grad_word_down: float32 [2048, 512], P('mp', 'dp')
- grad_char_gains: float32 [2, 256], replicated
- grad_pool_vector: float32 [256], replicated
- grad_word_gains: float32 [2, 512], replicated
The draws below stay inside these ranges and needn't reach their ends.
Inputs may be any that keep to these rules, and one draw needn't show every extreme that they name: `char_counts`: each word has 1 to 16 present character slots, the first ones; some word has all 16 in every draw. `word_source`: a permutation of the sequence-layout positions; a bucket row and the position it names stand at the same index of mp; at most 64 of the words held by one device belong to one sequence, and exactly 64 for some pair in every draw. `segment_ids`: each sequence holds five documents numbered 0 to 4 in order; document 2 begins at or before position 128 of its sequence and ends at or after position 895.
All inputs are finite; a program needn't handle non-finite values.
Results may differ from the reference program's by a relative error of at most 0.022.
The reference program's roundings to bfloat16 on the way count: a program that leaves them out, or rounds other values in their place, can miss the bound.
Values may be sent and summed in bfloat16 or wider, within the bound.
A program may use at most 256 MiB of HBM per device.

```python
import jax
import jax.numpy as jnp
from jax import lax

D = 512
HEADS = 8
FF = 2048
CD = 256
CHAR_HEADS = 4
CFF = 1024
CHARS = 16
WORD_DEV = 256
SEQ_LEN = 1024
WORDS = 8192
N_DP = 8
N_MP = 4


def draw_char_counts(key, part):
    key = jax.random.fold_in(key, 11)
    key_top, key_pick, key_rest = jax.random.split(key, 3)
    blocks_count = WORDS // WORD_DEV
    ceilings = jax.random.randint(key_top, (blocks_count,), 3, CHARS + 1)
    chosen = jax.random.randint(key_pick, (), 0, blocks_count)
    ceilings = jnp.where(jnp.arange(blocks_count) == chosen, CHARS, ceilings)
    per_word = jnp.repeat(ceilings, WORD_DEV)
    counts_drawn = 1 + jax.random.randint(key_rest, (WORDS,), 0, per_word)
    counts_drawn = jnp.where(jnp.arange(WORDS) == chosen * WORD_DEV, CHARS, counts_drawn)
    return counts_drawn.astype(jnp.int32)


def draw_segment_ids(key, part):
    key = jax.random.fold_in(key, 23)
    subkeys = jax.random.split(key, 4)
    eighth = SEQ_LEN // 8
    cut_second = jax.random.randint(subkeys[0], (N_DP, 1), 2, eighth + 1)
    cut_first = jax.random.randint(subkeys[1], (N_DP, 1), 1, cut_second)
    cut_third = jax.random.randint(subkeys[2], (N_DP, 1), SEQ_LEN - eighth, SEQ_LEN - 1)
    cut_fourth = jax.random.randint(subkeys[3], (N_DP, 1), cut_third + 1, SEQ_LEN)
    places = jnp.arange(SEQ_LEN)[None, :]
    segment_number = (places >= cut_first).astype(jnp.int32) + (places >= cut_second).astype(jnp.int32)
    segment_number = segment_number + (places >= cut_third).astype(jnp.int32) + (places >= cut_fourth).astype(jnp.int32)
    return segment_number.reshape(WORDS).astype(jnp.int32)


def draw_word_source(key, part):
    key = jax.random.fold_in(key, 37)
    groups = N_DP
    half_groups = groups // 2
    base_count = WORD_DEV // groups
    extra_count = WORD_DEV % groups

    def one_class(class_key):
        subkeys = jax.random.split(class_key, 4)
        amounts = base_count + (jnp.arange(groups) < extra_count).astype(jnp.int32)
        lower_half = amounts[:half_groups]
        upper_half = amounts[half_groups:]
        moved = jax.random.randint(subkeys[0], (half_groups,), 0, upper_half + 1)
        moved = moved.at[0].set(upper_half[0])
        amounts = jnp.concatenate([lower_half + moved, upper_half - moved])
        row_perm = jax.random.permutation(subkeys[1], groups)
        col_perm = jax.random.permutation(subkeys[2], groups)
        counts_pair = amounts[(col_perm[None, :] - row_perm[:, None]) % groups]
        orders = jax.vmap(lambda order_key: jax.random.permutation(order_key, WORD_DEV))(jax.random.split(subkeys[3], groups))
        col_start = jnp.cumsum(counts_pair, 0) - counts_pair
        row_end = jnp.cumsum(counts_pair, 1)
        row_start = row_end - counts_pair
        slots = jnp.arange(WORD_DEV)
        owner_of = jnp.sum((slots[None, :, None] >= row_end[:, None, :]).astype(jnp.int32), axis=2)
        within = slots[None, :] - jnp.take_along_axis(row_start, owner_of, 1)
        start_in_owner = jnp.take_along_axis(col_start, owner_of, 1) + within
        positions = orders[owner_of, start_in_owner]
        return (owner_of, positions)
    class_keys = jax.random.split(key, N_MP + 1)
    owner_of, positions = jax.vmap(one_class)(class_keys[:N_MP])
    classes = jnp.arange(N_MP)[:, None, None]
    global_index = (owner_of * N_MP + classes) * WORD_DEV + positions
    layout = jnp.transpose(global_index, (1, 0, 2))
    shuffles = jax.vmap(lambda shuffle_key: jax.random.permutation(shuffle_key, WORD_DEV))(jax.random.split(class_keys[N_MP], groups * N_MP))
    layout = jnp.take_along_axis(layout, shuffles.reshape(groups, N_MP, WORD_DEV), 2)
    return layout.reshape(WORDS).astype(jnp.int32)


def level_of(rng, extent, pieces, least, top_value):
    gain = 1.0
    for axis_at, parts in pieces:
        steps = jax.random.uniform(jax.random.fold_in(jax.random.fold_in(rng, 6), axis_at), (parts,), jnp.float32, least / len(pieces), top_value / len(pieces))
        gain = gain * jnp.repeat(jnp.exp(steps), extent[axis_at] // parts).reshape((-1,) + (1,) * (len(extent) - 1 - axis_at))
    return gain


def noise(rng, extent, scale, bound, cuts=(), dtype=jnp.bfloat16):
    level = level_of(rng, extent, cuts, -0.22, 0.18) if cuts else 1.0
    values = jax.random.normal(rng, extent, jnp.float32) * scale * level
    return jnp.minimum(jnp.maximum(values, -bound), bound).astype(dtype)


def setup_inputs(seed: int = 0) -> dict:
    key_of = jax.random.split(jax.random.key(seed), 18)
    return {
        "char_input": noise(key_of[0], (WORDS, CHARS * CD), 1.0, 6.0, ((0, 32),)),
        "char_counts": draw_char_counts(jax.random.fold_in(key_of[17], 71), 0),
        "word_source": draw_word_source(jax.random.fold_in(key_of[17], 71), 0),
        "segment_ids": draw_segment_ids(jax.random.fold_in(key_of[17], 71), 0),
        "cotangent": noise(key_of[4], (WORDS, D), 1.0, 6.0, ((0, 32),)),
        "char_norm_gains": jnp.clip(1.0 + 0.18 * jax.random.normal(key_of[5], (2, CD), jnp.float32), 0.099609375, 1.8984375).astype(jnp.bfloat16),
        "char_qkv": noise(key_of[6], (CD, 3 * CD), CD ** -0.5, 0.375),
        "char_out": noise(key_of[7], (CD, CD), (CD // 4) ** -0.5, 0.75),
        "char_up": noise(key_of[8], (CD, CFF), CD ** -0.5, 0.375),
        "char_down": noise(key_of[9], (CFF, CD), CFF ** -0.5, 0.1875),
        "pool_vector": noise(key_of[10], (CD,), CD ** -0.5, 0.375),
        "char_proj": noise(key_of[11], (CD, D), CD ** -0.5, 0.375),
        "word_norm_gains": jnp.clip(1.0 + 0.18 * jax.random.normal(key_of[12], (2, D), jnp.float32), 0.099609375, 1.8984375).astype(jnp.bfloat16),
        "word_qkv": noise(key_of[13], (3, D, D), D ** -0.5, 0.25, ((2, 4),)),
        "word_out": noise(key_of[14], (D, D), (max(1, 8 * D // SEQ_LEN)) ** -0.5, 3.0, ((0, 4),)),
        "word_up": noise(key_of[15], (D, FF), D ** -0.5, 0.25, ((1, 4),)),
        "word_down": noise(key_of[16], (FF, D), FF ** -0.5, 0.125, ((0, 4),)),
    }


EPSILON = 1e-05
NEGATIVE = -1e+30
HIGHEST = lax.Precision.HIGHEST

@jax.custom_vjp
def low(v):
    return lax.optimization_barrier(v.astype(jnp.bfloat16)).astype(jnp.float32)

@jax.custom_vjp
def low_back(v):
    return v

def low_keep(v):
    return (low(v), None)

def low_pass(kept, grad):
    return (grad,)

def back_keep(v):
    return (v, None)

def back_low(kept, grad):
    return (low(grad),)
low.defvjp(low_keep, low_pass)
low_back.defvjp(back_keep, back_low)

def norm_rows(values, gain_vec):
    row_mean = lax.optimization_barrier(jnp.mean(values, -1, keepdims=True))
    centered = values - row_mean
    variance = lax.optimization_barrier(jnp.mean(centered * centered, -1, keepdims=True))
    return centered * lax.rsqrt(variance + EPSILON) * gain_vec

def pool_words(final_rows, pool_vec, present):
    pool_scores = lax.optimization_barrier(jnp.sum(final_rows * pool_vec, -1))
    pool_scores = jnp.where(present, pool_scores, NEGATIVE)
    pool_weights = jax.nn.softmax(pool_scores, axis=-1)
    return lax.optimization_barrier(jnp.sum(pool_weights[..., None] * final_rows, 1))

def char_block(chars_in, present, char_weights):
    norm_gains, qkv_weight, out_weight, up_weight, down_weight, pool_weight, proj_weight = char_weights
    word_count = chars_in.shape[0]
    char_width = chars_in.shape[-1]
    head_size = char_width // CHAR_HEADS
    normed = low(norm_rows(chars_in, norm_gains[0]))
    projected = low_back(low(jnp.einsum('wcd,de->wce', normed, qkv_weight, precision=HIGHEST)))
    projected = projected.reshape(word_count, CHARS, 3, CHAR_HEADS, head_size)
    scores = low_back(jnp.einsum('wqhe,wkhe->whqk', projected[:, :, 0], projected[:, :, 1], precision=HIGHEST) * head_size ** (-0.5))
    scores = jnp.where(present[:, None, None, :], scores, NEGATIVE)
    softmaxed = low(jax.nn.softmax(scores, axis=-1))
    mixed_heads = jnp.einsum('whqk,wkhe->wqhe', softmaxed, projected[:, :, 2], precision=HIGHEST)
    mixed_heads = low_back(low(mixed_heads.reshape(word_count, CHARS, char_width)))
    middle = chars_in + low_back(jnp.einsum('wcd,de->wce', mixed_heads, out_weight, precision=HIGHEST))
    normed_two = low(norm_rows(middle, norm_gains[1]))
    hidden = low_back(jnp.einsum('wcd,de->wce', normed_two, up_weight, precision=HIGHEST))
    activated = low(jax.nn.gelu(hidden))
    final_rows = middle + low_back(jnp.einsum('wcd,de->wce', activated, down_weight, precision=HIGHEST))
    pooled = low(pool_words(final_rows, pool_weight, present))
    return jnp.dot(pooled, proj_weight, precision=HIGHEST)

def word_block(rows_in, segments, word_weights):
    norm_gains, qkv_weight, out_weight, up_weight, down_weight = word_weights
    length, model_width = rows_in.shape
    head_size = model_width // HEADS
    normed = low(norm_rows(rows_in, norm_gains[0]))
    projected = low_back(low(jnp.einsum('ld,kde->kle', normed, qkv_weight, precision=HIGHEST)))
    projected = projected.reshape(3, length, HEADS, head_size)
    scores = low_back(jnp.einsum('qhe,khe->hqk', projected[0], projected[1], precision=HIGHEST) * head_size ** (-0.5))
    places = jnp.arange(length)
    allowed = (places[None, :] <= places[:, None]) & (segments[None, :] == segments[:, None])
    scores = jnp.where(allowed[None], scores, NEGATIVE)
    softmaxed = low(jax.nn.softmax(scores, axis=-1))
    mixed_heads = jnp.einsum('hqk,khe->qhe', softmaxed, projected[2], precision=HIGHEST)
    mixed_heads = low_back(low(mixed_heads.reshape(length, model_width)))
    middle = rows_in + low_back(jnp.dot(mixed_heads, out_weight, precision=HIGHEST))
    normed_two = low(norm_rows(middle, norm_gains[1]))
    hidden = low_back(jnp.dot(normed_two, up_weight, precision=HIGHEST))
    activated = low(jax.nn.gelu(hidden))
    return middle + low_back(jnp.dot(activated, down_weight, precision=HIGHEST))

def reference(char_input, char_counts, word_source, segment_ids, cotangent, char_norm_gains, char_qkv, char_out, char_up, char_down, pool_vector, char_proj, word_norm_gains, word_qkv, word_out, word_up, word_down):
    chars = char_input.astype(jnp.float32).reshape(WORDS, CHARS, CD)
    present = (jnp.arange(CHARS)[None, :] < char_counts[:, None]).reshape(N_DP * N_MP, WORD_DEV, CHARS)
    segments = segment_ids.reshape(N_DP, SEQ_LEN)
    char_weights = tuple((weight.astype(jnp.float32) for weight in (char_norm_gains, char_qkv, char_out, char_up, char_down, pool_vector, char_proj)))
    word_weights = tuple((weight.astype(jnp.float32) for weight in (word_norm_gains, word_qkv, word_out, word_up, word_down)))
    char_step = jax.checkpoint(char_block)
    word_step = jax.checkpoint(word_block)

    def forward(chars_all, char_params, word_params):

        def char_map(block_item):
            return char_step(block_item[0], block_item[1], char_params)
        word_vec = lax.map(char_map, (chars_all.reshape(N_DP * N_MP, WORD_DEV, CHARS, CD), present))
        sent = low_back(low(word_vec.reshape(WORDS, D)))
        ordered = jnp.zeros((WORDS, D), jnp.float32).at[word_source].set(sent)

        def word_map(block_item):
            return word_step(block_item[0], block_item[1], word_params)
        result = lax.map(word_map, (ordered.reshape(N_DP, SEQ_LEN, D), segments))
        return result.reshape(WORDS, D)
    output, pullback = jax.vjp(forward, chars, char_weights, word_weights)
    d_chars, char_grads, word_grads = pullback(cotangent.astype(jnp.float32))
    return (output.astype(jnp.bfloat16), d_chars.reshape(WORDS, CHARS * CD), char_grads[1], char_grads[2], char_grads[3], char_grads[4], char_grads[6], word_grads[1], word_grads[2], word_grads[3], word_grads[4], char_grads[0], char_grads[5], word_grads[0])
```

```python
import functools
from functools import partial

import jax
import jax.numpy as jnp
from jax import lax
from jax.experimental import pallas as pl
from jax.experimental.pallas import tpu as pltpu
from jax.sharding import PartitionSpec as P

CHARS = 16
CHAR_HEADS = 4
EPSILON = 1e-05
NEGATIVE = -1e30
GELU_A = 0.7978845608028654
GELU_B = 0.044715
F32 = jnp.float32
BF16 = jnp.bfloat16
VMEM_LIMIT = 60 * 1024 * 1024


def dot_nn(left, right):
    return jnp.dot(left, right, preferred_element_type=F32)


def dot_nt(left, right):
    return lax.dot_general(left, right, (((1,), (1,)), ((), ())), preferred_element_type=F32)


def dot_tn(left, right):
    return lax.dot_general(left, right, (((0,), (0,)), ((), ())), preferred_element_type=F32)


def head_stack(values, heads, factor):
    width = values.shape[1] // heads
    lane = lax.broadcasted_iota(jnp.int32, (1, values.shape[1]), 1) // width
    return jnp.concatenate(
        [values * jnp.where(lane == h, factor, 0.0).astype(values.dtype) for h in range(heads)], 0
    )


def gelu_both(hidden):
    square = hidden * hidden
    inner = hidden * (GELU_A + (GELU_A * GELU_B) * square)
    tanh = jnp.tanh(inner)
    half = 0.5 + 0.5 * tanh
    slope = half + (0.5 * hidden) * (1.0 - tanh * tanh) * (GELU_A + (3.0 * GELU_A * GELU_B) * square)
    return hidden * half, slope


def char_fwd_body(
    x_ref, cnt_ref, gains_ref, wqkv_ref, wout_ref, wup_ref, wdown_ref, pool_ref, wproj_ref,
    e_ref, n1_ref, p_ref, a_ref, o_ref, n2_ref, rs1_ref, rs2_ref, act_ref, dg_ref, f_ref, aw_ref, pooled_ref,
):
    words, wide = x_ref.shape
    width = wide // CHARS
    blocks = words // 8
    gains = gains_ref[...].astype(F32)
    pieces = []
    for g in range(words // 16):
        xt = x_ref[16 * g : 16 * g + 16, :].astype(F32)
        for half in range(2):
            for c in range(CHARS):
                pieces.append(xt[8 * half : 8 * half + 8, width * c : width * c + width])
    x = jnp.concatenate(pieces, 0)

    def norm(v, gain):
        mean = jnp.mean(v, -1, keepdims=True)
        centered = v - mean
        rstd = lax.rsqrt(jnp.mean(centered * centered, -1, keepdims=True) + EPSILON)
        return (centered * rstd * gain).astype(BF16), rstd

    n1, rs1 = norm(x, gains[0:1])
    n1_ref[...] = n1
    rs1_ref[...] = rs1
    p_ref[...] = dot_nn(n1, wqkv_ref[...]).astype(BF16)
    row_w = lax.broadcasted_iota(jnp.int32, (8, 128), 0)
    lane_w = lax.broadcasted_iota(jnp.int32, (8, 128), 1) % 8
    same = row_w == lane_w
    slot = lax.broadcasted_iota(jnp.int32, (CHARS, 8, 128), 0)
    for b in range(blocks):
        rows = slice(128 * b, 128 * b + 128)
        counts = jnp.broadcast_to(cnt_ref[8 * b : 8 * b + 8, :], (8, 128))
        here = slot < counts[None]
        q = p_ref[rows, 0:width]
        k = p_ref[rows, width : 2 * width]
        v = p_ref[rows, 2 * width : 3 * width]
        st = dot_nt(head_stack(k, CHAR_HEADS, (width // CHAR_HEADS) ** -0.5), q)
        st = st.reshape(CHAR_HEADS, CHARS, 8, 128)
        st = jnp.where(here[None], st, NEGATIVE)
        e = jnp.exp(st - jnp.max(st, 1, keepdims=True))
        r = jnp.where(same[None, None], 1.0 / jnp.sum(e, 1, keepdims=True), 0.0)
        a = (e * r).reshape(CHAR_HEADS * 128, 128).astype(BF16)
        a_ref[CHAR_HEADS * 128 * b : CHAR_HEADS * 128 * (b + 1), :] = a
        o_ref[rows, :] = dot_tn(a, head_stack(v, CHAR_HEADS, 1.0)).astype(BF16)
    m = x + dot_nn(o_ref[...], wout_ref[...])
    n2, rs2 = norm(m, gains[1:2])
    n2_ref[...] = n2
    rs2_ref[...] = rs2
    act, slope = gelu_both(dot_nn(n2, wup_ref[...]))
    act = act.astype(BF16)
    act_ref[...] = act
    dg_ref[...] = slope.astype(BF16)
    f = m + dot_nn(act, wdown_ref[...])
    f_ref[...] = f.astype(BF16)
    t = jnp.sum(f * pool_ref[...].astype(F32), -1, keepdims=True).reshape(blocks, CHARS, 8, 1)
    counts = cnt_ref[...].reshape(blocks, 1, 8, 1)
    t = jnp.where(lax.broadcasted_iota(jnp.int32, t.shape, 1) < counts, t, NEGATIVE)
    et = jnp.exp(t - jnp.max(t, 1, keepdims=True))
    aw = et / jnp.sum(et, 1, keepdims=True)
    aw_ref[...] = aw.reshape(words * CHARS, 1)
    pooled = jnp.sum(aw * f.reshape(blocks, CHARS, 8, width), 1).reshape(words, width).astype(BF16)
    pooled_ref[...] = pooled
    e_ref[...] = dot_nn(pooled, wproj_ref[...]).astype(BF16)


def char_forward(x, counts, gains, wqkv, wout, wup, wdown, pool, wproj, step_words=32):
    words, wide = x.shape
    width = wide // CHARS
    rows = words * CHARS
    step_rows = step_words * CHARS
    full = lambda arr: pl.BlockSpec(arr.shape, lambda i: (0,) * arr.ndim)
    blk = lambda n, w: pl.BlockSpec((n, w), lambda i: (i, 0))
    hid = wup.shape[1]
    dw = wproj.shape[1]
    outs = [
        (words, step_words, dw, BF16), (rows, step_rows, width, BF16), (rows, step_rows, 3 * width, BF16),
        (rows * CHAR_HEADS, step_rows * CHAR_HEADS, 128, BF16), (rows, step_rows, width, BF16),
        (rows, step_rows, width, BF16), (rows, step_rows, 1, F32), (rows, step_rows, 1, F32),
        (rows, step_rows, hid, BF16), (rows, step_rows, hid, BF16), (rows, step_rows, width, BF16),
        (rows, step_rows, 1, F32), (words, step_words, width, BF16),
    ]
    return pl.pallas_call(
        char_fwd_body,
        grid=(words // step_words,),
        in_specs=[blk(step_words, wide), blk(step_words, 1)] + [full(w) for w in (gains, wqkv, wout, wup, wdown, pool, wproj)],
        out_specs=[blk(b, w) for _, b, w, _ in outs],
        out_shape=[jax.ShapeDtypeStruct((n, w), d) for n, _, w, d in outs],
        compiler_params=pltpu.CompilerParams(vmem_limit_bytes=VMEM_LIMIT),
        name="char_forward",
    )(x, counts, gains, wqkv, wout, wup, wdown, pool, wproj)


def char_bwd_body(
    de_ref, gains_ref, wqkv_ref, wout_ref, wup_ref, wdown_ref, pool_ref, wproj_ref,
    n1_ref, p_ref, a_ref, o_ref, n2_ref, rs1_ref, rs2_ref, act_ref, dg_ref, f_ref, aw_ref, pooled_ref,
    dx_ref, gqkv_ref, gout_ref, gup_ref, gdown_ref, gproj_ref, ggain_ref, gpool_ref,
    dp_ref, do_ref,
):
    words = de_ref.shape[0]
    width = n1_ref.shape[1]
    blocks = words // 8
    rows = words * CHARS
    gains = gains_ref[...].astype(F32)

    @pl.when(pl.program_id(0) == 0)
    def _():
        for ref in (gqkv_ref, gout_ref, gup_ref, gdown_ref, gproj_ref, ggain_ref, gpool_ref):
            ref[...] = jnp.zeros_like(ref)

    de = de_ref[...]
    gproj_ref[...] += dot_tn(pooled_ref[...], de)
    dpool = dot_nt(de, wproj_ref[...]).reshape(blocks, 1, 8, width)
    f = f_ref[...].astype(F32).reshape(blocks, CHARS, 8, width)
    aw = aw_ref[...].reshape(blocks, CHARS, 8, 1)
    g = jnp.sum(f * dpool, -1, keepdims=True)
    dt = aw * (g - jnp.sum(aw * g, 1, keepdims=True))
    gpool_ref[...] += jnp.sum((dt * f).reshape(rows // 8, 8, width), 0)
    df = (aw * dpool + dt * pool_ref[...].astype(F32)).reshape(rows, width)
    dfb = df.astype(BF16)
    gdown_ref[...] += dot_tn(act_ref[...], dfb)
    dh = (dg_ref[...].astype(F32) * dot_nt(dfb, wdown_ref[...])).astype(BF16)
    n2 = n2_ref[...]
    gup_ref[...] += dot_tn(n2, dh)
    dn2 = dot_nt(dh, wup_ref[...])

    def norm_back(dn, n, rstd, gain, row):
        d1 = dn * gain
        dnn = dn * n.astype(F32)
        ggain_ref[row] += jnp.sum(dnn.reshape(rows // 8, 8, width), 0)
        m1 = jnp.mean(d1, -1, keepdims=True)
        m2 = jnp.mean(dnn, -1, keepdims=True)
        return rstd * (d1 - m1 - n.astype(F32) * (1.0 / gain) * m2)

    dm = df + norm_back(dn2, n2, rs2_ref[...], gains[1:2], 1)
    dmb = dm.astype(BF16)
    gout_ref[...] += dot_tn(o_ref[...], dmb)
    do_ref[...] = dot_nt(dmb, wout_ref[...]).astype(BF16)
    scale = (width // CHAR_HEADS) ** -0.5
    for b in range(blocks):
        sl = slice(128 * b, 128 * b + 128)
        q = p_ref[sl, 0:width]
        k = p_ref[sl, width : 2 * width]
        v = p_ref[sl, 2 * width : 3 * width]
        do = do_ref[sl, :]
        ab = a_ref[CHAR_HEADS * 128 * b : CHAR_HEADS * 128 * (b + 1), :]
        a = ab.astype(F32).reshape(CHAR_HEADS, CHARS, 8, 128)
        dpt = dot_nt(head_stack(v, CHAR_HEADS, 1.0), do).reshape(CHAR_HEADS, CHARS, 8, 128)
        delta = jnp.sum(a * dpt, 1, keepdims=True)
        ds = (a * (dpt - delta)).reshape(CHAR_HEADS * 128, 128).astype(BF16)
        wide_ds = jnp.concatenate([ds[128 * h : 128 * h + 128] for h in range(CHAR_HEADS)], 1)
        wide_a = jnp.concatenate([ab[128 * h : 128 * h + 128] for h in range(CHAR_HEADS)], 1)
        dp_ref[sl, 0:width] = dot_tn(ds, head_stack(k, CHAR_HEADS, scale)).astype(BF16)
        dp_ref[sl, width : 2 * width] = dot_nn(wide_ds, head_stack(q, CHAR_HEADS, scale)).astype(BF16)
        dp_ref[sl, 2 * width : 3 * width] = dot_nn(wide_a, head_stack(do, CHAR_HEADS, 1.0)).astype(BF16)
    n1 = n1_ref[...]
    dp = dp_ref[...]
    gqkv_ref[...] += dot_tn(n1, dp)
    dn1 = dot_nt(dp, wqkv_ref[...])
    dx = dm + norm_back(dn1, n1, rs1_ref[...], gains[0:1], 0)
    for b in range(blocks):
        for c in range(CHARS):
            dx_ref[8 * b : 8 * b + 8, width * c : width * c + width] = dx[128 * b + 8 * c : 128 * b + 8 * c + 8]


def char_backward(de, kept, gains, wqkv, wout, wup, wdown, pool, wproj, step_words=32):
    words = de.shape[0]
    width = wout.shape[0]
    rows = words * CHARS
    step_rows = step_words * CHARS
    full = lambda arr: pl.BlockSpec(arr.shape, lambda i: (0,) * arr.ndim)
    blk = lambda n, w: pl.BlockSpec((n, w), lambda i: (i, 0))
    steps = words // step_words
    weights = (gains, wqkv, wout, wup, wdown, pool, wproj)
    outs = [wqkv.shape, wout.shape, wup.shape, wdown.shape, wproj.shape, (2, 8, width), (8, width)]
    return pl.pallas_call(
        char_bwd_body,
        grid=(steps,),
        in_specs=[blk(step_words, de.shape[1])] + [full(w) for w in weights]
        + [blk(r.shape[0] // steps, r.shape[1]) for r in kept],
        out_specs=[blk(step_words, CHARS * width)]
        + [pl.BlockSpec(s, lambda i, n=len(s): (0,) * n) for s in outs],
        out_shape=[jax.ShapeDtypeStruct((words, CHARS * width), F32)]
        + [jax.ShapeDtypeStruct(s, F32) for s in outs],
        scratch_shapes=[pltpu.VMEM((step_rows, 3 * width), BF16), pltpu.VMEM((step_rows, width), BF16)],
        compiler_params=pltpu.CompilerParams(vmem_limit_bytes=VMEM_LIMIT),
        name="char_backward",
    )(de, *weights, *kept)


MESH = pl.DeviceIdType.MESH
CHAR_ROWS = 224
WORD_ROWS = 768


def fold_half(block):
    half = block.shape[0] // 2
    return jnp.concatenate([block[:half], block[half:]], 1)


def unfold_half(block):
    return jnp.concatenate([block[:, :64], block[:, 64:]], 0)


def add_into(total_ref, other_ref, lead):
    def step(i, carry):
        total_ref[i] = (total_ref[i].astype(F32) + other_ref[i].astype(F32)).astype(total_ref.dtype)
        return carry
    lax.fori_loop(0, lead, step, 0)


def reduce_body(
    n_z,
    cqkv_ref, cout_ref, cup_ref, cdown_ref, cproj_ref, cgain_ref, cpool_ref, cg_ref,
    wqkv_ref, wout_ref, wup_ref, wdown_ref, wgain_ref,
    oqkv_ref, oout_ref, oup_ref, odown_ref, oproj_ref, owqkv_ref, owout_ref, owup_ref, owdown_ref,
    ocgain_ref, opool_ref, owgain_ref,
    cbuf, cr_a, cr_b, cr_c, cr_d, wbuf, wr_c, wr_d, small, sr, ssem, rsem,
):
    dp, mp = lax.axis_index("dp"), lax.axis_index("mp")
    z, x = dp // 2, dp % 2
    y, core = mp // 2, mp % 2
    peers = [(dp, y * 2 + 1 - core), (dp, (1 - y) * 2 + core), (z * 2 + 1 - x, mp)]
    z_peers = [(lax.rem(z + k, n_z) * 2 + x, mp) for k in range(1, n_z)]
    barrier = pltpu.get_barrier_semaphore()
    for peer in peers + z_peers:
        pl.semaphore_signal(barrier, inc=1, device_id=peer, device_id_type=MESH)

    def send(src, dst, slot, peer):
        copy = pltpu.make_async_remote_copy(
            src_ref=src, dst_ref=dst, send_sem=ssem.at[slot], recv_sem=rsem.at[slot],
            device_id=peer, device_id_type=MESH,
        )
        copy.start()
        return copy

    for d in range(2 * n_z):
        for t in range(3):
            wbuf[d % 2, d // 2, 64 * t : 64 * t + 64, :] = wqkv_ref[t, 64 * d : 64 * d + 64, :].astype(BF16)
        wbuf[d % 2, d // 2, 192:256, :] = wout_ref[64 * d : 64 * d + 64, :].astype(BF16)
        for t in range(4):
            wbuf[d % 2, d // 2, 256 + 64 * t : 320 + 64 * t, :] = wup_ref[64 * d : 64 * d + 64, 128 * t : 128 * t + 128].astype(BF16)
            wbuf[d % 2, d // 2, 512 + 64 * t : 576 + 64 * t, :] = wdown_ref[64 * d : 64 * d + 64, 128 * t : 128 * t + 128].astype(BF16)
    for d in range(2 * n_z):
        qkv = cqkv_ref[32 * d : 32 * d + 32, :]
        out = cout_ref[32 * d : 32 * d + 32, :]
        down = cdown_ref[128 * d : 128 * d + 128, :]
        for p in range(4):
            block = cbuf.at[p % 2, p // 2, d % 2, d // 2]
            part = qkv[:, 192 * p : 192 * p + 192]
            block[0:32, :] = part[:, 0:128].astype(BF16)
            block[32:48, :] = fold_half(part[:, 128:192]).astype(BF16)
            block[48:64, :] = fold_half(out[:, 64 * p : 64 * p + 64]).astype(BF16)
            block[64:96, :] = cup_ref[32 * d : 32 * d + 32, 256 * p : 256 * p + 128].astype(BF16)
            block[96:128, :] = cup_ref[32 * d : 32 * d + 32, 256 * p + 128 : 256 * p + 256].astype(BF16)
            block[128:192, :] = fold_half(down[:, 64 * p : 64 * p + 64]).astype(BF16)
            block[192:224, :] = cproj_ref[32 * d : 32 * d + 32, 128 * p : 128 * p + 128].astype(BF16)
    gains = cg_ref[...].astype(F32)
    rows = []
    for j in range(2):
        total = jnp.sum(cgain_ref[j], 0, keepdims=True) / gains[j : j + 1]
        rows += [total[:, 0:128], total[:, 128:256]]
    total = jnp.sum(cpool_ref[...], 0, keepdims=True)
    rows += [total[:, 0:128], total[:, 128:256]]
    for j in range(2):
        rows += [wgain_ref[j : j + 1, 128 * t : 128 * t + 128] for t in range(4)]
    rows.append(jnp.zeros((2, 128), F32))
    small[0] = jnp.concatenate(rows, 0)

    pl.semaphore_wait(barrier, len(peers) + len(z_peers))
    w_c = send(wbuf.at[1 - x], wr_c, 0, peers[2])
    c_a = send(cbuf.at[1 - core], cr_a, 1, peers[0])
    s_a = send(small.at[0], sr.at[0], 2, peers[0])
    s_a.wait()
    small[1] = small[0] + sr[0]
    s_b = send(small.at[1], sr.at[1], 3, peers[1])
    c_a.wait()
    mine = cbuf.at[core]
    for i in range(2):
        for j in range(2):
            add_into(mine.at[i, j], cr_a.at[i, j], n_z)
    c_b = send(mine.at[1 - y], cr_b, 4, peers[1])
    s_b.wait()
    small[2] = small[1] + sr[1]
    s_c = send(small.at[2], sr.at[2], 5, peers[2])
    w_c.wait()
    wmine = wbuf.at[x]
    add_into(wmine, wr_c, n_z)
    w_d = []
    for k in range(1, n_z):
        w_d.append(send(wmine.at[lax.rem(z + k, n_z)], wr_d.at[k - 1], 5 + k, z_peers[k - 1]))
    c_b.wait()
    mine2 = mine.at[y]
    for j in range(2):
        add_into(mine2.at[j], cr_b.at[j], n_z)
    c_c = send(mine2.at[1 - x], cr_c, 5 + n_z, peers[2])
    s_c.wait()
    small[3] = small[2] + sr[2]
    base = 5 + n_z
    s_d = [send(small.at[3], sr.at[2 + k], base + k, z_peers[k - 1]) for k in range(1, n_z)]
    c_c.wait()
    mine3 = mine2.at[x]
    add_into(mine3, cr_c, n_z)
    base = base + n_z - 1
    c_d = [send(mine3.at[lax.rem(z + k, n_z)], cr_d.at[k - 1], base + k, z_peers[k - 1]) for k in range(1, n_z)]
    for copy in w_d:
        copy.wait()
    word = wmine[z].astype(F32)
    for k in range(n_z - 1):
        word += wr_d[k].astype(F32)
    for t in range(3):
        owqkv_ref[t] = word[64 * t : 64 * t + 64]
    owout_ref[...] = word[192:256].T
    for t in range(4):
        owup_ref[:, 128 * t : 128 * t + 128] = word[256 + 64 * t : 320 + 64 * t]
        owdown_ref[128 * t : 128 * t + 128, :] = word[512 + 64 * t : 576 + 64 * t].T
    for copy in s_d:
        copy.wait()
    total = small[3]
    for k in range(n_z - 1):
        total += sr[3 + k]
    for j in range(2):
        for t in range(2):
            ocgain_ref[j : j + 1, 128 * t : 128 * t + 128] = total[2 * j + t : 2 * j + t + 1]
        for t in range(4):
            owgain_ref[j : j + 1, 128 * t : 128 * t + 128] = total[6 + 4 * j + t : 7 + 4 * j + t]
    for t in range(2):
        opool_ref[:, 128 * t : 128 * t + 128] = total[4 + t : 5 + t]
    for copy in c_d:
        copy.wait()
    char = mine3[z].astype(F32)
    for k in range(n_z - 1):
        char += cr_d[k].astype(F32)
    oqkv_ref[:, 0:128] = char[0:32]
    oqkv_ref[:, 128:192] = unfold_half(char[32:48])
    oout_ref[...] = unfold_half(char[48:64])
    oup_ref[:, 0:128] = char[64:96]
    oup_ref[:, 128:256] = char[96:128]
    odown_ref[...] = unfold_half(char[128:192])
    oproj_ref[...] = char[192:224]


def reduce_grads(n_dp, char_parts, char_gains, word_parts):
    n_z = n_dp // 2
    vm = pl.BlockSpec(memory_space=pltpu.VMEM)
    outs = [(32, 192), (32, 64), (32, 256), (128, 64), (32, 128), (3, 64, 128), (128, 64), (64, 512), (512, 64), (2, 256), (1, 256), (2, 512)]
    args = (*char_parts, char_gains, *word_parts)
    n_sem = 5 + n_z + 2 * (n_z - 1) + 1
    return pl.pallas_call(
        functools.partial(reduce_body, n_z),
        in_specs=[vm] * len(args),
        out_specs=[vm] * len(outs),
        out_shape=[jax.ShapeDtypeStruct(s, F32) for s in outs],
        scratch_shapes=[
            pltpu.VMEM((2, 2, 2, n_z, CHAR_ROWS, 128), BF16),
            pltpu.VMEM((2, 2, n_z, CHAR_ROWS, 128), BF16),
            pltpu.VMEM((2, n_z, CHAR_ROWS, 128), BF16),
            pltpu.VMEM((n_z, CHAR_ROWS, 128), BF16),
            pltpu.VMEM((n_z - 1, CHAR_ROWS, 128), BF16),
            pltpu.VMEM((2, n_z, WORD_ROWS, 128), BF16),
            pltpu.VMEM((n_z, WORD_ROWS, 128), BF16),
            pltpu.VMEM((n_z - 1, WORD_ROWS, 128), BF16),
            pltpu.VMEM((4, 16, 128), F32),
            pltpu.VMEM((2 + n_z, 16, 128), F32),
            pltpu.SemaphoreType.DMA((n_sem,)),
            pltpu.SemaphoreType.DMA((n_sem,)),
        ],
        compiler_params=pltpu.CompilerParams(collective_id=1, has_side_effects=True, vmem_limit_bytes=VMEM_LIMIT),
        name="reduce_gradients",
    )(*args)


HEADS = 8


def norm_rows(values, gain_vec):
    row_mean = jnp.mean(values, -1, keepdims=True)
    centered = values - row_mean
    variance = jnp.mean(centered * centered, -1, keepdims=True)
    return centered * lax.rsqrt(variance + EPSILON) * gain_vec


def flat_dot(left, right):
    return jnp.dot(left, right, preferred_element_type=jnp.float32)


def inner_dot(left, right):
    return lax.dot_general(
        left, right, (((0,), (0,)), ((), ())), preferred_element_type=jnp.float32
    )


def outer_dot(left, right):
    return lax.dot_general(
        left, right, (((1,), (1,)), ((), ())), preferred_element_type=jnp.float32
    )


def gather_rows(rows_in):
    return lax.all_gather(rows_in, "mp", axis=0, tiled=True)


def sum_rows(partial_rows):
    return lax.psum_scatter(partial_rows, "mp", scatter_dimension=0, tiled=True)


def attention_scores(q_block, keys_in, segments, seg_block, block_start, block_rows, scale_value):
    places = jnp.arange(segments.shape[0])
    rows_here = block_start + jnp.arange(block_rows)
    allowed = (places[None, :] <= rows_here[:, None]) & (segments[None, :] == seg_block[:, None])
    scores = (
        jnp.einsum("qhe,khe->hqk", q_block, keys_in, preferred_element_type=jnp.float32)
        * scale_value
    )
    return jnp.where(allowed[None], scores, NEGATIVE)


def word_attention(queries, keys_in, values_in, segments, block_rows):
    length = queries.shape[0]
    scale_value = queries.shape[-1] ** (-0.5)

    def one_block(block_start):
        q_block = lax.dynamic_slice_in_dim(queries, block_start, block_rows, 0)
        seg_block = lax.dynamic_slice_in_dim(segments, block_start, block_rows, 0)
        scores = attention_scores(
            q_block, keys_in, segments, seg_block, block_start, block_rows, scale_value
        )
        row_top = jnp.max(scores, -1, keepdims=True)
        raw_weights = jnp.exp(scores - row_top)
        row_total = jnp.sum(raw_weights, -1, keepdims=True)
        softmaxed = (raw_weights / row_total).astype(jnp.bfloat16)
        result = jnp.einsum(
            "hqk,khe->qhe", softmaxed, values_in, preferred_element_type=jnp.float32
        )
        return (result, (row_top + jnp.log(row_total))[..., 0])

    starts = jnp.arange(length // block_rows) * block_rows
    results, log_totals = lax.map(one_block, starts)
    return (results.reshape(length, queries.shape[1], queries.shape[2]), log_totals)


def word_attention_back(queries, keys_in, values_in, segments, log_totals, d_mixed, block_rows):
    length = queries.shape[0]
    scale_value = queries.shape[-1] ** (-0.5)

    def one_block(sums_carry, block_inputs):
        d_keys, d_values = sums_carry
        block_start, log_block = block_inputs
        q_block = lax.dynamic_slice_in_dim(queries, block_start, block_rows, 0)
        seg_block = lax.dynamic_slice_in_dim(segments, block_start, block_rows, 0)
        d_block = lax.dynamic_slice_in_dim(d_mixed, block_start, block_rows, 0)
        scores = attention_scores(
            q_block, keys_in, segments, seg_block, block_start, block_rows, scale_value
        )
        softmaxed = jnp.exp(scores - log_block[..., None])
        d_soft = jnp.einsum("qhe,khe->hqk", d_block, values_in, preferred_element_type=jnp.float32)
        row_delta = jnp.sum(softmaxed * d_soft, -1, keepdims=True)
        d_scores = (softmaxed * (d_soft - row_delta)).astype(jnp.bfloat16)
        d_query_block = (
            jnp.einsum("hqk,khe->qhe", d_scores, keys_in, preferred_element_type=jnp.float32)
            * scale_value
        )
        d_keys = (
            d_keys
            + jnp.einsum("hqk,qhe->khe", d_scores, q_block, preferred_element_type=jnp.float32)
            * scale_value
        )
        d_values = d_values + jnp.einsum(
            "hqk,qhe->khe",
            softmaxed.astype(jnp.bfloat16),
            d_block,
            preferred_element_type=jnp.float32,
        )
        return ((d_keys, d_values), d_query_block)

    starts = jnp.arange(length // block_rows) * block_rows
    empty = jnp.zeros(keys_in.shape, jnp.float32)
    (d_keys, d_values), d_queries = lax.scan(one_block, (empty, empty), (starts, log_totals))
    return (d_queries.reshape(queries.shape), d_keys, d_values)


def plain_reduce(char_parts, char_gains, word_parts):
    *char_mats, gain_rows, pool_rows = char_parts
    grad_word_qkv, grad_word_out, grad_word_up, grad_word_down, grad_word_gains = word_parts
    gain_sums = jnp.sum(gain_rows, 1) / char_gains.astype(F32)
    small = lax.psum((gain_sums, jnp.sum(pool_rows, 0), grad_word_gains), ("dp", "mp"))
    mats = []
    for grad in char_mats:
        part = lax.psum_scatter(grad, "dp", scatter_dimension=0, tiled=True)
        part = lax.psum_scatter(part.astype(BF16), "mp", scatter_dimension=1, tiled=True)
        mats.append(part.astype(F32))
    return (
        *mats,
        lax.psum_scatter(grad_word_qkv, "dp", scatter_dimension=1, tiled=True),
        lax.psum_scatter(grad_word_out, "dp", scatter_dimension=0, tiled=True).T,
        lax.psum_scatter(grad_word_up, "dp", scatter_dimension=0, tiled=True),
        lax.psum_scatter(grad_word_down, "dp", scatter_dimension=0, tiled=True).T,
        *small,
    )


def per_device(
    char_input,
    char_counts,
    word_source,
    segment_ids,
    cotangent,
    char_norm_gains,
    char_qkv,
    char_out,
    char_up,
    char_down,
    pool_vector,
    char_proj,
    word_norm_gains,
    word_qkv,
    word_out,
    word_up,
    word_down,
):
    words_here = char_counts.shape[0]
    char_width = char_proj.shape[0]
    model_width = word_out.shape[1]
    char_weights = (
        char_norm_gains, char_qkv, char_out, char_up, char_down, pool_vector.reshape(1, -1), char_proj
    )
    word_vec, *char_kept = char_forward(char_input, char_counts.reshape(-1, 1), *char_weights)
    groups = lax.axis_size("dp")
    capacity = (2 * words_here + groups - 1) // groups
    seq_length = words_here * lax.axis_size("mp")
    owner_index = word_source // seq_length
    row_in_owner = word_source % words_here
    owner_hits = (owner_index[:, None] == jnp.arange(groups)[None, :]).astype(jnp.int32)
    earlier_hits = jnp.cumsum(owner_hits, 0) - owner_hits
    slot_rank = jnp.sum(earlier_hits * owner_hits, 1)
    send_slot = owner_index * capacity + slot_rank
    send_vec = (
        jnp.zeros((groups * capacity, model_width), jnp.bfloat16)
        .at[send_slot]
        .set(word_vec.astype(jnp.bfloat16))
    )
    send_rows = (
        jnp.full((groups * capacity,), words_here, jnp.int32).at[send_slot].set(row_in_owner)
    )
    got_vec, got_rows = (
        lax.all_to_all(
            send_vec.reshape(groups, capacity, model_width),
            "dp",
            split_axis=0,
            concat_axis=0,
            tiled=True,
        ),
        lax.all_to_all(
            send_rows.reshape(groups, capacity), "dp", split_axis=0, concat_axis=0, tiled=True
        ),
    )
    got_rows = got_rows.reshape(groups * capacity)
    rows_low = (
        jnp.zeros((words_here, model_width), jnp.bfloat16)
        .at[got_rows]
        .set(got_vec.reshape(groups * capacity, model_width), mode="drop")
    )
    rows_in = rows_low.astype(jnp.float32)
    head_size = model_width // HEADS
    local_heads = word_qkv.shape[2] // head_size
    block_rows = min(512, seq_length)
    gain_first = word_norm_gains[0].astype(jnp.float32)
    gain_second = word_norm_gains[1].astype(jnp.float32)
    normed = norm_rows(rows_in, gain_first).astype(jnp.bfloat16)
    normed_all, segments_all = (
        lax.all_gather(normed, "mp", axis=0, tiled=True),
        lax.all_gather(segment_ids, "mp", axis=0, tiled=True),
    )
    projected = jnp.einsum(
        "ld,kde->kle", normed_all, word_qkv, preferred_element_type=jnp.float32
    ).astype(jnp.bfloat16)
    queries = projected[0].reshape(seq_length, local_heads, head_size)
    keys_in = projected[1].reshape(seq_length, local_heads, head_size)
    values_in = projected[2].reshape(seq_length, local_heads, head_size)
    attended, log_totals = word_attention(queries, keys_in, values_in, segments_all, block_rows)
    mixed_heads = attended.reshape(seq_length, local_heads * head_size).astype(jnp.bfloat16)
    middle = rows_in + sum_rows(flat_dot(mixed_heads, word_out))
    normed_two = norm_rows(middle, gain_second).astype(jnp.bfloat16)
    normed_two_all = gather_rows(normed_two)
    hidden = flat_dot(normed_two_all, word_up)
    activated = jax.nn.gelu(hidden).astype(jnp.bfloat16)
    output = middle + sum_rows(flat_dot(activated, word_down))
    d_output = cotangent.astype(jnp.float32)
    d_branch_all = gather_rows(cotangent)
    grad_word_down = inner_dot(d_branch_all, activated)
    d_activated = outer_dot(d_branch_all, word_down)
    unused_gelu, gelu_back = jax.vjp(jax.nn.gelu, hidden)
    d_hidden = gelu_back(d_activated)[0].astype(jnp.bfloat16)
    grad_word_up = inner_dot(normed_two_all, d_hidden)
    d_normed_two = sum_rows(outer_dot(d_hidden, word_up))
    unused_second, norm_back_second = jax.vjp(norm_rows, middle, gain_second)
    d_middle_norm, grad_gain_second = norm_back_second(d_normed_two)
    d_middle = d_output + d_middle_norm
    d_attended_all = gather_rows(d_middle.astype(jnp.bfloat16))
    grad_word_out = inner_dot(d_attended_all, mixed_heads)
    d_mixed = (
        outer_dot(d_attended_all, word_out)
        .astype(jnp.bfloat16)
        .reshape(seq_length, local_heads, head_size)
    )
    d_queries, d_keys, d_values = word_attention_back(
        queries, keys_in, values_in, segments_all, log_totals, d_mixed, block_rows
    )
    d_projected = (
        jnp.stack([d_queries, d_keys, d_values], 0)
        .reshape(3, seq_length, local_heads * head_size)
        .astype(jnp.bfloat16)
    )
    grad_word_qkv = jnp.einsum(
        "ld,kle->kde", normed_all, d_projected, preferred_element_type=jnp.float32
    )
    d_normed = sum_rows(
        jnp.einsum("kle,kde->ld", d_projected, word_qkv, preferred_element_type=jnp.float32)
    )
    unused_first, norm_back_first = jax.vjp(norm_rows, rows_in, gain_first)
    d_rows_norm, grad_gain_first = norm_back_first(d_normed)
    d_rows = (d_middle + d_rows_norm).astype(jnp.bfloat16)
    back_rows = jnp.take(d_rows, got_rows, axis=0, mode="fill", fill_value=0)
    returned = lax.all_to_all(
        back_rows.reshape(groups, capacity, model_width),
        "dp",
        split_axis=0,
        concat_axis=0,
        tiled=True,
    )
    d_word = returned.reshape(groups * capacity, model_width)[send_slot]
    d_chars, *char_parts = char_backward(d_word, char_kept, *char_weights)
    grad_word_gains = jnp.stack([grad_gain_first, grad_gain_second], 0)
    word_parts = (grad_word_qkv, grad_word_out, grad_word_up, grad_word_down, grad_word_gains)
    if groups == 8:
        reduced = reduce_grads(groups, char_parts, char_norm_gains, word_parts)
    else:
        reduced = plain_reduce(char_parts, char_norm_gains, word_parts)
    (
        grad_qkv, grad_out, grad_up, grad_down, grad_proj,
        grad_word_qkv, grad_word_out, grad_word_up, grad_word_down,
        grad_char_gains, grad_pool, grad_word_gains,
    ) = reduced
    return (
        output.astype(jnp.bfloat16),
        d_chars,
        grad_qkv,
        grad_out,
        grad_up,
        grad_down,
        grad_proj,
        grad_word_qkv,
        grad_word_out,
        grad_word_up,
        grad_word_down,
        grad_char_gains,
        grad_pool.reshape(-1),
        grad_word_gains,
    )


def solution(mesh):
    placed = (
        P(("dp", "mp"), None),
        P(("dp", "mp")),
        P(("dp", "mp")),
        P(("dp", "mp")),
        P(("dp", "mp"), None),
        P(),
        P(),
        P(),
        P(),
        P(),
        P(),
        P(),
        P(),
        P(None, None, "mp"),
        P("mp", None),
        P(None, "mp"),
        P("mp", None),
    )
    return jax.shard_map(
        per_device,
        mesh=mesh,
        in_specs=placed,
        out_specs=(
            P(("dp", "mp"), None),
            P(("dp", "mp"), None),
            P("dp", "mp"),
            P("dp", "mp"),
            P("dp", "mp"),
            P("dp", "mp"),
            P("dp", "mp"),
            P(None, "dp", "mp"),
            P("mp", "dp"),
            P("dp", "mp"),
            P("mp", "dp"),
            P(),
            P(),
            P(),
        ),
        check_vma=False,
    )
```

```python
import functools
import jax
import jax.numpy as jnp
from jax import lax
from jax.experimental import pallas as pl
from jax.experimental.pallas import tpu as pltpu
from jax.sharding import PartitionSpec as P

HEADS = 8
CHARS = 16
CHAR_HEADS = 4
EPSILON = 1e-05
NEGATIVE = -1e30
GELU_A = 0.7978845608028654
GELU_B = 0.044715
F32 = jnp.float32
BF16 = jnp.bfloat16
VMEM_LIMIT = 60 * 1024 * 1024


def dot_nn(left, right):
    return jnp.dot(left, right, preferred_element_type=F32)


def dot_nt(left, right):
    return lax.dot_general(left, right, (((1,), (1,)), ((), ())), preferred_element_type=F32)


def dot_tn(left, right):
    return lax.dot_general(left, right, (((0,), (0,)), ((), ())), preferred_element_type=F32)


def head_stack(values, heads, factor):
    width = values.shape[1] // heads
    lane = lax.broadcasted_iota(jnp.int32, (1, values.shape[1]), 1) // width
    return jnp.concatenate(
        [values * jnp.where(lane == h, factor, 0.0).astype(values.dtype) for h in range(heads)], 0
    )


def gelu_both(hidden):
    square = hidden * hidden
    inner = hidden * (GELU_A + (GELU_A * GELU_B) * square)
    tanh = jnp.tanh(inner)
    half = 0.5 + 0.5 * tanh
    slope = half + (0.5 * hidden) * (1.0 - tanh * tanh) * (GELU_A + (3.0 * GELU_A * GELU_B) * square)
    return hidden * half, slope


def char_fwd_body(
    x_ref, cnt_ref, gains_ref, wqkv_ref, wout_ref, wup_ref, wdown_ref, pool_ref, wproj_ref,
    e_ref, n1_ref, p_ref, a_ref, o_ref, n2_ref, rs1_ref, rs2_ref, act_ref, dg_ref, f_ref, aw_ref, pooled_ref,
):
    words, wide = x_ref.shape
    width = wide // CHARS
    blocks = words // 8
    gains = gains_ref[...].astype(F32)
    pieces = []
    for g in range(words // 16):
        xt = x_ref[16 * g : 16 * g + 16, :].astype(F32)
        for half in range(2):
            for c in range(CHARS):
                pieces.append(xt[8 * half : 8 * half + 8, width * c : width * c + width])
    x = jnp.concatenate(pieces, 0)

    def norm(v, gain):
        mean = jnp.mean(v, -1, keepdims=True)
        centered = v - mean
        rstd = lax.rsqrt(jnp.mean(centered * centered, -1, keepdims=True) + EPSILON)
        return (centered * rstd * gain).astype(BF16), rstd

    n1, rs1 = norm(x, gains[0:1])
    n1_ref[...] = n1
    rs1_ref[...] = rs1
    p_ref[...] = dot_nn(n1, wqkv_ref[...]).astype(BF16)
    row_w = lax.broadcasted_iota(jnp.int32, (8, 128), 0)
    lane_w = lax.broadcasted_iota(jnp.int32, (8, 128), 1) % 8
    same = row_w == lane_w
    slot = lax.broadcasted_iota(jnp.int32, (CHARS, 8, 128), 0)
    for b in range(blocks):
        rows = slice(128 * b, 128 * b + 128)
        counts = jnp.broadcast_to(cnt_ref[8 * b : 8 * b + 8, :], (8, 128))
        here = slot < counts[None]
        q = p_ref[rows, 0:width]
        k = p_ref[rows, width : 2 * width]
        v = p_ref[rows, 2 * width : 3 * width]
        st = dot_nt(head_stack(k, CHAR_HEADS, (width // CHAR_HEADS) ** -0.5), q)
        st = st.reshape(CHAR_HEADS, CHARS, 8, 128)
        st = jnp.where(here[None], st, NEGATIVE)
        e = jnp.exp(st - jnp.max(st, 1, keepdims=True))
        r = jnp.where(same[None, None], 1.0 / jnp.sum(e, 1, keepdims=True), 0.0)
        a = (e * r).reshape(CHAR_HEADS * 128, 128).astype(BF16)
        a_ref[CHAR_HEADS * 128 * b : CHAR_HEADS * 128 * (b + 1), :] = a
        o_ref[rows, :] = dot_tn(a, head_stack(v, CHAR_HEADS, 1.0)).astype(BF16)
    m = x + dot_nn(o_ref[...], wout_ref[...])
    n2, rs2 = norm(m, gains[1:2])
    n2_ref[...] = n2
    rs2_ref[...] = rs2
    act, slope = gelu_both(dot_nn(n2, wup_ref[...]))
    act = act.astype(BF16)
    act_ref[...] = act
    dg_ref[...] = slope.astype(BF16)
    f = m + dot_nn(act, wdown_ref[...])
    f_ref[...] = f.astype(BF16)
    t = jnp.sum(f * pool_ref[...].astype(F32), -1, keepdims=True).reshape(blocks, CHARS, 8, 1)
    counts = cnt_ref[...].reshape(blocks, 1, 8, 1)
    t = jnp.where(lax.broadcasted_iota(jnp.int32, t.shape, 1) < counts, t, NEGATIVE)
    et = jnp.exp(t - jnp.max(t, 1, keepdims=True))
    aw = et / jnp.sum(et, 1, keepdims=True)
    aw_ref[...] = aw.reshape(words * CHARS, 1)
    pooled = jnp.sum(aw * f.reshape(blocks, CHARS, 8, width), 1).reshape(words, width).astype(BF16)
    pooled_ref[...] = pooled
    e_ref[...] = dot_nn(pooled, wproj_ref[...]).astype(BF16)


def char_forward(x, counts, gains, wqkv, wout, wup, wdown, pool, wproj, step_words=32):
    words, wide = x.shape
    width = wide // CHARS
    rows = words * CHARS
    step_rows = step_words * CHARS
    full = lambda arr: pl.BlockSpec(arr.shape, lambda i: (0,) * arr.ndim)
    blk = lambda n, w: pl.BlockSpec((n, w), lambda i: (i, 0))
    hid = wup.shape[1]
    dw = wproj.shape[1]
    outs = [
        (words, step_words, dw, BF16), (rows, step_rows, width, BF16), (rows, step_rows, 3 * width, BF16),
        (rows * CHAR_HEADS, step_rows * CHAR_HEADS, 128, BF16), (rows, step_rows, width, BF16),
        (rows, step_rows, width, BF16), (rows, step_rows, 1, F32), (rows, step_rows, 1, F32),
        (rows, step_rows, hid, BF16), (rows, step_rows, hid, BF16), (rows, step_rows, width, BF16),
        (rows, step_rows, 1, F32), (words, step_words, width, BF16),
    ]
    return pl.pallas_call(
        char_fwd_body,
        grid=(words // step_words,),
        in_specs=[blk(step_words, wide), blk(step_words, 1)] + [full(w) for w in (gains, wqkv, wout, wup, wdown, pool, wproj)],
        out_specs=[blk(b, w) for _, b, w, _ in outs],
        out_shape=[jax.ShapeDtypeStruct((n, w), d) for n, _, w, d in outs],
        compiler_params=pltpu.CompilerParams(vmem_limit_bytes=VMEM_LIMIT),
        name="char_forward",
    )(x, counts, gains, wqkv, wout, wup, wdown, pool, wproj)


def char_bwd_body(
    de_ref, gains_ref, wqkv_ref, wout_ref, wup_ref, wdown_ref, pool_ref, wproj_ref,
    n1_ref, p_ref, a_ref, o_ref, n2_ref, rs1_ref, rs2_ref, act_ref, dg_ref, f_ref, aw_ref, pooled_ref,
    dx_ref, gqkv_ref, gout_ref, gup_ref, gdown_ref, gproj_ref, ggain_ref, gpool_ref,
    dp_ref, do_ref,
):
    words = de_ref.shape[0]
    width = n1_ref.shape[1]
    blocks = words // 8
    rows = words * CHARS
    gains = gains_ref[...].astype(F32)

    @pl.when(pl.program_id(0) == 0)
    def _():
        for ref in (gqkv_ref, gout_ref, gup_ref, gdown_ref, gproj_ref, ggain_ref, gpool_ref):
            ref[...] = jnp.zeros_like(ref)

    de = de_ref[...]
    gproj_ref[...] += dot_tn(pooled_ref[...], de)
    dpool = dot_nt(de, wproj_ref[...]).reshape(blocks, 1, 8, width)
    f = f_ref[...].astype(F32).reshape(blocks, CHARS, 8, width)
    aw = aw_ref[...].reshape(blocks, CHARS, 8, 1)
    g = jnp.sum(f * dpool, -1, keepdims=True)
    dt = aw * (g - jnp.sum(aw * g, 1, keepdims=True))
    gpool_ref[...] += jnp.sum((dt * f).reshape(rows // 8, 8, width), 0)
    df = (aw * dpool + dt * pool_ref[...].astype(F32)).reshape(rows, width)
    dfb = df.astype(BF16)
    gdown_ref[...] += dot_tn(act_ref[...], dfb)
    dh = (dg_ref[...].astype(F32) * dot_nt(dfb, wdown_ref[...])).astype(BF16)
    n2 = n2_ref[...]
    gup_ref[...] += dot_tn(n2, dh)
    dn2 = dot_nt(dh, wup_ref[...])

    def norm_back(dn, n, rstd, gain, row):
        d1 = dn * gain
        dnn = dn * n.astype(F32)
        ggain_ref[row] += jnp.sum(dnn.reshape(rows // 8, 8, width), 0)
        m1 = jnp.mean(d1, -1, keepdims=True)
        m2 = jnp.mean(dnn, -1, keepdims=True)
        return rstd * (d1 - m1 - n.astype(F32) * (1.0 / gain) * m2)

    dm = df + norm_back(dn2, n2, rs2_ref[...], gains[1:2], 1)
    dmb = dm.astype(BF16)
    gout_ref[...] += dot_tn(o_ref[...], dmb)
    do_ref[...] = dot_nt(dmb, wout_ref[...]).astype(BF16)
    scale = (width // CHAR_HEADS) ** -0.5
    for b in range(blocks):
        sl = slice(128 * b, 128 * b + 128)
        q = p_ref[sl, 0:width]
        k = p_ref[sl, width : 2 * width]
        v = p_ref[sl, 2 * width : 3 * width]
        do = do_ref[sl, :]
        ab = a_ref[CHAR_HEADS * 128 * b : CHAR_HEADS * 128 * (b + 1), :]
        a = ab.astype(F32).reshape(CHAR_HEADS, CHARS, 8, 128)
        dpt = dot_nt(head_stack(v, CHAR_HEADS, 1.0), do).reshape(CHAR_HEADS, CHARS, 8, 128)
        delta = jnp.sum(a * dpt, 1, keepdims=True)
        ds = (a * (dpt - delta)).reshape(CHAR_HEADS * 128, 128).astype(BF16)
        wide_ds = jnp.concatenate([ds[128 * h : 128 * h + 128] for h in range(CHAR_HEADS)], 1)
        wide_a = jnp.concatenate([ab[128 * h : 128 * h + 128] for h in range(CHAR_HEADS)], 1)
        dp_ref[sl, 0:width] = dot_tn(ds, head_stack(k, CHAR_HEADS, scale)).astype(BF16)
        dp_ref[sl, width : 2 * width] = dot_nn(wide_ds, head_stack(q, CHAR_HEADS, scale)).astype(BF16)
        dp_ref[sl, 2 * width : 3 * width] = dot_nn(wide_a, head_stack(do, CHAR_HEADS, 1.0)).astype(BF16)
    n1 = n1_ref[...]
    dp = dp_ref[...]
    gqkv_ref[...] += dot_tn(n1, dp)
    dn1 = dot_nt(dp, wqkv_ref[...])
    dx = dm + norm_back(dn1, n1, rs1_ref[...], gains[0:1], 0)
    for b in range(blocks):
        for c in range(CHARS):
            dx_ref[8 * b : 8 * b + 8, width * c : width * c + width] = dx[128 * b + 8 * c : 128 * b + 8 * c + 8]


def char_backward(de, kept, gains, wqkv, wout, wup, wdown, pool, wproj, step_words=32):
    words = de.shape[0]
    width = wout.shape[0]
    rows = words * CHARS
    step_rows = step_words * CHARS
    full = lambda arr: pl.BlockSpec(arr.shape, lambda i: (0,) * arr.ndim)
    blk = lambda n, w: pl.BlockSpec((n, w), lambda i: (i, 0))
    steps = words // step_words
    weights = (gains, wqkv, wout, wup, wdown, pool, wproj)
    outs = [wqkv.shape, wout.shape, wup.shape, wdown.shape, wproj.shape, (2, 8, width), (8, width)]
    return pl.pallas_call(
        char_bwd_body,
        grid=(steps,),
        in_specs=[blk(step_words, de.shape[1])] + [full(w) for w in weights]
        + [blk(r.shape[0] // steps, r.shape[1]) for r in kept],
        out_specs=[blk(step_words, CHARS * width)]
        + [pl.BlockSpec(s, lambda i, n=len(s): (0,) * n) for s in outs],
        out_shape=[jax.ShapeDtypeStruct((words, CHARS * width), F32)]
        + [jax.ShapeDtypeStruct(s, F32) for s in outs],
        scratch_shapes=[pltpu.VMEM((step_rows, 3 * width), BF16), pltpu.VMEM((step_rows, width), BF16)],
        compiler_params=pltpu.CompilerParams(vmem_limit_bytes=VMEM_LIMIT),
        name="char_backward",
    )(de, *weights, *kept)


MESH = pl.DeviceIdType.MESH
CHAR_ROWS = 224
WORD_ROWS = 768
SEMS = 8


def fold_half(block):
    half = block.shape[0] // 2
    return jnp.concatenate([block[:half], block[half:]], 1)


def unfold_half(block):
    return jnp.concatenate([block[:, :64], block[:, 64:]], 0)


def coordinates():
    dp, mp = lax.axis_index("dp"), lax.axis_index("mp")
    return dp // 2, dp % 2, mp // 2, mp % 2


def device_of(z, x, y, core):
    return (z * 2 + x, y * 2 + core)


def remote_copy(src, dst, ssem, rsem, slot, peer):
    return pltpu.make_async_remote_copy(
        src_ref=src, dst_ref=dst, send_sem=ssem.at[slot], recv_sem=rsem.at[slot],
        device_id=peer, device_id_type=MESH,
    )


class Halving:
    def __init__(self, n_z, work, got, ssem, rsem, base, order):
        self.n_z, self.work, self.got = n_z, work, got
        self.ssem, self.rsem, self.base, self.order = ssem, rsem, base, order
        self.z, self.x, self.y, self.core = coordinates()

    def copies(self, phase):
        z, x, y, core = self.z, self.x, self.y, self.core
        work = self.work
        slot = self.base + phase
        step = "c" if phase == 0 else self.order[phase - 1]
        if step == "c":
            pairs = [(work.at[1 - core], self.got[0], device_of(z, x, y, 1 - core))]
        elif step == "y":
            src = work.at[core, 1 - y] if phase == 1 else work.at[core, 1 - y, x]
            pairs = [(src, self.got[phase], device_of(z, x, 1 - y, core))]
        elif step == "x":
            src = work.at[core, :, 1 - x] if phase == 1 else work.at[core, y, 1 - x]
            pairs = [(src, self.got[phase], device_of(z, 1 - x, y, core))]
        else:
            pairs = []
            for k in range(1, self.n_z):
                other = lax.rem(z + k, self.n_z)
                pairs.append((work.at[core, y, x, other], self.got[3].at[k - 1], device_of(other, x, y, core)))
        return [remote_copy(s, d, self.ssem, self.rsem, slot + i, peer) for i, (s, d, peer) in enumerate(pairs)]

    def start(self, phase):
        for copy in self.copies(phase):
            copy.start()

    def finish(self, phase):
        for copy in self.copies(phase):
            copy.wait()
        x, y, core = self.x, self.y, self.core
        work, got, n_z = self.work, self.got[phase], self.n_z
        step = "c" if phase == 0 else self.order[phase - 1]

        def add(mine, other):
            def body(i, carry):
                mine[i] = (mine[i].astype(F32) + other[i].astype(F32)).astype(BF16)
                return carry
            lax.fori_loop(0, n_z, body, 0)

        if step == "c":
            for i in range(2):
                for j in range(2):
                    add(work.at[core, i, j], got.at[i, j])
        elif step == "y" and phase == 1:
            for j in range(2):
                add(work.at[core, y, j], got.at[j])
        elif step == "x" and phase == 1:
            for i in range(2):
                add(work.at[core, i, x], got.at[i])
        elif step in "yx":
            add(work.at[core, y, x], got)

    def total(self):
        value = self.work[self.core, self.y, self.x, self.z].astype(F32)
        for k in range(self.n_z - 1):
            value += self.got[3][k].astype(F32)
        return value

    @staticmethod
    def got_shapes(n_z, rows):
        return [
            pltpu.VMEM((2, 2, n_z, rows, 128), BF16), pltpu.VMEM((2, n_z, rows, 128), BF16),
            pltpu.VMEM((n_z, rows, 128), BF16), pltpu.VMEM((n_z - 1, rows, 128), BF16),
        ]


def pack_char(n_z, cqkv_ref, cout_ref, cup_ref, cdown_ref, cproj_ref, cbuf):
    for d in range(2 * n_z):
        qkv = cqkv_ref[32 * d : 32 * d + 32, :]
        out = cout_ref[32 * d : 32 * d + 32, :]
        down = cdown_ref[128 * d : 128 * d + 128, :]
        for p in range(4):
            block = cbuf.at[p % 2, p // 2, d % 2, d // 2]
            part = qkv[:, 192 * p : 192 * p + 192]
            block[0:32, :] = part[:, 0:128].astype(BF16)
            block[32:48, :] = fold_half(part[:, 128:192]).astype(BF16)
            block[48:64, :] = fold_half(out[:, 64 * p : 64 * p + 64]).astype(BF16)
            block[64:96, :] = cup_ref[32 * d : 32 * d + 32, 256 * p : 256 * p + 128].astype(BF16)
            block[96:128, :] = cup_ref[32 * d : 32 * d + 32, 256 * p + 128 : 256 * p + 256].astype(BF16)
            block[128:192, :] = fold_half(down[:, 64 * p : 64 * p + 64]).astype(BF16)
            block[192:224, :] = cproj_ref[32 * d : 32 * d + 32, 128 * p : 128 * p + 128].astype(BF16)


def pack_small(cgain_ref, cpool_ref, cg_ref, wgain_ref):
    gains = cg_ref[...].astype(F32)
    rows = []
    for j in range(2):
        total = jnp.sum(cgain_ref[j], 0, keepdims=True) / gains[j : j + 1]
        rows += [total[:, 0:128], total[:, 128:256]]
    total = jnp.sum(cpool_ref[...], 0, keepdims=True)
    rows += [total[:, 0:128], total[:, 128:256]]
    for j in range(2):
        rows += [wgain_ref[j : j + 1, 128 * t : 128 * t + 128] for t in range(4)]
    rows.append(jnp.zeros((2, 128), F32))
    return jnp.concatenate(rows, 0)


def reduce_body(
    n_z,
    cqkv_ref, cout_ref, cup_ref, cdown_ref, cproj_ref, cgain_ref, cpool_ref, cg_ref, wbuf_in, wgain_ref,
    char_ref, word_ref, small_ref,
    cbuf, *refs,
):
    c_got, wa_got, wb_got = refs[0:4], refs[4:8], refs[8:12]
    wbuf, small, sgot, ssem, rsem, lsem = refs[12:]
    z, x, y, core = coordinates()
    peers = [device_of(z, x, y, 1 - core), device_of(z, x, 1 - y, core), device_of(z, 1 - x, y, core)]
    z_peers = [device_of(lax.rem(z + k, n_z), x, y, core) for k in range(1, n_z)]
    barrier = pltpu.get_barrier_semaphore()
    for peer in peers + z_peers:
        pl.semaphore_signal(barrier, inc=1, device_id=peer, device_id_type=MESH)
    load = pltpu.make_async_copy(wbuf_in, wbuf, lsem)
    load.start()
    half = WORD_ROWS // 2
    first = Halving(n_z, wbuf.at[:, :, :, :, 0:half], wa_got, ssem, rsem, 0, "yxz")
    second = Halving(n_z, wbuf.at[:, :, :, :, half:], wb_got, ssem, rsem, SEMS, "xyz")
    chars = Halving(n_z, cbuf, c_got, ssem, rsem, 2 * SEMS, "yxz")
    tiny = 3 * SEMS
    load.wait()
    pl.semaphore_wait(barrier, len(peers) + len(z_peers))
    first.start(0)
    second.start(0)
    pack_char(n_z, cqkv_ref, cout_ref, cup_ref, cdown_ref, cproj_ref, cbuf)
    small[0] = pack_small(cgain_ref, cpool_ref, cg_ref, wgain_ref)
    chars.start(0)
    for i in range(3):
        copy = remote_copy(small.at[i], sgot.at[i], ssem, rsem, tiny + i, peers[i])
        copy.start()
        for part in (first, second, chars):
            part.finish(i)
            part.start(i + 1)
        copy.wait()
        small[i + 1] = small[i] + sgot[i]
    tail = [remote_copy(small.at[3], sgot.at[2 + k], ssem, rsem, tiny + 2 + k, z_peers[k - 1]) for k in range(1, n_z)]
    for copy in tail:
        copy.start()
    for copy in tail:
        copy.wait()
    total = small[3]
    for k in range(1, n_z):
        total += sgot[2 + k]
    small_ref[...] = total
    first.finish(3)
    word_ref[0:half, :] = first.total()
    second.finish(3)
    word_ref[half:, :] = second.total()
    chars.finish(3)
    char_ref[...] = chars.total()


def reduce_grads(n_dp, char_parts, char_gains, wbuf, wgain):
    n_z = n_dp // 2
    vm = pl.BlockSpec(memory_space=pltpu.VMEM)
    args = (*char_parts, char_gains, wbuf, wgain)
    specs = [vm] * len(args)
    specs[-2] = pl.BlockSpec(memory_space=pl.ANY)
    outs = [(CHAR_ROWS, 128), (WORD_ROWS, 128), (16, 128)]
    return pl.pallas_call(
        functools.partial(reduce_body, n_z),
        in_specs=specs,
        out_specs=[vm] * len(outs),
        out_shape=[jax.ShapeDtypeStruct(s, F32) for s in outs],
        scratch_shapes=[pltpu.VMEM((2, 2, 2, n_z, CHAR_ROWS, 128), BF16)]
        + Halving.got_shapes(n_z, CHAR_ROWS)
        + Halving.got_shapes(n_z, WORD_ROWS // 2) * 2
        + [
            pltpu.VMEM((2, 2, 2, n_z, WORD_ROWS, 128), BF16),
            pltpu.VMEM((4, 16, 128), F32),
            pltpu.VMEM((2 + n_z, 16, 128), F32),
            pltpu.SemaphoreType.DMA((4 * SEMS,)),
            pltpu.SemaphoreType.DMA((4 * SEMS,)),
            pltpu.SemaphoreType.DMA,
        ],
        compiler_params=pltpu.CompilerParams(collective_id=1, has_side_effects=True, vmem_limit_bytes=VMEM_LIMIT),
        name="reduce_gradients",
    )(*args)


def unpack_body(
    char_ref, word_ref, small_ref,
    oqkv_ref, oout_ref, oup_ref, odown_ref, oproj_ref, owqkv_ref, owout_ref, owup_ref, owdown_ref,
    ocgain_ref, opool_ref, owgain_ref,
):
    char, word, total = char_ref[...], word_ref[...], small_ref[...]
    oqkv_ref[:, 0:128] = char[0:32]
    oqkv_ref[:, 128:192] = unfold_half(char[32:48])
    oout_ref[...] = unfold_half(char[48:64])
    oup_ref[:, 0:128] = char[64:96]
    oup_ref[:, 128:256] = char[96:128]
    odown_ref[...] = unfold_half(char[128:192])
    oproj_ref[...] = char[192:224]
    for t in range(3):
        owqkv_ref[t] = word[64 * t : 64 * t + 64]
    owout_ref[...] = word[192:256].T
    for t in range(4):
        owup_ref[:, 128 * t : 128 * t + 128] = word[256 + 64 * t : 320 + 64 * t]
        owdown_ref[128 * t : 128 * t + 128, :] = word[512 + 64 * t : 576 + 64 * t].T
    for j in range(2):
        for t in range(2):
            ocgain_ref[j : j + 1, 128 * t : 128 * t + 128] = total[2 * j + t : 2 * j + t + 1]
        for t in range(4):
            owgain_ref[j : j + 1, 128 * t : 128 * t + 128] = total[6 + 4 * j + t : 7 + 4 * j + t]
    for t in range(2):
        opool_ref[:, 128 * t : 128 * t + 128] = total[4 + t : 5 + t]


def unpack_grads(char, word, small):
    vm = pl.BlockSpec(memory_space=pltpu.VMEM)
    outs = [(32, 192), (32, 64), (32, 256), (128, 64), (32, 128), (3, 64, 128), (128, 64), (64, 512), (512, 64), (2, 256), (1, 256), (2, 512)]
    return pl.pallas_call(
        unpack_body,
        in_specs=[vm] * 3,
        out_specs=[vm] * len(outs),
        out_shape=[jax.ShapeDtypeStruct(s, F32) for s in outs],
        name="unpack_gradients",
    )(char, word, small)


def norm_fwd(values, gain):
    mean = jnp.mean(values, -1, keepdims=True)
    centered = values - mean
    rstd = lax.rsqrt(jnp.mean(centered * centered, -1, keepdims=True) + EPSILON)
    return (centered * rstd * gain).astype(BF16), rstd


def norm_bwd(dn, n, rstd, gain):
    n = n.astype(F32)
    d1 = dn * gain
    dnn = dn * n
    m1 = jnp.mean(d1, -1, keepdims=True)
    m2 = jnp.mean(dnn, -1, keepdims=True)
    return rstd * (d1 - m1 - n * (1.0 / gain) * m2), jnp.sum(dnn, 0, keepdims=True) / gain


def as_column(row):
    return jnp.transpose(jnp.broadcast_to(row.astype(F32), (128, row.shape[1])))


def word_body(
    n_dp, cap, packed,
    e_ref, src_ref, seg_ref, cot_ref, gains_ref, wqkv_ref, wout_ref, wup_ref, wdown_ref,
    *refs,
):
    if packed:
        out_ref, de_ref, gbuf_ref, ggain_ref, *refs = refs
    else:
        out_ref, de_ref, gqkv_ref, gout_ref, gup_ref, gdown_ref, ggain_ref, *refs = refs
    (
        onehot, place, vec_send, vec_got, row_send, row_got, seg_all, segc_all, rows_ref, normed, rstd_a,
        qkv_send, qkv_all, weights, o_send, o_all, act_ref, dh_ref, dact_ref, dm_ref,
        do_send, do_all, dk_acc, dv_acc, dqkv_send, dqkv_all, back_send, ret,
        ssem, rsem,
    ) = refs
    dp, mp = lax.axis_index("dp"), lax.axis_index("mp")
    n_mp = 4
    words, width = e_ref.shape
    slots = n_dp * cap
    pair = 2 * (width // HEADS)
    scale = (width // HEADS) ** -0.5
    to_dp = [(lax.rem(dp + k, n_dp), mp) for k in range(n_dp)]
    from_dp = [(lax.rem(dp + n_dp - k, n_dp), mp) for k in range(n_dp)]
    mates = [(mp // 2 * 2 + (mp + 1) % 2), (mp + 2) % 4, ((mp // 2 * 2 + 2) % 4 + (mp + 1) % 2)]
    barrier = pltpu.get_barrier_semaphore()
    for k in range(1, n_dp):
        pl.semaphore_signal(barrier, inc=1, device_id=to_dp[k], device_id_type=MESH)
    for mate in mates:
        pl.semaphore_signal(barrier, inc=1, device_id=(dp, mate), device_id_type=MESH)
    next_slot = [0]

    def send(src, dst, peer):
        slot = next_slot[0]
        next_slot[0] += 1
        copy = pltpu.make_async_remote_copy(
            src_ref=src, dst_ref=dst, send_sem=ssem.at[slot], recv_sem=rsem.at[slot],
            device_id=peer, device_id_type=MESH,
        )
        copy.start()
        return copy

    source = src_ref[...]
    owner = source // (words * n_mp)
    owner_c = as_column(owner)[:, 0:1]
    index_r = lax.broadcasted_iota(jnp.int32, (words, words), 0)
    index_c = lax.broadcasted_iota(jnp.int32, (words, words), 1)
    earlier = (owner_c == owner.astype(F32)) & (index_r < index_c)
    rank = jnp.sum(jnp.where(earlier, 1.0, 0.0), 0, keepdims=True).astype(jnp.int32)
    slot_of = lax.rem(owner - dp + n_dp, n_dp) * cap + rank
    onehot[...] = jnp.where(lax.broadcasted_iota(jnp.int32, (slots, words), 0) == slot_of, 1.0, 0.0).astype(BF16)
    row_mat = as_column(lax.rem(source, words) + 1).astype(BF16)
    row_send[...] = dot_nn(onehot[...], row_mat).astype(BF16).reshape(n_dp, cap, 128)
    seg_all[mp] = jnp.broadcast_to(seg_ref[...], (8, words))
    vec_send[...] = dot_nn(onehot[...], e_ref[...]).astype(BF16).reshape(n_dp, cap, width)

    pl.semaphore_wait(barrier, n_dp - 1 + 3)
    row_copies = [send(row_send.at[k], row_got.at[k], to_dp[k]) for k in range(1, n_dp)]
    vec_copies = [send(vec_send.at[k], vec_got.at[k], to_dp[k]) for k in range(1, n_dp)]
    seg_copies = [send(seg_all.at[mp], seg_all.at[mp], (dp, mate)) for mate in mates]
    row_got[0] = row_send[0]
    vec_got[0] = vec_send[0]
    gains = gains_ref[...].astype(F32)
    cot = cot_ref[...]
    for p in range(n_mp):
        dact_ref[p] = dot_nt(cot, wdown_ref[p])
    for copy in seg_copies:
        copy.wait()
    for j in range(n_mp):
        segc_all[words * j : words * j + words, :] = as_column(seg_all[j, 0:1, :])
    for copy in row_copies:
        copy.wait()
    at_row = row_got[...].reshape(slots, 128)[:, 0:1].astype(F32) - 1.0
    lanes = lax.broadcasted_iota(jnp.int32, (slots, words), 1).astype(F32)
    place[...] = jnp.where(lanes == at_row, 1.0, 0.0).astype(BF16)
    for copy in vec_copies:
        copy.wait()
    rows = dot_tn(place[...], vec_got[...].reshape(slots, width))
    rows_ref[...] = rows
    n_w, rstd = norm_fwd(rows, gains[0:1])
    normed[0] = n_w
    rstd_a[0] = rstd
    qkv_copies = []
    for mate in reversed(mates):
        qkv_send[mate] = dot_nn(n_w, wqkv_ref[mate]).astype(BF16)
        qkv_copies.append(send(qkv_send.at[mate], qkv_all.at[mp], (dp, mate)))
    qkv_all[mp] = dot_nn(n_w, wqkv_ref[mp]).astype(BF16)
    for copy in qkv_copies:
        copy.wait()

    head_lane = lax.broadcasted_iota(jnp.int32, (1, pair), 1) // (pair // 2)
    head_mask = [jnp.where(head_lane == h, 1.0, 0.0).astype(BF16) for h in range(2)]
    o_copies = []
    for i in reversed(range(n_mp)):
        keys = words * (i + 1)
        q = qkv_all[i, :, 0:pair]
        k = qkv_all[0 : i + 1, :, pair : 2 * pair].reshape(keys, pair)
        v = qkv_all[0 : i + 1, :, 2 * pair : 3 * pair].reshape(keys, pair)
        same = segc_all[0:keys, 0:1] == seg_all[i, 0:1, :].astype(F32)
        key_at = lax.broadcasted_iota(jnp.int32, (keys, words), 0)
        query_at = lax.broadcasted_iota(jnp.int32, (keys, words), 1) + words * i
        allowed = same & (key_at <= query_at)
        total = None
        for h in range(2):
            st = dot_nt(k * (head_mask[h] * scale).astype(BF16), q)
            st = jnp.where(allowed, st, NEGATIVE)
            ex = jnp.exp(st - jnp.max(st, 0, keepdims=True))
            at = (ex * (1.0 / jnp.sum(ex, 0, keepdims=True))).astype(BF16)
            weights[i, h, 0:keys, :] = at
            part = dot_tn(at, v * head_mask[h])
            total = part if total is None else total + part
        o_send[i] = total.astype(BF16)
    for mate in reversed(mates):
        o_copies.append(send(o_send.at[mate], o_all.at[mp], (dp, mate)))
    o_all[mp] = o_send[mp]
    for copy in o_copies:
        copy.wait()
    attended = jnp.concatenate([o_all[p] for p in range(n_mp)], 1)
    mid = rows_ref[...] + dot_nn(attended, wout_ref[...].reshape(width, width))
    n_w2, rstd2 = norm_fwd(mid, gains[1:2])
    normed[1] = n_w2
    out = mid
    dn2 = jnp.zeros((words, width), F32)
    for p in range(n_mp):
        act, slope = gelu_both(dot_nn(n_w2, wup_ref[p]))
        act = act.astype(BF16)
        act_ref[p] = act
        dh = (slope * dact_ref[p]).astype(BF16)
        dh_ref[p] = dh
        out = out + dot_nn(act, wdown_ref[p])
        dn2 = dn2 + dot_nt(dh, wup_ref[p])
    out_ref[...] = out.astype(BF16)
    d_norm, gain_b = norm_bwd(dn2, n_w2, rstd2, gains[1:2])
    d_mid = cot.astype(F32) + d_norm
    dm_ref[...] = d_mid
    d_att = d_mid.astype(BF16)
    do_copies = []
    for mate in reversed(mates):
        do_send[mate] = dot_nt(d_att, wout_ref[mate]).astype(BF16)
        do_copies.append(send(do_send.at[mate], do_all.at[mp], (dp, mate)))
    do_all[mp] = dot_nt(d_att, wout_ref[mp]).astype(BF16)

    def put(base, p, grad):
        if packed:
            block = words // 4
            for d in range(n_dp):
                for t in range(grad.shape[1] // 128):
                    gbuf_ref[p % 2, p // 2, d % 2, d // 2, base + block * t : base + block * t + block, :] = (
                        grad[block * d : block * d + block, 128 * t : 128 * t + 128].astype(BF16)
                    )
        else:
            ref = {0: gqkv_ref, 192: gout_ref, 256: gup_ref, 512: gdown_ref}[base]
            ref[p] = grad

    for p in range(n_mp):
        put(512, p, dot_tn(cot, act_ref[p]))
        put(256, p, dot_tn(n_w2, dh_ref[p]))
        put(192, p, dot_tn(d_att, o_all[p]))
    dk_acc[...] = jnp.zeros_like(dk_acc)
    dv_acc[...] = jnp.zeros_like(dv_acc)
    for copy in do_copies:
        copy.wait()
    for i in reversed(range(n_mp)):
        keys = words * (i + 1)
        q = qkv_all[i, :, 0:pair]
        k = qkv_all[0 : i + 1, :, pair : 2 * pair].reshape(keys, pair)
        v = qkv_all[0 : i + 1, :, 2 * pair : 3 * pair].reshape(keys, pair)
        do = do_all[i]
        dq = None
        for h in range(2):
            at = weights[i, h, 0:keys, :]
            dpt = dot_nt(v * head_mask[h], do)
            af = at.astype(F32)
            delta = jnp.sum(af * dpt, 0, keepdims=True)
            ds = (af * (dpt - delta)).astype(BF16)
            scaled = (head_mask[h] * scale).astype(BF16)
            part = dot_tn(ds, k * scaled)
            dq = part if dq is None else dq + part
            dk_acc[0:keys, :] += dot_nn(ds, q * scaled)
            dv_acc[0:keys, :] += dot_nn(at, do * head_mask[h])
        dqkv_send[i, :, 0:pair] = dq.astype(BF16)
        dqkv_send[i, :, pair : 2 * pair] = dk_acc[words * i : keys, :].astype(BF16)
        dqkv_send[i, :, 2 * pair : 3 * pair] = dv_acc[words * i : keys, :].astype(BF16)
    dqkv_copies = []
    for mate in reversed(mates):
        dqkv_copies.append(send(dqkv_send.at[mate], dqkv_all.at[mp], (dp, mate)))
    dqkv_all[mp] = dqkv_send[mp]
    for copy in dqkv_copies:
        copy.wait()
    d_normed = jnp.zeros((words, width), F32)
    for p in range(n_mp):
        d_normed = d_normed + dot_nt(dqkv_all[p], wqkv_ref[p])
    d_first, gain_a = norm_bwd(d_normed, normed[0], rstd_a[0], gains[0:1])
    d_rows = (dm_ref[...] + d_first).astype(BF16)
    ggain_ref[0:1, :] = gain_a
    ggain_ref[1:2, :] = gain_b
    back_send[...] = dot_nn(place[...], d_rows).astype(BF16).reshape(n_dp, cap, width)
    back_copies = [send(back_send.at[k], ret.at[k], from_dp[k]) for k in range(1, n_dp)]
    ret[0] = back_send[0]
    for p in range(n_mp):
        put(0, p, dot_tn(normed[0], dqkv_all[p]))
    for copy in back_copies:
        copy.wait()
    de_ref[...] = dot_tn(onehot[...], ret[...].reshape(slots, width)).astype(BF16)


def word_layer(n_dp, word_vec, source, segments, cotangent, gains, wqkv, wout, wup, wdown):
    words, width = word_vec.shape
    n_mp = wqkv.shape[0]
    cap = -(-2 * words // n_dp // 16) * 16
    slots = cap * n_dp
    pair = 2 * (width // HEADS)
    packed = n_dp == 8
    outs = [((words, width), BF16), ((words, width), BF16)]
    if packed:
        outs.append(((2, 2, 2, n_dp // 2, WORD_ROWS, 128), BF16))
    else:
        outs += [((n_mp, width, n), F32) for n in (3 * pair, pair, wup.shape[2], wup.shape[2])]
    outs.append(((2, width), F32))
    hid = wup.shape[2]
    n_sem = 3 * (n_dp - 1) + 5 * 3
    vm = pl.BlockSpec(memory_space=pltpu.VMEM)
    args = (word_vec, source.reshape(1, -1), segments.reshape(1, -1), cotangent, gains, wqkv, wout, wup, wdown)
    shapes = [
        ((slots, words), BF16), ((slots, words), BF16), ((n_dp, cap, width), BF16), ((n_dp, cap, width), BF16),
        ((n_dp, cap, 128), BF16), ((n_dp, cap, 128), BF16), ((n_mp, 8, words), jnp.int32), ((n_mp * words, 128), F32),
        ((words, width), F32), ((2, words, width), BF16), ((1, words, 1), F32),
        ((n_mp, words, 3 * pair), BF16), ((n_mp, words, 3 * pair), BF16), ((n_mp, 2, n_mp * words, words), BF16),
        ((n_mp, words, pair), BF16), ((n_mp, words, pair), BF16),
        ((n_mp, words, hid), BF16), ((n_mp, words, hid), BF16), ((n_mp, words, hid), F32), ((words, width), F32),
        ((n_mp, words, pair), BF16), ((n_mp, words, pair), BF16), ((n_mp * words, pair), F32), ((n_mp * words, pair), F32),
        ((n_mp, words, 3 * pair), BF16), ((n_mp, words, 3 * pair), BF16), ((n_dp, cap, width), BF16), ((n_dp, cap, width), BF16),
    ]
    return pl.pallas_call(
        functools.partial(word_body, n_dp, cap, packed),
        in_specs=[vm] * len(args),
        out_specs=[vm] * len(outs),
        out_shape=[jax.ShapeDtypeStruct(s, d) for s, d in outs],
        scratch_shapes=[pltpu.VMEM(s, d) for s, d in shapes]
        + [pltpu.SemaphoreType.DMA((n_sem,)), pltpu.SemaphoreType.DMA((n_sem,))],
        compiler_params=pltpu.CompilerParams(collective_id=0, has_side_effects=True, vmem_limit_bytes=VMEM_LIMIT),
        name="word_layer",
    )(*args)


def plain_reduce(char_parts, char_gains, word_parts, word_gains):
    *char_mats, gain_rows, pool_rows = char_parts
    gain_sums = jnp.sum(gain_rows, 1) / char_gains.astype(F32)
    small = lax.psum((gain_sums, jnp.sum(pool_rows, 0), word_gains), ("dp", "mp"))
    mats = []
    for grad in char_mats:
        part = lax.psum_scatter(grad, "dp", scatter_dimension=0, tiled=True)
        part = lax.psum_scatter(part.astype(BF16), "mp", scatter_dimension=1, tiled=True)
        mats.append(part.astype(F32))
    words = []
    for grad in word_parts:
        part = lax.psum_scatter(grad, "dp", scatter_dimension=1, tiled=True)
        words.append(lax.psum_scatter(part, "mp", scatter_dimension=0, tiled=False))
    qkv, out, up, down = words
    qkv = jnp.transpose(qkv.reshape(qkv.shape[0], 3, -1), (1, 0, 2))
    return (*mats, qkv, out.T, up, down.T, *small)


def per_device(
    char_input,
    char_counts,
    word_source,
    segment_ids,
    cotangent,
    char_norm_gains,
    char_qkv,
    char_out,
    char_up,
    char_down,
    pool_vector,
    char_proj,
    word_norm_gains,
    word_qkv,
    word_out,
    word_up,
    word_down,
):
    groups = lax.axis_size("dp")
    char_weights = (
        char_norm_gains, char_qkv, char_out, char_up, char_down, pool_vector.reshape(1, -1), char_proj
    )
    word_weights = [
        lax.all_gather(w, "mp", axis=0, tiled=False)
        for w in (
            jnp.transpose(word_qkv, (1, 0, 2)).reshape(word_qkv.shape[1], -1), word_out, word_up, word_down,
        )
    ]
    word_vec, *char_kept = char_forward(char_input, char_counts.reshape(-1, 1), *char_weights)
    output, d_word, *word_parts, word_gains = word_layer(
        groups, word_vec, word_source, segment_ids, cotangent, word_norm_gains, *word_weights
    )
    d_chars, *char_parts = char_backward(d_word, char_kept, *char_weights)
    if groups == 8:
        sums = reduce_grads(groups, char_parts, char_norm_gains, word_parts[0], word_gains)
        grads = unpack_grads(*sums)
    else:
        grads = plain_reduce(char_parts, char_norm_gains, word_parts, word_gains)
    *mats, grad_char_gains, grad_pool, grad_word_gains = grads
    return (output, d_chars, *mats, grad_char_gains, grad_pool.reshape(-1), grad_word_gains)


def solution(mesh):
    placed = (
        P(("dp", "mp"), None),
        P(("dp", "mp")),
        P(("dp", "mp")),
        P(("dp", "mp")),
        P(("dp", "mp"), None),
        P(),
        P(),
        P(),
        P(),
        P(),
        P(),
        P(),
        P(),
        P(None, None, "mp"),
        P("mp", None),
        P(None, "mp"),
        P("mp", None),
    )
    return jax.shard_map(
        per_device,
        mesh=mesh,
        in_specs=placed,
        out_specs=(
            P(("dp", "mp"), None),
            P(("dp", "mp"), None),
            P("dp", "mp"),
            P("dp", "mp"),
            P("dp", "mp"),
            P("dp", "mp"),
            P("dp", "mp"),
            P(None, "dp", "mp"),
            P("mp", "dp"),
            P("dp", "mp"),
            P("mp", "dp"),
            P(),
            P(),
            P(),
        ),
        check_vma=False,
    )
```

```python
import functools
import jax
import jax.numpy as jnp
from jax import lax
from jax.experimental import pallas as pl
from jax.experimental.pallas import tpu as pltpu
from jax.sharding import PartitionSpec as P

HEADS = 8
CHARS = 16
CHAR_HEADS = 4
EPSILON = 1e-05
NEGATIVE = -1e30
GELU_A = 0.7978845608028654
GELU_B = 0.044715
F32 = jnp.float32
BF16 = jnp.bfloat16
MESH = pl.DeviceIdType.MESH
VMEM_LIMIT = 60 * 1024 * 1024


def dot_nn(left, right):
    return jnp.dot(left, right, preferred_element_type=F32)


def dot_nt(left, right):
    return lax.dot_general(left, right, (((1,), (1,)), ((), ())), preferred_element_type=F32)


def dot_tn(left, right):
    return lax.dot_general(left, right, (((0,), (0,)), ((), ())), preferred_element_type=F32)


def as_column(row):
    return jnp.transpose(jnp.broadcast_to(row.astype(F32), (128, row.shape[1])))


def head_stack(values, heads, factor):
    width = values.shape[1] // heads
    lane = lax.broadcasted_iota(jnp.int32, (1, values.shape[1]), 1) // width
    return jnp.concatenate(
        [values * jnp.where(lane == h, factor, 0.0).astype(values.dtype) for h in range(heads)], 0
    )


def gelu_both(hidden):
    square = hidden * hidden
    inner = hidden * (GELU_A + (GELU_A * GELU_B) * square)
    tanh = jnp.tanh(inner)
    half = 0.5 + 0.5 * tanh
    slope = half + (0.5 * hidden) * (1.0 - tanh * tanh) * (GELU_A + (3.0 * GELU_A * GELU_B) * square)
    return hidden * half, slope


def char_fwd_body(
    n_dp, cap,
    x_ref, cnt_ref, gains_ref, wqkv_ref, wout_ref, wup_ref, wdown_ref, pool_ref, wproj_ref,
    src_ref, seg_ref, s_qkv, s_out, s_up, s_down,
    e_ref, n1_ref, p_ref, a_ref, o_ref, n2_ref, rs1_ref, rs2_ref, act_ref, dg_ref, f_ref, aw_ref, pooled_ref,
    onehot_ref, place_ref, seg_out, g_qkv, g_out, g_up, g_down,
    row_send, row_got, seg_all, ssem, rsem,
):
    gather_step(
        n_dp, cap, src_ref, seg_ref, (s_qkv, s_out, s_up, s_down), (g_qkv, g_out, g_up, g_down),
        onehot_ref, place_ref, seg_out, row_send, row_got, seg_all, ssem, rsem,
    )
    words, wide = x_ref.shape
    width = wide // CHARS
    blocks = words // 8
    gains = gains_ref[...].astype(F32)
    pieces = []
    for g in range(words // 16):
        xt = x_ref[16 * g : 16 * g + 16, :].astype(F32)
        for half in range(2):
            for c in range(CHARS):
                pieces.append(xt[8 * half : 8 * half + 8, width * c : width * c + width])
    x = jnp.concatenate(pieces, 0)

    def norm(v, gain):
        mean = jnp.mean(v, -1, keepdims=True)
        centered = v - mean
        rstd = lax.rsqrt(jnp.mean(centered * centered, -1, keepdims=True) + EPSILON)
        return (centered * rstd * gain).astype(BF16), rstd

    n1, rs1 = norm(x, gains[0:1])
    n1_ref[...] = n1
    rs1_ref[...] = rs1
    p_ref[...] = dot_nn(n1, wqkv_ref[...]).astype(BF16)
    row_w = lax.broadcasted_iota(jnp.int32, (8, 128), 0)
    lane_w = lax.broadcasted_iota(jnp.int32, (8, 128), 1) % 8
    same = row_w == lane_w
    slot = lax.broadcasted_iota(jnp.int32, (CHARS, 8, 128), 0)
    for b in range(blocks):
        rows = slice(128 * b, 128 * b + 128)
        counts = jnp.broadcast_to(cnt_ref[8 * b : 8 * b + 8, :], (8, 128))
        here = slot < counts[None]
        q = p_ref[rows, 0:width]
        k = p_ref[rows, width : 2 * width]
        v = p_ref[rows, 2 * width : 3 * width]
        st = dot_nt(head_stack(k, CHAR_HEADS, (width // CHAR_HEADS) ** -0.5), q)
        st = st.reshape(CHAR_HEADS, CHARS, 8, 128)
        st = jnp.where(here[None], st, NEGATIVE)
        e = jnp.exp(st - jnp.max(st, 1, keepdims=True))
        r = jnp.where(same[None, None], 1.0 / jnp.sum(e, 1, keepdims=True), 0.0)
        a = (e * r).reshape(CHAR_HEADS * 128, 128).astype(BF16)
        a_ref[CHAR_HEADS * 128 * b : CHAR_HEADS * 128 * (b + 1), :] = a
        o_ref[rows, :] = dot_tn(a, head_stack(v, CHAR_HEADS, 1.0)).astype(BF16)
    m = x + dot_nn(o_ref[...], wout_ref[...])
    n2, rs2 = norm(m, gains[1:2])
    n2_ref[...] = n2
    rs2_ref[...] = rs2
    act, slope = gelu_both(dot_nn(n2, wup_ref[...]))
    act = act.astype(BF16)
    act_ref[...] = act
    dg_ref[...] = slope.astype(BF16)
    f = m + dot_nn(act, wdown_ref[...])
    f_ref[...] = f.astype(BF16)
    t = jnp.sum(f * pool_ref[...].astype(F32), -1, keepdims=True).reshape(blocks, CHARS, 8, 1)
    counts = cnt_ref[...].reshape(blocks, 1, 8, 1)
    t = jnp.where(lax.broadcasted_iota(jnp.int32, t.shape, 1) < counts, t, NEGATIVE)
    et = jnp.exp(t - jnp.max(t, 1, keepdims=True))
    aw = et / jnp.sum(et, 1, keepdims=True)
    aw_ref[...] = aw.reshape(words * CHARS, 1)
    pooled = jnp.sum(aw * f.reshape(blocks, CHARS, 8, width), 1).reshape(words, width).astype(BF16)
    pooled_ref[...] = pooled
    e_ref[...] = dot_nn(pooled, wproj_ref[...]).astype(BF16)

    @pl.when(pl.program_id(0) == pl.num_programs(0) - 1)
    def _():
        gather_end((g_qkv, g_out, g_up, g_down), (s_qkv, s_out, s_up, s_down), ssem, rsem)


def gather_step(
    n_dp, cap, src_ref, seg_ref, slices, wholes,
    onehot_ref, place_ref, seg_out, row_send, row_got, seg_all, ssem, rsem,
):
    step, last = pl.program_id(0), pl.num_programs(0) - 1
    dp, mp = lax.axis_index("dp"), lax.axis_index("mp")
    sibling = mp // 2 * 2 + (mp + 1) % 2
    across = (mp + 2) % 4
    mates = [sibling, across, across // 2 * 2 + (across + 1) % 2]
    words = src_ref.shape[1]
    slots = n_dp * cap
    parts = len(slices)

    def copy(src, dst, slot, peer):
        return pltpu.make_async_remote_copy(
            src_ref=src, dst_ref=dst, send_sem=ssem.at[slot], recv_sem=rsem.at[slot],
            device_id=peer, device_id_type=MESH,
        )

    def far(i):
        return copy(slices[i], wholes[i].at[mp], i, (dp, across))

    def near(i):
        return copy(slices[i], wholes[i].at[mp], parts + i, (dp, sibling))

    def relay(i):
        return copy(wholes[i].at[across], wholes[i].at[across], 2 * parts + i, (dp, sibling))

    def row_copy(k):
        return copy(row_send.at[k], row_got.at[k], 3 * parts + k, (lax.rem(dp + k, n_dp), mp))

    def seg_copy(j):
        return copy(seg_all.at[mp], seg_all.at[mp], 3 * parts + n_dp + j, (dp, mates[j]))

    @pl.when(step == 0)
    def _():
        barrier = pltpu.get_barrier_semaphore()
        for k in range(1, n_dp):
            pl.semaphore_signal(barrier, inc=1, device_id=(lax.rem(dp + k, n_dp), mp), device_id_type=MESH)
        for mate in mates:
            pl.semaphore_signal(barrier, inc=1, device_id=(dp, mate), device_id_type=MESH)
        source = src_ref[...]
        owner = source // (words * 4)
        owner_c = as_column(owner)[:, 0:1]
        index_r = lax.broadcasted_iota(jnp.int32, (words, words), 0)
        index_c = lax.broadcasted_iota(jnp.int32, (words, words), 1)
        earlier = (owner_c == owner.astype(F32)) & (index_r < index_c)
        rank = jnp.sum(jnp.where(earlier, 1.0, 0.0), 0, keepdims=True).astype(jnp.int32)
        slot_of = lax.rem(owner - dp + n_dp, n_dp) * cap + rank
        at_slot = lax.broadcasted_iota(jnp.int32, (slots, words), 0) == slot_of
        onehot_ref[...] = jnp.where(at_slot, 1.0, 0.0).astype(BF16)
        row_mat = as_column(lax.rem(source, words) + 1).astype(BF16)
        row_send[...] = dot_nn(onehot_ref[...], row_mat).astype(BF16).reshape(n_dp, cap, 128)
        seg_all[mp] = jnp.broadcast_to(seg_ref[...], (8, words))
        pl.semaphore_wait(barrier, n_dp - 1 + 3)
        far(0).start()
        far(1).start()
        for i in range(parts):
            near(i).start()
        for k in range(1, n_dp):
            row_copy(k).start()
        for j in range(3):
            seg_copy(j).start()
        row_got[0] = row_send[0]

    @pl.when(step == 2)
    def _():
        far(2).start()

    @pl.when(step == 3)
    def _():
        far(0).wait()
        relay(0).start()
        far(1).wait()
        relay(1).start()

    @pl.when(step == 4)
    def _():
        far(3).start()

    @pl.when(step == 6)
    def _():
        far(2).wait()
        relay(2).start()

    @pl.when(step == last)
    def _():
        far(3).wait()
        relay(3).start()

    @pl.when(step == last)
    def _():
        for k in range(1, n_dp):
            row_copy(k).wait()
        for j in range(3):
            seg_copy(j).wait()
        at_row = row_got[...].reshape(slots, 128)[:, 0:1].astype(F32) - 1.0
        lanes = lax.broadcasted_iota(jnp.int32, (slots, words), 1).astype(F32)
        place_ref[...] = jnp.where(lanes == at_row, 1.0, 0.0).astype(BF16)
        seg_out[...] = seg_all[...]


def gather_end(wholes, slices, ssem, rsem):
    dp, mp = lax.axis_index("dp"), lax.axis_index("mp")
    sibling = mp // 2 * 2 + (mp + 1) % 2
    across = (mp + 2) % 4
    parts = len(slices)
    for i in range(parts):
        for slot, at in ((parts + i, mp), (2 * parts + i, across)):
            pltpu.make_async_remote_copy(
                src_ref=slices[i] if slot < 2 * parts else wholes[i].at[across], dst_ref=wholes[i].at[at],
                send_sem=ssem.at[slot], recv_sem=rsem.at[slot], device_id=(dp, sibling), device_id_type=MESH,
            ).wait()


def char_forward(n_dp, x, counts, gains, wqkv, wout, wup, wdown, pool, wproj, source, segments, slices, step_words=32):
    words, wide = x.shape
    width = wide // CHARS
    rows = words * CHARS
    step_rows = step_words * CHARS
    cap = -(-2 * words // n_dp // 16) * 16
    slots = n_dp * cap
    full = lambda arr: pl.BlockSpec(arr.shape, lambda i: (0,) * arr.ndim)
    blk = lambda n, w: pl.BlockSpec((n, w), lambda i: (i, 0))
    hid = wup.shape[1]
    dw = wproj.shape[1]
    outs = [
        (words, step_words, dw, BF16), (rows, step_rows, width, BF16), (rows, step_rows, 3 * width, BF16),
        (rows * CHAR_HEADS, step_rows * CHAR_HEADS, 128, BF16), (rows, step_rows, width, BF16),
        (rows, step_rows, width, BF16), (rows, step_rows, 1, F32), (rows, step_rows, 1, F32),
        (rows, step_rows, hid, BF16), (rows, step_rows, hid, BF16), (rows, step_rows, width, BF16),
        (rows, step_rows, 1, F32), (words, step_words, width, BF16),
    ]
    fixed = [((slots, words), BF16), ((slots, words), BF16), ((4, 8, words), jnp.int32)]
    any_spec = pl.BlockSpec(memory_space=pl.ANY)
    n_sem = 3 * len(slices) + n_dp + 3
    return pl.pallas_call(
        functools.partial(char_fwd_body, n_dp, cap),
        grid=(words // step_words,),
        in_specs=[blk(step_words, wide), blk(step_words, 1)]
        + [full(w) for w in (gains, wqkv, wout, wup, wdown, pool, wproj, source, segments)]
        + [any_spec] * len(slices),
        out_specs=[blk(b, w) for _, b, w, _ in outs]
        + [pl.BlockSpec(s, lambda i, n=len(s): (0,) * n) for s, _ in fixed]
        + [any_spec] * len(slices),
        out_shape=[jax.ShapeDtypeStruct((n, w), d) for n, _, w, d in outs]
        + [jax.ShapeDtypeStruct(s, d) for s, d in fixed]
        + [jax.ShapeDtypeStruct((4, *s.shape), s.dtype) for s in slices],
        scratch_shapes=[
            pltpu.VMEM((n_dp, cap, 128), BF16), pltpu.VMEM((n_dp, cap, 128), BF16), pltpu.VMEM((4, 8, words), jnp.int32),
            pltpu.SemaphoreType.DMA((n_sem,)), pltpu.SemaphoreType.DMA((n_sem,)),
        ],
        compiler_params=pltpu.CompilerParams(collective_id=2, has_side_effects=True, vmem_limit_bytes=VMEM_LIMIT),
        name="char_forward",
    )(x, counts, gains, wqkv, wout, wup, wdown, pool, wproj, source, segments, *slices)


CHAR_A = 160
CHAR_B = 64
WORD_ROWS = 768
WORD_CHUNKS = 4
ORDERS = ("yxz", "xyz", "yxz", "xyz")
SEMS = 8


def fold_half(block):
    half = block.shape[0] // 2
    return jnp.concatenate([block[:half], block[half:]], 1)


def unfold_half(block):
    return jnp.concatenate([block[:, :64], block[:, 64:]], 0)


def coordinates():
    dp, mp = lax.axis_index("dp"), lax.axis_index("mp")
    return dp // 2, dp % 2, mp // 2, mp % 2


def device_of(z, x, y, core):
    return (z * 2 + x, y * 2 + core)


def remote_copy(src, dst, ssem, rsem, slot, peer):
    return pltpu.make_async_remote_copy(
        src_ref=src, dst_ref=dst, send_sem=ssem.at[slot], recv_sem=rsem.at[slot],
        device_id=peer, device_id_type=MESH,
    )


class Halving:
    def __init__(self, n_z, sent, work, got, ssem, rsem, base, order):
        self.n_z, self.sent, self.work, self.got = n_z, sent, work, got
        self.ssem, self.rsem, self.base, self.order = ssem, rsem, base, order
        self.z, self.x, self.y, self.core = coordinates()

    def copies(self, phase):
        z, x, y, core = self.z, self.x, self.y, self.core
        work = self.work
        slot = self.base + phase
        step = "c" if phase == 0 else self.order[phase - 1]
        if step == "c":
            pairs = [(self.sent, self.got[0], device_of(z, x, y, 1 - core))]
        elif step == "y":
            src = work.at[1 - y] if phase == 1 else work.at[1 - y, x]
            pairs = [(src, self.got[phase], device_of(z, x, 1 - y, core))]
        elif step == "x":
            src = work.at[:, 1 - x] if phase == 1 else work.at[y, 1 - x]
            pairs = [(src, self.got[phase], device_of(z, 1 - x, y, core))]
        else:
            pairs = []
            for k in range(1, self.n_z):
                other = lax.rem(z + k, self.n_z)
                pairs.append((work.at[y, x, other], self.got[3].at[k - 1], device_of(other, x, y, core)))
        return [remote_copy(s, d, self.ssem, self.rsem, slot + i, peer) for i, (s, d, peer) in enumerate(pairs)]

    def start(self, phase):
        for copy in self.copies(phase):
            copy.start()

    def finish(self, phase):
        for copy in self.copies(phase):
            copy.wait()
        x, y = self.x, self.y
        work, got = self.work, self.got[phase]
        step = "c" if phase == 0 else self.order[phase - 1]

        def add(mine, other):
            def body(i, carry):
                mine[i] = mine[i] + other[i]
                return carry
            lax.fori_loop(0, self.n_z, body, 0)

        if step == "c":
            for i in range(2):
                for j in range(2):
                    add(work.at[i, j], got.at[i, j])
        elif step == "y" and phase == 1:
            for j in range(2):
                add(work.at[y, j], got.at[j])
        elif step == "x" and phase == 1:
            for i in range(2):
                add(work.at[i, x], got.at[i])
        elif step in "yx":
            add(work.at[y, x], got)

    def total(self):
        value = self.work[self.y, self.x, self.z].astype(F32)
        for k in range(self.n_z - 1):
            value += self.got[3][k].astype(F32)
        return value

    @staticmethod
    def got_shapes(n_z, rows):
        return [
            pltpu.VMEM((2, 2, n_z, rows, 128), BF16), pltpu.VMEM((2, n_z, rows, 128), BF16),
            pltpu.VMEM((n_z, rows, 128), BF16), pltpu.VMEM((n_z - 1, rows, 128), BF16),
        ]


class GradientSums:
    def __init__(self, n_z, gbuf, refs):
        self.n_z, self.gbuf = n_z, gbuf
        abuf, bbuf, wbuf, small, sgot, ssem, rsem, lsem, *got = refs
        self.abuf, self.bbuf, self.wbuf, self.small, self.sgot = abuf, bbuf, wbuf, small, sgot
        self.ssem, self.rsem, self.lsem = ssem, rsem, lsem
        self.core = lax.axis_index("mp") % 2
        part = WORD_ROWS // WORD_CHUNKS
        sent = gbuf.at[1 - self.core]
        self.chunks = [
            Halving(
                n_z, sent.at[:, :, :, part * i : part * i + part], wbuf.at[:, :, :, part * i : part * i + part],
                got[4 * i : 4 * i + 4], ssem, rsem, SEMS * i, ORDERS[i],
            )
            for i in range(WORD_CHUNKS)
        ]
        base = SEMS * WORD_CHUNKS
        at = 4 * WORD_CHUNKS
        self.parta = Halving(
            n_z, abuf.at[1 - self.core], abuf.at[self.core], got[at : at + 4], ssem, rsem, base, "yxz"
        )
        self.partb = Halving(
            n_z, bbuf.at[1 - self.core], bbuf.at[self.core], got[at + 4 : at + 8], ssem, rsem, base + SEMS, "yxz"
        )
        self.tiny = base + 2 * SEMS

    @staticmethod
    def scratch(n_z):
        n_sem = SEMS * (WORD_CHUNKS + 3)
        shapes = [
            pltpu.VMEM((2, 2, 2, n_z, CHAR_A, 128), BF16), pltpu.VMEM((2, 2, 2, n_z, CHAR_B, 128), BF16),
            pltpu.VMEM((2, 2, n_z, WORD_ROWS, 128), BF16),
            pltpu.VMEM((4, 16, 128), F32), pltpu.VMEM((2 + n_z, 16, 128), F32),
            pltpu.SemaphoreType.DMA((n_sem,)), pltpu.SemaphoreType.DMA((n_sem,)), pltpu.SemaphoreType.DMA,
        ]
        for _ in range(WORD_CHUNKS):
            shapes += Halving.got_shapes(n_z, WORD_ROWS // WORD_CHUNKS)
        return shapes + Halving.got_shapes(n_z, CHAR_A) + Halving.got_shapes(n_z, CHAR_B)

    def begin(self, step):
        z, x, y, core = coordinates()
        chunks = self.chunks
        load = pltpu.make_async_copy(self.gbuf.at[core], self.wbuf, self.lsem)

        def advance(at, moves):
            @pl.when(step == at)
            def _():
                for i, phase in moves:
                    chunks[i].finish(phase)
                    if phase < 3:
                        chunks[i].start(phase + 1)

        @pl.when(step == 0)
        def _():
            load.start()
            barrier = pltpu.get_barrier_semaphore()
            peers = [device_of(z, x, y, 1 - core), device_of(z, x, 1 - y, core), device_of(z, 1 - x, y, core)]
            peers += [device_of(lax.rem(z + k, self.n_z), x, y, core) for k in range(1, self.n_z)]
            for peer in peers:
                pl.semaphore_signal(barrier, inc=1, device_id=peer, device_id_type=MESH)
            pl.semaphore_wait(barrier, len(peers))
            for i in range(WORD_CHUNKS):
                chunks[i].start(0)
            load.wait()

        for at, moves in SCHEDULE:
            advance(at, moves)

    def middle(self, step, half, gup_ref, gdown_ref, gproj_ref):
        n_z, abuf, part = self.n_z, self.abuf, self.parta

        @pl.when(step == half - 1)
        def _():
            for d in range(2 * n_z):
                down = gdown_ref[128 * d : 128 * d + 128, :]
                for p in range(4):
                    block = abuf.at[p % 2, p // 2, d % 2, d // 2]
                    block[0:32, :] = gup_ref[32 * d : 32 * d + 32, 256 * p : 256 * p + 128].astype(BF16)
                    block[32:64, :] = gup_ref[32 * d : 32 * d + 32, 256 * p + 128 : 256 * p + 256].astype(BF16)
                    block[64:128, :] = fold_half(down[:, 64 * p : 64 * p + 64]).astype(BF16)
                    block[128:160, :] = gproj_ref[32 * d : 32 * d + 32, 128 * p : 128 * p + 128].astype(BF16)
            part.start(0)

        for phase, at in enumerate(PART_STEPS):
            @pl.when(step == half + at)
            def _():
                part.finish(phase)
                part.start(phase + 1)

    def end(
        self, step, gqkv_ref, gout_ref, ggain_ref, gpool_ref, gains_ref, wgain_ref,
        outa_ref, outb_ref, word_ref, small_ref,
    ):
        n_z, bbuf, small, sgot = self.n_z, self.bbuf, self.small, self.sgot
        z, x, y, core = coordinates()
        peers = [device_of(z, x, y, 1 - core), device_of(z, x, 1 - y, core), device_of(z, 1 - x, y, core)]
        z_peers = [device_of(lax.rem(z + k, n_z), x, y, core) for k in range(1, n_z)]

        @pl.when(step == pl.num_programs(0) - 1)
        def _():
            for d in range(2 * n_z):
                qkv = gqkv_ref[32 * d : 32 * d + 32, :]
                out = gout_ref[32 * d : 32 * d + 32, :]
                for p in range(4):
                    block = bbuf.at[p % 2, p // 2, d % 2, d // 2]
                    own = qkv[:, 192 * p : 192 * p + 192]
                    block[0:32, :] = own[:, 0:128].astype(BF16)
                    block[32:48, :] = fold_half(own[:, 128:192]).astype(BF16)
                    block[48:64, :] = fold_half(out[:, 64 * p : 64 * p + 64]).astype(BF16)
            self.partb.start(0)
            small[0] = pack_small(ggain_ref, gpool_ref, gains_ref, wgain_ref)
            for i in range(3):
                copy = remote_copy(small.at[i], sgot.at[i], self.ssem, self.rsem, self.tiny + i, peers[i])
                copy.start()
                self.partb.finish(i)
                self.partb.start(i + 1)
                copy.wait()
                small[i + 1] = small[i] + sgot[i]
            tail = [
                remote_copy(small.at[3], sgot.at[2 + k], self.ssem, self.rsem, self.tiny + 2 + k, z_peers[k - 1])
                for k in range(1, n_z)
            ]
            for copy in tail:
                copy.start()
            part = WORD_ROWS // WORD_CHUNKS
            for i in range(WORD_CHUNKS):
                word_ref[part * i : part * i + part, :] = self.chunks[i].total()
            self.parta.finish(3)
            outa_ref[...] = self.parta.total()
            for copy in tail:
                copy.wait()
            total = small[3]
            for k in range(1, n_z):
                total += sgot[2 + k]
            small_ref[...] = total
            self.partb.finish(3)
            outb_ref[...] = self.partb.total()


SCHEDULE = (
    (1, ((0, 0), (1, 0))),
    (2, ((2, 0), (3, 0))),
    (5, ((0, 1), (1, 1))),
    (8, ((2, 1), (3, 1), (0, 2), (1, 2))),
    (11, ((2, 2), (3, 2))),
    (14, ((0, 3), (1, 3), (2, 3), (3, 3))),
)
PART_STEPS = (0, 3, 5)


def pack_small(cgain_ref, cpool_ref, cg_ref, wgain_ref):
    gains = cg_ref[...].astype(F32)
    rows = []
    for j in range(2):
        total = jnp.sum(cgain_ref[j], 0, keepdims=True) / gains[j : j + 1]
        rows += [total[:, 0:128], total[:, 128:256]]
    total = jnp.sum(cpool_ref[...], 0, keepdims=True)
    rows += [total[:, 0:128], total[:, 128:256]]
    for j in range(2):
        rows += [wgain_ref[j : j + 1, 128 * t : 128 * t + 128] for t in range(4)]
    rows.append(jnp.zeros((2, 128), F32))
    return jnp.concatenate(rows, 0)


def unpack_body(
    parta_ref, partb_ref, word_ref, small_ref,
    oqkv_ref, oout_ref, oup_ref, odown_ref, oproj_ref, owqkv_ref, owout_ref, owup_ref, owdown_ref,
    ocgain_ref, opool_ref, owgain_ref,
):
    parta, partb, word, total = parta_ref[...], partb_ref[...], word_ref[...], small_ref[...]
    oqkv_ref[:, 0:128] = partb[0:32]
    oqkv_ref[:, 128:192] = unfold_half(partb[32:48])
    oout_ref[...] = unfold_half(partb[48:64])
    oup_ref[:, 0:128] = parta[0:32]
    oup_ref[:, 128:256] = parta[32:64]
    odown_ref[...] = unfold_half(parta[64:128])
    oproj_ref[...] = parta[128:160]
    for t in range(3):
        owqkv_ref[t] = word[64 * t : 64 * t + 64]
    owout_ref[...] = word[192:256].T
    for t in range(4):
        owup_ref[:, 128 * t : 128 * t + 128] = word[256 + 64 * t : 320 + 64 * t]
        owdown_ref[128 * t : 128 * t + 128, :] = word[512 + 64 * t : 576 + 64 * t].T
    for j in range(2):
        for t in range(2):
            ocgain_ref[j : j + 1, 128 * t : 128 * t + 128] = total[2 * j + t : 2 * j + t + 1]
        for t in range(4):
            owgain_ref[j : j + 1, 128 * t : 128 * t + 128] = total[6 + 4 * j + t : 7 + 4 * j + t]
    for t in range(2):
        opool_ref[:, 128 * t : 128 * t + 128] = total[4 + t : 5 + t]


def unpack_grads(*sums):
    vm = pl.BlockSpec(memory_space=pltpu.VMEM)
    outs = [(32, 192), (32, 64), (32, 256), (128, 64), (32, 128), (3, 64, 128), (128, 64), (64, 512), (512, 64), (2, 256), (1, 256), (2, 512)]
    return pl.pallas_call(
        unpack_body,
        in_specs=[vm] * 4,
        out_specs=[vm] * len(outs),
        out_shape=[jax.ShapeDtypeStruct(s, F32) for s in outs],
        name="unpack_gradients",
    )(*sums)


def char_bwd_body(
    n_dp, fused,
    de_ref, gains_ref, wqkv_ref, wout_ref, wup_ref, wdown_ref, pool_ref, wproj_ref,
    n1_ref, p_ref, a_ref, o_ref, n2_ref, rs1_ref, rs2_ref, act_ref, dg_ref, f_ref, aw_ref, pooled_ref,
    *refs,
):
    if fused:
        gbuf_any, wgain_ref, dx_ref, outa_ref, outb_ref, word_ref, small_ref, *refs = refs
        dm_ref, dp_ref, do_ref, *refs = refs
    else:
        dx_ref, *refs = refs
    gqkv_ref, gout_ref, gup_ref, gdown_ref, gproj_ref, ggain_ref, gpool_ref, *refs = refs
    if not fused:
        dm_ref, dp_ref, do_ref = refs
    step = pl.program_id(0)
    half = pl.num_programs(0) // 2
    words = de_ref.shape[0]
    width = n1_ref.shape[1]
    blocks = words // 8
    rows = words * CHARS
    gains = gains_ref[...].astype(F32)
    if fused:
        sums = GradientSums(n_dp // 2, gbuf_any, refs)
        sums.begin(step)

    @pl.when(step == 0)
    def _():
        for ref in (gqkv_ref, gout_ref, gup_ref, gdown_ref, gproj_ref, ggain_ref, gpool_ref):
            ref[...] = jnp.zeros_like(ref)

    def norm_back(dn, n, rstd, gain, row):
        d1 = dn * gain
        dnn = dn * n.astype(F32)
        ggain_ref[row] += jnp.sum(dnn.reshape(rows // 8, 8, width), 0)
        m1 = jnp.mean(d1, -1, keepdims=True)
        m2 = jnp.mean(dnn, -1, keepdims=True)
        return rstd * (d1 - m1 - n.astype(F32) * (1.0 / gain) * m2)

    @pl.when(step < half)
    def _():
        de = de_ref[...]
        gproj_ref[...] += dot_tn(pooled_ref[...], de)
        dpool = dot_nt(de, wproj_ref[...]).reshape(blocks, 1, 8, width)
        f = f_ref[...].astype(F32).reshape(blocks, CHARS, 8, width)
        aw = aw_ref[...].reshape(blocks, CHARS, 8, 1)
        g = jnp.sum(f * dpool, -1, keepdims=True)
        dt = aw * (g - jnp.sum(aw * g, 1, keepdims=True))
        gpool_ref[...] += jnp.sum((dt * f).reshape(rows // 8, 8, width), 0)
        df = (aw * dpool + dt * pool_ref[...].astype(F32)).reshape(rows, width)
        dfb = df.astype(BF16)
        gdown_ref[...] += dot_tn(act_ref[...], dfb)
        dh = (dg_ref[...].astype(F32) * dot_nt(dfb, wdown_ref[...])).astype(BF16)
        n2 = n2_ref[...]
        gup_ref[...] += dot_tn(n2, dh)
        dn2 = dot_nt(dh, wup_ref[...])
        dm_ref[pl.ds(pl.multiple_of(step * rows, rows), rows), :] = df + norm_back(dn2, n2, rs2_ref[...], gains[1:2], 1)

    @pl.when(step >= half)
    def _():
        dm = dm_ref[pl.ds(pl.multiple_of((step - half) * rows, rows), rows), :]
        dmb = dm.astype(BF16)
        gout_ref[...] += dot_tn(o_ref[...], dmb)
        do_ref[...] = dot_nt(dmb, wout_ref[...]).astype(BF16)
        scale = (width // CHAR_HEADS) ** -0.5
        for b in range(blocks):
            sl = slice(128 * b, 128 * b + 128)
            q = p_ref[sl, 0:width]
            k = p_ref[sl, width : 2 * width]
            v = p_ref[sl, 2 * width : 3 * width]
            do = do_ref[sl, :]
            ab = a_ref[CHAR_HEADS * 128 * b : CHAR_HEADS * 128 * (b + 1), :]
            a = ab.astype(F32).reshape(CHAR_HEADS, CHARS, 8, 128)
            dpt = dot_nt(head_stack(v, CHAR_HEADS, 1.0), do).reshape(CHAR_HEADS, CHARS, 8, 128)
            delta = jnp.sum(a * dpt, 1, keepdims=True)
            ds = (a * (dpt - delta)).reshape(CHAR_HEADS * 128, 128).astype(BF16)
            wide_ds = jnp.concatenate([ds[128 * h : 128 * h + 128] for h in range(CHAR_HEADS)], 1)
            wide_a = jnp.concatenate([ab[128 * h : 128 * h + 128] for h in range(CHAR_HEADS)], 1)
            dp_ref[sl, 0:width] = dot_tn(ds, head_stack(k, CHAR_HEADS, scale)).astype(BF16)
            dp_ref[sl, width : 2 * width] = dot_nn(wide_ds, head_stack(q, CHAR_HEADS, scale)).astype(BF16)
            dp_ref[sl, 2 * width : 3 * width] = dot_nn(wide_a, head_stack(do, CHAR_HEADS, 1.0)).astype(BF16)
        n1 = n1_ref[...]
        dp = dp_ref[...]
        gqkv_ref[...] += dot_tn(n1, dp)
        dn1 = dot_nt(dp, wqkv_ref[...])
        dx = dm + norm_back(dn1, n1, rs1_ref[...], gains[0:1], 0)
        for b in range(blocks):
            for c in range(CHARS):
                dx_ref[8 * b : 8 * b + 8, width * c : width * c + width] = dx[128 * b + 8 * c : 128 * b + 8 * c + 8]

    if fused:
        sums.middle(step, half, gup_ref, gdown_ref, gproj_ref)
        sums.end(
            step, gqkv_ref, gout_ref, ggain_ref, gpool_ref, gains_ref, wgain_ref,
            outa_ref, outb_ref, word_ref, small_ref,
        )


def char_backward(n_dp, de, kept, gains, wqkv, wout, wup, wdown, pool, wproj, gbuf, wgain, step_words=32):
    words = de.shape[0]
    width = wout.shape[0]
    rows = words * CHARS
    step_rows = step_words * CHARS
    steps = words // step_words
    fused = gbuf is not None
    full = lambda arr: pl.BlockSpec(arr.shape, lambda i: (0,) * arr.ndim)
    fixed = lambda s: pl.BlockSpec(s, lambda i: (0,) * len(s))
    early = lambda n, w: pl.BlockSpec((n, w), lambda i: (lax.min(i, steps - 1), 0))
    late = lambda n, w: pl.BlockSpec((n, w), lambda i: (lax.max(i - steps, 0), 0))
    weights = (gains, wqkv, wout, wup, wdown, pool, wproj)
    when = [late, late, late, late, early, late, early, early, early, early, early, early]
    grads = [wqkv.shape, wout.shape, wup.shape, wdown.shape, wproj.shape, (2, 8, width), (8, width)]
    scratch = [pltpu.VMEM((rows, width), F32), pltpu.VMEM((step_rows, 3 * width), BF16), pltpu.VMEM((step_rows, width), BF16)]
    args = [de, *weights, *kept]
    in_specs = [early(step_words, de.shape[1])] + [full(w) for w in weights]
    in_specs += [f(r.shape[0] // steps, r.shape[1]) for f, r in zip(when, kept)]
    params = dict(vmem_limit_bytes=VMEM_LIMIT)
    if fused:
        outs = [(CHAR_A, 128), (CHAR_B, 128), (WORD_ROWS, 128), (16, 128)]
        args += [gbuf, wgain]
        in_specs += [pl.BlockSpec(memory_space=pl.ANY), full(wgain)]
        scratch += [pltpu.VMEM(s, F32) for s in grads] + GradientSums.scratch(n_dp // 2)
        params.update(collective_id=1, has_side_effects=True)
    else:
        outs = grads
    return pl.pallas_call(
        functools.partial(char_bwd_body, n_dp, fused),
        grid=(2 * steps,),
        in_specs=in_specs,
        out_specs=[late(step_words, CHARS * width)] + [fixed(s) for s in outs],
        out_shape=[jax.ShapeDtypeStruct((words, CHARS * width), F32)] + [jax.ShapeDtypeStruct(s, F32) for s in outs],
        scratch_shapes=scratch,
        compiler_params=pltpu.CompilerParams(**params),
        name="char_backward",
    )(*args)


def norm_fwd(values, gain):
    mean = jnp.mean(values, -1, keepdims=True)
    centered = values - mean
    rstd = lax.rsqrt(jnp.mean(centered * centered, -1, keepdims=True) + EPSILON)
    return (centered * rstd * gain).astype(BF16), rstd


def norm_bwd(dn, n, rstd, gain):
    n = n.astype(F32)
    d1 = dn * gain
    dnn = dn * n
    m1 = jnp.mean(d1, -1, keepdims=True)
    m2 = jnp.mean(dnn, -1, keepdims=True)
    return rstd * (d1 - m1 - n * (1.0 / gain) * m2), jnp.sum(dnn, 0, keepdims=True) / gain


def word_body(
    n_dp, cap, packed,
    e_ref, onehot, place, seg_all, cot_ref, gains_ref, *refs,
):
    slices, wholes, refs = refs[:4], refs[4:8], refs[8:]
    if packed:
        out_ref, de_ref, gbuf_ref, ggain_ref, *refs = refs
    else:
        out_ref, de_ref, gqkv_ref, gout_ref, gup_ref, gdown_ref, ggain_ref, *refs = refs
    (
        wqkv_ref, wout_ref, wup_ref, wdown_ref, vec_send, vec_got, segc_all, rows_ref, normed, rstd_a,
        qkv_send, qkv_all, weights, o_send, o_all, act_ref, dh_ref, dact_ref, dm_ref,
        do_send, do_all, dk_acc, dv_acc, dqkv_send, dqkv_all, back_send, ret,
        ssem, rsem, lsem,
    ) = refs
    dp, mp = lax.axis_index("dp"), lax.axis_index("mp")
    n_mp = 4
    words, width = e_ref.shape
    slots = n_dp * cap
    pair = 2 * (width // HEADS)
    scale = (width // HEADS) ** -0.5
    to_dp = [(lax.rem(dp + k, n_dp), mp) for k in range(n_dp)]
    from_dp = [(lax.rem(dp + n_dp - k, n_dp), mp) for k in range(n_dp)]
    mates = [(mp // 2 * 2 + (mp + 1) % 2), (mp + 2) % 4, ((mp // 2 * 2 + 2) % 4 + (mp + 1) % 2)]
    barrier = pltpu.get_barrier_semaphore()
    for k in range(1, n_dp):
        pl.semaphore_signal(barrier, inc=1, device_id=to_dp[k], device_id_type=MESH)
    for mate in mates:
        pl.semaphore_signal(barrier, inc=1, device_id=(dp, mate), device_id_type=MESH)
    next_slot = [0]

    def send(src, dst, peer):
        slot = next_slot[0]
        next_slot[0] += 1
        copy = pltpu.make_async_remote_copy(
            src_ref=src, dst_ref=dst, send_sem=ssem.at[slot], recv_sem=rsem.at[slot],
            device_id=peer, device_id_type=MESH,
        )
        copy.start()
        return copy

    loads = []
    for i, held in ((3, wdown_ref), (0, wqkv_ref), (1, wout_ref), (2, wup_ref)):
        loads.append([pltpu.make_async_copy(slices[i], held.at[mp], lsem.at[i, 0])])
        loads[-1] += [
            pltpu.make_async_copy(wholes[i].at[mate], held.at[mate], lsem.at[i, 1 + j]) for j, mate in enumerate(mates)
        ]
        for load in loads[-1]:
            load.start()
    vec_send[...] = dot_nn(onehot[...], e_ref[...]).astype(BF16).reshape(n_dp, cap, width)

    pl.semaphore_wait(barrier, n_dp - 1 + 3)
    vec_copies = [send(vec_send.at[k], vec_got.at[k], to_dp[k]) for k in range(1, n_dp)]
    vec_got[0] = vec_send[0]
    gains = gains_ref[...].astype(F32)
    cot = cot_ref[...]
    for load in loads[0]:
        load.wait()
    for p in range(n_mp):
        dact_ref[p] = dot_nt(cot, wdown_ref[p])
    for j in range(n_mp):
        segc_all[words * j : words * j + words, :] = as_column(seg_all[j, 0:1, :])
    for load in loads[1] + loads[2] + loads[3]:
        load.wait()
    for copy in vec_copies:
        copy.wait()
    rows = dot_tn(place[...], vec_got[...].reshape(slots, width))
    rows_ref[...] = rows
    n_w, rstd = norm_fwd(rows, gains[0:1])
    normed[0] = n_w
    rstd_a[0] = rstd
    qkv_copies = []
    for mate in reversed(mates):
        qkv_send[mate] = dot_nn(n_w, wqkv_ref[mate]).astype(BF16)
        qkv_copies.append(send(qkv_send.at[mate], qkv_all.at[mp], (dp, mate)))
    qkv_all[mp] = dot_nn(n_w, wqkv_ref[mp]).astype(BF16)
    for copy in qkv_copies:
        copy.wait()

    head_lane = lax.broadcasted_iota(jnp.int32, (1, pair), 1) // (pair // 2)
    head_mask = [jnp.where(head_lane == h, 1.0, 0.0).astype(BF16) for h in range(2)]
    o_copies = []
    for i in reversed(range(n_mp)):
        keys = words * (i + 1)
        q = qkv_all[i, :, 0:pair]
        k = qkv_all[0 : i + 1, :, pair : 2 * pair].reshape(keys, pair)
        v = qkv_all[0 : i + 1, :, 2 * pair : 3 * pair].reshape(keys, pair)
        same = segc_all[0:keys, 0:1] == seg_all[i, 0:1, :].astype(F32)
        key_at = lax.broadcasted_iota(jnp.int32, (keys, words), 0)
        query_at = lax.broadcasted_iota(jnp.int32, (keys, words), 1) + words * i
        allowed = same & (key_at <= query_at)
        total = None
        for h in range(2):
            st = dot_nt(k * (head_mask[h] * scale).astype(BF16), q)
            st = jnp.where(allowed, st, NEGATIVE)
            ex = jnp.exp(st - jnp.max(st, 0, keepdims=True))
            at = (ex * (1.0 / jnp.sum(ex, 0, keepdims=True))).astype(BF16)
            weights[i, h, 0:keys, :] = at
            part = dot_tn(at, v * head_mask[h])
            total = part if total is None else total + part
        o_send[i] = total.astype(BF16)
    for mate in reversed(mates):
        o_copies.append(send(o_send.at[mate], o_all.at[mp], (dp, mate)))
    o_all[mp] = o_send[mp]
    for copy in o_copies:
        copy.wait()
    attended = jnp.concatenate([o_all[p] for p in range(n_mp)], 1)
    mid = rows_ref[...] + dot_nn(attended, wout_ref[...].reshape(width, width))
    n_w2, rstd2 = norm_fwd(mid, gains[1:2])
    normed[1] = n_w2
    out = mid
    dn2 = jnp.zeros((words, width), F32)
    for p in range(n_mp):
        act, slope = gelu_both(dot_nn(n_w2, wup_ref[p]))
        act = act.astype(BF16)
        act_ref[p] = act
        dh = (slope * dact_ref[p]).astype(BF16)
        dh_ref[p] = dh
        out = out + dot_nn(act, wdown_ref[p])
        dn2 = dn2 + dot_nt(dh, wup_ref[p])
    out_ref[...] = out.astype(BF16)
    d_norm, gain_b = norm_bwd(dn2, n_w2, rstd2, gains[1:2])
    d_mid = cot.astype(F32) + d_norm
    dm_ref[...] = d_mid
    d_att = d_mid.astype(BF16)
    do_copies = []
    for mate in reversed(mates):
        do_send[mate] = dot_nt(d_att, wout_ref[mate]).astype(BF16)
        do_copies.append(send(do_send.at[mate], do_all.at[mp], (dp, mate)))
    do_all[mp] = dot_nt(d_att, wout_ref[mp]).astype(BF16)

    def put(base, p, grad):
        if packed:
            block = words // 4
            for d in range(n_dp):
                for t in range(grad.shape[1] // 128):
                    gbuf_ref[p % 2, p // 2, d % 2, d // 2, base + block * t : base + block * t + block, :] = (
                        grad[block * d : block * d + block, 128 * t : 128 * t + 128].astype(BF16)
                    )
        else:
            ref = {0: gqkv_ref, 192: gout_ref, 256: gup_ref, 512: gdown_ref}[base]
            ref[p] = grad

    for p in range(n_mp):
        put(512, p, dot_tn(cot, act_ref[p]))
        put(256, p, dot_tn(n_w2, dh_ref[p]))
        put(192, p, dot_tn(d_att, o_all[p]))
    dk_acc[...] = jnp.zeros_like(dk_acc)
    dv_acc[...] = jnp.zeros_like(dv_acc)
    for copy in do_copies:
        copy.wait()
    for i in reversed(range(n_mp)):
        keys = words * (i + 1)
        q = qkv_all[i, :, 0:pair]
        k = qkv_all[0 : i + 1, :, pair : 2 * pair].reshape(keys, pair)
        v = qkv_all[0 : i + 1, :, 2 * pair : 3 * pair].reshape(keys, pair)
        do = do_all[i]
        dq = None
        for h in range(2):
            at = weights[i, h, 0:keys, :]
            dpt = dot_nt(v * head_mask[h], do)
            af = at.astype(F32)
            delta = jnp.sum(af * dpt, 0, keepdims=True)
            ds = (af * (dpt - delta)).astype(BF16)
            scaled = (head_mask[h] * scale).astype(BF16)
            part = dot_tn(ds, k * scaled)
            dq = part if dq is None else dq + part
            dk_acc[0:keys, :] += dot_nn(ds, q * scaled)
            dv_acc[0:keys, :] += dot_nn(at, do * head_mask[h])
        dqkv_send[i, :, 0:pair] = dq.astype(BF16)
        dqkv_send[i, :, pair : 2 * pair] = dk_acc[words * i : keys, :].astype(BF16)
        dqkv_send[i, :, 2 * pair : 3 * pair] = dv_acc[words * i : keys, :].astype(BF16)
    dqkv_copies = []
    for mate in reversed(mates):
        dqkv_copies.append(send(dqkv_send.at[mate], dqkv_all.at[mp], (dp, mate)))
    dqkv_all[mp] = dqkv_send[mp]
    for copy in dqkv_copies:
        copy.wait()
    d_normed = jnp.zeros((words, width), F32)
    for p in range(n_mp):
        d_normed = d_normed + dot_nt(dqkv_all[p], wqkv_ref[p])
    d_first, gain_a = norm_bwd(d_normed, normed[0], rstd_a[0], gains[0:1])
    d_rows = (dm_ref[...] + d_first).astype(BF16)
    ggain_ref[0:1, :] = gain_a
    ggain_ref[1:2, :] = gain_b
    back_send[...] = dot_nn(place[...], d_rows).astype(BF16).reshape(n_dp, cap, width)
    back_copies = [send(back_send.at[k], ret.at[k], from_dp[k]) for k in range(1, n_dp)]
    ret[0] = back_send[0]
    for p in range(n_mp):
        put(0, p, dot_tn(normed[0], dqkv_all[p]))
    for copy in back_copies:
        copy.wait()
    de_ref[...] = dot_tn(onehot[...], ret[...].reshape(slots, width)).astype(BF16)


def word_layer(n_dp, word_vec, onehot, place, segments, cotangent, gains, slices, wholes):
    words, width = word_vec.shape
    wqkv, wout, wup, wdown = wholes
    n_mp = wqkv.shape[0]
    cap = -(-2 * words // n_dp // 16) * 16
    slots = cap * n_dp
    pair = 2 * (width // HEADS)
    packed = n_dp == 8
    outs = [((words, width), BF16), ((words, width), BF16)]
    if packed:
        outs.append(((2, 2, 2, n_dp // 2, WORD_ROWS, 128), BF16))
    else:
        outs += [((n_mp, width, n), F32) for n in (3 * pair, pair, wup.shape[2], wup.shape[2])]
    outs.append(((2, width), F32))
    hid = wup.shape[2]
    n_sem = 2 * (n_dp - 1) + 4 * 3
    vm = pl.BlockSpec(memory_space=pltpu.VMEM)
    args = (word_vec, onehot, place, segments, cotangent, gains, *slices, *wholes)
    shapes = [
        (wqkv.shape, BF16), (wout.shape, BF16), (wup.shape, BF16), (wdown.shape, BF16),
        ((n_dp, cap, width), BF16), ((n_dp, cap, width), BF16), ((n_mp * words, 128), F32),
        ((words, width), F32), ((2, words, width), BF16), ((1, words, 1), F32),
        ((n_mp, words, 3 * pair), BF16), ((n_mp, words, 3 * pair), BF16), ((n_mp, 2, n_mp * words, words), BF16),
        ((n_mp, words, pair), BF16), ((n_mp, words, pair), BF16),
        ((n_mp, words, hid), BF16), ((n_mp, words, hid), BF16), ((n_mp, words, hid), F32), ((words, width), F32),
        ((n_mp, words, pair), BF16), ((n_mp, words, pair), BF16), ((n_mp * words, pair), F32), ((n_mp * words, pair), F32),
        ((n_mp, words, 3 * pair), BF16), ((n_mp, words, 3 * pair), BF16), ((n_dp, cap, width), BF16), ((n_dp, cap, width), BF16),
    ]
    return pl.pallas_call(
        functools.partial(word_body, n_dp, cap, packed),
        in_specs=[vm] * (len(args) - 8) + [pl.BlockSpec(memory_space=pl.ANY)] * 8,
        out_specs=[vm] * len(outs),
        out_shape=[jax.ShapeDtypeStruct(s, d) for s, d in outs],
        scratch_shapes=[pltpu.VMEM(s, d) for s, d in shapes]
        + [pltpu.SemaphoreType.DMA((n_sem,)), pltpu.SemaphoreType.DMA((n_sem,)), pltpu.SemaphoreType.DMA((4, 4))],
        compiler_params=pltpu.CompilerParams(collective_id=0, has_side_effects=True, vmem_limit_bytes=VMEM_LIMIT),
        name="word_layer",
    )(*args)


def plain_reduce(char_parts, char_gains, word_parts, word_gains):
    *char_mats, gain_rows, pool_rows = char_parts
    gain_sums = jnp.sum(gain_rows, 1) / char_gains.astype(F32)
    small = lax.psum((gain_sums, jnp.sum(pool_rows, 0), word_gains), ("dp", "mp"))
    mats = []
    for grad in char_mats:
        part = lax.psum_scatter(grad, "dp", scatter_dimension=0, tiled=True)
        part = lax.psum_scatter(part.astype(BF16), "mp", scatter_dimension=1, tiled=True)
        mats.append(part.astype(F32))
    words = []
    for grad in word_parts:
        part = lax.psum_scatter(grad, "dp", scatter_dimension=1, tiled=True)
        words.append(lax.psum_scatter(part, "mp", scatter_dimension=0, tiled=False))
    qkv, out, up, down = words
    qkv = jnp.transpose(qkv.reshape(qkv.shape[0], 3, -1), (1, 0, 2))
    return (*mats, qkv, out.T, up, down.T, *small)


def per_device(
    char_input,
    char_counts,
    word_source,
    segment_ids,
    cotangent,
    char_norm_gains,
    char_qkv,
    char_out,
    char_up,
    char_down,
    pool_vector,
    char_proj,
    word_norm_gains,
    word_qkv,
    word_out,
    word_up,
    word_down,
):
    groups = lax.axis_size("dp")
    char_weights = (
        char_norm_gains, char_qkv, char_out, char_up, char_down, pool_vector.reshape(1, -1), char_proj
    )
    slices = (
        jnp.transpose(word_qkv, (1, 0, 2)).reshape(word_qkv.shape[1], -1), word_out, word_up, word_down,
    )
    word_vec, *kept = char_forward(
        groups, char_input, char_counts.reshape(-1, 1), *char_weights,
        word_source.reshape(1, -1), segment_ids.reshape(1, -1), slices,
    )
    char_kept, (onehot, place, segments, *word_weights) = kept[:12], kept[12:]
    output, d_word, *word_parts, word_gains = word_layer(
        groups, word_vec, onehot, place, segments, cotangent, word_norm_gains, slices, word_weights
    )
    fused = groups == 8
    d_chars, *char_parts = char_backward(
        groups, d_word, char_kept, *char_weights, word_parts[0] if fused else None, word_gains
    )
    if fused:
        grads = unpack_grads(*char_parts)
    else:
        grads = plain_reduce(char_parts, char_norm_gains, word_parts, word_gains)
    *mats, grad_char_gains, grad_pool, grad_word_gains = grads
    return (output, d_chars, *mats, grad_char_gains, grad_pool.reshape(-1), grad_word_gains)


def solution(mesh):
    placed = (
        P(("dp", "mp"), None),
        P(("dp", "mp")),
        P(("dp", "mp")),
        P(("dp", "mp")),
        P(("dp", "mp"), None),
        P(),
        P(),
        P(),
        P(),
        P(),
        P(),
        P(),
        P(),
        P(None, None, "mp"),
        P("mp", None),
        P(None, "mp"),
        P("mp", None),
    )
    return jax.shard_map(
        per_device,
        mesh=mesh,
        in_specs=placed,
        out_specs=(
            P(("dp", "mp"), None),
            P(("dp", "mp"), None),
            P("dp", "mp"),
            P("dp", "mp"),
            P("dp", "mp"),
            P("dp", "mp"),
            P("dp", "mp"),
            P(None, "dp", "mp"),
            P("mp", "dp"),
            P("dp", "mp"),
            P("mp", "dp"),
            P(),
            P(),
            P(),
        ),
        check_vma=False,
    )
```

```python
import functools
import jax
import jax.numpy as jnp
from jax import lax
from jax.experimental import pallas as pl
from jax.experimental.pallas import tpu as pltpu
from jax.sharding import PartitionSpec as P

HEADS = 8
CHARS = 16
CHAR_HEADS = 4
EPSILON = 1e-05
NEGATIVE = -1e30
GELU_A = 0.7978845608028654
GELU_B = 0.044715
F32 = jnp.float32
BF16 = jnp.bfloat16
MESH = pl.DeviceIdType.MESH
VMEM_LIMIT = 62 * 1024 * 1024
STEP_WORDS = 64
HIDDEN_CUT = 256


def dot_nn(left, right):
    return jnp.dot(left, right, preferred_element_type=F32)


def dot_nt(left, right):
    return lax.dot_general(left, right, (((1,), (1,)), ((), ())), preferred_element_type=F32)


def dot_tn(left, right):
    return lax.dot_general(left, right, (((0,), (0,)), ((), ())), preferred_element_type=F32)


def as_column(row):
    return jnp.transpose(jnp.broadcast_to(row.astype(F32), (128, row.shape[1])))


def head_stack(values, heads, factor):
    width = values.shape[1] // heads
    lane = lax.broadcasted_iota(jnp.int32, (1, values.shape[1]), 1) // width
    return jnp.concatenate(
        [values * jnp.where(lane == h, factor, 0.0).astype(values.dtype) for h in range(heads)], 0
    )


def gelu_both(hidden):
    c = lambda value: jnp.asarray(value, hidden.dtype)
    square = hidden * hidden
    tanh = jnp.tanh(hidden * (c(GELU_A) + c(GELU_A * GELU_B) * square))
    half = c(0.5) + c(0.5) * tanh
    slope = half + (c(0.5) * hidden) * (c(1.0) - tanh * tanh) * (c(GELU_A) + c(3.0 * GELU_A * GELU_B) * square)
    return hidden * half, slope


def norm_fwd(values, gain):
    mean = jnp.mean(values, -1, keepdims=True)
    centered = values - mean
    rstd = lax.rsqrt(jnp.mean(centered * centered, -1, keepdims=True) + EPSILON)
    return (centered * rstd * gain).astype(BF16), rstd


def norm_bwd(dn, n, rstd, gain):
    n = n.astype(F32)
    d1 = dn * gain
    dnn = dn * n
    m1 = jnp.mean(d1, -1, keepdims=True)
    m2 = jnp.mean(dnn, -1, keepdims=True)
    return rstd * (d1 - m1 - n * (1.0 / gain) * m2), dnn


def coordinates():
    dp, mp = lax.axis_index("dp"), lax.axis_index("mp")
    return dp // 2, dp % 2, mp // 2, mp % 2


def device_of(z, x, y, core):
    return (z * 2 + x, y * 2 + core)


def remote_copy(src, dst, ssem, rsem, slot, peer):
    return pltpu.make_async_remote_copy(
        src_ref=src, dst_ref=dst, send_sem=ssem.at[slot], recv_sem=rsem.at[slot],
        device_id=peer, device_id_type=MESH,
    )


class WeightGather:
    def __init__(self, slices, wholes, ssem, rsem):
        self.slices, self.wholes, self.ssem, self.rsem = slices, wholes, ssem, rsem
        self.z, self.x, self.y, self.core = coordinates()
        self.mp = self.y * 2 + self.core
        self.across = (1 - self.y) * 2 + self.core

    @staticmethod
    def half(ref, axis, which):
        rows = ref.shape[axis] // 2
        return ref.at[(slice(None),) * axis + (pl.ds(pl.multiple_of(which * rows, rows), rows),)]

    def copy(self, i, kind):
        z, x, y, core = self.z, self.x, self.y, self.core
        piece, whole = self.slices[i], self.wholes[i]
        axis = len(piece.shape) - 2
        far = whole.at[self.across]
        if kind == "far":
            src, dst = self.half(piece, axis, x), self.half(whole.at[self.mp], axis, x)
            peer = device_of(z, x, 1 - y, core)
        elif kind == "near":
            src, dst, peer = piece, whole.at[self.mp], device_of(z, x, y, 1 - core)
        else:
            which = 1 - x if kind == "late" else x
            src = dst = self.half(far, axis, which)
            peer = device_of(z, 1 - x, y, core) if kind == "side" else device_of(z, x, y, 1 - core)
        slot = i * 5 + ("far", "near", "side", "early", "late").index(kind)
        return remote_copy(src, dst, self.ssem, self.rsem, slot, peer)

    def peers(self):
        z, x, y, core = self.z, self.x, self.y, self.core
        return [device_of(z, x, 1 - y, core), device_of(z, x, y, 1 - core), device_of(z, 1 - x, y, core)]

    def begin(self):
        for i in range(len(self.slices)):
            self.copy(i, "far").start()
        for i in range(len(self.slices)):
            self.copy(i, "near").start()

    def pass_on(self, i):
        self.copy(i, "far").wait()
        self.copy(i, "side").start()
        self.copy(i, "early").start()

    def pass_last(self, i):
        self.copy(i, "side").wait()
        self.copy(i, "late").start()

    def finish(self):
        for i in range(len(self.slices)):
            for kind in ("near", "early", "late"):
                self.copy(i, kind).wait()


def char_fwd_body(
    n_dp, cap,
    x_ref, cnt_ref, gains_ref, wqkv_ref, wout_ref, wup_ref, wdown_ref, pool_ref, wproj_ref,
    src_ref, seg_ref, s_qkv, s_out, s_up, s_down,
    e_ref, n1_ref, p_ref, a_ref, o_ref, n2_ref, rs1_ref, rs2_ref, act_ref, dg_ref, f_ref, aw_ref, pooled_ref,
    onehot_ref, place_ref, seg_out, g_qkv, g_out, g_up, g_down,
    cnt_col, row_send, row_got, seg_all, ssem, rsem, wsend, wrecv,
):
    step, last = pl.program_id(0), pl.num_programs(0) - 1
    dp, mp = lax.axis_index("dp"), lax.axis_index("mp")
    gather = WeightGather((s_qkv, s_out, s_up, s_down), (g_qkv, g_out, g_up, g_down), wsend, wrecv)
    mates = [mp // 2 * 2 + (mp + 1) % 2, (mp + 2) % 4, (mp // 2 * 2 + 2) % 4 + (mp + 1) % 2]
    all_words = src_ref.shape[1]
    slots = n_dp * cap
    row_copy = lambda k: remote_copy(row_send.at[k], row_got.at[k], ssem, rsem, k, (lax.rem(dp + k, n_dp), mp))
    seg_copy = lambda j: remote_copy(seg_all.at[mp], seg_all.at[mp], ssem, rsem, n_dp + j, (dp, mates[j]))

    @pl.when(step == 0)
    def _():
        barrier = pltpu.get_barrier_semaphore()
        greeted = [(lax.rem(dp + k, n_dp), mp) for k in range(1, n_dp)] + [(dp, mate) for mate in mates]
        for peer in greeted:
            pl.semaphore_signal(barrier, inc=1, device_id=peer, device_id_type=MESH)
        source = src_ref[...]
        owner = source // (all_words * 4)
        owner_c = as_column(owner)[:, 0:1]
        index_r = lax.broadcasted_iota(jnp.int32, (all_words, all_words), 0)
        index_c = lax.broadcasted_iota(jnp.int32, (all_words, all_words), 1)
        earlier = (owner_c == owner.astype(F32)) & (index_r < index_c)
        rank = jnp.sum(jnp.where(earlier, 1.0, 0.0), 0, keepdims=True).astype(jnp.int32)
        slot_of = lax.rem(owner - dp + n_dp, n_dp) * cap + rank
        at_slot = lax.broadcasted_iota(jnp.int32, (slots, all_words), 0) == slot_of
        onehot_ref[...] = jnp.where(at_slot, 1.0, 0.0).astype(BF16)
        row_mat = as_column(lax.rem(source, all_words) + 1).astype(BF16)
        row_send[...] = dot_nn(onehot_ref[...], row_mat).astype(BF16).reshape(n_dp, cap, 128)
        seg_all[mp] = jnp.broadcast_to(seg_ref[...], (8, all_words))
        cnt_col[...] = as_column(cnt_ref[...])
        pl.semaphore_wait(barrier, len(greeted))
        gather.begin()
        for k in range(1, n_dp):
            row_copy(k).start()
        for j in range(3):
            seg_copy(j).start()
        row_got[0] = row_send[0]

    @pl.when(step == 2)
    def _():
        gather.pass_on(0)
        gather.pass_on(1)

    words, wide = x_ref.shape
    width = wide // CHARS
    blocks = words // 8
    gains = gains_ref[...].astype(F32)
    counts_here = cnt_col[pl.ds(pl.multiple_of(step * words, words), words), :].astype(jnp.int32)
    pieces = []
    for g in range(words // 16):
        xt = x_ref[16 * g : 16 * g + 16, :].astype(F32)
        for half in range(2):
            for c in range(CHARS):
                pieces.append(xt[8 * half : 8 * half + 8, width * c : width * c + width])
    x = jnp.concatenate(pieces, 0)
    n1, rs1 = norm_fwd(x, gains[0:1])
    n1_ref[...] = n1
    rs1_ref[...] = rs1
    p_ref[...] = dot_nn(n1, wqkv_ref[...]).astype(BF16)
    row_w = lax.broadcasted_iota(jnp.int32, (8, 128), 0)
    lane_w = lax.broadcasted_iota(jnp.int32, (8, 128), 1) % 8
    same = row_w == lane_w
    slot = lax.broadcasted_iota(jnp.int32, (CHARS, 8, 128), 0)
    size = CHAR_HEADS * 128
    scale = (width // CHAR_HEADS) ** -0.5
    scores = []
    for b in range(blocks):
        sl = slice(128 * b, 128 * b + 128)
        scores.append(dot_nt(head_stack(p_ref[sl, width : 2 * width], CHAR_HEADS, scale), p_ref[sl, 0:width]))
    for b in range(blocks):
        here = slot < counts_here[8 * b : 8 * b + 8][None]
        st = jnp.where(here[None], scores[b].reshape(CHAR_HEADS, CHARS, 8, 128), NEGATIVE)
        e = jnp.exp(st - jnp.max(st, 1, keepdims=True))
        r = jnp.where(same[None, None], 1.0 / jnp.sum(e, 1, keepdims=True), 0.0)
        a_ref[size * b : size * b + size, :] = (e * r).reshape(size, 128).astype(BF16)
    for b in range(blocks):
        sl = slice(128 * b, 128 * b + 128)
        a = a_ref[size * b : size * b + size, :]
        o_ref[sl, :] = dot_tn(a, head_stack(p_ref[sl, 2 * width : 3 * width], CHAR_HEADS, 1.0)).astype(BF16)
    m = x + dot_nn(o_ref[...], wout_ref[...])
    n2, rs2 = norm_fwd(m, gains[1:2])
    n2_ref[...] = n2
    rs2_ref[...] = rs2

    f = m
    for j in range(0, wup_ref.shape[1], HIDDEN_CUT):
        cut = slice(j, j + HIDDEN_CUT)
        act, slope = gelu_both(dot_nn(n2, wup_ref[:, cut]).astype(BF16))
        act_ref[:, cut] = act
        dg_ref[:, cut] = slope
        f = f + dot_nn(act, wdown_ref[cut, :])
    f_ref[...] = f.astype(BF16)
    t = jnp.sum(f * pool_ref[...].astype(F32).reshape(1, width), -1, keepdims=True).reshape(blocks, CHARS, 8, 1)
    counts = counts_here[:, 0:1].reshape(blocks, 1, 8, 1)
    t = jnp.where(lax.broadcasted_iota(jnp.int32, t.shape, 1) < counts, t, NEGATIVE)
    et = jnp.exp(t - jnp.max(t, 1, keepdims=True))
    aw = et / jnp.sum(et, 1, keepdims=True)
    aw_ref[...] = aw.reshape(words * CHARS, 1)
    pooled = jnp.sum(aw * f.reshape(blocks, CHARS, 8, width), 1).reshape(words, width).astype(BF16)
    pooled_ref[...] = pooled
    e_ref[...] = dot_nn(pooled, wproj_ref[...]).astype(BF16)

    @pl.when(step == 2)
    def _():
        gather.pass_on(2)

    @pl.when(step == last)
    def _():
        gather.pass_on(3)
        for i in range(3):
            gather.pass_last(i)
        for k in range(1, n_dp):
            row_copy(k).wait()
        for j in range(3):
            seg_copy(j).wait()
        at_row = row_got[...].reshape(slots, 128)[:, 0:1].astype(F32) - 1.0
        lanes = lax.broadcasted_iota(jnp.int32, (slots, all_words), 1).astype(F32)
        place_ref[...] = jnp.where(lanes == at_row, 1.0, 0.0).astype(BF16)
        seg_out[...] = seg_all[...]
        gather.pass_last(3)
        gather.finish()


def char_forward(n_dp, x, counts, gains, wqkv, wout, wup, wdown, pool, wproj, source, segments, slices):
    words, wide = x.shape
    width = wide // CHARS
    rows = words * CHARS
    step_rows = STEP_WORDS * CHARS
    cap = -(-2 * words // n_dp // 16) * 16
    slots = n_dp * cap
    full = lambda arr: pl.BlockSpec(arr.shape, lambda i: (0,) * arr.ndim)
    blk = lambda n, w: pl.BlockSpec((n, w), lambda i: (i, 0))
    hid = wup.shape[1]
    dw = wproj.shape[1]
    outs = [
        (words, STEP_WORDS, dw, BF16), (rows, step_rows, width, BF16), (rows, step_rows, 3 * width, BF16),
        (rows * CHAR_HEADS, step_rows * CHAR_HEADS, 128, BF16), (rows, step_rows, width, BF16),
        (rows, step_rows, width, BF16), (rows, step_rows, 1, F32), (rows, step_rows, 1, F32),
        (rows, step_rows, hid, BF16), (rows, step_rows, hid, BF16), (rows, step_rows, width, BF16),
        (rows, step_rows, 1, F32), (words, STEP_WORDS, width, BF16),
    ]
    fixed = [((slots, words), BF16), ((slots, words), BF16), ((4, 8, words), jnp.int32)]
    any_spec = pl.BlockSpec(memory_space=pl.ANY)
    return pl.pallas_call(
        functools.partial(char_fwd_body, n_dp, cap),
        grid=(words // STEP_WORDS,),
        in_specs=[blk(STEP_WORDS, wide)]
        + [full(w) for w in (counts, gains, wqkv, wout, wup, wdown, pool, wproj, source, segments)]
        + [any_spec] * len(slices),
        out_specs=[blk(b, w) for _, b, w, _ in outs]
        + [pl.BlockSpec(s, lambda i, n=len(s): (0,) * n) for s, _ in fixed]
        + [any_spec] * len(slices),
        out_shape=[jax.ShapeDtypeStruct((n, w), d) for n, _, w, d in outs]
        + [jax.ShapeDtypeStruct(s, d) for s, d in fixed]
        + [jax.ShapeDtypeStruct((4, *s.shape), s.dtype) for s in slices],
        scratch_shapes=[
            pltpu.VMEM((words, 128), F32),
            pltpu.VMEM((n_dp, cap, 128), BF16), pltpu.VMEM((n_dp, cap, 128), BF16), pltpu.VMEM((4, 8, words), jnp.int32),
            pltpu.SemaphoreType.DMA((n_dp + 3,)), pltpu.SemaphoreType.DMA((n_dp + 3,)),
            pltpu.SemaphoreType.DMA((5 * len(slices),)), pltpu.SemaphoreType.DMA((5 * len(slices),)),
        ],
        compiler_params=pltpu.CompilerParams(collective_id=2, has_side_effects=True, vmem_limit_bytes=VMEM_LIMIT),
        name="char_forward",
    )(x, counts, gains, wqkv, wout, wup, wdown, pool, wproj, source, segments, *slices)


CHAR_A = 176
CHAR_B = 48
WORD_ROWS = 768
CHUNK_ROWS = 192
SEMS = 8


def fold_half(block):
    half = block.shape[0] // 2
    return jnp.concatenate([block[:half], block[half:]], 1)


def unfold_half(block):
    return jnp.concatenate([block[:, :64], block[:, 64:]], 0)


class Halving:
    def __init__(self, n_z, sent, work, got, ssem, rsem, base, order):
        self.n_z, self.sent, self.work, self.got = n_z, sent, work, got
        self.ssem, self.rsem, self.base, self.order = ssem, rsem, base, order
        self.z, self.x, self.y, self.core = coordinates()

    def copies(self, phase):
        z, x, y, core = self.z, self.x, self.y, self.core
        work = self.work
        step = "c" if phase == 0 else self.order[phase - 1]
        if step == "c":
            pairs = [(self.sent, self.got[0], device_of(z, x, y, 1 - core))]
        elif step == "y":
            src = work.at[1 - y] if phase == 1 else work.at[1 - y, x]
            pairs = [(src, self.got[phase], device_of(z, x, 1 - y, core))]
        elif step == "x":
            src = work.at[:, 1 - x] if phase == 1 else work.at[y, 1 - x]
            pairs = [(src, self.got[phase], device_of(z, 1 - x, y, core))]
        else:
            pairs = []
            for k in range(1, self.n_z):
                other = lax.rem(z + k, self.n_z)
                pairs.append((work.at[y, x, other], self.got[3].at[k - 1], device_of(other, x, y, core)))
        return [
            remote_copy(src, dst, self.ssem, self.rsem, self.base + phase + i, peer)
            for i, (src, dst, peer) in enumerate(pairs)
        ]

    def start(self, phase):
        for copy in self.copies(phase):
            copy.start()

    def finish(self, phase):
        for copy in self.copies(phase):
            copy.wait()
        x, y = self.x, self.y
        work, got = self.work, self.got[phase]
        step = "c" if phase == 0 else self.order[phase - 1]

        def add(mine, other):
            def body(i, carry):
                mine[i] = mine[i] + other[i]
                return carry
            lax.fori_loop(0, self.n_z, body, 0)

        if step == "c":
            for i in range(2):
                for j in range(2):
                    add(work.at[i, j], got.at[i, j])
        elif step == "y" and phase == 1:
            for j in range(2):
                add(work.at[y, j], got.at[j])
        elif step == "x" and phase == 1:
            for i in range(2):
                add(work.at[i, x], got.at[i])
        elif step in "yx":
            add(work.at[y, x], got)

    def advance(self, phase):
        self.finish(phase)
        self.start(phase + 1)

    def total(self):
        value = self.work[self.y, self.x, self.z].astype(F32)
        for k in range(self.n_z - 1):
            value += self.got[3][k].astype(F32)
        return value

    @staticmethod
    def got_shapes(n_z, rows, first=0):
        shapes = [(2, 2, n_z, rows, 128), (2, n_z, rows, 128), (n_z, rows, 128), (n_z - 1, rows, 128)]
        return [pltpu.VMEM(s, BF16) for s in shapes[first:]]


class GradientSums:
    def __init__(self, n_z, word_sum, refs):
        self.n_z, self.word_sum = n_z, word_sum
        abuf, bbuf, wbuf, small, sgot, ssem, rsem, lsem, *got = refs
        self.abuf, self.bbuf, self.wbuf, self.small, self.sgot = abuf, bbuf, wbuf, small, sgot
        self.ssem, self.rsem, self.lsem = ssem, rsem, lsem
        self.z, self.x, self.y, self.core = coordinates()
        self.chunks = []
        for i, order in enumerate(("xyz", "yxz", "yxz", "yxz")):
            rows = wbuf.at[:, :, :, CHUNK_ROWS * i : CHUNK_ROWS * i + CHUNK_ROWS]
            self.chunks.append(
                Halving(n_z, None, rows, [None, *got[3 * i : 3 * i + 3]], ssem, rsem, SEMS * i, order)
            )
        core = self.core
        self.parta = Halving(n_z, abuf.at[1 - core], abuf.at[core], got[12:16], ssem, rsem, 4 * SEMS, "yxz")
        self.partb = Halving(n_z, bbuf.at[1 - core], bbuf.at[core], got[16:20], ssem, rsem, 5 * SEMS, "yxz")
        self.tiny = 6 * SEMS

    @staticmethod
    def scratch(n_z):
        n_sem = 7 * SEMS
        shapes = [
            pltpu.VMEM((2, 2, 2, n_z, CHAR_A, 128), BF16), pltpu.VMEM((2, 2, 2, n_z, CHAR_B, 128), BF16),
            pltpu.VMEM((2, 2, n_z, WORD_ROWS, 128), BF16),
            pltpu.VMEM((4, 16, 128), F32), pltpu.VMEM((2 + n_z, 16, 128), F32),
            pltpu.SemaphoreType.DMA((n_sem,)), pltpu.SemaphoreType.DMA((n_sem,)), pltpu.SemaphoreType.DMA,
        ]
        for _ in range(4):
            shapes += Halving.got_shapes(n_z, CHUNK_ROWS, 1)
        return shapes + Halving.got_shapes(n_z, CHAR_A) + Halving.got_shapes(n_z, CHAR_B)

    def peers(self):
        z, x, y, core = self.z, self.x, self.y, self.core
        near = [device_of(z, x, y, 1 - core), device_of(z, x, 1 - y, core), device_of(z, 1 - x, y, core)]
        return near, [device_of(lax.rem(z + k, self.n_z), x, y, core) for k in range(1, self.n_z)]

    def begin(self):
        load = pltpu.make_async_copy(self.word_sum, self.wbuf, self.lsem)
        load.start()
        near, along = self.peers()
        barrier = pltpu.get_barrier_semaphore()
        for peer in near + along:
            pl.semaphore_signal(barrier, inc=1, device_id=peer, device_id_type=MESH)
        pl.semaphore_wait(barrier, len(near + along))
        load.wait()
        self.chunks[0].start(1)
        self.chunks[1].start(1)
        self.chunks[3].start(2)

    def pack_a(self, gup_ref, gdown_ref, gproj_ref, gout_ref):
        for d in range(2 * self.n_z):
            down = gdown_ref[128 * d : 128 * d + 128, :]
            out = gout_ref[32 * d : 32 * d + 32, :]
            for p in range(4):
                block = self.abuf.at[p % 2, p // 2, d % 2, d // 2]
                block[0:32, :] = gup_ref[32 * d : 32 * d + 32, 256 * p : 256 * p + 128].astype(BF16)
                block[32:64, :] = gup_ref[32 * d : 32 * d + 32, 256 * p + 128 : 256 * p + 256].astype(BF16)
                block[64:128, :] = fold_half(down[:, 64 * p : 64 * p + 64]).astype(BF16)
                block[128:160, :] = gproj_ref[32 * d : 32 * d + 32, 128 * p : 128 * p + 128].astype(BF16)
                block[160:176, :] = fold_half(out[:, 64 * p : 64 * p + 64]).astype(BF16)
        self.parta.start(0)

    def pack_b(self, gqkv_ref):
        for d in range(2 * self.n_z):
            qkv = gqkv_ref[32 * d : 32 * d + 32, :]
            for p in range(4):
                block = self.bbuf.at[p % 2, p // 2, d % 2, d // 2]
                own = qkv[:, 192 * p : 192 * p + 192]
                block[0:32, :] = own[:, 0:128].astype(BF16)
                block[32:48, :] = fold_half(own[:, 128:192]).astype(BF16)
        self.partb.start(0)

    def tiny_copies(self, phase):
        near, along = self.peers()
        small, sgot = self.small, self.sgot
        if phase < 3:
            return [remote_copy(small.at[phase], sgot.at[phase], self.ssem, self.rsem, self.tiny + phase, near[phase])]
        return [
            remote_copy(small.at[3], sgot.at[3 + k], self.ssem, self.rsem, self.tiny + 3 + k, peer)
            for k, peer in enumerate(along)
        ]

    def tiny_start(self, phase):
        for copy in self.tiny_copies(phase):
            copy.start()

    def tiny_finish(self, phase):
        for copy in self.tiny_copies(phase):
            copy.wait()
        small, sgot = self.small, self.sgot
        if phase < 3:
            small[phase + 1] = small[phase] + sgot[phase]
            return None
        total = small[3]
        for k in range(1, self.n_z):
            total += sgot[2 + k]
        return total


def pack_small(cgain_ref, cpool_ref, gqkv_ref, wqkv_ref, gains_ref, wgain_ref):
    gains = gains_ref[...].astype(F32)
    width = gains.shape[1]
    first = jnp.sum(gqkv_ref[...] * wqkv_ref[...].astype(F32), -1, keepdims=True)
    first = jnp.transpose(jnp.broadcast_to(first, (width, 128)))[0:1, :]
    sums = [
        first / gains[0:1], jnp.sum(cgain_ref[...], 0, keepdims=True) / gains[1:2],
        jnp.sum(cpool_ref[...], 0, keepdims=True), wgain_ref[0:1, :], wgain_ref[1:2, :],
    ]
    rows = [v[:, t : t + 128] for v in sums for t in range(0, v.shape[1], 128)]
    rows.append(jnp.zeros((2, 128), F32))
    return jnp.concatenate(rows, 0)


def finish_body(
    dx_ref, wide_ref, parta_ref, partb_ref, word_ref, small_ref,
    odx_ref, owide_ref, oqkv_ref, oout_ref, oup_ref, odown_ref, oproj_ref, owqkv_ref, owout_ref, owup_ref, owdown_ref,
    ocgain_ref, opool_ref, owgain_ref,
):
    odx_ref[...] = dx_ref[...].astype(F32)

    @pl.when(pl.program_id(0) == 0)
    def _():
        parta, partb, word, total = parta_ref[...], partb_ref[...], word_ref[...], small_ref[...]
        owide_ref[...] = wide_ref[...]
        oqkv_ref[:, 0:128] = partb[0:32]
        oqkv_ref[:, 128:192] = unfold_half(partb[32:48])
        oout_ref[...] = unfold_half(parta[160:176])
        oup_ref[:, 0:128] = parta[0:32]
        oup_ref[:, 128:256] = parta[32:64]
        odown_ref[...] = unfold_half(parta[64:128]).T
        oproj_ref[...] = parta[128:160]
        for t in range(3):
            owqkv_ref[t] = word[64 * t : 64 * t + 64]
        owout_ref[...] = word[192:256]
        for t in range(4):
            owup_ref[:, 128 * t : 128 * t + 128] = word[256 + 64 * t : 320 + 64 * t]
            owdown_ref[:, 128 * t : 128 * t + 128] = word[512 + 64 * t : 576 + 64 * t]
        for j in range(2):
            for t in range(2):
                ocgain_ref[j : j + 1, 128 * t : 128 * t + 128] = total[2 * j + t : 2 * j + t + 1]
            for t in range(4):
                owgain_ref[j : j + 1, 128 * t : 128 * t + 128] = total[6 + 4 * j + t : 7 + 4 * j + t]
        for t in range(2):
            opool_ref[:, 128 * t : 128 * t + 128] = total[4 + t : 5 + t]


def finish(d_chars, word_out, *sums):
    words, wide = d_chars.shape
    steps = words // STEP_WORDS
    full = lambda s: pl.BlockSpec(s, lambda i: (0,) * len(s))
    blk = pl.BlockSpec((STEP_WORDS, wide), lambda i: (i, 0))
    outs = [
        word_out.shape, (32, 192), (32, 64), (32, 256), (64, 128), (32, 128),
        (3, 64, 128), (64, 128), (64, 512), (64, 512), (2, 256), (1, 256), (2, 512),
    ]
    result = pl.pallas_call(
        finish_body,
        grid=(steps,),
        in_specs=[blk, full(word_out.shape)] + [full(s.shape) for s in sums],
        out_specs=[blk] + [full(s) for s in outs],
        out_shape=[jax.ShapeDtypeStruct((words, wide), F32), jax.ShapeDtypeStruct(outs[0], BF16)]
        + [jax.ShapeDtypeStruct(s, F32) for s in outs[1:]],
        compiler_params=pltpu.CompilerParams(vmem_limit_bytes=VMEM_LIMIT),
        name="finish",
    )(d_chars, word_out, *sums)
    dx, out, qkv, cout, up, down, proj, wqkv, wout, wup, wdown, cgain, pool, wgain = result
    return (out, dx, qkv, cout, up, down.T, proj, wqkv, wout.T, wup, wdown.T, cgain, pool.reshape(-1), wgain)


def char_bwd_body(
    n_dp, fused,
    de_ref, gains_ref, wqkv_ref, wout_ref, wup_ref, wdown_ref, pool_ref, wproj_ref,
    n1_ref, p_ref, a_ref, o_ref, n2_ref, rs1_ref, rs2_ref, act_ref, dg_ref, f_ref, aw_ref, pooled_ref,
    *refs,
):
    if fused:
        word_sum, wgain_ref, dx_ref, outa_ref, outb_ref, word_ref, small_ref, *refs = refs
    else:
        dx_ref, *refs = refs
        outs, refs = refs[:7], refs[7:]
    gqkv_ref, gout_ref, gup_ref, gdown_ref, gproj_ref, ggain_ref, gpool_ref, *refs = refs
    dm_ref, dp_ref, do_ref, ds_ref, *refs = refs
    step = pl.program_id(0)
    part = pl.num_programs(0) // 3
    words = de_ref.shape[0]
    width = n1_ref.shape[1]
    blocks = words // 8
    rows = words * CHARS
    size = CHAR_HEADS * 128
    gains = gains_ref[...].astype(F32)
    here = pl.ds(pl.multiple_of(lax.rem(step, part) * rows, rows), rows)
    sums = GradientSums(n_dp // 2, word_sum, refs) if fused else None
    chunks = sums.chunks if fused else None

    def at(when, act):
        if fused:
            pl.when(step == when)(act)

    @pl.when(step == 0)
    def _():
        if fused:
            sums.begin()
        for ref in (gqkv_ref, gout_ref, gup_ref, gdown_ref, gproj_ref, ggain_ref, gpool_ref):
            ref[...] = jnp.zeros_like(ref)

    def events_start():
        def second():
            chunks[3].advance(2)
            chunks[0].advance(1)
            chunks[1].advance(1)
            chunks[2].start(1)
        at(2, second)

        def third():
            chunks[3].finish(3)
            chunks[0].advance(2)
            chunks[1].advance(2)
        at(3, third)

        def fourth():
            chunks[2].advance(1)
            sums.parta.advance(0)
        at(4, fourth)

        def sixth():
            chunks[2].advance(2)
            chunks[0].finish(3)
            chunks[1].finish(3)
        at(6, sixth)

        def seventh():
            sums.parta.advance(1)
        at(7, seventh)

        def ninth():
            sums.partb.advance(0)
            sums.tiny_finish(0)
            sums.tiny_start(1)
            sums.parta.advance(2)
        at(9, ninth)

        def eleventh():
            sums.partb.advance(1)
            sums.tiny_finish(1)
            sums.tiny_start(2)
            chunks[2].finish(3)
            for i in range(4):
                word_ref[CHUNK_ROWS * i : CHUNK_ROWS * i + CHUNK_ROWS, :] = chunks[i].total()
        at(11, eleventh)

    events_start()

    @pl.when(step < part)
    def _():
        de = de_ref[...]
        gproj_ref[...] += dot_tn(pooled_ref[...], de)
        dpool = dot_nt(de, wproj_ref[...]).reshape(blocks, 1, 8, width)
        f = f_ref[...].astype(F32).reshape(blocks, CHARS, 8, width)
        aw = aw_ref[...].reshape(blocks, CHARS, 8, 1)
        g = jnp.sum(f * dpool, -1, keepdims=True)
        dt = aw * (g - jnp.sum(aw * g, 1, keepdims=True))
        gpool_ref[...] += jnp.sum((dt * f).reshape(rows // 8, 8, width), 0)
        df = (aw * dpool + dt * pool_ref[...].astype(F32).reshape(1, width)).reshape(rows, width)
        dfb = df.astype(BF16)
        n2 = n2_ref[...]
        dn2 = None
        for j in range(0, wup_ref.shape[1], HIDDEN_CUT):
            cut = slice(j, j + HIDDEN_CUT)
            gdown_ref[cut, :] += dot_tn(act_ref[:, cut], dfb)
            dh = dg_ref[:, cut] * dot_nt(dfb, wdown_ref[cut, :]).astype(BF16)
            gup_ref[:, cut] += dot_tn(n2, dh)
            term = dot_nt(dh, wup_ref[:, cut])
            dn2 = term if dn2 is None else dn2 + term
        d_norm, dnn = norm_bwd(dn2, n2, rs2_ref[...], gains[1:2])
        ggain_ref[...] += jnp.sum(dnn.reshape(rows // 8, 8, width), 0)
        dm = df + d_norm
        dm_ref[here, :] = dm
        dmb = dm.astype(BF16)
        gout_ref[...] += dot_tn(o_ref[...], dmb)
        do_ref[here, :] = dot_nt(dmb, wout_ref[...]).astype(BF16)

    at(part - 1, lambda: sums.pack_a(gup_ref, gdown_ref, gproj_ref, gout_ref))

    @pl.when((step >= part) & (step < 2 * part))
    def _():
        scale = (width // CHAR_HEADS) ** -0.5
        base = lax.rem(step, part) * rows
        spot = lambda b: pl.ds(pl.multiple_of(base + 128 * b, 128), 128)
        raw = []
        for b in range(blocks):
            sl = slice(128 * b, 128 * b + 128)
            raw.append(dot_nt(head_stack(p_ref[sl, 2 * width : 3 * width], CHAR_HEADS, 1.0), do_ref[spot(b), :]))
        for b in range(blocks):
            a = a_ref[size * b : size * b + size, :].astype(F32).reshape(CHAR_HEADS, CHARS, 8, 128)
            dpt = raw[b].reshape(CHAR_HEADS, CHARS, 8, 128)
            delta = jnp.sum(a * dpt, 1, keepdims=True)
            ds_ref[size * b : size * b + size, :] = (a * (dpt - delta)).reshape(size, 128).astype(BF16)
        for b in range(blocks):
            sl = slice(128 * b, 128 * b + 128)
            ds = ds_ref[size * b : size * b + size, :]
            k = head_stack(p_ref[sl, width : 2 * width], CHAR_HEADS, scale)
            dp_ref[spot(b), 0:width] = dot_tn(ds, k).astype(BF16)
        for b in range(blocks):
            sl = slice(128 * b, 128 * b + 128)
            cut = lambda h: ds_ref[size * b + 128 * h : size * b + 128 * h + 128, :]
            wide = jnp.concatenate([cut(h) for h in range(CHAR_HEADS)], 1)
            q = head_stack(p_ref[sl, 0:width], CHAR_HEADS, scale)
            dp_ref[spot(b), width : 2 * width] = dot_nn(wide, q).astype(BF16)
        for b in range(blocks):
            cut = lambda h: a_ref[size * b + 128 * h : size * b + 128 * h + 128, :]
            wide = jnp.concatenate([cut(h) for h in range(CHAR_HEADS)], 1)
            do = head_stack(do_ref[spot(b), :], CHAR_HEADS, 1.0)
            dp_ref[spot(b), 2 * width : 3 * width] = dot_nn(wide, do).astype(BF16)
        gqkv_ref[...] += dot_tn(n1_ref[...], dp_ref[here, :])

    def begin_b():
        sums.pack_b(gqkv_ref)
        sums.small[0] = pack_small(ggain_ref, gpool_ref, gqkv_ref, wqkv_ref, gains_ref, wgain_ref)
        sums.tiny_start(0)
    at(2 * part - 1, begin_b)

    @pl.when(step >= 2 * part)
    def _():
        dn1 = dot_nt(dp_ref[here, :], wqkv_ref[...])
        d_norm, _ = norm_bwd(dn1, n1_ref[...], rs1_ref[...], gains[0:1])
        dx = dm_ref[here, :] + d_norm
        for b in range(0, blocks, 2):
            for c in range(CHARS):
                pair = [dx[128 * i + 8 * c : 128 * i + 8 * c + 8] for i in (b, b + 1)]
                dx_ref[8 * b : 8 * b + 16, width * c : width * c + width] = jnp.concatenate(pair, 0).astype(BF16)

    def end():
        sums.partb.advance(2)
        sums.tiny_finish(2)
        sums.tiny_start(3)
        sums.parta.finish(3)
        outa_ref[...] = sums.parta.total()
        small_ref[...] = sums.tiny_finish(3)
        sums.partb.finish(3)
        outb_ref[...] = sums.partb.total()
    at(3 * part - 1, end)

    if not fused:
        @pl.when(step == 3 * part - 1)
        def _():
            for out, ref in zip(outs, (gqkv_ref, gout_ref, gup_ref, gdown_ref, gproj_ref, ggain_ref, gpool_ref)):
                out[...] = ref[...]


def char_backward(n_dp, de, kept, gains, wqkv, wout, wup, wdown, pool, wproj, word_sum, wgain):
    words = de.shape[0]
    width = wout.shape[0]
    rows = words * CHARS
    step_rows = STEP_WORDS * CHARS
    steps = words // STEP_WORDS
    fused = word_sum is not None
    full = lambda arr: pl.BlockSpec(arr.shape, lambda i: (0,) * arr.ndim)
    fixed = lambda s: pl.BlockSpec(s, lambda i: (0,) * len(s))
    first = lambda n, w: pl.BlockSpec((n, w), lambda i: (lax.min(i, steps - 1), 0))
    second = lambda n, w: pl.BlockSpec((n, w), lambda i: (lax.clamp(0, i - steps, steps - 1), 0))
    third = lambda n, w: pl.BlockSpec((n, w), lambda i: (lax.max(i - 2 * steps, 0), 0))
    twice = lambda n, w: pl.BlockSpec((n, w), lambda i: (lax.rem(lax.max(i - steps, 0), steps), 0))
    weights = (gains, wqkv, wout, wup, wdown, pool, wproj)
    when = [twice, second, second, first, first, third, first, first, first, first, first, first]
    grads = [wqkv.shape, wout.shape, wup.shape, wdown.shape, wproj.shape, (8, width), (8, width)]
    scratch = [pltpu.VMEM(s, F32) for s in grads] + [
        pltpu.VMEM((rows, width), F32), pltpu.VMEM((rows, 3 * width), BF16), pltpu.VMEM((rows, width), BF16),
        pltpu.VMEM((step_rows * CHAR_HEADS, 128), BF16),
    ]
    args = [de, *weights, *kept]
    in_specs = [first(STEP_WORDS, de.shape[1])] + [full(w) for w in weights]
    in_specs += [f(r.shape[0] // steps, r.shape[1]) for f, r in zip(when, kept)]
    params = dict(vmem_limit_bytes=VMEM_LIMIT)
    if fused:
        outs = [(CHAR_A, 128), (CHAR_B, 128), (WORD_ROWS, 128), (16, 128)]
        args += [word_sum, wgain]
        in_specs += [pl.BlockSpec(memory_space=pl.ANY), full(wgain)]
        scratch += GradientSums.scratch(n_dp // 2)
        params.update(collective_id=1, has_side_effects=True)
    else:
        outs = grads
    return pl.pallas_call(
        functools.partial(char_bwd_body, n_dp, fused),
        grid=(3 * steps,),
        in_specs=in_specs,
        out_specs=[third(STEP_WORDS, CHARS * width)] + [fixed(s) for s in outs],
        out_shape=[jax.ShapeDtypeStruct((words, CHARS * width), BF16)] + [jax.ShapeDtypeStruct(s, F32) for s in outs],
        scratch_shapes=scratch,
        compiler_params=pltpu.CompilerParams(**params),
        name="char_backward",
    )(*args)


def word_body(
    n_dp, cap, packed,
    e_ref, onehot, place, seg_all, cot_ref, gains_ref, *refs,
):
    slices, wholes, refs = refs[:4], refs[4:8], refs[8:]
    if packed:
        out_ref, de_ref, gsum_ref, ggain_ref, gbuf_ref, got_a, got_y, *refs = refs
    else:
        out_ref, de_ref, gqkv_ref, gout_ref, gup_ref, gdown_ref, ggain_ref, *refs = refs
    (
        wqkv_ref, wout_ref, wup_ref, wdown_ref, vec_send, vec_got, segc_all, rows_ref, normed, rstd_a,
        qkv_send, qkv_all, weights, o_send, o_all, act_ref, dh_ref, dact_ref, dm_ref,
        do_send, do_all, dk_acc, dv_acc, dqkv_send, dqkv_all, back_send, ret,
        ssem, rsem, lsem,
    ) = refs
    dp, mp = lax.axis_index("dp"), lax.axis_index("mp")
    n_mp = 4
    words, width = e_ref.shape
    slots = n_dp * cap
    pair = 2 * (width // HEADS)
    scale = (width // HEADS) ** -0.5
    to_dp = [(lax.rem(dp + k, n_dp), mp) for k in range(n_dp)]
    from_dp = [(lax.rem(dp + n_dp - k, n_dp), mp) for k in range(n_dp)]
    mates = [(mp // 2 * 2 + (mp + 1) % 2), (mp + 2) % 4, ((mp // 2 * 2 + 2) % 4 + (mp + 1) % 2)]
    barrier = pltpu.get_barrier_semaphore()
    for k in range(1, n_dp):
        pl.semaphore_signal(barrier, inc=1, device_id=to_dp[k], device_id_type=MESH)
    for mate in mates:
        pl.semaphore_signal(barrier, inc=1, device_id=(dp, mate), device_id_type=MESH)
    next_slot = [0]

    def send(src, dst, peer):
        slot = next_slot[0]
        next_slot[0] += 1
        copy = pltpu.make_async_remote_copy(
            src_ref=src, dst_ref=dst, send_sem=ssem.at[slot], recv_sem=rsem.at[slot],
            device_id=peer, device_id_type=MESH,
        )
        copy.start()
        return copy

    loads = []
    for i, held in ((3, wdown_ref), (0, wqkv_ref), (1, wout_ref), (2, wup_ref)):
        loads.append([])
        for j, at in enumerate([mp, *mates]):
            src = slices[i] if j == 0 else wholes[i].at[at]
            if i == 0:
                for t in range(3):
                    dst = held.at[at, :, pair * t : pair * t + pair]
                    loads[-1].append(pltpu.make_async_copy(src.at[t], dst, lsem.at[4 + t, j]))
            else:
                loads[-1].append(pltpu.make_async_copy(src, held.at[at], lsem.at[i, j]))
        for load in loads[-1]:
            load.start()
    vec_send[...] = dot_nn(onehot[...], e_ref[...]).astype(BF16).reshape(n_dp, cap, width)

    pl.semaphore_wait(barrier, n_dp - 1 + 3)
    vec_copies = [send(vec_send.at[k], vec_got.at[k], to_dp[k]) for k in range(1, n_dp)]
    vec_got[0] = vec_send[0]
    gains = gains_ref[...].astype(F32)
    cot = cot_ref[...]
    for load in loads[0]:
        load.wait()
    for p in range(n_mp):
        dact_ref[p] = dot_nt(cot, wdown_ref[p]).astype(BF16)
    for j in range(n_mp):
        segc_all[words * j : words * j + words, :] = as_column(seg_all[j, 0:1, :])
    for load in loads[1] + loads[2] + loads[3]:
        load.wait()
    for copy in vec_copies:
        copy.wait()
    rows = dot_tn(place[...], vec_got[...].reshape(slots, width))
    rows_ref[...] = rows
    n_w, rstd = norm_fwd(rows, gains[0:1])
    normed[0] = n_w
    rstd_a[0] = rstd
    qkv_copies = []
    for mate in reversed(mates):
        qkv_send[mate] = dot_nn(n_w, wqkv_ref[mate]).astype(BF16)
        qkv_copies.append(send(qkv_send.at[mate], qkv_all.at[mp], (dp, mate)))
    qkv_all[mp] = dot_nn(n_w, wqkv_ref[mp]).astype(BF16)
    for copy in qkv_copies:
        copy.wait()

    head_lane = lax.broadcasted_iota(jnp.int32, (1, pair), 1) // (pair // 2)
    head_mask = [jnp.where(head_lane == h, 1.0, 0.0).astype(BF16) for h in range(2)]
    o_copies = []
    for i in reversed(range(n_mp)):
        keys = words * (i + 1)
        q = qkv_all[i, :, 0:pair]
        k = qkv_all[0 : i + 1, :, pair : 2 * pair].reshape(keys, pair)
        v = qkv_all[0 : i + 1, :, 2 * pair : 3 * pair].reshape(keys, pair)
        same = segc_all[0:keys, 0:1] == seg_all[i, 0:1, :].astype(F32)
        key_at = lax.broadcasted_iota(jnp.int32, (keys, words), 0)
        query_at = lax.broadcasted_iota(jnp.int32, (keys, words), 1) + words * i
        allowed = same & (key_at <= query_at)
        total = None
        for h in range(2):
            st = dot_nt(k * (head_mask[h] * scale).astype(BF16), q)
            st = jnp.where(allowed, st, NEGATIVE)
            ex = jnp.exp(st - jnp.max(st, 0, keepdims=True))
            at = (ex * (1.0 / jnp.sum(ex, 0, keepdims=True))).astype(BF16)
            weights[i, h, 0:keys, :] = at
            part = dot_tn(at, v * head_mask[h])
            total = part if total is None else total + part
        o_send[i] = total.astype(BF16)
    for mate in reversed(mates):
        o_copies.append(send(o_send.at[mate], o_all.at[mp], (dp, mate)))
    o_all[mp] = o_send[mp]
    for copy in o_copies:
        copy.wait()
    attended = jnp.concatenate([o_all[p] for p in range(n_mp)], 1)
    mid = rows_ref[...] + dot_nn(attended, wout_ref[...].reshape(width, width))
    n_w2, rstd2 = norm_fwd(mid, gains[1:2])
    normed[1] = n_w2
    out = mid
    dn2 = jnp.zeros((words, width), F32)
    for p in range(n_mp):
        act, slope = gelu_both(dot_nn(n_w2, wup_ref[p]).astype(BF16))
        act_ref[p] = act
        dh = slope * dact_ref[p]
        dh_ref[p] = dh
        out = out + dot_nn(act, wdown_ref[p])
        dn2 = dn2 + dot_nt(dh, wup_ref[p])
    out_ref[...] = out.astype(BF16)
    d_norm, dnn = norm_bwd(dn2, n_w2, rstd2, gains[1:2])
    gain_b = jnp.sum(dnn, 0, keepdims=True) / gains[1:2]
    d_mid = cot.astype(F32) + d_norm
    dm_ref[...] = d_mid
    d_att = d_mid.astype(BF16)
    do_copies = []
    for mate in reversed(mates):
        do_send[mate] = dot_nt(d_att, wout_ref[mate]).astype(BF16)
        do_copies.append(send(do_send.at[mate], do_all.at[mp], (dp, mate)))
    do_all[mp] = dot_nt(d_att, wout_ref[mp]).astype(BF16)

    z, x, y, core = coordinates()

    def pair_sum(low, high):
        src = gbuf_ref.at[1 - core, :, :, :, low:high]
        return send(src, got_a.at[:, :, :, low:high], device_of(z, x, y, 1 - core))

    def pair_add(low, high):
        def add(i, carry):
            b, c, d = i // n_dp, (i // (n_dp // 2)) % 2, lax.rem(i, n_dp // 2)
            gsum_ref[b, c, d, low:high] = gbuf_ref[core, b, c, d, low:high] + got_a[b, c, d, low:high]
            return carry
        lax.fori_loop(0, 2 * n_dp, add, 0)

    def put(base, p, grad):
        if packed:
            block = words // 4
            for d in range(n_dp):
                for t in range(grad.shape[1] // 128):
                    gbuf_ref[p % 2, p // 2, d % 2, d // 2, base + block * t : base + block * t + block, :] = (
                        grad[block * d : block * d + block, 128 * t : 128 * t + 128].astype(BF16)
                    )
        else:
            ref = {0: gqkv_ref, 192: gout_ref, 256: gup_ref, 512: gdown_ref}[base]
            ref[p] = grad

    for p in range(n_mp):
        put(512, p, dot_tn(cot, act_ref[p]))
        put(256, p, dot_tn(n_w2, dh_ref[p]))
        put(192, p, dot_tn(d_att, o_all[p]))
    if packed:
        early_sum = pair_sum(CHUNK_ROWS, WORD_ROWS)
    dk_acc[...] = jnp.zeros_like(dk_acc)
    dv_acc[...] = jnp.zeros_like(dv_acc)
    for copy in do_copies:
        copy.wait()
    for i in reversed(range(n_mp)):
        keys = words * (i + 1)
        q = qkv_all[i, :, 0:pair]
        k = qkv_all[0 : i + 1, :, pair : 2 * pair].reshape(keys, pair)
        v = qkv_all[0 : i + 1, :, 2 * pair : 3 * pair].reshape(keys, pair)
        do = do_all[i]
        dq = None
        for h in range(2):
            at = weights[i, h, 0:keys, :]
            dpt = dot_nt(v * head_mask[h], do)
            af = at.astype(F32)
            delta = jnp.sum(af * dpt, 0, keepdims=True)
            ds = (af * (dpt - delta)).astype(BF16)
            scaled = (head_mask[h] * scale).astype(BF16)
            part = dot_tn(ds, k * scaled)
            dq = part if dq is None else dq + part
            dk_acc[0:keys, :] += dot_nn(ds, q * scaled)
            dv_acc[0:keys, :] += dot_nn(at, do * head_mask[h])
        dqkv_send[i, :, 0:pair] = dq.astype(BF16)
        dqkv_send[i, :, pair : 2 * pair] = dk_acc[words * i : keys, :].astype(BF16)
        dqkv_send[i, :, 2 * pair : 3 * pair] = dv_acc[words * i : keys, :].astype(BF16)
    dqkv_copies = []
    for mate in reversed(mates):
        dqkv_copies.append(send(dqkv_send.at[mate], dqkv_all.at[mp], (dp, mate)))
    dqkv_all[mp] = dqkv_send[mp]
    if packed:
        early_sum.wait()
        pair_add(CHUNK_ROWS, WORD_ROWS)
    for copy in dqkv_copies:
        copy.wait()
    if packed:
        y_sum = send(gsum_ref.at[1 - y, :, :, WORD_ROWS - CHUNK_ROWS :], got_y, device_of(z, x, 1 - y, core))
    d_normed = jnp.zeros((words, width), F32)
    for p in range(n_mp):
        d_normed = d_normed + dot_nt(dqkv_all[p], wqkv_ref[p])
    d_first, dnn = norm_bwd(d_normed, normed[0], rstd_a[0], gains[0:1])
    gain_a = jnp.sum(dnn, 0, keepdims=True) / gains[0:1]
    d_rows = (dm_ref[...] + d_first).astype(BF16)
    ggain_ref[0:1, :] = gain_a
    ggain_ref[1:2, :] = gain_b
    back_send[...] = dot_nn(place[...], d_rows).astype(BF16).reshape(n_dp, cap, width)
    back_copies = [send(back_send.at[k], ret.at[k], from_dp[k]) for k in range(1, n_dp)]
    ret[0] = back_send[0]
    for p in range(n_mp):
        put(0, p, dot_tn(normed[0], dqkv_all[p]))
    if packed:
        late_sum = pair_sum(0, CHUNK_ROWS)
        late_sum.wait()
        pair_add(0, CHUNK_ROWS)
        y_sum.wait()
        for c in range(2):
            for d in range(n_dp // 2):
                gsum_ref[y, c, d, WORD_ROWS - CHUNK_ROWS :] += got_y[c, d]
    for copy in back_copies:
        copy.wait()
    de_ref[...] = dot_tn(onehot[...], ret[...].reshape(slots, width)).astype(BF16)


def word_layer(n_dp, word_vec, onehot, place, segments, cotangent, gains, slices, wholes):
    words, width = word_vec.shape
    wqkv, wout, wup, wdown = wholes
    n_mp = wqkv.shape[0]
    cap = -(-2 * words // n_dp // 16) * 16
    slots = cap * n_dp
    pair = 2 * (width // HEADS)
    packed = n_dp == 8
    outs = [((words, width), BF16), ((words, width), BF16)]
    if packed:
        outs.append(((2, 2, n_dp // 2, WORD_ROWS, 128), BF16))
    else:
        outs += [((n_mp, width, n), F32) for n in (3 * pair, pair, wup.shape[2], wup.shape[2])]
    outs.append(((2, width), F32))
    hid = wup.shape[2]
    n_sem = 2 * (n_dp - 1) + 4 * 3 + 3
    vm = pl.BlockSpec(memory_space=pltpu.VMEM)
    args = (word_vec, onehot, place, segments, cotangent, gains, *slices, *wholes)
    shapes = [
        ((n_mp, width, 3 * pair), BF16), (wout.shape, BF16), (wup.shape, BF16), (wdown.shape, BF16),
        ((n_dp, cap, width), BF16), ((n_dp, cap, width), BF16), ((n_mp * words, 128), F32),
        ((words, width), F32), ((2, words, width), BF16), ((1, words, 1), F32),
        ((n_mp, words, 3 * pair), BF16), ((n_mp, words, 3 * pair), BF16), ((n_mp, 2, n_mp * words, words), BF16),
        ((n_mp, words, pair), BF16), ((n_mp, words, pair), BF16),
        ((n_mp, words, hid), BF16), ((n_mp, words, hid), BF16), ((n_mp, words, hid), BF16), ((words, width), F32),
        ((n_mp, words, pair), BF16), ((n_mp, words, pair), BF16), ((n_mp * words, pair), F32), ((n_mp * words, pair), F32),
        ((n_mp, words, 3 * pair), BF16), ((n_mp, words, 3 * pair), BF16), ((n_dp, cap, width), BF16), ((n_dp, cap, width), BF16),
    ]
    if packed:
        shapes = [
            ((2, 2, 2, n_dp // 2, WORD_ROWS, 128), BF16), ((2, 2, n_dp // 2, WORD_ROWS, 128), BF16),
            ((2, n_dp // 2, CHUNK_ROWS, 128), BF16), *shapes,
        ]
    return pl.pallas_call(
        functools.partial(word_body, n_dp, cap, packed),
        in_specs=[vm] * (len(args) - 8) + [pl.BlockSpec(memory_space=pl.ANY)] * 8,
        out_specs=[vm] * len(outs),
        out_shape=[jax.ShapeDtypeStruct(s, d) for s, d in outs],
        scratch_shapes=[pltpu.VMEM(s, d) for s, d in shapes]
        + [pltpu.SemaphoreType.DMA((n_sem,)), pltpu.SemaphoreType.DMA((n_sem,)), pltpu.SemaphoreType.DMA((7, 4))],
        compiler_params=pltpu.CompilerParams(collective_id=0, has_side_effects=True, vmem_limit_bytes=VMEM_LIMIT),
        name="word_layer",
    )(*args)


def plain_reduce(char_parts, char_gains, char_qkv, word_parts, word_gains):
    *char_mats, gain_rows, pool_rows = char_parts
    gain_sums = jnp.stack([jnp.sum(char_mats[0] * char_qkv.astype(F32), 1), jnp.sum(gain_rows, 0)]) / char_gains.astype(F32)
    small = lax.psum((gain_sums, jnp.sum(pool_rows, 0), word_gains), ("dp", "mp"))
    mats = []
    for grad in char_mats:
        part = lax.psum_scatter(grad, "dp", scatter_dimension=0, tiled=True)
        part = lax.psum_scatter(part.astype(BF16), "mp", scatter_dimension=1, tiled=True)
        mats.append(part.astype(F32))
    words = []
    for grad in word_parts:
        part = lax.psum_scatter(grad, "dp", scatter_dimension=1, tiled=True)
        words.append(lax.psum_scatter(part, "mp", scatter_dimension=0, tiled=False))
    qkv, out, up, down = words
    qkv = jnp.transpose(qkv.reshape(qkv.shape[0], 3, -1), (1, 0, 2))
    return (*mats, qkv, out.T, up, down.T, *small)


def per_device(
    char_input,
    char_counts,
    word_source,
    segment_ids,
    cotangent,
    char_norm_gains,
    char_qkv,
    char_out,
    char_up,
    char_down,
    pool_vector,
    char_proj,
    word_norm_gains,
    word_qkv,
    word_out,
    word_up,
    word_down,
):
    groups = lax.axis_size("dp")
    char_weights = (char_norm_gains, char_qkv, char_out, char_up, char_down, pool_vector, char_proj)
    slices = (word_qkv, word_out, word_up, word_down)
    word_vec, *kept = char_forward(
        groups, char_input, char_counts.reshape(1, -1), *char_weights,
        word_source.reshape(1, -1), segment_ids.reshape(1, -1), slices,
    )
    char_kept, (onehot, place, segments, *word_weights) = kept[:12], kept[12:]
    output, d_word, *word_parts, word_gains = word_layer(
        groups, word_vec, onehot, place, segments, cotangent, word_norm_gains, slices, word_weights
    )
    fused = groups == 8
    d_chars, *char_parts = char_backward(
        groups, d_word, char_kept, *char_weights, word_parts[0] if fused else None, word_gains
    )
    if fused:
        return finish(d_chars, output, *char_parts)
    *mats, grad_char_gains, grad_pool, grad_word_gains = plain_reduce(
        char_parts, char_norm_gains, char_qkv, word_parts, word_gains
    )
    return (output, d_chars.astype(F32), *mats, grad_char_gains, grad_pool, grad_word_gains)


def solution(mesh):
    placed = (
        P(("dp", "mp"), None),
        P(("dp", "mp")),
        P(("dp", "mp")),
        P(("dp", "mp")),
        P(("dp", "mp"), None),
        P(),
        P(),
        P(),
        P(),
        P(),
        P(),
        P(),
        P(),
        P(None, None, "mp"),
        P("mp", None),
        P(None, "mp"),
        P("mp", None),
    )
    return jax.shard_map(
        per_device,
        mesh=mesh,
        in_specs=placed,
        out_specs=(
            P(("dp", "mp"), None),
            P(("dp", "mp"), None),
            P("dp", "mp"),
            P("dp", "mp"),
            P("dp", "mp"),
            P("dp", "mp"),
            P("dp", "mp"),
            P(None, "dp", "mp"),
            P("mp", "dp"),
            P("dp", "mp"),
            P("mp", "dp"),
            P(),
            P(),
            P(),
        ),
        check_vma=False,
    )
```

```python
import functools
import jax
import jax.numpy as jnp
from jax import lax
from jax.experimental import pallas as pl
from jax.experimental.pallas import tpu as pltpu
from jax.sharding import PartitionSpec as P

HEADS = 8
CHARS = 16
CHAR_HEADS = 4
EPSILON = 1e-05
NEGATIVE = -1e30
GELU_A = 0.7978845608028654
GELU_B = 0.044715
F32 = jnp.float32
BF16 = jnp.bfloat16
MESH = pl.DeviceIdType.MESH
VMEM_LIMIT = 62 * 1024 * 1024
STEP_WORDS = 64
HIDDEN_CUT = 256


def dot_nn(left, right):
    return jnp.dot(left, right, preferred_element_type=F32)


def dot_nt(left, right):
    return lax.dot_general(left, right, (((1,), (1,)), ((), ())), preferred_element_type=F32)


def dot_tn(left, right):
    return lax.dot_general(left, right, (((0,), (0,)), ((), ())), preferred_element_type=F32)


def as_column(row):
    return jnp.transpose(jnp.broadcast_to(row.astype(F32), (128, row.shape[1])))


def head_stack(values, heads, factor):
    width = values.shape[1] // heads
    lane = lax.broadcasted_iota(jnp.int32, (1, values.shape[1]), 1) // width
    return jnp.concatenate(
        [values * jnp.where(lane == h, factor, 0.0).astype(values.dtype) for h in range(heads)], 0
    )


def gelu_both(hidden):
    c = lambda value: jnp.asarray(value, hidden.dtype)
    square = hidden * hidden
    tanh = jnp.tanh(hidden * (c(GELU_A) + c(GELU_A * GELU_B) * square))
    half = c(0.5) + c(0.5) * tanh
    slope = half + (c(0.5) * hidden) * (c(1.0) - tanh * tanh) * (c(GELU_A) + c(3.0 * GELU_A * GELU_B) * square)
    return hidden * half, slope


def norm_fwd(values, gain):
    mean = jnp.mean(values, -1, keepdims=True)
    centered = values - mean
    rstd = lax.rsqrt(jnp.mean(centered * centered, -1, keepdims=True) + EPSILON)
    return (centered * rstd * gain).astype(BF16), rstd


def norm_bwd(dn, n, rstd, gain):
    n = n.astype(F32)
    d1 = dn * gain
    dnn = dn * n
    m1 = jnp.mean(d1, -1, keepdims=True)
    m2 = jnp.mean(dnn, -1, keepdims=True)
    return rstd * (d1 - m1 - n * (1.0 / gain) * m2), dnn


def coordinates():
    dp, mp = lax.axis_index("dp"), lax.axis_index("mp")
    return dp // 2, dp % 2, mp // 2, mp % 2


def device_of(z, x, y, core):
    return (z * 2 + x, y * 2 + core)


def remote_copy(src, dst, ssem, rsem, slot, peer):
    return pltpu.make_async_remote_copy(
        src_ref=src, dst_ref=dst, send_sem=ssem.at[slot], recv_sem=rsem.at[slot],
        device_id=peer, device_id_type=MESH,
    )


class WeightGather:
    def __init__(self, slices, wholes, ssem, rsem):
        self.slices, self.wholes, self.ssem, self.rsem = slices, wholes, ssem, rsem
        self.z, self.x, self.y, self.core = coordinates()
        self.mp = self.y * 2 + self.core
        self.across = (1 - self.y) * 2 + self.core

    @staticmethod
    def half(ref, axis, which):
        rows = ref.shape[axis] // 2
        return ref.at[(slice(None),) * axis + (pl.ds(pl.multiple_of(which * rows, rows), rows),)]

    def copy(self, i, kind):
        z, x, y, core = self.z, self.x, self.y, self.core
        piece, whole = self.slices[i], self.wholes[i]
        axis = len(piece.shape) - 2
        far = whole.at[self.across]
        if kind == "far":
            src, dst = self.half(piece, axis, x), self.half(whole.at[self.mp], axis, x)
            peer = device_of(z, x, 1 - y, core)
        elif kind == "near":
            src, dst, peer = piece, whole.at[self.mp], device_of(z, x, y, 1 - core)
        else:
            which = 1 - x if kind == "late" else x
            src = dst = self.half(far, axis, which)
            peer = device_of(z, 1 - x, y, core) if kind == "side" else device_of(z, x, y, 1 - core)
        slot = i * 5 + ("far", "near", "side", "early", "late").index(kind)
        return remote_copy(src, dst, self.ssem, self.rsem, slot, peer)

    def peers(self):
        z, x, y, core = self.z, self.x, self.y, self.core
        return [device_of(z, x, 1 - y, core), device_of(z, x, y, 1 - core), device_of(z, 1 - x, y, core)]

    def begin(self):
        self.copy(0, "far").start()
        self.copy(1, "far").start()
        for i in range(len(self.slices)):
            self.copy(i, "near").start()

    def begin_far(self, i):
        self.copy(i, "far").start()

    def pass_on(self, i):
        self.copy(i, "far").wait()
        if i < len(self.slices) - 1:
            self.copy(i, "side").start()
        self.copy(i, "early").start()

    def pass_last(self, i):
        self.copy(i, "side").wait()
        self.copy(i, "late").start()

    def finish(self):
        for i in range(len(self.slices)):
            for kind in ("near", "early", "late")[: 3 - (i == len(self.slices) - 1)]:
                self.copy(i, kind).wait()


def char_fwd_body(
    n_dp, cap,
    x_ref, cnt_ref, gains_ref, wqkv_ref, wout_ref, wup_ref, wdown_ref, pool_ref,
    src_ref, seg_ref, s_qkv, s_out, s_up, s_down,
    pooled_ref, n1_ref, p_ref, a_ref, o_ref, n2_ref, rs1_ref, rs2_ref, act_ref, dg_ref, f_ref, aw_ref,
    onehot_ref, place_ref, seg_out, g_qkv, g_out, g_up, g_down,
    cnt_col, row_send, row_got, seg_all, ssem, rsem, wsend, wrecv,
):
    step, last = pl.program_id(0), pl.num_programs(0) - 1
    dp, mp = lax.axis_index("dp"), lax.axis_index("mp")
    gather = WeightGather((s_qkv, s_out, s_up, s_down), (g_qkv, g_out, g_up, g_down), wsend, wrecv)
    mates = [mp // 2 * 2 + (mp + 1) % 2, (mp + 2) % 4, (mp // 2 * 2 + 2) % 4 + (mp + 1) % 2]
    all_words = src_ref.shape[1]
    slots = n_dp * cap
    row_copy = lambda k: remote_copy(row_send.at[k], row_got.at[k], ssem, rsem, k, (lax.rem(dp + k, n_dp), mp))
    seg_copy = lambda j: remote_copy(seg_all.at[mp], seg_all.at[mp], ssem, rsem, n_dp + j, (dp, mates[j]))

    @pl.when(step == 0)
    def _():
        barrier = pltpu.get_barrier_semaphore()
        greeted = [(lax.rem(dp + k, n_dp), mp) for k in range(1, n_dp)] + [(dp, mate) for mate in mates]
        for peer in greeted:
            pl.semaphore_signal(barrier, inc=1, device_id=peer, device_id_type=MESH)
        source = src_ref[...]
        owner = source // (all_words * 4)
        owner_c = as_column(owner)[:, 0:1]
        index_r = lax.broadcasted_iota(jnp.int32, (all_words, all_words), 0)
        index_c = lax.broadcasted_iota(jnp.int32, (all_words, all_words), 1)
        earlier = (owner_c == owner.astype(F32)) & (index_r < index_c)
        rank = jnp.sum(jnp.where(earlier, 1.0, 0.0), 0, keepdims=True).astype(jnp.int32)
        slot_of = lax.rem(owner - dp + n_dp, n_dp) * cap + rank
        at_slot = lax.broadcasted_iota(jnp.int32, (slots, all_words), 0) == slot_of
        onehot_ref[...] = jnp.where(at_slot, 1.0, 0.0).astype(BF16)
        row_mat = as_column(lax.rem(source, all_words) + 1).astype(BF16)
        row_send[...] = dot_nn(onehot_ref[...], row_mat).astype(BF16).reshape(n_dp, cap, 128)
        seg_all[mp] = jnp.broadcast_to(seg_ref[...], (8, all_words))
        cnt_col[...] = as_column(cnt_ref[...])
        pl.semaphore_wait(barrier, len(greeted))
        gather.begin()
        for k in range(1, n_dp):
            row_copy(k).start()
        for j in range(3):
            seg_copy(j).start()
        row_got[0] = row_send[0]

    @pl.when(step == last)
    def _():
        gather.pass_last(0)
        gather.pass_last(1)

    words, wide = x_ref.shape
    width = wide // CHARS
    blocks = words // 8
    gains = gains_ref[...].astype(F32)
    counts_here = cnt_col[pl.ds(pl.multiple_of(step * words, words), words), :].astype(jnp.int32)
    pieces = []
    for g in range(words // 16):
        xt = x_ref[16 * g : 16 * g + 16, :].astype(F32)
        for half in range(2):
            for c in range(CHARS):
                pieces.append(xt[8 * half : 8 * half + 8, width * c : width * c + width])
    x = jnp.concatenate(pieces, 0)
    n1, rs1 = norm_fwd(x, gains[0:1])
    n1_ref[...] = n1
    rs1_ref[...] = rs1
    p_ref[...] = dot_nn(n1, wqkv_ref[...]).astype(BF16)
    row_w = lax.broadcasted_iota(jnp.int32, (8, 128), 0)
    lane_w = lax.broadcasted_iota(jnp.int32, (8, 128), 1) % 8
    same = row_w == lane_w
    slot = lax.broadcasted_iota(jnp.int32, (CHARS, 8, 128), 0)
    size = CHAR_HEADS * 128
    scale = (width // CHAR_HEADS) ** -0.5
    scores = []
    for b in range(blocks):
        sl = slice(128 * b, 128 * b + 128)
        scores.append(dot_nt(head_stack(p_ref[sl, width : 2 * width], CHAR_HEADS, scale), p_ref[sl, 0:width]))
    for b in range(blocks):
        here = slot < counts_here[8 * b : 8 * b + 8][None]
        st = jnp.where(here[None], scores[b].reshape(CHAR_HEADS, CHARS, 8, 128), NEGATIVE)
        e = jnp.exp(st - jnp.max(st, 1, keepdims=True))
        r = jnp.where(same[None, None], 1.0 / jnp.sum(e, 1, keepdims=True), 0.0)
        a_ref[size * b : size * b + size, :] = (e * r).reshape(size, 128).astype(BF16)
    for b in range(blocks):
        sl = slice(128 * b, 128 * b + 128)
        a = a_ref[size * b : size * b + size, :]
        o_ref[sl, :] = dot_tn(a, head_stack(p_ref[sl, 2 * width : 3 * width], CHAR_HEADS, 1.0)).astype(BF16)
    m = x + dot_nn(o_ref[...], wout_ref[...])
    n2, rs2 = norm_fwd(m, gains[1:2])
    n2_ref[...] = n2
    rs2_ref[...] = rs2

    @pl.when(step == 0)
    def _():
        gather.begin_far(2)

    @pl.when(step == 1)
    def _():
        gather.pass_on(0)
        gather.pass_on(1)
        gather.begin_far(3)

    @pl.when(step == 2)
    def _():
        gather.pass_on(2)

    @pl.when(step == last)
    def _():
        gather.pass_last(2)
        gather.pass_on(3)

    f = m
    for j in range(0, wup_ref.shape[1], HIDDEN_CUT):
        cut = slice(j, j + HIDDEN_CUT)
        act, slope = gelu_both(dot_nn(n2, wup_ref[:, cut]).astype(BF16))
        act_ref[:, cut] = act
        dg_ref[:, cut] = slope
        f = f + dot_nn(act, wdown_ref[cut, :])
    f_ref[...] = f.astype(BF16)
    t = jnp.sum(f * pool_ref[...].astype(F32).reshape(1, width), -1, keepdims=True).reshape(blocks, CHARS, 8, 1)
    counts = counts_here[:, 0:1].reshape(blocks, 1, 8, 1)
    t = jnp.where(lax.broadcasted_iota(jnp.int32, t.shape, 1) < counts, t, NEGATIVE)
    et = jnp.exp(t - jnp.max(t, 1, keepdims=True))
    aw = et / jnp.sum(et, 1, keepdims=True)
    aw_ref[...] = aw.reshape(words * CHARS, 1)
    pooled_ref[...] = jnp.sum(aw * f.reshape(blocks, CHARS, 8, width), 1).reshape(words, width).astype(BF16)

    @pl.when(step == last)
    def _():
        for k in range(1, n_dp):
            row_copy(k).wait()
        for j in range(3):
            seg_copy(j).wait()
        at_row = row_got[...].reshape(slots, 128)[:, 0:1].astype(F32) - 1.0
        lanes = lax.broadcasted_iota(jnp.int32, (slots, all_words), 1).astype(F32)
        place_ref[...] = jnp.where(lanes == at_row, 1.0, 0.0).astype(BF16)
        seg_out[...] = seg_all[...]
        gather.finish()


def char_forward(n_dp, x, counts, gains, wqkv, wout, wup, wdown, pool, source, segments, slices):
    words, wide = x.shape
    width = wide // CHARS
    rows = words * CHARS
    step_rows = STEP_WORDS * CHARS
    cap = -(-2 * words // n_dp // 16) * 16
    slots = n_dp * cap
    full = lambda arr: pl.BlockSpec(arr.shape, lambda i: (0,) * arr.ndim)
    blk = lambda n, w: pl.BlockSpec((n, w), lambda i: (i, 0))
    hid = wup.shape[1]
    outs = [
        (words, STEP_WORDS, width, BF16), (rows, step_rows, width, BF16), (rows, step_rows, 3 * width, BF16),
        (rows * CHAR_HEADS, step_rows * CHAR_HEADS, 128, BF16), (rows, step_rows, width, BF16),
        (rows, step_rows, width, BF16), (rows, step_rows, 1, F32), (rows, step_rows, 1, F32),
        (rows, step_rows, hid, BF16), (rows, step_rows, hid, BF16), (rows, step_rows, width, BF16),
        (rows, step_rows, 1, F32),
    ]
    fixed = [((slots, words), BF16), ((slots, words), BF16), ((4, 8, words), jnp.int32)]
    any_spec = pl.BlockSpec(memory_space=pl.ANY)
    return pl.pallas_call(
        functools.partial(char_fwd_body, n_dp, cap),
        grid=(words // STEP_WORDS,),
        in_specs=[blk(STEP_WORDS, wide)]
        + [full(w) for w in (counts, gains, wqkv, wout, wup, wdown, pool, source, segments)]
        + [any_spec] * len(slices),
        out_specs=[blk(b, w) for _, b, w, _ in outs]
        + [pl.BlockSpec(s, lambda i, n=len(s): (0,) * n) for s, _ in fixed]
        + [any_spec] * len(slices),
        out_shape=[jax.ShapeDtypeStruct((n, w), d) for n, _, w, d in outs]
        + [jax.ShapeDtypeStruct(s, d) for s, d in fixed]
        + [jax.ShapeDtypeStruct((4, *s.shape), s.dtype) for s in slices],
        scratch_shapes=[
            pltpu.VMEM((words, 128), F32),
            pltpu.VMEM((n_dp, cap, 128), BF16), pltpu.VMEM((n_dp, cap, 128), BF16), pltpu.VMEM((4, 8, words), jnp.int32),
            pltpu.SemaphoreType.DMA((n_dp + 3,)), pltpu.SemaphoreType.DMA((n_dp + 3,)),
            pltpu.SemaphoreType.DMA((5 * len(slices),)), pltpu.SemaphoreType.DMA((5 * len(slices),)),
        ],
        compiler_params=pltpu.CompilerParams(collective_id=2, has_side_effects=True, vmem_limit_bytes=VMEM_LIMIT),
        name="char_forward",
    )(x, counts, gains, wqkv, wout, wup, wdown, pool, source, segments, *slices)


CHAR_A = 144
CHAR_CUT = 80
CHAR_B = 48
WORD_ROWS = 800
CHUNK_ROWS = 192
CHUNKS = ((0, 224), (224, 416), (416, 608), (608, 800))
ROW_QKV, ROW_PROJ, ROW_OUT, ROW_UP, ROW_DOWN = 0, 192, 224, 288, 544
SEMS = 8


def fold_half(block):
    half = block.shape[0] // 2
    return jnp.concatenate([block[:half], block[half:]], 1)


def unfold_half(block):
    return jnp.concatenate([block[:, :64], block[:, 64:]], 0)


class Halving:
    def __init__(self, n_z, sent, work, got, ssem, rsem, base, order):
        self.n_z, self.sent, self.work, self.got = n_z, sent, work, got
        self.ssem, self.rsem, self.base, self.order = ssem, rsem, base, order
        self.z, self.x, self.y, self.core = coordinates()

    def copies(self, phase):
        z, x, y, core = self.z, self.x, self.y, self.core
        work = self.work
        step = "c" if phase == 0 else self.order[phase - 1]
        if step == "c":
            pairs = [(self.sent, self.got[0], device_of(z, x, y, 1 - core))]
        elif step == "y":
            src = work.at[1 - y] if phase == 1 else work.at[1 - y, x]
            pairs = [(src, self.got[phase], device_of(z, x, 1 - y, core))]
        elif step == "x":
            src = work.at[:, 1 - x] if phase == 1 else work.at[y, 1 - x]
            pairs = [(src, self.got[phase], device_of(z, 1 - x, y, core))]
        else:
            pairs = []
            for k in range(1, self.n_z):
                other = lax.rem(z + k, self.n_z)
                pairs.append((work.at[y, x, other], self.got[3].at[k - 1], device_of(other, x, y, core)))
        return [
            remote_copy(src, dst, self.ssem, self.rsem, self.base + phase + i, peer)
            for i, (src, dst, peer) in enumerate(pairs)
        ]

    def start(self, phase):
        for copy in self.copies(phase):
            copy.start()

    def finish(self, phase):
        for copy in self.copies(phase):
            copy.wait()
        x, y = self.x, self.y
        work, got = self.work, self.got[phase]
        step = "c" if phase == 0 else self.order[phase - 1]

        def add(mine, other):
            def body(i, carry):
                mine[i] = mine[i] + other[i]
                return carry
            lax.fori_loop(0, self.n_z, body, 0)

        if step == "c":
            for i in range(2):
                for j in range(2):
                    add(work.at[i, j], got.at[i, j])
        elif step == "y" and phase == 1:
            for j in range(2):
                add(work.at[y, j], got.at[j])
        elif step == "x" and phase == 1:
            for i in range(2):
                add(work.at[i, x], got.at[i])
        elif step in "yx":
            add(work.at[y, x], got)

    def advance(self, phase):
        self.finish(phase)
        self.start(phase + 1)

    def total(self):
        value = self.work[self.y, self.x, self.z].astype(F32)
        for k in range(self.n_z - 1):
            value += self.got[3][k].astype(F32)
        return value

    @staticmethod
    def got_shapes(n_z, rows, first=0):
        shapes = [(2, 2, n_z, rows, 128), (2, n_z, rows, 128), (n_z, rows, 128), (n_z - 1, rows, 128)]
        return [pltpu.VMEM(s, BF16) for s in shapes[first:]]


class DirectSum:
    def __init__(self, n_dp, buf, got_mp, held, got_dp, ssem, rsem, base):
        self.n_dp, self.buf, self.got_mp, self.held, self.got_dp = n_dp, buf, got_mp, held, got_dp
        self.ssem, self.rsem, self.base = ssem, rsem, base
        self.dp, self.mp = lax.axis_index("dp"), lax.axis_index("mp")

    def copies(self, phase):
        dp, mp, n_dp = self.dp, self.mp, self.n_dp
        make = lambda src, dst, slot, peer: remote_copy(src, dst, self.ssem, self.rsem, self.base + slot, peer)
        if phase == 0:
            to = [lax.rem(mp + k, 4) for k in range(1, 4)]
            return [make(self.buf.at[p], self.got_mp.at[k], k, (dp, p)) for k, p in enumerate(to)]
        to = [lax.rem(dp + k, n_dp) for k in range(1, n_dp)]
        return [make(self.held.at[d], self.got_dp.at[k], 3 + k, (d, mp)) for k, d in enumerate(to)]

    def start(self, phase):
        for copy in self.copies(phase):
            copy.start()

    def advance(self):
        for copy in self.copies(0):
            copy.wait()
        got, buf, mp = self.got_mp, self.buf, self.mp

        def add(d, carry):
            total = buf[mp, d].astype(F32) + got[0, d].astype(F32)
            total = total + got[1, d].astype(F32) + got[2, d].astype(F32)
            self.held[d] = total.astype(self.held.dtype)
            return carry
        lax.fori_loop(0, self.n_dp, add, 0)
        self.start(1)

    def total(self):
        for copy in self.copies(1):
            copy.wait()
        value = self.held[self.dp].astype(F32)
        for k in range(self.n_dp - 1):
            value += self.got_dp[k].astype(F32)
        return value

    @staticmethod
    def shapes(n_dp, rows, dtype):
        shapes = [(4, n_dp, rows, 128), (3, n_dp, rows, 128), (n_dp, rows, 128), (n_dp - 1, rows, 128)]
        return [pltpu.VMEM(s, dtype) for s in shapes]


class GradientSums:
    def __init__(self, n_z, word_sum, refs):
        self.n_z, self.word_sum = n_z, word_sum
        abuf, wbuf, small, sgot, ssem, rsem, lsem, *got = refs
        self.abuf, self.wbuf, self.small, self.sgot = abuf, wbuf, small, sgot
        self.ssem, self.rsem, self.lsem = ssem, rsem, lsem
        self.z, self.x, self.y, self.core = coordinates()
        self.chunks = []
        for i, order in enumerate(("yxz", "yxz", "xyz", "xyz")):
            rows = wbuf.at[:, :, :, CHUNKS[i][0] : CHUNKS[i][1]]
            self.chunks.append(
                Halving(n_z, None, rows, [None, *got[3 * i : 3 * i + 3]], ssem, rsem, SEMS * i, order)
            )
        core = self.core
        self.parts = []
        for i, (low, high, order) in enumerate(((0, CHAR_CUT, "yxz"), (CHAR_CUT, CHAR_A, "xyz"))):
            rows = abuf.at[:, :, :, :, low:high]
            at = 12 + 4 * i
            self.parts.append(
                Halving(n_z, rows.at[1 - core], rows.at[core], got[at : at + 4], ssem, rsem, (4 + i) * SEMS, order)
            )
        self.partb = DirectSum(2 * n_z, *got[20:24], ssem, rsem, 6 * SEMS)
        self.tiny = 8 * SEMS

    @staticmethod
    def scratch(n_z):
        n_sem = 10 * SEMS
        shapes = [
            pltpu.VMEM((2, 2, 2, n_z, CHAR_A, 128), BF16), pltpu.VMEM((2, 2, n_z, WORD_ROWS, 128), BF16),
            pltpu.VMEM((2, 16, 128), F32), pltpu.VMEM((2 + 2 * n_z, 16, 128), F32),
            pltpu.SemaphoreType.DMA((n_sem,)), pltpu.SemaphoreType.DMA((n_sem,)), pltpu.SemaphoreType.DMA,
        ]
        for low, high in CHUNKS:
            shapes += Halving.got_shapes(n_z, high - low, 1)
        for rows in (CHAR_CUT, CHAR_A - CHAR_CUT):
            shapes += Halving.got_shapes(n_z, rows)
        return shapes + DirectSum.shapes(2 * n_z, CHAR_B, BF16)

    def begin(self):
        load = pltpu.make_async_copy(self.word_sum, self.wbuf, self.lsem)
        load.start()
        dp, mp, n_dp = self.partb.dp, self.partb.mp, 2 * self.n_z
        peers = [(lax.rem(dp + k, n_dp), mp) for k in range(1, n_dp)] + [(dp, lax.rem(mp + k, 4)) for k in range(1, 4)]
        barrier = pltpu.get_barrier_semaphore()
        for peer in peers:
            pl.semaphore_signal(barrier, inc=1, device_id=peer, device_id_type=MESH)
        pl.semaphore_wait(barrier, len(peers))
        load.wait()
        for i, phase in enumerate((1, 2, 2, 2)):
            self.chunks[i].start(phase)

    def pack_a(self, gup_ref, gdown_ref, gout_ref):
        for d in range(2 * self.n_z):
            down = gdown_ref[128 * d : 128 * d + 128, :]
            out = gout_ref[32 * d : 32 * d + 32, :]
            for p in range(4):
                block = self.abuf.at[p % 2, p // 2, d % 2, d // 2]
                block[0:32, :] = gup_ref[32 * d : 32 * d + 32, 256 * p : 256 * p + 128].astype(BF16)
                block[32:64, :] = gup_ref[32 * d : 32 * d + 32, 256 * p + 128 : 256 * p + 256].astype(BF16)
                block[64:128, :] = fold_half(down[:, 64 * p : 64 * p + 64]).astype(BF16)
                block[128:144, :] = fold_half(out[:, 64 * p : 64 * p + 64]).astype(BF16)
        for part in self.parts:
            part.start(0)

    def pack_b(self, gqkv_ref):
        for d in range(2 * self.n_z):
            qkv = gqkv_ref[32 * d : 32 * d + 32, :]
            for p in range(4):
                own = qkv[:, 192 * p : 192 * p + 192]
                self.partb.buf[p, d, 0:32, :] = own[:, 0:128].astype(BF16)
                self.partb.buf[p, d, 32:48, :] = fold_half(own[:, 128:192]).astype(BF16)
        self.partb.start(0)

    def tiny_copies(self, phase):
        dp, mp, n_dp = self.partb.dp, self.partb.mp, 2 * self.n_z
        if phase == 0:
            peers = [(dp, lax.rem(mp + k, 4)) for k in range(1, 4)]
        else:
            peers = [(lax.rem(dp + k, n_dp), mp) for k in range(1, n_dp)]
        at = 3 * phase
        return [
            remote_copy(self.small.at[phase], self.sgot.at[at + k], self.ssem, self.rsem, self.tiny + at + k, peer)
            for k, peer in enumerate(peers)
        ]

    def tiny_start(self, phase):
        for copy in self.tiny_copies(phase):
            copy.start()

    def tiny_finish(self, phase):
        copies = self.tiny_copies(phase)
        for copy in copies:
            copy.wait()
        total = self.small[phase]
        for k in range(len(copies)):
            total += self.sgot[3 * phase + k]
        return total


def pack_small(cgain_ref, cpool_ref, gqkv_ref, wqkv_ref, gains_ref, wgain_ref):
    gains = gains_ref[...].astype(F32)
    width = gains.shape[1]
    first = jnp.sum(gqkv_ref[...] * wqkv_ref[...].astype(F32), -1, keepdims=True)
    first = jnp.transpose(jnp.broadcast_to(first, (width, 128)))[0:1, :]
    sums = [
        first / gains[0:1], jnp.sum(cgain_ref[...], 0, keepdims=True) / gains[1:2],
        jnp.sum(cpool_ref[...], 0, keepdims=True), wgain_ref[0:1, :], wgain_ref[1:2, :],
    ]
    rows = [v[:, t : t + 128] for v in sums for t in range(0, v.shape[1], 128)]
    rows.append(jnp.zeros((2, 128), F32))
    return jnp.concatenate(rows, 0)


def finish_body(
    dx_ref, wide_ref, parta_ref, partb_ref, word_ref, small_ref,
    odx_ref, owide_ref, oqkv_ref, oout_ref, oup_ref, odown_ref, oproj_ref, owqkv_ref, owout_ref, owup_ref, owdown_ref,
    ocgain_ref, opool_ref, owgain_ref,
):
    odx_ref[...] = dx_ref[...].astype(F32)

    @pl.when(pl.program_id(0) == 0)
    def _():
        parta, partb, word, total = parta_ref[...], partb_ref[...], word_ref[...], small_ref[...]
        owide_ref[...] = wide_ref[...]
        oqkv_ref[:, 0:128] = partb[0:32]
        oqkv_ref[:, 128:192] = unfold_half(partb[32:48])
        oout_ref[...] = unfold_half(parta[128:144])
        oup_ref[:, 0:128] = parta[0:32]
        oup_ref[:, 128:256] = parta[32:64]
        odown_ref[...] = unfold_half(parta[64:128]).T
        oproj_ref[...] = word[ROW_PROJ : ROW_PROJ + 32]
        for t in range(3):
            owqkv_ref[t] = word[64 * t : 64 * t + 64]
        owout_ref[...] = word[ROW_OUT : ROW_OUT + 64]
        for t in range(4):
            owup_ref[:, 128 * t : 128 * t + 128] = word[ROW_UP + 64 * t : ROW_UP + 64 * t + 64]
            owdown_ref[:, 128 * t : 128 * t + 128] = word[ROW_DOWN + 64 * t : ROW_DOWN + 64 * t + 64]
        for j in range(2):
            for t in range(2):
                ocgain_ref[j : j + 1, 128 * t : 128 * t + 128] = total[2 * j + t : 2 * j + t + 1]
            for t in range(4):
                owgain_ref[j : j + 1, 128 * t : 128 * t + 128] = total[6 + 4 * j + t : 7 + 4 * j + t]
        for t in range(2):
            opool_ref[:, 128 * t : 128 * t + 128] = total[4 + t : 5 + t]


def finish(d_chars, word_out, *sums):
    words, wide = d_chars.shape
    steps = words // STEP_WORDS
    full = lambda s: pl.BlockSpec(s, lambda i: (0,) * len(s))
    blk = pl.BlockSpec((STEP_WORDS, wide), lambda i: (i, 0))
    outs = [
        word_out.shape, (32, 192), (32, 64), (32, 256), (64, 128), (32, 128),
        (3, 64, 128), (64, 128), (64, 512), (64, 512), (2, 256), (1, 256), (2, 512),
    ]
    result = pl.pallas_call(
        finish_body,
        grid=(steps,),
        in_specs=[blk, full(word_out.shape)] + [full(s.shape) for s in sums],
        out_specs=[blk] + [full(s) for s in outs],
        out_shape=[jax.ShapeDtypeStruct((words, wide), F32), jax.ShapeDtypeStruct(outs[0], BF16)]
        + [jax.ShapeDtypeStruct(s, F32) for s in outs[1:]],
        compiler_params=pltpu.CompilerParams(vmem_limit_bytes=VMEM_LIMIT),
        name="finish",
    )(d_chars, word_out, *sums)
    dx, out, qkv, cout, up, down, proj, wqkv, wout, wup, wdown, cgain, pool, wgain = result
    return (out, dx, qkv, cout, up, down.T, proj, wqkv, wout.T, wup, wdown.T, cgain, pool.reshape(-1), wgain)


def char_bwd_body(
    n_dp, fused,
    dpool_ref, gains_ref, wqkv_ref, wout_ref, wup_ref, wdown_ref, pool_ref,
    n1_ref, p_ref, a_ref, o_ref, n2_ref, rs1_ref, rs2_ref, act_ref, dg_ref, f_ref, aw_ref,
    *refs,
):
    if fused:
        word_sum, wgain_ref, dx_ref, outa_ref, outb_ref, word_ref, small_ref, *refs = refs
    else:
        dx_ref, *refs = refs
        outs, refs = refs[:6], refs[6:]
    gqkv_ref, gout_ref, gup_ref, gdown_ref, ggain_ref, gpool_ref, *refs = refs
    dm_ref, dp_ref, do_ref, ds_ref, *refs = refs
    step = pl.program_id(0)
    part = pl.num_programs(0) // 3
    words = dpool_ref.shape[0]
    width = n1_ref.shape[1]
    blocks = words // 8
    rows = words * CHARS
    size = CHAR_HEADS * 128
    gains = gains_ref[...].astype(F32)
    here = pl.ds(pl.multiple_of(lax.rem(step, part) * rows, rows), rows)
    sums = GradientSums(n_dp // 2, word_sum, refs) if fused else None
    chunks = sums.chunks if fused else None

    def at(when, act):
        if fused:
            pl.when(step == when)(act)

    @pl.when(step == 0)
    def _():
        if fused:
            sums.begin()
        for ref in (gqkv_ref, gout_ref, gup_ref, gdown_ref, ggain_ref, gpool_ref):
            ref[...] = jnp.zeros_like(ref)

    def event(when, *moves):
        def act():
            for sum_of, phase in moves:
                if phase < 3:
                    sum_of.advance(phase)
                else:
                    sum_of.finish(3)
        at(when, act)

    if fused:
        first, other = sums.parts
        event(2, (chunks[1], 2))
        event(4, (chunks[2], 2), (chunks[3], 2), (chunks[0], 1))
        event(5, (first, 0), (other, 0))
        event(6, (chunks[0], 2))
        event(8, (first, 1), (other, 1))
        event(11, (first, 2), (other, 2))

    @pl.when(step < part)
    def _():
        dpool = dpool_ref[...].astype(F32).reshape(blocks, 1, 8, width)
        f = f_ref[...].astype(F32).reshape(blocks, CHARS, 8, width)
        aw = aw_ref[...].reshape(blocks, CHARS, 8, 1)
        g = jnp.sum(f * dpool, -1, keepdims=True)
        dt = aw * (g - jnp.sum(aw * g, 1, keepdims=True))
        gpool_ref[...] += jnp.sum((dt * f).reshape(rows // 8, 8, width), 0)
        df = (aw * dpool + dt * pool_ref[...].astype(F32).reshape(1, width)).reshape(rows, width)
        dfb = df.astype(BF16)
        n2 = n2_ref[...]
        dn2 = None
        for j in range(0, wup_ref.shape[1], HIDDEN_CUT):
            cut = slice(j, j + HIDDEN_CUT)
            gdown_ref[cut, :] += dot_tn(act_ref[:, cut], dfb)
            dh = dg_ref[:, cut] * dot_nt(dfb, wdown_ref[cut, :]).astype(BF16)
            gup_ref[:, cut] += dot_tn(n2, dh)
            term = dot_nt(dh, wup_ref[:, cut])
            dn2 = term if dn2 is None else dn2 + term
        d_norm, dnn = norm_bwd(dn2, n2, rs2_ref[...], gains[1:2])
        ggain_ref[...] += jnp.sum(dnn.reshape(rows // 8, 8, width), 0)
        dm = df + d_norm
        dm_ref[here, :] = dm
        dmb = dm.astype(BF16)
        gout_ref[...] += dot_tn(o_ref[...], dmb)
        do_ref[here, :] = dot_nt(dmb, wout_ref[...]).astype(BF16)

    at(part - 1, lambda: sums.pack_a(gup_ref, gdown_ref, gout_ref))

    @pl.when((step >= part) & (step < 2 * part))
    def _():
        scale = (width // CHAR_HEADS) ** -0.5
        base = lax.rem(step, part) * rows
        spot = lambda b: pl.ds(pl.multiple_of(base + 128 * b, 128), 128)
        raw = []
        for b in range(blocks):
            sl = slice(128 * b, 128 * b + 128)
            raw.append(dot_nt(head_stack(p_ref[sl, 2 * width : 3 * width], CHAR_HEADS, 1.0), do_ref[spot(b), :]))
        for b in range(blocks):
            a = a_ref[size * b : size * b + size, :].astype(F32).reshape(CHAR_HEADS, CHARS, 8, 128)
            dpt = raw[b].reshape(CHAR_HEADS, CHARS, 8, 128)
            delta = jnp.sum(a * dpt, 1, keepdims=True)
            ds_ref[size * b : size * b + size, :] = (a * (dpt - delta)).reshape(size, 128).astype(BF16)
        for b in range(blocks):
            sl = slice(128 * b, 128 * b + 128)
            ds = ds_ref[size * b : size * b + size, :]
            k = head_stack(p_ref[sl, width : 2 * width], CHAR_HEADS, scale)
            dp_ref[spot(b), 0:width] = dot_tn(ds, k).astype(BF16)
        for b in range(blocks):
            sl = slice(128 * b, 128 * b + 128)
            cut = lambda h: ds_ref[size * b + 128 * h : size * b + 128 * h + 128, :]
            wide = jnp.concatenate([cut(h) for h in range(CHAR_HEADS)], 1)
            q = head_stack(p_ref[sl, 0:width], CHAR_HEADS, scale)
            dp_ref[spot(b), width : 2 * width] = dot_nn(wide, q).astype(BF16)
        for b in range(blocks):
            cut = lambda h: a_ref[size * b + 128 * h : size * b + 128 * h + 128, :]
            wide = jnp.concatenate([cut(h) for h in range(CHAR_HEADS)], 1)
            do = head_stack(do_ref[spot(b), :], CHAR_HEADS, 1.0)
            dp_ref[spot(b), 2 * width : 3 * width] = dot_nn(wide, do).astype(BF16)
        gqkv_ref[...] += dot_tn(n1_ref[...], dp_ref[here, :])

    def begin_b():
        sums.pack_b(gqkv_ref)
        sums.small[0] = pack_small(ggain_ref, gpool_ref, gqkv_ref, wqkv_ref, gains_ref, wgain_ref)
        sums.tiny_start(0)
    at(2 * part - 1, begin_b)

    @pl.when(step >= 2 * part)
    def _():
        dn1 = dot_nt(dp_ref[here, :], wqkv_ref[...])
        d_norm, _ = norm_bwd(dn1, n1_ref[...], rs1_ref[...], gains[0:1])
        dx = dm_ref[here, :] + d_norm
        for b in range(0, blocks, 2):
            for c in range(CHARS):
                pair = [dx[128 * i + 8 * c : 128 * i + 8 * c + 8] for i in (b, b + 1)]
                dx_ref[8 * b : 8 * b + 16, width * c : width * c + width] = jnp.concatenate(pair, 0).astype(BF16)

    def end():
        sums.partb.advance()
        sums.small[1] = sums.tiny_finish(0)
        sums.tiny_start(1)
        for i in range(4):
            chunks[i].finish(3)
            word_ref[CHUNKS[i][0] : CHUNKS[i][1], :] = chunks[i].total()
        for i, (low, high) in enumerate(((0, CHAR_CUT), (CHAR_CUT, CHAR_A))):
            sums.parts[i].finish(3)
            outa_ref[low:high, :] = sums.parts[i].total()
        small_ref[...] = sums.tiny_finish(1)
        outb_ref[...] = sums.partb.total()
    at(3 * part - 1, end)

    if not fused:
        @pl.when(step == 3 * part - 1)
        def _():
            for out, ref in zip(outs, (gqkv_ref, gout_ref, gup_ref, gdown_ref, ggain_ref, gpool_ref)):
                out[...] = ref[...]


def char_backward(n_dp, dpool, kept, gains, wqkv, wout, wup, wdown, pool, word_sum, wgain):
    words = dpool.shape[0]
    width = wout.shape[0]
    rows = words * CHARS
    step_rows = STEP_WORDS * CHARS
    steps = words // STEP_WORDS
    fused = word_sum is not None
    full = lambda arr: pl.BlockSpec(arr.shape, lambda i: (0,) * arr.ndim)
    fixed = lambda s: pl.BlockSpec(s, lambda i: (0,) * len(s))
    first = lambda n, w: pl.BlockSpec((n, w), lambda i: (lax.min(i, steps - 1), 0))
    second = lambda n, w: pl.BlockSpec((n, w), lambda i: (lax.clamp(0, i - steps, steps - 1), 0))
    third = lambda n, w: pl.BlockSpec((n, w), lambda i: (lax.max(i - 2 * steps, 0), 0))
    twice = lambda n, w: pl.BlockSpec((n, w), lambda i: (lax.rem(lax.max(i - steps, 0), steps), 0))
    weights = (gains, wqkv, wout, wup, wdown, pool)
    when = [twice, second, second, first, first, third, first, first, first, first, first]
    grads = [wqkv.shape, wout.shape, wup.shape, wdown.shape, (8, width), (8, width)]
    scratch = [pltpu.VMEM(s, F32) for s in grads] + [
        pltpu.VMEM((rows, width), F32), pltpu.VMEM((rows, 3 * width), BF16), pltpu.VMEM((rows, width), BF16),
        pltpu.VMEM((step_rows * CHAR_HEADS, 128), BF16),
    ]
    args = [dpool, *weights, *kept]
    in_specs = [first(STEP_WORDS, width)] + [full(w) for w in weights]
    in_specs += [f(r.shape[0] // steps, r.shape[1]) for f, r in zip(when, kept)]
    params = dict(vmem_limit_bytes=VMEM_LIMIT)
    if fused:
        outs = [(CHAR_A, 128), (CHAR_B, 128), (WORD_ROWS, 128), (16, 128)]
        args += [word_sum, wgain]
        in_specs += [pl.BlockSpec(memory_space=pl.ANY), full(wgain)]
        scratch += GradientSums.scratch(n_dp // 2)
        params.update(collective_id=1, has_side_effects=True)
    else:
        outs = grads
    return pl.pallas_call(
        functools.partial(char_bwd_body, n_dp, fused),
        grid=(3 * steps,),
        in_specs=in_specs,
        out_specs=[third(STEP_WORDS, CHARS * width)] + [fixed(s) for s in outs],
        out_shape=[jax.ShapeDtypeStruct((words, CHARS * width), BF16)] + [jax.ShapeDtypeStruct(s, F32) for s in outs],
        scratch_shapes=scratch,
        compiler_params=pltpu.CompilerParams(**params),
        name="char_backward",
    )(*args)


def word_body(
    n_dp, cap, packed,
    pooled_ref, onehot, place, seg_all, cot_ref, gains_ref, wproj_ref, *refs,
):
    slices, wholes, refs = refs[:4], refs[4:8], refs[8:]
    if packed:
        out_ref, dpool_ref, gsum_ref, ggain_ref, gbuf_ref, got_a, got_x, got_y, *refs = refs
    else:
        out_ref, dpool_ref, gqkv_ref, gout_ref, gup_ref, gdown_ref, gproj_ref, ggain_ref, *refs = refs
    (
        wqkv_ref, wout_ref, wup_ref, wdown_ref, vec_send, vec_got, segc_all, pooled_rows, rows_ref, normed, rstd_a,
        qkv_send, qkv_all, weights, o_send, o_all, act_ref, dh_ref, dact_ref, dm_ref,
        do_send, do_all, dk_acc, dv_acc, dqkv_send, dqkv_all, back_send, ret,
        ssem, rsem, lsem,
    ) = refs
    dp, mp = lax.axis_index("dp"), lax.axis_index("mp")
    n_mp = 4
    words, narrow = pooled_ref.shape
    width = cot_ref.shape[1]
    slots = n_dp * cap
    pair = 2 * (width // HEADS)
    scale = (width // HEADS) ** -0.5
    to_dp = [(lax.rem(dp + k, n_dp), mp) for k in range(n_dp)]
    from_dp = [(lax.rem(dp + n_dp - k, n_dp), mp) for k in range(n_dp)]
    mates = [(mp // 2 * 2 + (mp + 1) % 2), (mp + 2) % 4, ((mp // 2 * 2 + 2) % 4 + (mp + 1) % 2)]
    barrier = pltpu.get_barrier_semaphore()
    for k in range(1, n_dp):
        pl.semaphore_signal(barrier, inc=1, device_id=to_dp[k], device_id_type=MESH)
    for mate in mates:
        pl.semaphore_signal(barrier, inc=1, device_id=(dp, mate), device_id_type=MESH)
    next_slot = [0]

    def send(src, dst, peer):
        slot = next_slot[0]
        next_slot[0] += 1
        copy = pltpu.make_async_remote_copy(
            src_ref=src, dst_ref=dst, send_sem=ssem.at[slot], recv_sem=rsem.at[slot],
            device_id=peer, device_id_type=MESH,
        )
        copy.start()
        return copy

    z, x, y, core = coordinates()
    loads = []
    for i, held in ((3, wdown_ref), (0, wqkv_ref), (1, wout_ref), (2, wup_ref)):
        loads.append([])
        for j, at in enumerate([mp, *mates]):
            src = slices[i] if j == 0 else wholes[i].at[at]
            if i == 0:
                for t in range(3):
                    dst = held.at[at, :, pair * t : pair * t + pair]
                    loads[-1].append(pltpu.make_async_copy(src.at[t], dst, lsem.at[4 + t, j]))
            elif i == 3 and j > 1:
                src, dst = WeightGather.half(src, 0, x), WeightGather.half(held.at[at], 0, x)
                loads[-1].append(pltpu.make_async_copy(src, dst, lsem.at[i, j]))
            else:
                loads[-1].append(pltpu.make_async_copy(src, held.at[at], lsem.at[i, j]))
        for load in loads[-1]:
            load.start()
    vec_send[...] = dot_nn(onehot[...], pooled_ref[...]).astype(BF16).reshape(n_dp, cap, narrow)

    pl.semaphore_wait(barrier, n_dp - 1 + 3)
    vec_copies = [send(vec_send.at[k], vec_got.at[k], to_dp[k]) for k in range(1, n_dp)]
    source = WeightGather.half(wholes[3].at[mates[1]], 0, x)
    down_side = send(source, WeightGather.half(wdown_ref.at[mates[1]], 0, x), device_of(z, 1 - x, y, core))
    vec_got[0] = vec_send[0]
    gains = gains_ref[...].astype(F32)
    cot = cot_ref[...]
    for j in range(n_mp):
        segc_all[words * j : words * j + words, :] = as_column(seg_all[j, 0:1, :])
    for load in loads[1] + loads[2] + loads[3]:
        load.wait()
    for copy in vec_copies:
        copy.wait()
    pooled_rows[...] = dot_tn(place[...], vec_got[...].reshape(slots, narrow)).astype(BF16)
    rows = dot_nn(pooled_rows[...], wproj_ref[...]).astype(BF16).astype(F32)
    rows_ref[...] = rows
    n_w, rstd = norm_fwd(rows, gains[0:1])
    normed[0] = n_w
    rstd_a[0] = rstd
    qkv_copies = []
    for mate in reversed(mates):
        qkv_send[mate] = dot_nn(n_w, wqkv_ref[mate]).astype(BF16)
        qkv_copies.append(send(qkv_send.at[mate], qkv_all.at[mp], (dp, mate)))
    qkv_all[mp] = dot_nn(n_w, wqkv_ref[mp]).astype(BF16)
    down_side.wait()
    source = WeightGather.half(wdown_ref.at[mates[1]], 0, 1 - x)
    down_late = send(source, source, (dp, mates[0]))
    for copy in qkv_copies:
        copy.wait()

    low_lane = lax.broadcasted_iota(jnp.int32, (1, pair), 1) < pair // 2
    low_mask = jnp.where(low_lane, 1.0, 0.0).astype(BF16)
    high_mask = jnp.where(low_lane, 0.0, 1.0).astype(BF16)

    def heads(v, factor):
        return jnp.concatenate([v * (low_mask * factor).astype(BF16), v * (high_mask * factor).astype(BF16)], 0)

    o_copies = []
    for i in reversed(range(n_mp)):
        keys = words * (i + 1)
        q = heads(qkv_all[i, :, 0:pair], scale)
        k = qkv_all[0 : i + 1, :, pair : 2 * pair].reshape(keys, pair)
        v = qkv_all[0 : i + 1, :, 2 * pair : 3 * pair].reshape(keys, pair)
        same = segc_all[0:keys, 0:1] == seg_all[i, 0:1, :].astype(F32)
        key_at = lax.broadcasted_iota(jnp.int32, (keys, words), 0)
        query_at = lax.broadcasted_iota(jnp.int32, (keys, words), 1) + words * i
        allowed = same & (key_at <= query_at)
        st = jnp.where(jnp.concatenate([allowed, allowed], 1), dot_nt(k, q), NEGATIVE)
        ex = jnp.exp(st - jnp.max(st, 0, keepdims=True))
        at = (ex * (1.0 / jnp.sum(ex, 0, keepdims=True))).astype(BF16)
        weights[i, 0:keys, :] = at
        both = dot_tn(at, v)
        o_send[i] = jnp.where(low_lane, both[:words], both[words:]).astype(BF16)
    for mate in reversed(mates):
        o_copies.append(send(o_send.at[mate], o_all.at[mp], (dp, mate)))
    o_all[mp] = o_send[mp]
    down_late.wait()
    for load in loads[0]:
        load.wait()
    for p in range(n_mp):
        dact_ref[p] = dot_nt(cot, wdown_ref[p]).astype(BF16)
    for copy in o_copies:
        copy.wait()
    attended = jnp.concatenate([o_all[p] for p in range(n_mp)], 1)
    mid = rows_ref[...] + dot_nn(attended, wout_ref[...].reshape(width, width))
    n_w2, rstd2 = norm_fwd(mid, gains[1:2])
    normed[1] = n_w2
    out = mid
    dn2 = jnp.zeros((words, width), F32)
    for p in range(n_mp):
        act, slope = gelu_both(dot_nn(n_w2, wup_ref[p]).astype(BF16))
        act_ref[p] = act
        dh = slope * dact_ref[p]
        dh_ref[p] = dh
        out = out + dot_nn(act, wdown_ref[p])
        dn2 = dn2 + dot_nt(dh, wup_ref[p])
    out_ref[...] = out.astype(BF16)
    d_norm, dnn = norm_bwd(dn2, n_w2, rstd2, gains[1:2])
    gain_b = jnp.sum(dnn, 0, keepdims=True) / gains[1:2]
    d_mid = cot.astype(F32) + d_norm
    dm_ref[...] = d_mid
    d_att = d_mid.astype(BF16)
    do_copies = []
    for mate in reversed(mates):
        do_send[mate] = dot_nt(d_att, wout_ref[mate]).astype(BF16)
        do_copies.append(send(do_send.at[mate], do_all.at[mp], (dp, mate)))
    do_all[mp] = dot_nt(d_att, wout_ref[mp]).astype(BF16)

    def pair_sum(i):
        low, high = CHUNKS[i]
        src = gbuf_ref.at[1 - core, :, :, :, low:high]
        return send(src, got_a.at[:, :, :, low:high], device_of(z, x, y, 1 - core))

    def pair_add(i):
        low, high = CHUNKS[i]

        def add(i, carry):
            b, c, d = i // n_dp, (i // (n_dp // 2)) % 2, lax.rem(i, n_dp // 2)
            gsum_ref[b, c, d, low:high] = gbuf_ref[core, b, c, d, low:high] + got_a[b, c, d, low:high]
            return carry
        lax.fori_loop(0, 2 * n_dp, add, 0)

    def x_sum(i):
        low, high = CHUNKS[i]
        return send(gsum_ref.at[:, 1 - x, :, low:high], got_x.at[i - 2], device_of(z, 1 - x, y, core))

    def x_add(i):
        low, high = CHUNKS[i]
        for b in range(2):
            for d in range(n_dp // 2):
                gsum_ref[b, x, d, low:high] += got_x[i - 2, b, d]

    def y_sum(i):
        low, high = CHUNKS[i]
        return send(gsum_ref.at[1 - y, :, :, low:high], got_y, device_of(z, x, 1 - y, core))

    def y_add(i):
        low, high = CHUNKS[i]
        for c in range(2):
            for d in range(n_dp // 2):
                gsum_ref[y, c, d, low:high] += got_y[c, d]

    def put(base, p, grad):
        if packed:
            block = grad.shape[0] // n_dp
            for d in range(n_dp):
                for t in range(grad.shape[1] // 128):
                    gbuf_ref[p % 2, p // 2, d % 2, d // 2, base + block * t : base + block * t + block, :] = (
                        grad[block * d : block * d + block, 128 * t : 128 * t + 128].astype(BF16)
                    )
        elif base == ROW_PROJ:
            gproj_ref[:, 128 * p : 128 * p + 128] = grad
        else:
            ref = {ROW_QKV: gqkv_ref, ROW_OUT: gout_ref, ROW_UP: gup_ref, ROW_DOWN: gdown_ref}[base]
            ref[p] = grad

    for p in range(n_mp):
        put(ROW_DOWN, p, dot_tn(cot, act_ref[p]))
    if packed:
        pair_three = pair_sum(3)
    for p in range(n_mp):
        put(ROW_UP, p, dot_tn(n_w2, dh_ref[p]))
    if packed:
        pair_two = pair_sum(2)
    for p in range(n_mp):
        put(ROW_OUT, p, dot_tn(d_att, o_all[p]))
    if packed:
        pair_one = pair_sum(1)
        pair_three.wait()
        pair_add(3)
        x_three = x_sum(3)
    dk_acc[...] = jnp.zeros_like(dk_acc)
    dv_acc[...] = jnp.zeros_like(dv_acc)
    for copy in do_copies:
        copy.wait()
    for i in reversed(range(n_mp)):
        keys = words * (i + 1)
        q = qkv_all[i, :, 0:pair]
        k = qkv_all[0 : i + 1, :, pair : 2 * pair].reshape(keys, pair)
        v = qkv_all[0 : i + 1, :, 2 * pair : 3 * pair].reshape(keys, pair)
        do = heads(do_all[i], 1.0)
        at = weights[i, 0:keys, :]
        af = at.astype(F32)
        dpt = dot_nt(v, do)
        ds = (af * (dpt - jnp.sum(af * dpt, 0, keepdims=True))).astype(BF16)
        both = dot_tn(ds, k)
        dq = jnp.where(low_lane, both[:words], both[words:]) * scale
        dk_acc[0:keys, :] += dot_nn(ds, heads(q, scale))
        dv_acc[0:keys, :] += dot_nn(at, do)
        dqkv_send[i, :, 0:pair] = dq.astype(BF16)
        dqkv_send[i, :, pair : 2 * pair] = dk_acc[words * i : keys, :].astype(BF16)
        dqkv_send[i, :, 2 * pair : 3 * pair] = dv_acc[words * i : keys, :].astype(BF16)
    if packed:
        pair_two.wait()
        pair_add(2)
        x_two = x_sum(2)
    dqkv_copies = []
    for mate in reversed(mates):
        dqkv_copies.append(send(dqkv_send.at[mate], dqkv_all.at[mp], (dp, mate)))
    dqkv_all[mp] = dqkv_send[mp]
    if packed:
        pair_one.wait()
        pair_add(1)
    for copy in dqkv_copies:
        copy.wait()
    if packed:
        y_one = y_sum(1)
    d_normed = jnp.zeros((words, width), F32)
    for p in range(n_mp):
        d_normed = d_normed + dot_nt(dqkv_all[p], wqkv_ref[p])
    d_first, dnn = norm_bwd(d_normed, normed[0], rstd_a[0], gains[0:1])
    gain_a = jnp.sum(dnn, 0, keepdims=True) / gains[0:1]
    d_rows = (dm_ref[...] + d_first).astype(BF16)
    ggain_ref[0:1, :] = gain_a
    ggain_ref[1:2, :] = gain_b
    d_pooled = dot_nt(d_rows, wproj_ref[...]).astype(BF16)
    back_send[...] = dot_nn(place[...], d_pooled).astype(BF16).reshape(n_dp, cap, narrow)
    back_copies = [send(back_send.at[k], ret.at[k], from_dp[k]) for k in range(1, n_dp)]
    ret[0] = back_send[0]
    grad_proj = dot_tn(pooled_rows[...], d_rows)
    for p in range(n_mp):
        put(ROW_QKV, p, dot_tn(normed[0], dqkv_all[p]))
        put(ROW_PROJ, p, grad_proj[:, 128 * p : 128 * p + 128])
    if packed:
        pair_zero = pair_sum(0)
        x_three.wait()
        x_add(3)
        x_two.wait()
        x_add(2)
        pair_zero.wait()
        pair_add(0)
    for copy in back_copies:
        copy.wait()
    dpool_ref[...] = dot_tn(onehot[...], ret[...].reshape(slots, narrow)).astype(BF16)
    if packed:
        y_one.wait()
        y_add(1)


def word_layer(n_dp, pooled, onehot, place, segments, cotangent, gains, wproj, slices, wholes):
    words, narrow = pooled.shape
    width = cotangent.shape[1]
    wqkv, wout, wup, wdown = wholes
    n_mp = wqkv.shape[0]
    cap = -(-2 * words // n_dp // 16) * 16
    slots = cap * n_dp
    pair = 2 * (width // HEADS)
    packed = n_dp == 8
    outs = [((words, width), BF16), ((words, narrow), BF16)]
    if packed:
        outs.append(((2, 2, n_dp // 2, WORD_ROWS, 128), BF16))
    else:
        outs += [((n_mp, width, n), F32) for n in (3 * pair, pair, wup.shape[2], wup.shape[2])]
        outs.append(((narrow, width), F32))
    outs.append(((2, width), F32))
    hid = wup.shape[2]
    n_sem = 2 * (n_dp - 1) + 4 * 3 + 3 + 7
    vm = pl.BlockSpec(memory_space=pltpu.VMEM)
    args = (pooled, onehot, place, segments, cotangent, gains, wproj, *slices, *wholes)
    shapes = [
        ((n_mp, width, 3 * pair), BF16), (wout.shape, BF16), (wup.shape, BF16), (wdown.shape, BF16),
        ((n_dp, cap, narrow), BF16), ((n_dp, cap, narrow), BF16), ((n_mp * words, 128), F32), ((words, narrow), BF16),
        ((words, width), F32), ((2, words, width), BF16), ((1, words, 1), F32),
        ((n_mp, words, 3 * pair), BF16), ((n_mp, words, 3 * pair), BF16), ((n_mp, n_mp * words, 2 * words), BF16),
        ((n_mp, words, pair), BF16), ((n_mp, words, pair), BF16),
        ((n_mp, words, hid), BF16), ((n_mp, words, hid), BF16), ((n_mp, words, hid), BF16), ((words, width), F32),
        ((n_mp, words, pair), BF16), ((n_mp, words, pair), BF16), ((n_mp * words, pair), F32), ((n_mp * words, pair), F32),
        ((n_mp, words, 3 * pair), BF16), ((n_mp, words, 3 * pair), BF16), ((n_dp, cap, narrow), BF16), ((n_dp, cap, narrow), BF16),
    ]
    if packed:
        shapes = [
            ((2, 2, 2, n_dp // 2, WORD_ROWS, 128), BF16), ((2, 2, n_dp // 2, WORD_ROWS, 128), BF16),
            ((2, 2, n_dp // 2, CHUNK_ROWS, 128), BF16), ((2, n_dp // 2, CHUNK_ROWS, 128), BF16), *shapes,
        ]
    return pl.pallas_call(
        functools.partial(word_body, n_dp, cap, packed),
        in_specs=[vm] * (len(args) - 8) + [pl.BlockSpec(memory_space=pl.ANY)] * 8,
        out_specs=[vm] * len(outs),
        out_shape=[jax.ShapeDtypeStruct(s, d) for s, d in outs],
        scratch_shapes=[pltpu.VMEM(s, d) for s, d in shapes]
        + [pltpu.SemaphoreType.DMA((n_sem,)), pltpu.SemaphoreType.DMA((n_sem,)), pltpu.SemaphoreType.DMA((7, 4))],
        compiler_params=pltpu.CompilerParams(collective_id=0, has_side_effects=True, vmem_limit_bytes=VMEM_LIMIT),
        name="word_layer",
    )(*args)


def plain_reduce(char_parts, char_gains, char_qkv, word_parts, word_gains):
    *char_mats, gain_rows, pool_rows = char_parts
    gain_sums = jnp.stack([jnp.sum(char_mats[0] * char_qkv.astype(F32), 1), jnp.sum(gain_rows, 0)]) / char_gains.astype(F32)
    small = lax.psum((gain_sums, jnp.sum(pool_rows, 0), word_gains), ("dp", "mp"))
    mats = []
    for grad in char_mats:
        part = lax.psum_scatter(grad, "dp", scatter_dimension=0, tiled=True)
        part = lax.psum_scatter(part.astype(BF16), "mp", scatter_dimension=1, tiled=True)
        mats.append(part.astype(F32))
    words = []
    for grad in word_parts:
        part = lax.psum_scatter(grad, "dp", scatter_dimension=1, tiled=True)
        words.append(lax.psum_scatter(part, "mp", scatter_dimension=0, tiled=False))
    qkv, out, up, down = words
    qkv = jnp.transpose(qkv.reshape(qkv.shape[0], 3, -1), (1, 0, 2))
    return (*mats, qkv, out.T, up, down.T, *small)


def per_device(
    char_input,
    char_counts,
    word_source,
    segment_ids,
    cotangent,
    char_norm_gains,
    char_qkv,
    char_out,
    char_up,
    char_down,
    pool_vector,
    char_proj,
    word_norm_gains,
    word_qkv,
    word_out,
    word_up,
    word_down,
):
    groups = lax.axis_size("dp")
    char_weights = (char_norm_gains, char_qkv, char_out, char_up, char_down, pool_vector)
    slices = (word_qkv, word_out, word_up, word_down)
    pooled, *kept = char_forward(
        groups, char_input, char_counts.reshape(1, -1), *char_weights,
        word_source.reshape(1, -1), segment_ids.reshape(1, -1), slices,
    )
    char_kept, (onehot, place, segments, *word_weights) = kept[:11], kept[11:]
    output, d_pooled, *word_parts, word_gains = word_layer(
        groups, pooled, onehot, place, segments, cotangent, word_norm_gains, char_proj, slices, word_weights
    )
    fused = groups == 8
    d_chars, *char_parts = char_backward(
        groups, d_pooled, char_kept, *char_weights, word_parts[0] if fused else None, word_gains
    )
    if fused:
        return finish(d_chars, output, *char_parts)
    *word_parts, grad_proj = word_parts
    char_parts = (*char_parts[:4], grad_proj, *char_parts[4:])
    *mats, grad_char_gains, grad_pool, grad_word_gains = plain_reduce(
        char_parts, char_norm_gains, char_qkv, word_parts, word_gains
    )
    return (output, d_chars.astype(F32), *mats, grad_char_gains, grad_pool, grad_word_gains)


def solution(mesh):
    placed = (
        P(("dp", "mp"), None),
        P(("dp", "mp")),
        P(("dp", "mp")),
        P(("dp", "mp")),
        P(("dp", "mp"), None),
        P(),
        P(),
        P(),
        P(),
        P(),
        P(),
        P(),
        P(),
        P(None, None, "mp"),
        P("mp", None),
        P(None, "mp"),
        P("mp", None),
    )
    return jax.shard_map(
        per_device,
        mesh=mesh,
        in_specs=placed,
        out_specs=(
            P(("dp", "mp"), None),
            P(("dp", "mp"), None),
            P("dp", "mp"),
            P("dp", "mp"),
            P("dp", "mp"),
            P("dp", "mp"),
            P("dp", "mp"),
            P(None, "dp", "mp"),
            P("mp", "dp"),
            P("dp", "mp"),
            P("mp", "dp"),
            P(),
            P(),
            P(),
        ),
        check_vma=False,
    )
```

```python
import functools
import jax
import jax.numpy as jnp
from jax import lax
from jax.experimental import pallas as pl
from jax.experimental.pallas import tpu as pltpu
from jax.sharding import PartitionSpec as P

HEADS = 8
CHARS = 16
CHAR_HEADS = 4
EPSILON = 1e-05
NEGATIVE = -1e30
GELU_A = 0.7978845608028654
GELU_B = 0.044715
F32 = jnp.float32
BF16 = jnp.bfloat16
MESH = pl.DeviceIdType.MESH
VMEM_LIMIT = 62 * 1024 * 1024
STEP_WORDS = 64
HIDDEN_CUT = 256


def dot_nn(left, right):
    return jnp.dot(left, right, preferred_element_type=F32)


def dot_nt(left, right):
    return lax.dot_general(left, right, (((1,), (1,)), ((), ())), preferred_element_type=F32)


def dot_tn(left, right):
    return lax.dot_general(left, right, (((0,), (0,)), ((), ())), preferred_element_type=F32)


def as_column(row):
    return jnp.transpose(jnp.broadcast_to(row.astype(F32), (128, row.shape[1])))


def head_stack(values, heads, factor):
    width = values.shape[1] // heads
    lane = lax.broadcasted_iota(jnp.int32, (1, values.shape[1]), 1) // width
    return jnp.concatenate(
        [values * jnp.where(lane == h, factor, 0.0).astype(values.dtype) for h in range(heads)], 0
    )


def gelu_both(hidden):
    c = lambda value: jnp.asarray(value, hidden.dtype)
    square = hidden * hidden
    tanh = jnp.tanh(hidden * (c(GELU_A) + c(GELU_A * GELU_B) * square))
    half = c(0.5) + c(0.5) * tanh
    slope = half + (c(0.5) * hidden) * (c(1.0) - tanh * tanh) * (c(GELU_A) + c(3.0 * GELU_A * GELU_B) * square)
    return hidden * half, slope


def norm_fwd(values, gain):
    mean = jnp.mean(values, -1, keepdims=True)
    centered = values - mean
    rstd = lax.rsqrt(jnp.mean(centered * centered, -1, keepdims=True) + EPSILON)
    return (centered * rstd * gain).astype(BF16), rstd


def norm_bwd(dn, n, rstd, gain):
    n = n.astype(F32)
    d1 = dn * gain
    dnn = dn * n
    m1 = jnp.mean(d1, -1, keepdims=True)
    m2 = jnp.mean(dnn, -1, keepdims=True)
    return rstd * (d1 - m1 - n * (1.0 / gain) * m2), dnn


def coordinates():
    dp, mp = lax.axis_index("dp"), lax.axis_index("mp")
    return dp // 2, dp % 2, mp // 2, mp % 2


def device_of(z, x, y, core):
    return (z * 2 + x, y * 2 + core)


def remote_copy(src, dst, ssem, rsem, slot, peer):
    return pltpu.make_async_remote_copy(
        src_ref=src, dst_ref=dst, send_sem=ssem.at[slot], recv_sem=rsem.at[slot],
        device_id=peer, device_id_type=MESH,
    )


class WeightGather:
    def __init__(self, slices, wholes, ssem, rsem):
        self.slices, self.wholes, self.ssem, self.rsem = slices, wholes, ssem, rsem
        self.z, self.x, self.y, self.core = coordinates()
        self.mp = self.y * 2 + self.core
        self.across = (1 - self.y) * 2 + self.core

    @staticmethod
    def half(ref, axis, which):
        rows = ref.shape[axis] // 2
        return ref.at[(slice(None),) * axis + (pl.ds(pl.multiple_of(which * rows, rows), rows),)]

    def copy(self, i, kind):
        z, x, y, core = self.z, self.x, self.y, self.core
        piece, whole = self.slices[i], self.wholes[i]
        axis = len(piece.shape) - 2
        far = whole.at[self.across]
        if kind == "far":
            src, dst = self.half(piece, axis, x), self.half(whole.at[self.mp], axis, x)
            peer = device_of(z, x, 1 - y, core)
        elif kind == "near":
            src, dst, peer = piece, whole.at[self.mp], device_of(z, x, y, 1 - core)
        else:
            which = 1 - x if kind == "late" else x
            src = dst = self.half(far, axis, which)
            peer = device_of(z, 1 - x, y, core) if kind == "side" else device_of(z, x, y, 1 - core)
        slot = i * 5 + ("far", "near", "side", "early", "late").index(kind)
        return remote_copy(src, dst, self.ssem, self.rsem, slot, peer)

    def peers(self):
        z, x, y, core = self.z, self.x, self.y, self.core
        return [device_of(z, x, 1 - y, core), device_of(z, x, y, 1 - core), device_of(z, 1 - x, y, core)]

    def begin(self):
        self.copy(0, "far").start()
        self.copy(1, "far").start()
        for i in range(len(self.slices)):
            self.copy(i, "near").start()

    def begin_far(self, i):
        self.copy(i, "far").start()

    def pass_on(self, i):
        self.copy(i, "far").wait()
        if i < len(self.slices) - 1:
            self.copy(i, "side").start()
        self.copy(i, "early").start()

    def pass_last(self, i):
        self.copy(i, "side").wait()
        self.copy(i, "late").start()

    def finish(self):
        for i in range(len(self.slices)):
            for kind in ("near", "early", "late")[: 3 - (i == len(self.slices) - 1)]:
                self.copy(i, kind).wait()


def char_fwd_body(
    n_dp, cap,
    x_ref, cnt_ref, gains_ref, wqkv_ref, wout_ref, wup_ref, wdown_ref, pool_ref,
    src_ref, seg_ref, s_qkv, s_out, s_up, s_down,
    pooled_ref, early_ref, late_ref, p_any, a_any, act_any,
    onehot_ref, place_ref, seg_out, g_qkv, g_out, g_up, g_down,
    cnt_col, row_send, row_got, seg_all, ssem, rsem, wsend, wrecv, p_buf, a_buf, act_buf, osem,
):
    step, last = pl.program_id(0), pl.num_programs(0) - 1
    dp, mp = lax.axis_index("dp"), lax.axis_index("mp")
    gather = WeightGather((s_qkv, s_out, s_up, s_down), (g_qkv, g_out, g_up, g_down), wsend, wrecv)
    mates = [mp // 2 * 2 + (mp + 1) % 2, (mp + 2) % 4, (mp // 2 * 2 + 2) % 4 + (mp + 1) % 2]
    all_words = src_ref.shape[1]
    slots = n_dp * cap
    row_copy = lambda k: remote_copy(row_send.at[k], row_got.at[k], ssem, rsem, k, (lax.rem(dp + k, n_dp), mp))
    seg_copy = lambda j: remote_copy(seg_all.at[mp], seg_all.at[mp], ssem, rsem, n_dp + j, (dp, mates[j]))

    @pl.when(step == 0)
    def _():
        barrier = pltpu.get_barrier_semaphore()
        greeted = [(lax.rem(dp + k, n_dp), mp) for k in range(1, n_dp)] + [(dp, mate) for mate in mates]
        for peer in greeted:
            pl.semaphore_signal(barrier, inc=1, device_id=peer, device_id_type=MESH)
        source = src_ref[...]
        owner = source // (all_words * 4)
        owner_c = as_column(owner)[:, 0:1]
        index_r = lax.broadcasted_iota(jnp.int32, (all_words, all_words), 0)
        index_c = lax.broadcasted_iota(jnp.int32, (all_words, all_words), 1)
        earlier = (owner_c == owner.astype(F32)) & (index_r < index_c)
        rank = jnp.sum(jnp.where(earlier, 1.0, 0.0), 0, keepdims=True).astype(jnp.int32)
        slot_of = lax.rem(owner - dp + n_dp, n_dp) * cap + rank
        at_slot = lax.broadcasted_iota(jnp.int32, (slots, all_words), 0) == slot_of
        onehot_ref[...] = jnp.where(at_slot, 1.0, 0.0).astype(BF16)
        row_mat = as_column(lax.rem(source, all_words) + 1).astype(BF16)
        row_send[...] = dot_nn(onehot_ref[...], row_mat).astype(BF16).reshape(n_dp, cap, 128)
        seg_all[mp] = jnp.broadcast_to(seg_ref[...], (8, all_words))
        cnt_col[...] = as_column(cnt_ref[...])
        pl.semaphore_wait(barrier, len(greeted))
        gather.begin()
        for k in range(1, n_dp):
            row_copy(k).start()
        for j in range(3):
            seg_copy(j).start()
        row_got[0] = row_send[0]

    @pl.when(step == last)
    def _():
        gather.pass_last(0)
        gather.pass_last(1)

    words, wide = x_ref.shape
    width = wide // CHARS
    blocks = words // 8
    gains = gains_ref[...].astype(F32)
    counts_here = cnt_col[pl.ds(pl.multiple_of(step * words, words), words), :].astype(jnp.int32)
    pieces = []
    for g in range(words // 16):
        xt = x_ref[16 * g : 16 * g + 16, :].astype(F32)
        for half in range(2):
            for c in range(CHARS):
                pieces.append(xt[8 * half : 8 * half + 8, width * c : width * c + width])
    x = jnp.concatenate(pieces, 0)
    hid = wup_ref.shape[1]
    rows = words * CHARS
    cuts = range(0, hid, HIDDEN_CUT)
    held = lax.rem(step, 2)
    p_ref, a_ref, act_ref = p_buf.at[held], a_buf.at[held], act_buf.at[held]

    def out_copies(of):
        slot = lax.rem(of, 2)
        at = lambda n: pl.ds(pl.multiple_of(of * n, n), n)
        heads = rows * CHAR_HEADS
        copies = [
            pltpu.make_async_copy(p_buf.at[slot], p_any.at[at(rows)], osem.at[slot, 0]),
            pltpu.make_async_copy(a_buf.at[slot], a_any.at[at(heads)], osem.at[slot, 1]),
        ]
        for i in range(2 * hid // HIDDEN_CUT):
            cut = pl.ds(HIDDEN_CUT * i, HIDDEN_CUT)
            copies.append(pltpu.make_async_copy(act_buf.at[slot, :, cut], act_any.at[at(rows), cut], osem.at[slot, 2 + i]))
        return copies

    leaving = out_copies(step)

    @pl.when(step >= 2)
    def _():
        for copy in out_copies(step - 2):
            copy.wait()

    n1, rs1 = norm_fwd(x, gains[0:1])
    lane = lax.broadcasted_iota(jnp.int32, (rows, 128), 1)
    late_ref[:, 0:width] = n1
    late_ref[:, width:] = jnp.where(lane == 0, rs1, 0.0).astype(BF16)
    p_ref[...] = dot_nn(n1, wqkv_ref[...]).astype(BF16)
    row_w = lax.broadcasted_iota(jnp.int32, (8, 128), 0)
    lane_w = lax.broadcasted_iota(jnp.int32, (8, 128), 1) % 8
    same = row_w == lane_w
    slot = lax.broadcasted_iota(jnp.int32, (CHARS, 8, 128), 0)
    size = CHAR_HEADS * 128
    scale = (width // CHAR_HEADS) ** -0.5
    scores = []
    for b in range(blocks):
        sl = slice(128 * b, 128 * b + 128)
        scores.append(dot_nt(head_stack(p_ref[sl, width : 2 * width], CHAR_HEADS, scale), p_ref[sl, 0:width]))
    for b in range(blocks):
        here = slot < counts_here[8 * b : 8 * b + 8][None]
        st = jnp.where(here[None], scores[b].reshape(CHAR_HEADS, CHARS, 8, 128), NEGATIVE)
        e = jnp.exp(st - jnp.max(st, 1, keepdims=True))
        r = jnp.where(same[None, None], 1.0 / jnp.sum(e, 1, keepdims=True), 0.0)
        a_ref[size * b : size * b + size, :] = (e * r).reshape(size, 128).astype(BF16)
    for b in range(blocks):
        sl = slice(128 * b, 128 * b + 128)
        a = a_ref[size * b : size * b + size, :]
        early_ref[sl, 0:width] = dot_tn(a, head_stack(p_ref[sl, 2 * width : 3 * width], CHAR_HEADS, 1.0)).astype(BF16)
    leaving[0].start()
    leaving[1].start()
    m = x + dot_nn(early_ref[:, 0:width], wout_ref[...])
    n2, rs2 = norm_fwd(m, gains[1:2])
    early_ref[:, width : 2 * width] = n2

    @pl.when(step == 0)
    def _():
        gather.begin_far(2)

    @pl.when(step == 1)
    def _():
        gather.pass_on(0)
        gather.pass_on(1)
        gather.begin_far(3)

    @pl.when(step == 2)
    def _():
        gather.pass_on(2)

    @pl.when(step == last)
    def _():
        gather.pass_last(2)
        gather.pass_on(3)

    f = m
    for i, j in enumerate(cuts):
        cut = slice(j, j + HIDDEN_CUT)
        act, slope = gelu_both(dot_nn(n2, wup_ref[:, cut]).astype(BF16))
        act_ref[:, cut] = act
        act_ref[:, hid + j : hid + j + HIDDEN_CUT] = slope
        leaving[2 + i].start()
        leaving[2 + len(cuts) + i].start()
        f = f + dot_nn(act, wdown_ref[cut, :])
    early_ref[:, 2 * width : 3 * width] = f.astype(BF16)
    t = jnp.sum(f * pool_ref[...].astype(F32).reshape(1, width), -1, keepdims=True).reshape(blocks, CHARS, 8, 1)
    counts = counts_here[:, 0:1].reshape(blocks, 1, 8, 1)
    t = jnp.where(lax.broadcasted_iota(jnp.int32, t.shape, 1) < counts, t, NEGATIVE)
    et = jnp.exp(t - jnp.max(t, 1, keepdims=True))
    aw = et / jnp.sum(et, 1, keepdims=True)
    early_ref[:, 3 * width :] = jnp.where(lane == 0, rs2, aw.reshape(rows, 1)).astype(BF16)
    pooled_ref[...] = jnp.sum(aw * f.reshape(blocks, CHARS, 8, width), 1).reshape(words, width).astype(BF16)

    @pl.when(step == last)
    def _():
        for k in range(1, n_dp):
            row_copy(k).wait()
        for j in range(3):
            seg_copy(j).wait()
        at_row = row_got[...].reshape(slots, 128)[:, 0:1].astype(F32) - 1.0
        lanes = lax.broadcasted_iota(jnp.int32, (slots, all_words), 1).astype(F32)
        place_ref[...] = jnp.where(lanes == at_row, 1.0, 0.0).astype(BF16)
        seg_out[...] = seg_all[...]
        gather.finish()
        for copy in out_copies(step - 1) + leaving:
            copy.wait()


def char_forward(n_dp, x, counts, gains, wqkv, wout, wup, wdown, pool, source, segments, slices):
    words, wide = x.shape
    width = wide // CHARS
    rows = words * CHARS
    step_rows = STEP_WORDS * CHARS
    cap = -(-2 * words // n_dp // 16) * 16
    slots = n_dp * cap
    full = lambda arr: pl.BlockSpec(arr.shape, lambda i: (0,) * arr.ndim)
    blk = lambda n, w: pl.BlockSpec((n, w), lambda i: (i, 0))
    hid = wup.shape[1]
    outs = [
        (words, STEP_WORDS, width), (rows, step_rows, 3 * width + 128), (rows, step_rows, width + 128),
        (rows, None, 3 * width), (rows * CHAR_HEADS, None, 128), (rows, None, 2 * hid),
    ]
    fixed = [((slots, words), BF16), ((slots, words), BF16), ((4, 8, words), jnp.int32)]
    any_spec = pl.BlockSpec(memory_space=pl.ANY)
    return pl.pallas_call(
        functools.partial(char_fwd_body, n_dp, cap),
        grid=(words // STEP_WORDS,),
        in_specs=[blk(STEP_WORDS, wide)]
        + [full(w) for w in (counts, gains, wqkv, wout, wup, wdown, pool, source, segments)]
        + [any_spec] * len(slices),
        out_specs=[blk(b, w) if b else any_spec for _, b, w in outs]
        + [pl.BlockSpec(s, lambda i, n=len(s): (0,) * n) for s, _ in fixed]
        + [any_spec] * len(slices),
        out_shape=[jax.ShapeDtypeStruct((n, w), BF16) for n, _, w in outs]
        + [jax.ShapeDtypeStruct(s, d) for s, d in fixed]
        + [jax.ShapeDtypeStruct((4, *s.shape), s.dtype) for s in slices],
        scratch_shapes=[
            pltpu.VMEM((words, 128), F32),
            pltpu.VMEM((n_dp, cap, 128), BF16), pltpu.VMEM((n_dp, cap, 128), BF16), pltpu.VMEM((4, 8, words), jnp.int32),
            pltpu.SemaphoreType.DMA((n_dp + 3,)), pltpu.SemaphoreType.DMA((n_dp + 3,)),
            pltpu.SemaphoreType.DMA((5 * len(slices),)), pltpu.SemaphoreType.DMA((5 * len(slices),)),
            pltpu.VMEM((2, step_rows, 3 * width), BF16), pltpu.VMEM((2, step_rows * CHAR_HEADS, 128), BF16),
            pltpu.VMEM((2, step_rows, 2 * hid), BF16),
            pltpu.SemaphoreType.DMA((2, 2 + 2 * (hid // HIDDEN_CUT))),
        ],
        compiler_params=pltpu.CompilerParams(collective_id=2, has_side_effects=True, vmem_limit_bytes=VMEM_LIMIT),
        name="char_forward",
    )(x, counts, gains, wqkv, wout, wup, wdown, pool, source, segments, *slices)


CHAR_A = 144
CHAR_CUT = 80
CHAR_B = 48
WORD_ROWS = 800
CHUNK_ROWS = 192
CHUNKS = ((0, 192), (192, 224), (224, 416), (416, 608), (608, 800))
ROW_QKV, ROW_PROJ, ROW_OUT, ROW_UP, ROW_DOWN = 0, 192, 224, 288, 544
SEMS = 8


def fold_half(block):
    half = block.shape[0] // 2
    return jnp.concatenate([block[:half], block[half:]], 1)


def unfold_half(block):
    return jnp.concatenate([block[:, :64], block[:, 64:]], 0)


class Halving:
    def __init__(self, n_z, sent, work, got, ssem, rsem, base, order):
        self.n_z, self.sent, self.work, self.got = n_z, sent, work, got
        self.ssem, self.rsem, self.base, self.order = ssem, rsem, base, order
        self.z, self.x, self.y, self.core = coordinates()

    def copies(self, phase):
        z, x, y, core = self.z, self.x, self.y, self.core
        work = self.work
        step = "c" if phase == 0 else self.order[phase - 1]
        if step == "c":
            pairs = [(self.sent, self.got[0], device_of(z, x, y, 1 - core))]
        elif step == "y":
            src = work.at[1 - y] if phase == 1 else work.at[1 - y, x]
            pairs = [(src, self.got[phase], device_of(z, x, 1 - y, core))]
        elif step == "x":
            src = work.at[:, 1 - x] if phase == 1 else work.at[y, 1 - x]
            pairs = [(src, self.got[phase], device_of(z, 1 - x, y, core))]
        else:
            pairs = []
            for k in range(1, self.n_z):
                other = lax.rem(z + k, self.n_z)
                pairs.append((work.at[y, x, other], self.got[3].at[k - 1], device_of(other, x, y, core)))
        return [
            remote_copy(src, dst, self.ssem, self.rsem, self.base + phase + i, peer)
            for i, (src, dst, peer) in enumerate(pairs)
        ]

    def start(self, phase):
        for copy in self.copies(phase):
            copy.start()

    def finish(self, phase):
        for copy in self.copies(phase):
            copy.wait()
        x, y = self.x, self.y
        work, got = self.work, self.got[phase]
        step = "c" if phase == 0 else self.order[phase - 1]

        def add(mine, other):
            def body(i, carry):
                mine[i] = mine[i] + other[i]
                return carry
            lax.fori_loop(0, self.n_z, body, 0)

        if step == "c":
            for i in range(2):
                for j in range(2):
                    add(work.at[i, j], got.at[i, j])
        elif step == "y" and phase == 1:
            for j in range(2):
                add(work.at[y, j], got.at[j])
        elif step == "x" and phase == 1:
            for i in range(2):
                add(work.at[i, x], got.at[i])
        elif step in "yx":
            add(work.at[y, x], got)

    def advance(self, phase):
        self.finish(phase)
        self.start(phase + 1)

    def total(self):
        value = self.work[self.y, self.x, self.z].astype(F32)
        for k in range(self.n_z - 1):
            value += self.got[3][k].astype(F32)
        return value

    @staticmethod
    def got_shapes(n_z, rows, first=0):
        shapes = [(2, 2, n_z, rows, 128), (2, n_z, rows, 128), (n_z, rows, 128), (n_z - 1, rows, 128)]
        return [pltpu.VMEM(s, BF16) for s in shapes[first:]]


class DirectSum:
    def __init__(self, n_dp, buf, got_mp, held, got_dp, ssem, rsem, base):
        self.n_dp, self.buf, self.got_mp, self.held, self.got_dp = n_dp, buf, got_mp, held, got_dp
        self.ssem, self.rsem, self.base = ssem, rsem, base
        self.dp, self.mp = lax.axis_index("dp"), lax.axis_index("mp")

    def copies(self, phase):
        dp, mp, n_dp = self.dp, self.mp, self.n_dp
        make = lambda src, dst, slot, peer: remote_copy(src, dst, self.ssem, self.rsem, self.base + slot, peer)
        if phase == 0:
            to = [lax.rem(mp + k, 4) for k in range(1, 4)]
            return [make(self.buf.at[p], self.got_mp.at[k], k, (dp, p)) for k, p in enumerate(to)]
        to = [lax.rem(dp + k, n_dp) for k in range(1, n_dp)]
        return [make(self.held.at[d], self.got_dp.at[k], 3 + k, (d, mp)) for k, d in enumerate(to)]

    def start(self, phase):
        for copy in self.copies(phase):
            copy.start()

    def advance(self):
        for copy in self.copies(0):
            copy.wait()
        got, buf, mp = self.got_mp, self.buf, self.mp

        def add(d, carry):
            total = buf[mp, d].astype(F32) + got[0, d].astype(F32)
            total = total + got[1, d].astype(F32) + got[2, d].astype(F32)
            self.held[d] = total.astype(self.held.dtype)
            return carry
        lax.fori_loop(0, self.n_dp, add, 0)
        self.start(1)

    def total(self):
        for copy in self.copies(1):
            copy.wait()
        value = self.held[self.dp].astype(F32)
        for k in range(self.n_dp - 1):
            value += self.got_dp[k].astype(F32)
        return value

    @staticmethod
    def shapes(n_dp, rows, dtype):
        shapes = [(4, n_dp, rows, 128), (3, n_dp, rows, 128), (n_dp, rows, 128), (n_dp - 1, rows, 128)]
        return [pltpu.VMEM(s, dtype) for s in shapes]


class GradientSums:
    def __init__(self, n_z, word_sum, refs):
        self.n_z, self.word_sum = n_z, word_sum
        abuf, wbuf, small, sgot, ssem, rsem, lsem, *got = refs
        self.abuf, self.wbuf, self.small, self.sgot = abuf, wbuf, small, sgot
        self.ssem, self.rsem, self.lsem = ssem, rsem, lsem
        self.z, self.x, self.y, self.core = coordinates()
        self.chunks = []
        for i, order in enumerate(("yxz", "yxz", "yxz", "xyz", "xyz")):
            rows = wbuf.at[:, :, :, CHUNKS[i][0] : CHUNKS[i][1]]
            self.chunks.append(
                Halving(n_z, None, rows, [None, *got[3 * i : 3 * i + 3]], ssem, rsem, SEMS * i, order)
            )
        core = self.core
        self.parts = []
        for i, (low, high, order) in enumerate(((0, CHAR_CUT, "yxz"), (CHAR_CUT, CHAR_A, "xyz"))):
            rows = abuf.at[:, :, :, :, low:high]
            at = 3 * len(CHUNKS) + 4 * i
            self.parts.append(
                Halving(n_z, rows.at[1 - core], rows.at[core], got[at : at + 4], ssem, rsem, (5 + i) * SEMS, order)
            )
        at = 3 * len(CHUNKS) + 8
        self.partb = DirectSum(2 * n_z, *got[at : at + 4], ssem, rsem, 7 * SEMS)
        self.tiny = 9 * SEMS

    @staticmethod
    def scratch(n_z):
        n_sem = 11 * SEMS
        shapes = [
            pltpu.VMEM((2, 2, 2, n_z, CHAR_A, 128), BF16), pltpu.VMEM((2, 2, n_z, WORD_ROWS, 128), BF16),
            pltpu.VMEM((2, 16, 128), F32), pltpu.VMEM((2 + 2 * n_z, 16, 128), F32),
            pltpu.SemaphoreType.DMA((n_sem,)), pltpu.SemaphoreType.DMA((n_sem,)), pltpu.SemaphoreType.DMA,
        ]
        for low, high in CHUNKS:
            shapes += Halving.got_shapes(n_z, high - low, 1)
        for rows in (CHAR_CUT, CHAR_A - CHAR_CUT):
            shapes += Halving.got_shapes(n_z, rows)
        return shapes + DirectSum.shapes(2 * n_z, CHAR_B, BF16)

    def begin(self):
        load = pltpu.make_async_copy(self.word_sum, self.wbuf, self.lsem)
        load.start()
        dp, mp, n_dp = self.partb.dp, self.partb.mp, 2 * self.n_z
        peers = [(lax.rem(dp + k, n_dp), mp) for k in range(1, n_dp)] + [(dp, lax.rem(mp + k, 4)) for k in range(1, 4)]
        barrier = pltpu.get_barrier_semaphore()
        for peer in peers:
            pl.semaphore_signal(barrier, inc=1, device_id=peer, device_id_type=MESH)
        pl.semaphore_wait(barrier, len(peers))
        load.wait()
        for i, phase in enumerate((3, 1, 1, 1, 2)):
            self.chunks[i].start(phase)

    def pack_a(self, gup_ref, gdown_ref, gout_ref):
        for d in range(2 * self.n_z):
            down = gdown_ref[128 * d : 128 * d + 128, :]
            out = gout_ref[32 * d : 32 * d + 32, :]
            for p in range(4):
                block = self.abuf.at[p % 2, p // 2, d % 2, d // 2]
                block[0:32, :] = gup_ref[32 * d : 32 * d + 32, 256 * p : 256 * p + 128].astype(BF16)
                block[32:64, :] = gup_ref[32 * d : 32 * d + 32, 256 * p + 128 : 256 * p + 256].astype(BF16)
                block[64:128, :] = fold_half(down[:, 64 * p : 64 * p + 64]).astype(BF16)
                block[128:144, :] = fold_half(out[:, 64 * p : 64 * p + 64]).astype(BF16)
        for part in self.parts:
            part.start(0)

    def pack_b(self, gqkv_ref):
        for d in range(2 * self.n_z):
            qkv = gqkv_ref[32 * d : 32 * d + 32, :]
            for p in range(4):
                own = qkv[:, 192 * p : 192 * p + 192]
                self.partb.buf[p, d, 0:32, :] = own[:, 0:128].astype(BF16)
                self.partb.buf[p, d, 32:48, :] = fold_half(own[:, 128:192]).astype(BF16)
        self.partb.start(0)

    def tiny_copies(self, phase):
        dp, mp, n_dp = self.partb.dp, self.partb.mp, 2 * self.n_z
        if phase == 0:
            peers = [(dp, lax.rem(mp + k, 4)) for k in range(1, 4)]
        else:
            peers = [(lax.rem(dp + k, n_dp), mp) for k in range(1, n_dp)]
        at = 3 * phase
        return [
            remote_copy(self.small.at[phase], self.sgot.at[at + k], self.ssem, self.rsem, self.tiny + at + k, peer)
            for k, peer in enumerate(peers)
        ]

    def tiny_start(self, phase):
        for copy in self.tiny_copies(phase):
            copy.start()

    def tiny_finish(self, phase):
        copies = self.tiny_copies(phase)
        for copy in copies:
            copy.wait()
        total = self.small[phase]
        for k in range(len(copies)):
            total += self.sgot[3 * phase + k]
        return total


def pack_small(cgain_ref, cpool_ref, gqkv_ref, wqkv_ref, gains_ref, wgain_ref):
    gains = gains_ref[...].astype(F32)
    width = gains.shape[1]
    first = jnp.sum(gqkv_ref[...] * wqkv_ref[...].astype(F32), -1, keepdims=True)
    first = jnp.transpose(jnp.broadcast_to(first, (width, 128)))[0:1, :]
    sums = [
        first / gains[0:1], jnp.sum(cgain_ref[...], 0, keepdims=True) / gains[1:2],
        jnp.sum(cpool_ref[...], 0, keepdims=True), wgain_ref[0:1, :], wgain_ref[1:2, :],
    ]
    rows = [v[:, t : t + 128] for v in sums for t in range(0, v.shape[1], 128)]
    rows.append(jnp.zeros((2, 128), F32))
    return jnp.concatenate(rows, 0)


def finish_body(
    dx_ref, wide_ref, sums_ref,
    odx_ref, owide_ref, oqkv_ref, oout_ref, oup_ref, odown_ref, oproj_ref, owqkv_ref, owout_ref, owup_ref, owdown_ref,
    ocgain_ref, opool_ref, owgain_ref,
):
    odx_ref[...] = dx_ref[...].astype(F32)

    @pl.when(pl.program_id(0) == 0)
    def _():
        base = WORD_ROWS
        owide_ref[...] = wide_ref[...]
        for t in range(3):
            owqkv_ref[t] = sums_ref[64 * t : 64 * t + 64, :]
        oproj_ref[...] = sums_ref[ROW_PROJ : ROW_PROJ + 32, :]
        owout_ref[...] = sums_ref[ROW_OUT : ROW_OUT + 64, :]
        for t in range(4):
            owup_ref[:, 128 * t : 128 * t + 128] = sums_ref[ROW_UP + 64 * t : ROW_UP + 64 * t + 64, :]
            owdown_ref[:, 128 * t : 128 * t + 128] = sums_ref[ROW_DOWN + 64 * t : ROW_DOWN + 64 * t + 64, :]
        oup_ref[:, 0:128] = sums_ref[base : base + 32, :]
        oup_ref[:, 128:256] = sums_ref[base + 32 : base + 64, :]
        odown_ref[...] = unfold_half(sums_ref[base + 64 : base + 128, :]).T
        oout_ref[...] = unfold_half(sums_ref[base + 128 : base + 144, :])
        base = WORD_ROWS + CHAR_A
        oqkv_ref[:, 0:128] = sums_ref[base : base + 32, :]
        oqkv_ref[:, 128:192] = unfold_half(sums_ref[base + 32 : base + 48, :])
        total = sums_ref[base + CHAR_B : base + CHAR_B + 16, :]
        for j in range(2):
            for t in range(2):
                ocgain_ref[j : j + 1, 128 * t : 128 * t + 128] = total[2 * j + t : 2 * j + t + 1]
            for t in range(4):
                owgain_ref[j : j + 1, 128 * t : 128 * t + 128] = total[6 + 4 * j + t : 7 + 4 * j + t]
        for t in range(2):
            opool_ref[:, 128 * t : 128 * t + 128] = total[4 + t : 5 + t]


def finish(d_chars, word_out, sums):
    words, wide = d_chars.shape
    steps = 2
    full = lambda s: pl.BlockSpec(s, lambda i: (0,) * len(s))
    blk = pl.BlockSpec((words // steps, wide), lambda i: (i, 0))
    outs = [
        word_out.shape, (32, 192), (32, 64), (32, 256), (64, 128), (32, 128),
        (3, 64, 128), (64, 128), (64, 512), (64, 512), (2, 256), (1, 256), (2, 512),
    ]
    result = pl.pallas_call(
        finish_body,
        grid=(steps,),
        in_specs=[blk, full(word_out.shape), full(sums.shape)],
        out_specs=[blk] + [full(s) for s in outs],
        out_shape=[jax.ShapeDtypeStruct((words, wide), F32), jax.ShapeDtypeStruct(outs[0], BF16)]
        + [jax.ShapeDtypeStruct(s, F32) for s in outs[1:]],
        compiler_params=pltpu.CompilerParams(vmem_limit_bytes=VMEM_LIMIT),
        name="finish",
    )(d_chars, word_out, sums)
    dx, out, qkv, cout, up, down, proj, wqkv, wout, wup, wdown, cgain, pool, wgain = result
    return (out, dx, qkv, cout, up, down.T, proj, wqkv, wout.T, wup, wdown.T, cgain, pool.reshape(-1), wgain)


def char_bwd_body(
    n_dp, fused,
    dpool_ref, gains_ref, pool_ref, wqkv_any, wout_any, wup_any, wdown_any,
    early_ref, late_ref, p_ref, a_ref, act_ref,
    *refs,
):
    if fused:
        word_sum, wgain_ref, dx_ref, sums_ref, *refs = refs
    else:
        dx_ref, *refs = refs
        outs, refs = refs[:6], refs[6:]
    gqkv_ref, gout_ref, gup_ref, gdown_ref, ggain_ref, gpool_ref, *refs = refs
    dm_ref, dp_ref, do_ref, ds_ref, wqkv_ref, wout_ref, wup_ref, wdown_ref, dp_now, do_now, wsem, *refs = refs
    step = pl.program_id(0)
    part = pl.num_programs(0) // 3
    words = dpool_ref.shape[0]
    width = wout_ref.shape[0]
    hid = wup_ref.shape[1]
    blocks = words // 8
    rows = words * CHARS
    size = CHAR_HEADS * 128
    gains = gains_ref[...].astype(F32)
    here = pl.ds(pl.multiple_of(lax.rem(step, part) * rows, rows), rows)
    sums = GradientSums(n_dp // 2, word_sum, refs) if fused else None
    chunks = sums.chunks if fused else None

    def at(when, act):
        if fused:
            pl.when(step == when)(act)

    @pl.when(step == 0)
    def _():
        pairs = ((wdown_any, wdown_ref), (wup_any, wup_ref), (wout_any, wout_ref), (wqkv_any, wqkv_ref))
        loads = [pltpu.make_async_copy(src, dst, wsem.at[i]) for i, (src, dst) in enumerate(pairs)]
        for load in loads:
            load.start()
        if fused:
            sums.begin()
        for load in loads:
            load.wait()
        for ref in (gqkv_ref, gout_ref, gup_ref, gdown_ref, ggain_ref, gpool_ref):
            ref[...] = jnp.zeros_like(ref)

    def event(when, *moves):
        def act():
            for sum_of, phase in moves:
                if phase < 3:
                    sum_of.advance(phase)
                else:
                    sum_of.finish(3)
        at(when, act)

    if fused:
        first, other = sums.parts
        event(2, (chunks[1], 1), (chunks[3], 1))
        event(3, (chunks[2], 1), (chunks[4], 2))
        event(4, (chunks[1], 2), (chunks[3], 2))
        event(5, (first, 0), (other, 0))
        event(6, (chunks[2], 2))
        event(8, (first, 1), (other, 1))
        event(11, (first, 2), (other, 2))

    @pl.when(step < part)
    def _():
        dpool = dpool_ref[...].astype(F32).reshape(blocks, 1, 8, width)
        f = early_ref[:, 2 * width : 3 * width].astype(F32).reshape(blocks, CHARS, 8, width)
        stat = early_ref[:, 3 * width :].astype(F32)
        aw = stat[:, 1:2].reshape(blocks, CHARS, 8, 1)
        g = jnp.sum(f * dpool, -1, keepdims=True)
        dt = aw * (g - jnp.sum(aw * g, 1, keepdims=True))
        gpool_ref[...] += jnp.sum((dt * f).reshape(rows // 8, 8, width), 0)
        df = (aw * dpool + dt * pool_ref[...].astype(F32).reshape(1, width)).reshape(rows, width)
        dfb = df.astype(BF16)
        n2 = early_ref[:, width : 2 * width]
        dn2 = None
        for j in range(0, wup_ref.shape[1], HIDDEN_CUT):
            cut = slice(j, j + HIDDEN_CUT)
            gdown_ref[cut, :] += dot_tn(act_ref[:, cut], dfb)
            dh = act_ref[:, hid + j : hid + j + HIDDEN_CUT] * dot_nt(dfb, wdown_ref[cut, :]).astype(BF16)
            gup_ref[:, cut] += dot_tn(n2, dh)
            term = dot_nt(dh, wup_ref[:, cut])
            dn2 = term if dn2 is None else dn2 + term
        d_norm, dnn = norm_bwd(dn2, n2, stat[:, 0:1], gains[1:2])
        ggain_ref[...] += jnp.sum(dnn.reshape(rows // 8, 8, width), 0)
        dm = df + d_norm
        dmb = dm.astype(BF16)
        dm_ref[here, :] = dmb
        gout_ref[...] += dot_tn(early_ref[:, 0:width], dmb)
        do_ref[here, :] = dot_nt(dmb, wout_ref[...]).astype(BF16)

    at(part - 1, lambda: sums.pack_a(gup_ref, gdown_ref, gout_ref))

    @pl.when((step >= part) & (step < 2 * part))
    def _():
        scale = (width // CHAR_HEADS) ** -0.5
        do_now[...] = do_ref[here, :]
        raw = []
        for b in range(blocks):
            sl = slice(128 * b, 128 * b + 128)
            raw.append(dot_nt(head_stack(p_ref[sl, 2 * width : 3 * width], CHAR_HEADS, 1.0), do_now[128 * b : 128 * b + 128, :]))
        for b in range(blocks):
            a = a_ref[size * b : size * b + size, :].astype(F32).reshape(CHAR_HEADS, CHARS, 8, 128)
            dpt = raw[b].reshape(CHAR_HEADS, CHARS, 8, 128)
            delta = jnp.sum(a * dpt, 1, keepdims=True)
            ds_ref[size * b : size * b + size, :] = (a * (dpt - delta)).reshape(size, 128).astype(BF16)
        for b in range(blocks):
            sl = slice(128 * b, 128 * b + 128)
            ds = ds_ref[size * b : size * b + size, :]
            k = head_stack(p_ref[sl, width : 2 * width], CHAR_HEADS, scale)
            dp_now[128 * b : 128 * b + 128, 0:width] = dot_tn(ds, k).astype(BF16)
        for b in range(blocks):
            sl = slice(128 * b, 128 * b + 128)
            cut = lambda h: ds_ref[size * b + 128 * h : size * b + 128 * h + 128, :]
            wide = jnp.concatenate([cut(h) for h in range(CHAR_HEADS)], 1)
            q = head_stack(p_ref[sl, 0:width], CHAR_HEADS, scale)
            dp_now[128 * b : 128 * b + 128, width : 2 * width] = dot_nn(wide, q).astype(BF16)
        for b in range(blocks):
            cut = lambda h: a_ref[size * b + 128 * h : size * b + 128 * h + 128, :]
            wide = jnp.concatenate([cut(h) for h in range(CHAR_HEADS)], 1)
            do = head_stack(do_now[128 * b : 128 * b + 128, :], CHAR_HEADS, 1.0)
            dp_now[128 * b : 128 * b + 128, 2 * width : 3 * width] = dot_nn(wide, do).astype(BF16)
        dp = dp_now[...]
        dp_ref[here, :] = dp
        gqkv_ref[...] += dot_tn(late_ref[:, 0:width], dp)

    def begin_b():
        sums.pack_b(gqkv_ref)
        sums.small[0] = pack_small(ggain_ref, gpool_ref, gqkv_ref, wqkv_ref, gains_ref, wgain_ref)
        sums.tiny_start(0)
    at(2 * part - 1, begin_b)

    @pl.when(step >= 2 * part)
    def _():
        dn1 = dot_nt(dp_ref[here, :], wqkv_ref[...])
        rstd = late_ref[:, width:].astype(F32)[:, 0:1]
        d_norm, _ = norm_bwd(dn1, late_ref[:, 0:width], rstd, gains[0:1])
        dx = dm_ref[here, :].astype(F32) + d_norm
        for b in range(0, blocks, 2):
            for c in range(CHARS):
                pair = [dx[128 * i + 8 * c : 128 * i + 8 * c + 8] for i in (b, b + 1)]
                dx_ref[8 * b : 8 * b + 16, width * c : width * c + width] = jnp.concatenate(pair, 0).astype(BF16)

    def end():
        sums.partb.advance()
        sums.small[1] = sums.tiny_finish(0)
        sums.tiny_start(1)
        for i, (low, high) in enumerate(CHUNKS):
            chunks[i].finish(3)
            sums_ref[low:high, :] = chunks[i].total()
        base = WORD_ROWS
        for i, (low, high) in enumerate(((0, CHAR_CUT), (CHAR_CUT, CHAR_A))):
            sums.parts[i].finish(3)
            sums_ref[base + low : base + high, :] = sums.parts[i].total()
        base += CHAR_A
        sums_ref[base + CHAR_B : base + CHAR_B + 16, :] = sums.tiny_finish(1)
        sums_ref[base : base + CHAR_B, :] = sums.partb.total()
    at(3 * part - 1, end)

    if not fused:
        @pl.when(step == 3 * part - 1)
        def _():
            for out, ref in zip(outs, (gqkv_ref, gout_ref, gup_ref, gdown_ref, ggain_ref, gpool_ref)):
                out[...] = ref[...]


def char_backward(n_dp, dpool, kept, gains, wqkv, wout, wup, wdown, pool, word_sum, wgain):
    words = dpool.shape[0]
    width = wout.shape[0]
    rows = words * CHARS
    step_rows = STEP_WORDS * CHARS
    steps = words // STEP_WORDS
    fused = word_sum is not None
    full = lambda arr: pl.BlockSpec(arr.shape, lambda i: (0,) * arr.ndim)
    fixed = lambda s: pl.BlockSpec(s, lambda i: (0,) * len(s))
    first = lambda n, w: pl.BlockSpec((n, w), lambda i: (lax.min(i, steps - 1), 0))
    second = lambda n, w: pl.BlockSpec((n, w), lambda i: (lax.clamp(0, i - steps, steps - 1), 0))
    third = lambda n, w: pl.BlockSpec((n, w), lambda i: (lax.max(i - 2 * steps, 0), 0))
    twice = lambda n, w: pl.BlockSpec((n, w), lambda i: (lax.rem(lax.max(i - steps, 0), steps), 0))
    grads = [wqkv.shape, wout.shape, wup.shape, wdown.shape, (8, width), (8, width)]
    scratch = [pltpu.VMEM(s, F32) for s in grads] + [
        pltpu.VMEM((rows, width), BF16), pltpu.VMEM((rows, 3 * width), BF16), pltpu.VMEM((rows, width), BF16),
        pltpu.VMEM((step_rows * CHAR_HEADS, 128), BF16), *[pltpu.VMEM(w.shape, BF16) for w in (wqkv, wout, wup, wdown)],
        pltpu.VMEM((step_rows, 3 * width), BF16), pltpu.VMEM((step_rows, width), BF16), pltpu.SemaphoreType.DMA((4,)),
    ]
    any_spec = pl.BlockSpec(memory_space=pl.ANY)
    args = [dpool, gains, pool, wqkv, wout, wup, wdown, *kept]
    in_specs = [first(STEP_WORDS, width), full(gains), full(pool)] + [any_spec] * 4
    in_specs += [f(r.shape[0] // steps, r.shape[1]) for f, r in zip((first, twice, second, second, first), kept)]
    params = dict(vmem_limit_bytes=VMEM_LIMIT)
    if fused:
        outs = [(WORD_ROWS + CHAR_A + CHAR_B + 16, 128)]
        args += [word_sum, wgain]
        in_specs += [pl.BlockSpec(memory_space=pl.ANY), full(wgain)]
        scratch += GradientSums.scratch(n_dp // 2)
        params.update(collective_id=1, has_side_effects=True)
    else:
        outs = grads
    return pl.pallas_call(
        functools.partial(char_bwd_body, n_dp, fused),
        grid=(3 * steps,),
        in_specs=in_specs,
        out_specs=[third(STEP_WORDS, CHARS * width)] + [fixed(s) for s in outs],
        out_shape=[jax.ShapeDtypeStruct((words, CHARS * width), BF16)] + [jax.ShapeDtypeStruct(s, F32) for s in outs],
        scratch_shapes=scratch,
        compiler_params=pltpu.CompilerParams(**params),
        name="char_backward",
    )(*args)


def word_body(
    n_dp, cap, packed,
    pooled_ref, onehot, place, seg_all, cot_ref, gains_ref, wproj_ref, *refs,
):
    slices, wholes, refs = refs[:4], refs[4:8], refs[8:]
    if packed:
        out_ref, dpool_ref, gsum_ref, ggain_ref, gbuf_ref, got_a, got_x, gq_ref, got_q, *refs = refs
    else:
        out_ref, dpool_ref, gqkv_ref, gout_ref, gup_ref, gdown_ref, gproj_ref, ggain_ref, *refs = refs
    (
        wqkv_ref, wout_ref, wup_ref, wdown_ref, vec_send, vec_got, segc_all, pooled_rows, rows_ref, normed_all, rstd_a,
        qkv_all, weights, o_send, o_all, act_ref, dh_ref, dact_ref, dm_ref,
        do_send, do_all, dk_acc, dv_acc, dqkv_send, dqkv_all, back_send, ret,
        ssem, rsem, lsem,
    ) = refs
    dp, mp = lax.axis_index("dp"), lax.axis_index("mp")
    n_mp = 4
    words, narrow = pooled_ref.shape
    width = cot_ref.shape[1]
    slots = n_dp * cap
    pair = 2 * (width // HEADS)
    scale = (width // HEADS) ** -0.5
    to_dp = [(lax.rem(dp + k, n_dp), mp) for k in range(n_dp)]
    from_dp = [(lax.rem(dp + n_dp - k, n_dp), mp) for k in range(n_dp)]
    mates = [(mp // 2 * 2 + (mp + 1) % 2), (mp + 2) % 4, ((mp // 2 * 2 + 2) % 4 + (mp + 1) % 2)]
    barrier = pltpu.get_barrier_semaphore()
    for k in range(1, n_dp):
        pl.semaphore_signal(barrier, inc=1, device_id=to_dp[k], device_id_type=MESH)
    for mate in mates:
        pl.semaphore_signal(barrier, inc=1, device_id=(dp, mate), device_id_type=MESH)
    next_slot = [0]

    def send(src, dst, peer):
        slot = next_slot[0]
        next_slot[0] += 1
        copy = pltpu.make_async_remote_copy(
            src_ref=src, dst_ref=dst, send_sem=ssem.at[slot], recv_sem=rsem.at[slot],
            device_id=peer, device_id_type=MESH,
        )
        copy.start()
        return copy

    z, x, y, core = coordinates()
    loads = []
    for i, held in ((3, wdown_ref), (0, wqkv_ref), (1, wout_ref), (2, wup_ref)):
        loads.append([])
        for j, at in enumerate([mp, *mates]):
            src = slices[i] if j == 0 else wholes[i].at[at]
            if i == 0:
                for t in range(3):
                    dst = held.at[at, :, pair * t : pair * t + pair]
                    loads[-1].append(pltpu.make_async_copy(src.at[t], dst, lsem.at[4 + t, j]))
            elif i == 3 and j > 1:
                src, dst = WeightGather.half(src, 0, x), WeightGather.half(held.at[at], 0, x)
                loads[-1].append(pltpu.make_async_copy(src, dst, lsem.at[i, j]))
            else:
                loads[-1].append(pltpu.make_async_copy(src, held.at[at], lsem.at[i, j]))
        for load in loads[-1]:
            load.start()
    vec_send[...] = dot_nn(onehot[...], pooled_ref[...]).astype(BF16).reshape(n_dp, cap, narrow)

    pl.semaphore_wait(barrier, n_dp - 1 + 3)
    vec_copies = [send(vec_send.at[k], vec_got.at[k], to_dp[k]) for k in range(1, n_dp)]
    source = WeightGather.half(wholes[3].at[mates[1]], 0, x)
    down_side = send(source, WeightGather.half(wdown_ref.at[mates[1]], 0, x), device_of(z, 1 - x, y, core))
    vec_got[0] = vec_send[0]
    gains = gains_ref[...].astype(F32)
    cot = cot_ref[...]
    for j in range(n_mp):
        segc_all[words * j : words * j + words, :] = as_column(seg_all[j, 0:1, :])
    for load in loads[1] + loads[2] + loads[3]:
        load.wait()
    for copy in vec_copies:
        copy.wait()
    pooled_rows[mp] = dot_tn(place[...], vec_got[...].reshape(slots, narrow)).astype(BF16)
    row_copies = [send(pooled_rows.at[mp], pooled_rows.at[mp], (dp, mate)) for mate in reversed(mates)]
    for turn, at in enumerate([mp, *mates]):
        if turn > 0:
            row_copies[3 - turn].wait()
        rows = dot_nn(pooled_rows[at], wproj_ref[...]).astype(BF16).astype(F32)
        n_w, rstd = norm_fwd(rows, gains[0:1])
        normed_all[at] = n_w
        if turn == 0:
            rows_ref[...] = rows
            rstd_a[...] = rstd
        qkv_all[at] = dot_nn(n_w, wqkv_ref[mp]).astype(BF16)
    down_side.wait()
    source = WeightGather.half(wdown_ref.at[mates[1]], 0, 1 - x)
    down_late = send(source, source, (dp, mates[0]))

    low_lane = lax.broadcasted_iota(jnp.int32, (1, pair), 1) < pair // 2
    low_mask = jnp.where(low_lane, 1.0, 0.0).astype(BF16)
    high_mask = jnp.where(low_lane, 0.0, 1.0).astype(BF16)

    def heads(v, factor):
        return jnp.concatenate([v * (low_mask * factor).astype(BF16), v * (high_mask * factor).astype(BF16)], 0)

    o_copies = []
    for i in reversed(range(n_mp)):
        keys = words * (i + 1)
        q = heads(qkv_all[i, :, 0:pair], scale)
        k = qkv_all[0 : i + 1, :, pair : 2 * pair].reshape(keys, pair)
        v = qkv_all[0 : i + 1, :, 2 * pair : 3 * pair].reshape(keys, pair)
        same = segc_all[0:keys, 0:1] == seg_all[i, 0:1, :].astype(F32)
        key_at = lax.broadcasted_iota(jnp.int32, (keys, words), 0)
        query_at = lax.broadcasted_iota(jnp.int32, (keys, words), 1) + words * i
        allowed = same & (key_at <= query_at)
        st = jnp.where(jnp.concatenate([allowed, allowed], 1), dot_nt(k, q), NEGATIVE)
        ex = jnp.exp(st - jnp.max(st, 0, keepdims=True))
        at = (ex * (1.0 / jnp.sum(ex, 0, keepdims=True))).astype(BF16)
        weights[i, 0:keys, :] = at
        both = dot_tn(at, v)
        o_send[i] = jnp.where(low_lane, both[:words], both[words:]).astype(BF16)
    for mate in reversed(mates):
        o_copies.append(send(o_send.at[mate], o_all.at[mp], (dp, mate)))
    o_all[mp] = o_send[mp]
    down_late.wait()
    for load in loads[0]:
        load.wait()
    for p in range(n_mp):
        dact_ref[p] = dot_nt(cot, wdown_ref[p]).astype(BF16)
    for copy in o_copies:
        copy.wait()
    attended = jnp.concatenate([o_all[p] for p in range(n_mp)], 1)
    mid = rows_ref[...] + dot_nn(attended, wout_ref[...].reshape(width, width))
    n_w2, rstd2 = norm_fwd(mid, gains[1:2])
    out = mid
    dn2 = jnp.zeros((words, width), F32)
    for p in range(n_mp):
        act, slope = gelu_both(dot_nn(n_w2, wup_ref[p]).astype(BF16))
        act_ref[p] = act
        dh = slope * dact_ref[p]
        dh_ref[p] = dh
        out = out + dot_nn(act, wdown_ref[p])
        dn2 = dn2 + dot_nt(dh, wup_ref[p])
    out_ref[...] = out.astype(BF16)
    d_norm, dnn = norm_bwd(dn2, n_w2, rstd2, gains[1:2])
    gain_b = jnp.sum(dnn, 0, keepdims=True) / gains[1:2]
    d_mid = cot.astype(F32) + d_norm
    dm_ref[...] = d_mid
    d_att = d_mid.astype(BF16)
    do_copies = []
    for mate in reversed(mates):
        do_send[mate] = dot_nt(d_att, wout_ref[mate]).astype(BF16)
        do_copies.append(send(do_send.at[mate], do_all.at[mp], (dp, mate)))
    do_all[mp] = dot_nt(d_att, wout_ref[mp]).astype(BF16)

    def pair_sum(i):
        low, high = CHUNKS[i]
        src = gbuf_ref.at[1 - core, :, :, :, low:high]
        return send(src, got_a.at[:, :, :, low:high], device_of(z, x, y, 1 - core))

    def pair_add(i):
        low, high = CHUNKS[i]

        def add(i, carry):
            b, c, d = i // n_dp, (i // (n_dp // 2)) % 2, lax.rem(i, n_dp // 2)
            gsum_ref[b, c, d, low:high] = gbuf_ref[core, b, c, d, low:high] + got_a[b, c, d, low:high]
            return carry
        lax.fori_loop(0, 2 * n_dp, add, 0)

    def x_sum(i):
        low, high = CHUNKS[i]
        return send(gsum_ref.at[:, 1 - x, :, low:high], got_x, device_of(z, 1 - x, y, core))

    def x_add(i):
        low, high = CHUNKS[i]
        for b in range(2):
            for d in range(n_dp // 2):
                gsum_ref[b, x, d, low:high] += got_x[b, d]

    def put(base, p, grad):
        if packed:
            block = grad.shape[0] // n_dp
            for d in range(n_dp):
                for t in range(grad.shape[1] // 128):
                    gbuf_ref[p % 2, p // 2, d % 2, d // 2, base + block * t : base + block * t + block, :] = (
                        grad[block * d : block * d + block, 128 * t : 128 * t + 128].astype(BF16)
                    )
        elif base == ROW_PROJ:
            gproj_ref[:, 128 * p : 128 * p + 128] = grad
        else:
            ref = {ROW_OUT: gout_ref, ROW_UP: gup_ref, ROW_DOWN: gdown_ref}[base]
            ref[p] = grad

    for p in range(n_mp):
        put(ROW_DOWN, p, dot_tn(cot, act_ref[p]))
    if packed:
        pair_three = pair_sum(4)
    for p in range(n_mp):
        put(ROW_UP, p, dot_tn(n_w2, dh_ref[p]))
    if packed:
        pair_two = pair_sum(3)
    for p in range(n_mp):
        put(ROW_OUT, p, dot_tn(d_att, o_all[p]))
    if packed:
        pair_one = pair_sum(2)
        pair_three.wait()
        pair_add(4)
        x_three = x_sum(4)
    dk_acc[...] = jnp.zeros_like(dk_acc)
    dv_acc[...] = jnp.zeros_like(dv_acc)
    for copy in do_copies:
        copy.wait()
    for i in reversed(range(n_mp)):
        keys = words * (i + 1)
        q = qkv_all[i, :, 0:pair]
        k = qkv_all[0 : i + 1, :, pair : 2 * pair].reshape(keys, pair)
        v = qkv_all[0 : i + 1, :, 2 * pair : 3 * pair].reshape(keys, pair)
        do = heads(do_all[i], 1.0)
        at = weights[i, 0:keys, :]
        af = at.astype(F32)
        dpt = dot_nt(v, do)
        ds = (af * (dpt - jnp.sum(af * dpt, 0, keepdims=True))).astype(BF16)
        both = dot_tn(ds, k)
        dq = jnp.where(low_lane, both[:words], both[words:]) * scale
        dk_acc[0:keys, :] += dot_nn(ds, heads(q, scale))
        dv_acc[0:keys, :] += dot_nn(at, do)
        dqkv_send[i, :, 0:pair] = dq.astype(BF16)
        dqkv_send[i, :, pair : 2 * pair] = dk_acc[words * i : keys, :].astype(BF16)
        dqkv_send[i, :, 2 * pair : 3 * pair] = dv_acc[words * i : keys, :].astype(BF16)
    dqkv_copies = []
    for mate in reversed(mates):
        dqkv_copies.append(send(dqkv_send.at[mate], dqkv_all.at[mp], (dp, mate)))
    dqkv_all[mp] = dqkv_send[mp]
    grad_qkv = dot_tn(normed_all[...].reshape(n_mp * words, width), dqkv_send[...].reshape(n_mp * words, 3 * pair))
    if packed:
        block = width // n_dp
        for d in range(n_dp):
            for t in range(3):
                gq_ref[d % 2, d // 2, block * t : block * t + block, :] = (
                    grad_qkv[block * d : block * d + block, 128 * t : 128 * t + 128].astype(BF16)
                )
        q_sum = send(gq_ref.at[1 - x], got_q, device_of(z, 1 - x, y, core))
        pair_two.wait()
        pair_add(3)
        pair_one.wait()
        pair_add(2)
    else:
        gqkv_ref[...] = grad_qkv
    for copy in dqkv_copies:
        copy.wait()
    d_normed = jnp.zeros((words, width), F32)
    for p in range(n_mp):
        d_normed = d_normed + dot_nt(dqkv_all[p], wqkv_ref[p])
    d_first, dnn = norm_bwd(d_normed, normed_all[mp], rstd_a[...], gains[0:1])
    gain_a = jnp.sum(dnn, 0, keepdims=True) / gains[0:1]
    d_rows = (dm_ref[...] + d_first).astype(BF16)
    ggain_ref[0:1, :] = gain_a
    ggain_ref[1:2, :] = gain_b
    d_pooled = dot_nt(d_rows, wproj_ref[...]).astype(BF16)
    back_send[...] = dot_nn(place[...], d_pooled).astype(BF16).reshape(n_dp, cap, narrow)
    back_copies = [send(back_send.at[k], ret.at[k], from_dp[k]) for k in range(1, n_dp)]
    ret[0] = back_send[0]
    grad_proj = dot_tn(pooled_rows[mp], d_rows)
    for p in range(n_mp):
        put(ROW_PROJ, p, grad_proj[:, 128 * p : 128 * p + 128])
    if packed:
        pair_zero = pair_sum(1)
        q_sum.wait()
        low, high = CHUNKS[0]
        gsum_ref[y, x, :, low:high] = gq_ref[x] + got_q[...]
        x_three.wait()
        x_add(4)
        pair_zero.wait()
        pair_add(1)
    for copy in back_copies:
        copy.wait()
    dpool_ref[...] = dot_tn(onehot[...], ret[...].reshape(slots, narrow)).astype(BF16)


def word_layer(n_dp, pooled, onehot, place, segments, cotangent, gains, wproj, slices, wholes):
    words, narrow = pooled.shape
    width = cotangent.shape[1]
    wqkv, wout, wup, wdown = wholes
    n_mp = wqkv.shape[0]
    cap = -(-2 * words // n_dp // 16) * 16
    slots = cap * n_dp
    pair = 2 * (width // HEADS)
    packed = n_dp == 8
    outs = [((words, width), BF16), ((words, narrow), BF16)]
    if packed:
        outs.append(((2, 2, n_dp // 2, WORD_ROWS, 128), BF16))
    else:
        outs.append(((width, 3 * pair), F32))
        outs += [((n_mp, width, n), F32) for n in (pair, wup.shape[2], wup.shape[2])]
        outs.append(((narrow, width), F32))
    outs.append(((2, width), F32))
    hid = wup.shape[2]
    n_sem = 2 * (n_dp - 1) + 4 * 3 + 3 + 6
    vm = pl.BlockSpec(memory_space=pltpu.VMEM)
    args = (pooled, onehot, place, segments, cotangent, gains, wproj, *slices, *wholes)
    shapes = [
        ((n_mp, width, 3 * pair), BF16), (wout.shape, BF16), (wup.shape, BF16), (wdown.shape, BF16),
        ((n_dp, cap, narrow), BF16), ((n_dp, cap, narrow), BF16), ((n_mp * words, 128), F32), ((n_mp, words, narrow), BF16),
        ((words, width), F32), ((n_mp, words, width), BF16), ((words, 1), F32),
        ((n_mp, words, 3 * pair), BF16), ((n_mp, n_mp * words, 2 * words), BF16),
        ((n_mp, words, pair), BF16), ((n_mp, words, pair), BF16),
        ((n_mp, words, hid), BF16), ((n_mp, words, hid), BF16), ((n_mp, words, hid), BF16), ((words, width), F32),
        ((n_mp, words, pair), BF16), ((n_mp, words, pair), BF16), ((n_mp * words, pair), F32), ((n_mp * words, pair), F32),
        ((n_mp, words, 3 * pair), BF16), ((n_mp, words, 3 * pair), BF16), ((n_dp, cap, narrow), BF16), ((n_dp, cap, narrow), BF16),
    ]
    if packed:
        shapes = [
            ((2, 2, 2, n_dp // 2, WORD_ROWS, 128), BF16), ((2, 2, n_dp // 2, WORD_ROWS, 128), BF16),
            ((2, n_dp // 2, CHUNK_ROWS, 128), BF16),
            ((2, n_dp // 2, CHUNK_ROWS, 128), BF16), ((n_dp // 2, CHUNK_ROWS, 128), BF16), *shapes,
        ]
    return pl.pallas_call(
        functools.partial(word_body, n_dp, cap, packed),
        in_specs=[vm] * (len(args) - 8) + [pl.BlockSpec(memory_space=pl.ANY)] * 8,
        out_specs=[vm] * len(outs),
        out_shape=[jax.ShapeDtypeStruct(s, d) for s, d in outs],
        scratch_shapes=[pltpu.VMEM(s, d) for s, d in shapes]
        + [pltpu.SemaphoreType.DMA((n_sem,)), pltpu.SemaphoreType.DMA((n_sem,)), pltpu.SemaphoreType.DMA((7, 4))],
        compiler_params=pltpu.CompilerParams(collective_id=0, has_side_effects=True, vmem_limit_bytes=VMEM_LIMIT),
        name="word_layer",
    )(*args)


def plain_reduce(char_parts, char_gains, char_qkv, word_parts, word_gains):
    *char_mats, gain_rows, pool_rows = char_parts
    gain_sums = jnp.stack([jnp.sum(char_mats[0] * char_qkv.astype(F32), 1), jnp.sum(gain_rows, 0)]) / char_gains.astype(F32)
    small = lax.psum((gain_sums, jnp.sum(pool_rows, 0), word_gains), ("dp", "mp"))
    mats = []
    for grad in char_mats:
        part = lax.psum_scatter(grad, "dp", scatter_dimension=0, tiled=True)
        part = lax.psum_scatter(part.astype(BF16), "mp", scatter_dimension=1, tiled=True)
        mats.append(part.astype(F32))
    qkv, *rest = word_parts
    words = []
    for grad in rest:
        part = lax.psum_scatter(grad, "dp", scatter_dimension=1, tiled=True)
        words.append(lax.psum_scatter(part, "mp", scatter_dimension=0, tiled=False))
    out, up, down = words
    qkv = lax.psum_scatter(qkv, "dp", scatter_dimension=0, tiled=True)
    qkv = jnp.transpose(qkv.reshape(qkv.shape[0], 3, -1), (1, 0, 2))
    return (*mats, qkv, out.T, up, down.T, *small)


def per_device(
    char_input,
    char_counts,
    word_source,
    segment_ids,
    cotangent,
    char_norm_gains,
    char_qkv,
    char_out,
    char_up,
    char_down,
    pool_vector,
    char_proj,
    word_norm_gains,
    word_qkv,
    word_out,
    word_up,
    word_down,
):
    groups = lax.axis_size("dp")
    char_weights = (char_norm_gains, char_qkv, char_out, char_up, char_down, pool_vector)
    slices = (word_qkv, word_out, word_up, word_down)
    pooled, *kept = char_forward(
        groups, char_input, char_counts.reshape(1, -1), *char_weights,
        word_source.reshape(1, -1), segment_ids.reshape(1, -1), slices,
    )
    char_kept, (onehot, place, segments, *word_weights) = kept[:5], kept[5:]
    output, d_pooled, *word_parts, word_gains = word_layer(
        groups, pooled, onehot, place, segments, cotangent, word_norm_gains, char_proj, slices, word_weights
    )
    fused = groups == 8
    d_chars, *char_parts = char_backward(
        groups, d_pooled, char_kept, *char_weights, word_parts[0] if fused else None, word_gains
    )
    if fused:
        return finish(d_chars, output, char_parts[0])
    *word_parts, grad_proj = word_parts
    char_parts = (*char_parts[:4], grad_proj, *char_parts[4:])
    *mats, grad_char_gains, grad_pool, grad_word_gains = plain_reduce(
        char_parts, char_norm_gains, char_qkv, word_parts, word_gains
    )
    return (output, d_chars.astype(F32), *mats, grad_char_gains, grad_pool, grad_word_gains)


def solution(mesh):
    placed = (
        P(("dp", "mp"), None),
        P(("dp", "mp")),
        P(("dp", "mp")),
        P(("dp", "mp")),
        P(("dp", "mp"), None),
        P(),
        P(),
        P(),
        P(),
        P(),
        P(),
        P(),
        P(),
        P(None, None, "mp"),
        P("mp", None),
        P(None, "mp"),
        P("mp", None),
    )
    return jax.shard_map(
        per_device,
        mesh=mesh,
        in_specs=placed,
        out_specs=(
            P(("dp", "mp"), None),
            P(("dp", "mp"), None),
            P("dp", "mp"),
            P("dp", "mp"),
            P("dp", "mp"),
            P("dp", "mp"),
            P("dp", "mp"),
            P(None, "dp", "mp"),
            P("mp", "dp"),
            P("dp", "mp"),
            P("mp", "dp"),
            P(),
            P(),
            P(),
        ),
        check_vma=False,
    )
```

```python
import functools
import jax
import jax.numpy as jnp
from jax import lax
from jax.experimental import pallas as pl
from jax.experimental.pallas import tpu as pltpu
from jax.sharding import PartitionSpec as P

HEADS = 8
CHARS = 16
CHAR_HEADS = 4
EPSILON = 1e-05
NEGATIVE = -1e30
GELU_A = 0.7978845608028654
GELU_B = 0.044715
F32 = jnp.float32
BF16 = jnp.bfloat16
MESH = pl.DeviceIdType.MESH
VMEM_LIMIT = 62 * 1024 * 1024
STEP_WORDS = 64
HIDDEN_CUT = 256


def dot_nn(left, right):
    return jnp.dot(left, right, preferred_element_type=F32)


def dot_nt(left, right):
    return lax.dot_general(left, right, (((1,), (1,)), ((), ())), preferred_element_type=F32)


def dot_tn(left, right):
    return lax.dot_general(left, right, (((0,), (0,)), ((), ())), preferred_element_type=F32)


def as_column(row):
    return jnp.transpose(jnp.broadcast_to(row.astype(F32), (128, row.shape[1])))


def head_stack(values, heads, factor):
    width = values.shape[1] // heads
    lane = lax.broadcasted_iota(jnp.int32, (1, values.shape[1]), 1) // width
    return jnp.concatenate(
        [values * jnp.where(lane == h, factor, 0.0).astype(values.dtype) for h in range(heads)], 0
    )


def gelu_both(hidden):
    c = lambda value: jnp.asarray(value, hidden.dtype)
    square = hidden * hidden
    tanh = jnp.tanh(hidden * (c(GELU_A) + c(GELU_A * GELU_B) * square))
    half = c(0.5) + c(0.5) * tanh
    slope = half + (c(0.5) * hidden) * (c(1.0) - tanh * tanh) * (c(GELU_A) + c(3.0 * GELU_A * GELU_B) * square)
    return hidden * half, slope


def norm_fwd(values, gain):
    mean = jnp.mean(values, -1, keepdims=True)
    centered = values - mean
    rstd = lax.rsqrt(jnp.mean(centered * centered, -1, keepdims=True) + EPSILON)
    return (centered * rstd * gain).astype(BF16), rstd


def norm_bwd(dn, n, rstd, gain):
    n = n.astype(F32)
    d1 = dn * gain
    dnn = dn * n
    m1 = jnp.mean(d1, -1, keepdims=True)
    m2 = jnp.mean(dnn, -1, keepdims=True)
    return rstd * (d1 - m1 - n * (1.0 / gain) * m2), dnn


def coordinates():
    dp, mp = lax.axis_index("dp"), lax.axis_index("mp")
    return dp // 2, dp % 2, mp // 2, mp % 2


def device_of(z, x, y, core):
    return (z * 2 + x, y * 2 + core)


def remote_copy(src, dst, ssem, rsem, slot, peer):
    return pltpu.make_async_remote_copy(
        src_ref=src, dst_ref=dst, send_sem=ssem.at[slot], recv_sem=rsem.at[slot],
        device_id=peer, device_id_type=MESH,
    )


class WeightGather:
    def __init__(self, slices, wholes, split, ssem, rsem):
        self.slices, self.wholes, self.split, self.ssem, self.rsem = slices, wholes, split, ssem, rsem
        self.z, self.x, self.y, self.core = coordinates()
        self.mp = self.y * 2 + self.core
        self.across = (1 - self.y) * 2 + self.core

    @staticmethod
    def half(ref, axis, which):
        rows = ref.shape[axis] // 2
        return ref.at[(slice(None),) * axis + (pl.ds(pl.multiple_of(which * rows, rows), rows),)]

    def copy(self, i, kind):
        z, x, y, core = self.z, self.x, self.y, self.core
        piece, whole = self.slices[i], self.wholes[i]
        axis = len(piece.shape) - 2
        far = whole.at[self.across]
        if kind == "far":
            src, dst = piece, whole.at[self.mp]
            if self.split[i]:
                src, dst = self.half(src, axis, x), self.half(dst, axis, x)
            peer = device_of(z, x, 1 - y, core)
        elif kind == "near":
            src, dst, peer = piece, whole.at[self.mp], device_of(z, x, y, 1 - core)
        else:
            which = 1 - x if kind == "late" else x
            src = dst = self.half(far, axis, which) if self.split[i] else far
            peer = device_of(z, 1 - x, y, core) if kind == "side" else device_of(z, x, y, 1 - core)
        slot = i * 5 + ("far", "near", "side", "early", "late").index(kind)
        return remote_copy(src, dst, self.ssem, self.rsem, slot, peer)

    def peers(self):
        z, x, y, core = self.z, self.x, self.y, self.core
        return [device_of(z, x, 1 - y, core), device_of(z, x, y, 1 - core), device_of(z, 1 - x, y, core)]

    def begin(self):
        for i in range(len(self.slices)):
            self.copy(i, "far").start()
        for i in range(len(self.slices)):
            self.copy(i, "near").start()

    def pass_on(self, i):
        self.copy(i, "far").wait()
        if self.split[i]:
            self.copy(i, "side").start()
        self.copy(i, "early").start()

    def pass_last(self, i):
        self.copy(i, "side").wait()
        self.copy(i, "late").start()

    def finish(self):
        for i in range(len(self.slices)):
            for kind in ("near", "early", "late")[: 2 + self.split[i]]:
                self.copy(i, kind).wait()


def char_fwd_body(
    n_dp, cap,
    x_ref, cnt_ref, gains_ref, wqkv_ref, wout_ref, wup_ref, wdown_ref, pool_ref,
    src_ref, seg_ref, s_qkv, s_out, s_up,
    pooled_ref, early_ref, late_ref, p_any, a_any, act_any,
    onehot_ref, place_ref, seg_out, g_qkv, g_out, g_up,
    cnt_col, row_send, row_got, seg_all, ssem, rsem, wsend, wrecv, p_buf, a_buf, act_buf, osem,
):
    step, last = pl.program_id(0), pl.num_programs(0) - 1
    dp, mp = lax.axis_index("dp"), lax.axis_index("mp")
    gather = WeightGather((s_qkv, s_out, s_up), (g_qkv, g_out, g_up), (True, True, False), wsend, wrecv)
    mates = [mp // 2 * 2 + (mp + 1) % 2, (mp + 2) % 4, (mp // 2 * 2 + 2) % 4 + (mp + 1) % 2]
    all_words = src_ref.shape[1]
    slots = n_dp * cap
    row_copy = lambda k: remote_copy(row_send.at[k], row_got.at[k], ssem, rsem, k, (lax.rem(dp + k, n_dp), mp))
    seg_copy = lambda j: remote_copy(seg_all.at[mp], seg_all.at[mp], ssem, rsem, n_dp + j, (dp, mates[j]))

    @pl.when(step == 0)
    def _():
        barrier = pltpu.get_barrier_semaphore()
        greeted = [(lax.rem(dp + k, n_dp), mp) for k in range(1, n_dp)] + [(dp, mate) for mate in mates]
        for peer in greeted:
            pl.semaphore_signal(barrier, inc=1, device_id=peer, device_id_type=MESH)
        source = src_ref[...]
        owner = source // (all_words * 4)
        owner_c = as_column(owner)[:, 0:1]
        index_r = lax.broadcasted_iota(jnp.int32, (all_words, all_words), 0)
        index_c = lax.broadcasted_iota(jnp.int32, (all_words, all_words), 1)
        earlier = (owner_c == owner.astype(F32)) & (index_r < index_c)
        rank = jnp.sum(jnp.where(earlier, 1.0, 0.0), 0, keepdims=True).astype(jnp.int32)
        slot_of = lax.rem(owner - dp + n_dp, n_dp) * cap + rank
        at_slot = lax.broadcasted_iota(jnp.int32, (slots, all_words), 0) == slot_of
        onehot_ref[...] = jnp.where(at_slot, 1.0, 0.0).astype(BF16)
        row_mat = as_column(lax.rem(source, all_words) + 1).astype(BF16)
        row_send[...] = dot_nn(onehot_ref[...], row_mat).astype(BF16).reshape(n_dp, cap, 128)
        seg_all[mp] = jnp.broadcast_to(seg_ref[...], (8, all_words))
        cnt_col[...] = as_column(cnt_ref[...])
        pl.semaphore_wait(barrier, len(greeted))
        gather.begin()
        for k in range(1, n_dp):
            row_copy(k).start()
        for j in range(3):
            seg_copy(j).start()
        row_got[0] = row_send[0]

    @pl.when(step == last)
    def _():
        gather.pass_last(0)
        gather.pass_last(1)

    words, wide = x_ref.shape
    width = wide // CHARS
    blocks = words // 8
    gains = gains_ref[...].astype(F32)
    counts_here = cnt_col[pl.ds(pl.multiple_of(step * words, words), words), :].astype(jnp.int32)
    pieces = []
    for g in range(words // 16):
        xt = x_ref[16 * g : 16 * g + 16, :].astype(F32)
        for half in range(2):
            for c in range(CHARS):
                pieces.append(xt[8 * half : 8 * half + 8, width * c : width * c + width])
    x = jnp.concatenate(pieces, 0)
    hid = wup_ref.shape[1]
    rows = words * CHARS
    cuts = range(0, hid, HIDDEN_CUT)
    held = lax.rem(step, 2)
    p_ref, a_ref, act_ref = p_buf.at[held], a_buf.at[held], act_buf.at[held]

    def out_copies(of):
        slot = lax.rem(of, 2)
        at = lambda n: pl.ds(pl.multiple_of(of * n, n), n)
        heads = rows * CHAR_HEADS
        copies = [
            pltpu.make_async_copy(p_buf.at[slot], p_any.at[at(rows)], osem.at[slot, 0]),
            pltpu.make_async_copy(a_buf.at[slot], a_any.at[at(heads)], osem.at[slot, 1]),
        ]
        for i in range(2 * hid // HIDDEN_CUT):
            cut = pl.ds(HIDDEN_CUT * i, HIDDEN_CUT)
            copies.append(pltpu.make_async_copy(act_buf.at[slot, :, cut], act_any.at[at(rows), cut], osem.at[slot, 2 + i]))
        return copies

    leaving = out_copies(step)

    @pl.when(step >= 2)
    def _():
        for copy in out_copies(step - 2):
            copy.wait()

    n1, rs1 = norm_fwd(x, gains[0:1])
    lane = lax.broadcasted_iota(jnp.int32, (rows, 128), 1)
    late_ref[:, 0:width] = n1
    late_ref[:, width:] = jnp.where(lane == 0, rs1, 0.0).astype(BF16)
    p_ref[...] = dot_nn(n1, wqkv_ref[...]).astype(BF16)
    row_w = lax.broadcasted_iota(jnp.int32, (8, 128), 0)
    lane_w = lax.broadcasted_iota(jnp.int32, (8, 128), 1) % 8
    same = row_w == lane_w
    slot = lax.broadcasted_iota(jnp.int32, (CHARS, 8, 128), 0)
    size = CHAR_HEADS * 128
    scale = (width // CHAR_HEADS) ** -0.5
    scores = []
    for b in range(blocks):
        sl = slice(128 * b, 128 * b + 128)
        scores.append(dot_nt(head_stack(p_ref[sl, width : 2 * width], CHAR_HEADS, scale), p_ref[sl, 0:width]))
    for b in range(blocks):
        here = slot < counts_here[8 * b : 8 * b + 8][None]
        st = jnp.where(here[None], scores[b].reshape(CHAR_HEADS, CHARS, 8, 128), NEGATIVE)
        e = jnp.exp(st - jnp.max(st, 1, keepdims=True))
        r = jnp.where(same[None, None], 1.0 / jnp.sum(e, 1, keepdims=True), 0.0)
        a_ref[size * b : size * b + size, :] = (e * r).reshape(size, 128).astype(BF16)
    for b in range(blocks):
        sl = slice(128 * b, 128 * b + 128)
        a = a_ref[size * b : size * b + size, :]
        early_ref[sl, 0:width] = dot_tn(a, head_stack(p_ref[sl, 2 * width : 3 * width], CHAR_HEADS, 1.0)).astype(BF16)
    leaving[0].start()
    leaving[1].start()
    m = x + dot_nn(early_ref[:, 0:width], wout_ref[...])
    n2, rs2 = norm_fwd(m, gains[1:2])
    early_ref[:, width : 2 * width] = n2

    @pl.when(step == 1)
    def _():
        gather.pass_on(0)
        gather.pass_on(1)


    @pl.when(step == last)
    def _():
        gather.pass_on(2)

    f = m
    for i, j in enumerate(cuts):
        cut = slice(j, j + HIDDEN_CUT)
        act, slope = gelu_both(dot_nn(n2, wup_ref[:, cut]).astype(BF16))
        act_ref[:, cut] = act
        act_ref[:, hid + j : hid + j + HIDDEN_CUT] = slope
        leaving[2 + i].start()
        leaving[2 + len(cuts) + i].start()
        f = f + dot_nn(act, wdown_ref[cut, :])
    early_ref[:, 2 * width : 3 * width] = f.astype(BF16)
    t = jnp.sum(f * pool_ref[...].astype(F32).reshape(1, width), -1, keepdims=True).reshape(blocks, CHARS, 8, 1)
    counts = counts_here[:, 0:1].reshape(blocks, 1, 8, 1)
    t = jnp.where(lax.broadcasted_iota(jnp.int32, t.shape, 1) < counts, t, NEGATIVE)
    et = jnp.exp(t - jnp.max(t, 1, keepdims=True))
    aw = et / jnp.sum(et, 1, keepdims=True)
    early_ref[:, 3 * width :] = jnp.where(lane == 0, rs2, aw.reshape(rows, 1)).astype(BF16)
    pooled_ref[...] = jnp.sum(aw * f.reshape(blocks, CHARS, 8, width), 1).reshape(words, width).astype(BF16)

    @pl.when(step == last)
    def _():
        for k in range(1, n_dp):
            row_copy(k).wait()
        for j in range(3):
            seg_copy(j).wait()
        at_row = row_got[...].reshape(slots, 128)[:, 0:1].astype(F32) - 1.0
        lanes = lax.broadcasted_iota(jnp.int32, (slots, all_words), 1).astype(F32)
        place_ref[...] = jnp.where(lanes == at_row, 1.0, 0.0).astype(BF16)
        seg_out[...] = seg_all[...]
        gather.finish()
        for copy in out_copies(step - 1) + leaving:
            copy.wait()


def char_forward(n_dp, x, counts, gains, wqkv, wout, wup, wdown, pool, source, segments, slices):
    words, wide = x.shape
    width = wide // CHARS
    rows = words * CHARS
    step_rows = STEP_WORDS * CHARS
    cap = -(-2 * words // n_dp // 16) * 16
    slots = n_dp * cap
    full = lambda arr: pl.BlockSpec(arr.shape, lambda i: (0,) * arr.ndim)
    blk = lambda n, w: pl.BlockSpec((n, w), lambda i: (i, 0))
    hid = wup.shape[1]
    outs = [
        (words, STEP_WORDS, width), (rows, step_rows, 3 * width + 128), (rows, step_rows, width + 128),
        (rows, None, 3 * width), (rows * CHAR_HEADS, None, 128), (rows, None, 2 * hid),
    ]
    fixed = [((slots, words), BF16), ((slots, words), BF16), ((4, 8, words), jnp.int32)]
    any_spec = pl.BlockSpec(memory_space=pl.ANY)
    return pl.pallas_call(
        functools.partial(char_fwd_body, n_dp, cap),
        grid=(words // STEP_WORDS,),
        in_specs=[blk(STEP_WORDS, wide)]
        + [full(w) for w in (counts, gains, wqkv, wout, wup, wdown, pool, source, segments)]
        + [any_spec] * len(slices),
        out_specs=[blk(b, w) if b else any_spec for _, b, w in outs]
        + [pl.BlockSpec(s, lambda i, n=len(s): (0,) * n) for s, _ in fixed]
        + [any_spec] * len(slices),
        out_shape=[jax.ShapeDtypeStruct((n, w), BF16) for n, _, w in outs]
        + [jax.ShapeDtypeStruct(s, d) for s, d in fixed]
        + [jax.ShapeDtypeStruct((4, *s.shape), s.dtype) for s in slices],
        scratch_shapes=[
            pltpu.VMEM((words, 128), F32),
            pltpu.VMEM((n_dp, cap, 128), BF16), pltpu.VMEM((n_dp, cap, 128), BF16), pltpu.VMEM((4, 8, words), jnp.int32),
            pltpu.SemaphoreType.DMA((n_dp + 3,)), pltpu.SemaphoreType.DMA((n_dp + 3,)),
            pltpu.SemaphoreType.DMA((5 * len(slices),)), pltpu.SemaphoreType.DMA((5 * len(slices),)),
            pltpu.VMEM((2, step_rows, 3 * width), BF16), pltpu.VMEM((2, step_rows * CHAR_HEADS, 128), BF16),
            pltpu.VMEM((2, step_rows, 2 * hid), BF16),
            pltpu.SemaphoreType.DMA((2, 2 + 2 * (hid // HIDDEN_CUT))),
        ],
        compiler_params=pltpu.CompilerParams(collective_id=2, has_side_effects=True, vmem_limit_bytes=VMEM_LIMIT),
        name="char_forward",
    )(x, counts, gains, wqkv, wout, wup, wdown, pool, source, segments, *slices)


CHAR_A = 144
CHAR_CUT = 80
CHAR_B = 48
WORD_ROWS = 800
CHUNK_ROWS = 192
CHUNKS = ((0, 192), (192, 224), (224, 416), (416, 608), (608, 800))
ROW_QKV, ROW_PROJ, ROW_OUT, ROW_UP, ROW_DOWN = 0, 192, 224, 288, 544
SEMS = 8


def fold_half(block):
    half = block.shape[0] // 2
    return jnp.concatenate([block[:half], block[half:]], 1)


def unfold_half(block):
    return jnp.concatenate([block[:, :64], block[:, 64:]], 0)


class Halving:
    def __init__(self, n_z, sent, work, got, ssem, rsem, base, order):
        self.n_z, self.sent, self.work, self.got = n_z, sent, work, got
        self.ssem, self.rsem, self.base, self.order = ssem, rsem, base, order
        self.z, self.x, self.y, self.core = coordinates()

    def copies(self, phase):
        z, x, y, core = self.z, self.x, self.y, self.core
        work = self.work
        step = "c" if phase == 0 else self.order[phase - 1]
        if step == "c":
            pairs = [(self.sent, self.got[0], device_of(z, x, y, 1 - core))]
        elif step == "y":
            src = work.at[1 - y] if phase == 1 else work.at[1 - y, x]
            pairs = [(src, self.got[phase], device_of(z, x, 1 - y, core))]
        elif step == "x":
            src = work.at[:, 1 - x] if phase == 1 else work.at[y, 1 - x]
            pairs = [(src, self.got[phase], device_of(z, 1 - x, y, core))]
        else:
            pairs = []
            for k in range(1, self.n_z):
                other = lax.rem(z + k, self.n_z)
                pairs.append((work.at[y, x, other], self.got[3].at[k - 1], device_of(other, x, y, core)))
        return [
            remote_copy(src, dst, self.ssem, self.rsem, self.base + phase + i, peer)
            for i, (src, dst, peer) in enumerate(pairs)
        ]

    def start(self, phase):
        for copy in self.copies(phase):
            copy.start()

    def finish(self, phase):
        for copy in self.copies(phase):
            copy.wait()
        x, y = self.x, self.y
        work, got = self.work, self.got[phase]
        step = "c" if phase == 0 else self.order[phase - 1]

        def add(mine, other):
            def body(i, carry):
                mine[i] = mine[i] + other[i]
                return carry
            lax.fori_loop(0, self.n_z, body, 0)

        if step == "c":
            for i in range(2):
                for j in range(2):
                    add(work.at[i, j], got.at[i, j])
        elif step == "y" and phase == 1:
            for j in range(2):
                add(work.at[y, j], got.at[j])
        elif step == "x" and phase == 1:
            for i in range(2):
                add(work.at[i, x], got.at[i])
        elif step in "yx":
            add(work.at[y, x], got)

    def advance(self, phase):
        self.finish(phase)
        self.start(phase + 1)

    def total(self):
        value = self.work[self.y, self.x, self.z].astype(F32)
        for k in range(self.n_z - 1):
            value += self.got[3][k].astype(F32)
        return value

    @staticmethod
    def got_shapes(n_z, rows, first=0):
        shapes = [(2, 2, n_z, rows, 128), (2, n_z, rows, 128), (n_z, rows, 128), (n_z - 1, rows, 128)]
        return [pltpu.VMEM(s, BF16) for s in shapes[first:]]


class DirectSum:
    def __init__(self, n_dp, buf, got_mp, held, got_dp, ssem, rsem, base):
        self.n_dp, self.buf, self.got_mp, self.held, self.got_dp = n_dp, buf, got_mp, held, got_dp
        self.ssem, self.rsem, self.base = ssem, rsem, base
        self.dp, self.mp = lax.axis_index("dp"), lax.axis_index("mp")

    def copies(self, phase):
        dp, mp, n_dp = self.dp, self.mp, self.n_dp
        make = lambda src, dst, slot, peer: remote_copy(src, dst, self.ssem, self.rsem, self.base + slot, peer)
        if phase == 0:
            to = [lax.rem(mp + k, 4) for k in range(1, 4)]
            return [make(self.buf.at[p], self.got_mp.at[k], k, (dp, p)) for k, p in enumerate(to)]
        to = [lax.rem(dp + k, n_dp) for k in range(1, n_dp)]
        return [make(self.held.at[d], self.got_dp.at[k], 3 + k, (d, mp)) for k, d in enumerate(to)]

    def start(self, phase):
        for copy in self.copies(phase):
            copy.start()

    def advance(self):
        for copy in self.copies(0):
            copy.wait()
        got, buf, mp = self.got_mp, self.buf, self.mp

        def add(d, carry):
            total = buf[mp, d].astype(F32) + got[0, d].astype(F32)
            total = total + got[1, d].astype(F32) + got[2, d].astype(F32)
            self.held[d] = total.astype(self.held.dtype)
            return carry
        lax.fori_loop(0, self.n_dp, add, 0)
        self.start(1)

    def total(self):
        for copy in self.copies(1):
            copy.wait()
        value = self.held[self.dp].astype(F32)
        for k in range(self.n_dp - 1):
            value += self.got_dp[k].astype(F32)
        return value

    @staticmethod
    def shapes(n_dp, rows, dtype):
        shapes = [(4, n_dp, rows, 128), (3, n_dp, rows, 128), (n_dp, rows, 128), (n_dp - 1, rows, 128)]
        return [pltpu.VMEM(s, dtype) for s in shapes]


class GradientSums:
    def __init__(self, n_z, word_sum, refs):
        self.n_z, self.word_sum = n_z, word_sum
        abuf, wbuf, small, sgot, ssem, rsem, lsem, *got = refs
        self.abuf, self.wbuf, self.small, self.sgot = abuf, wbuf, small, sgot
        self.ssem, self.rsem, self.lsem = ssem, rsem, lsem
        self.z, self.x, self.y, self.core = coordinates()
        self.chunks = []
        for i, order in enumerate(("yxz", "yxz", "yxz", "xyz", "xyz")):
            rows = wbuf.at[:, :, :, CHUNKS[i][0] : CHUNKS[i][1]]
            self.chunks.append(
                Halving(n_z, None, rows, [None, *got[3 * i : 3 * i + 3]], ssem, rsem, SEMS * i, order)
            )
        core = self.core
        self.parts = []
        for i, (low, high, order) in enumerate(((0, CHAR_CUT, "yxz"), (CHAR_CUT, CHAR_A, "xyz"))):
            rows = abuf.at[:, :, :, :, low:high]
            at = 3 * len(CHUNKS) + 4 * i
            self.parts.append(
                Halving(n_z, rows.at[1 - core], rows.at[core], got[at : at + 4], ssem, rsem, (5 + i) * SEMS, order)
            )
        at = 3 * len(CHUNKS) + 8
        self.partb = DirectSum(2 * n_z, *got[at : at + 4], ssem, rsem, 7 * SEMS)
        self.tiny = 9 * SEMS

    @staticmethod
    def scratch(n_z):
        n_sem = 11 * SEMS
        shapes = [
            pltpu.VMEM((2, 2, 2, n_z, CHAR_A, 128), BF16), pltpu.VMEM((2, 2, n_z, WORD_ROWS, 128), BF16),
            pltpu.VMEM((2, 16, 128), F32), pltpu.VMEM((2 + 2 * n_z, 16, 128), F32),
            pltpu.SemaphoreType.DMA((n_sem,)), pltpu.SemaphoreType.DMA((n_sem,)), pltpu.SemaphoreType.DMA,
        ]
        for low, high in CHUNKS:
            shapes += Halving.got_shapes(n_z, high - low, 1)
        for rows in (CHAR_CUT, CHAR_A - CHAR_CUT):
            shapes += Halving.got_shapes(n_z, rows)
        return shapes + DirectSum.shapes(2 * n_z, CHAR_B, BF16)

    def begin(self):
        load = pltpu.make_async_copy(self.word_sum, self.wbuf, self.lsem)
        load.start()
        dp, mp, n_dp = self.partb.dp, self.partb.mp, 2 * self.n_z
        peers = [(lax.rem(dp + k, n_dp), mp) for k in range(1, n_dp)] + [(dp, lax.rem(mp + k, 4)) for k in range(1, 4)]
        barrier = pltpu.get_barrier_semaphore()
        for peer in peers:
            pl.semaphore_signal(barrier, inc=1, device_id=peer, device_id_type=MESH)
        pl.semaphore_wait(barrier, len(peers))
        load.wait()
        for i, phase in enumerate((3, 1, 1, 1, 2)):
            self.chunks[i].start(phase)

    def pack_a(self, gup_ref, gdown_ref, gout_ref):
        for d in range(2 * self.n_z):
            down = gdown_ref[128 * d : 128 * d + 128, :]
            out = gout_ref[32 * d : 32 * d + 32, :]
            for p in range(4):
                block = self.abuf.at[p % 2, p // 2, d % 2, d // 2]
                block[0:32, :] = gup_ref[32 * d : 32 * d + 32, 256 * p : 256 * p + 128].astype(BF16)
                block[32:64, :] = gup_ref[32 * d : 32 * d + 32, 256 * p + 128 : 256 * p + 256].astype(BF16)
                block[64:128, :] = fold_half(down[:, 64 * p : 64 * p + 64]).astype(BF16)
                block[128:144, :] = fold_half(out[:, 64 * p : 64 * p + 64]).astype(BF16)
        for part in self.parts:
            part.start(0)

    def pack_b(self, gqkv_ref):
        for d in range(2 * self.n_z):
            qkv = gqkv_ref[32 * d : 32 * d + 32, :]
            for p in range(4):
                own = qkv[:, 192 * p : 192 * p + 192]
                self.partb.buf[p, d, 0:32, :] = own[:, 0:128].astype(BF16)
                self.partb.buf[p, d, 32:48, :] = fold_half(own[:, 128:192]).astype(BF16)
        self.partb.start(0)

    def tiny_copies(self, phase):
        dp, mp, n_dp = self.partb.dp, self.partb.mp, 2 * self.n_z
        if phase == 0:
            peers = [(dp, lax.rem(mp + k, 4)) for k in range(1, 4)]
        else:
            peers = [(lax.rem(dp + k, n_dp), mp) for k in range(1, n_dp)]
        at = 3 * phase
        return [
            remote_copy(self.small.at[phase], self.sgot.at[at + k], self.ssem, self.rsem, self.tiny + at + k, peer)
            for k, peer in enumerate(peers)
        ]

    def tiny_start(self, phase):
        for copy in self.tiny_copies(phase):
            copy.start()

    def tiny_finish(self, phase):
        copies = self.tiny_copies(phase)
        for copy in copies:
            copy.wait()
        total = self.small[phase]
        for k in range(len(copies)):
            total += self.sgot[3 * phase + k]
        return total


def pack_small(cgain_ref, cpool_ref, gqkv_ref, wqkv_ref, gains_ref, wgain_ref):
    gains = gains_ref[...].astype(F32)
    width = gains.shape[1]
    first = jnp.sum(gqkv_ref[...] * wqkv_ref[...].astype(F32), -1, keepdims=True)
    first = jnp.transpose(jnp.broadcast_to(first, (width, 128)))[0:1, :]
    sums = [
        first / gains[0:1], jnp.sum(cgain_ref[...], 0, keepdims=True) / gains[1:2],
        jnp.sum(cpool_ref[...], 0, keepdims=True), wgain_ref[0:1, :], wgain_ref[1:2, :],
    ]
    rows = [v[:, t : t + 128] for v in sums for t in range(0, v.shape[1], 128)]
    rows.append(jnp.zeros((2, 128), F32))
    return jnp.concatenate(rows, 0)


def finish_body(
    dx_ref, wide_ref, sums_ref,
    odx_ref, owide_ref, oqkv_ref, oout_ref, oup_ref, odown_ref, oproj_ref, owqkv_ref, owout_ref, owup_ref, owdown_ref,
    ocgain_ref, opool_ref, owgain_ref,
):
    odx_ref[...] = dx_ref[...].astype(F32)

    @pl.when(pl.program_id(0) == 0)
    def _():
        base = WORD_ROWS
        owide_ref[...] = wide_ref[...]
        for t in range(3):
            owqkv_ref[t] = sums_ref[64 * t : 64 * t + 64, :]
        oproj_ref[...] = sums_ref[ROW_PROJ : ROW_PROJ + 32, :]
        owout_ref[...] = sums_ref[ROW_OUT : ROW_OUT + 64, :]
        for t in range(4):
            owup_ref[:, 128 * t : 128 * t + 128] = sums_ref[ROW_UP + 64 * t : ROW_UP + 64 * t + 64, :]
            owdown_ref[:, 128 * t : 128 * t + 128] = sums_ref[ROW_DOWN + 64 * t : ROW_DOWN + 64 * t + 64, :]
        oup_ref[:, 0:128] = sums_ref[base : base + 32, :]
        oup_ref[:, 128:256] = sums_ref[base + 32 : base + 64, :]
        odown_ref[...] = unfold_half(sums_ref[base + 64 : base + 128, :]).T
        oout_ref[...] = unfold_half(sums_ref[base + 128 : base + 144, :])
        base = WORD_ROWS + CHAR_A
        oqkv_ref[:, 0:128] = sums_ref[base : base + 32, :]
        oqkv_ref[:, 128:192] = unfold_half(sums_ref[base + 32 : base + 48, :])
        total = sums_ref[base + CHAR_B : base + CHAR_B + 16, :]
        for j in range(2):
            for t in range(2):
                ocgain_ref[j : j + 1, 128 * t : 128 * t + 128] = total[2 * j + t : 2 * j + t + 1]
            for t in range(4):
                owgain_ref[j : j + 1, 128 * t : 128 * t + 128] = total[6 + 4 * j + t : 7 + 4 * j + t]
        for t in range(2):
            opool_ref[:, 128 * t : 128 * t + 128] = total[4 + t : 5 + t]


def finish(d_chars, word_out, sums):
    words, wide = d_chars.shape
    steps = 2
    full = lambda s: pl.BlockSpec(s, lambda i: (0,) * len(s))
    blk = pl.BlockSpec((words // steps, wide), lambda i: (i, 0))
    outs = [
        word_out.shape, (32, 192), (32, 64), (32, 256), (64, 128), (32, 128),
        (3, 64, 128), (64, 128), (64, 512), (64, 512), (2, 256), (1, 256), (2, 512),
    ]
    result = pl.pallas_call(
        finish_body,
        grid=(steps,),
        in_specs=[blk, full(word_out.shape), full(sums.shape)],
        out_specs=[blk] + [full(s) for s in outs],
        out_shape=[jax.ShapeDtypeStruct((words, wide), F32), jax.ShapeDtypeStruct(outs[0], BF16)]
        + [jax.ShapeDtypeStruct(s, F32) for s in outs[1:]],
        compiler_params=pltpu.CompilerParams(vmem_limit_bytes=VMEM_LIMIT),
        name="finish",
    )(d_chars, word_out, sums)
    dx, out, qkv, cout, up, down, proj, wqkv, wout, wup, wdown, cgain, pool, wgain = result
    return (out, dx, qkv, cout, up, down.T, proj, wqkv, wout.T, wup, wdown.T, cgain, pool.reshape(-1), wgain)


def char_bwd_body(
    n_dp, fused,
    dpool_ref, gains_ref, pool_ref, wqkv_any, wout_any, wup_any, wdown_any,
    early_ref, late_ref, p_ref, a_ref, act_ref,
    *refs,
):
    if fused:
        word_sum, wgain_ref, dx_ref, sums_ref, *refs = refs
    else:
        dx_ref, *refs = refs
        outs, refs = refs[:6], refs[6:]
    gqkv_ref, gout_ref, gup_ref, gdown_ref, ggain_ref, gpool_ref, *refs = refs
    dm_ref, dp_ref, do_ref, ds_ref, wqkv_ref, wout_ref, wup_ref, wdown_ref, dp_now, do_now, wsem, *refs = refs
    step = pl.program_id(0)
    part = pl.num_programs(0) // 3
    words = dpool_ref.shape[0]
    width = wout_ref.shape[0]
    hid = wup_ref.shape[1]
    blocks = words // 8
    rows = words * CHARS
    size = CHAR_HEADS * 128
    gains = gains_ref[...].astype(F32)
    here = pl.ds(pl.multiple_of(lax.rem(step, part) * rows, rows), rows)
    sums = GradientSums(n_dp // 2, word_sum, refs) if fused else None
    chunks = sums.chunks if fused else None

    def at(when, act):
        if fused:
            pl.when(step == when)(act)

    @pl.when(step == 0)
    def _():
        pairs = ((wdown_any, wdown_ref), (wup_any, wup_ref), (wout_any, wout_ref), (wqkv_any, wqkv_ref))
        loads = [pltpu.make_async_copy(src, dst, wsem.at[i]) for i, (src, dst) in enumerate(pairs)]
        for load in loads:
            load.start()
        if fused:
            sums.begin()
        for load in loads:
            load.wait()
        for ref in (gqkv_ref, gout_ref, gup_ref, gdown_ref, ggain_ref, gpool_ref):
            ref[...] = jnp.zeros_like(ref)

    def event(when, *moves):
        def act():
            for sum_of, phase in moves:
                if phase < 3:
                    sum_of.advance(phase)
                else:
                    sum_of.finish(3)
        at(when, act)

    if fused:
        first, other = sums.parts
        event(2, (chunks[1], 1), (chunks[3], 1))
        event(3, (chunks[2], 1), (chunks[4], 2))
        event(4, (chunks[1], 2), (chunks[3], 2))
        event(5, (first, 0), (other, 0))
        event(6, (chunks[2], 2))
        event(7, (first, 1), (other, 1))
        event(9, (first, 2), (other, 2))

    @pl.when(step < part)
    def _():
        dpool = dpool_ref[...].astype(F32).reshape(blocks, 1, 8, width)
        f = early_ref[:, 2 * width : 3 * width].astype(F32).reshape(blocks, CHARS, 8, width)
        stat = early_ref[:, 3 * width :].astype(F32)
        aw = stat[:, 1:2].reshape(blocks, CHARS, 8, 1)
        g = jnp.sum(f * dpool, -1, keepdims=True)
        dt = aw * (g - jnp.sum(aw * g, 1, keepdims=True))
        gpool_ref[...] += jnp.sum((dt * f).reshape(rows // 8, 8, width), 0)
        df = (aw * dpool + dt * pool_ref[...].astype(F32).reshape(1, width)).reshape(rows, width)
        dfb = df.astype(BF16)
        n2 = early_ref[:, width : 2 * width]
        dn2 = None
        for j in range(0, wup_ref.shape[1], HIDDEN_CUT):
            cut = slice(j, j + HIDDEN_CUT)
            gdown_ref[cut, :] += dot_tn(act_ref[:, cut], dfb)
            dh = act_ref[:, hid + j : hid + j + HIDDEN_CUT] * dot_nt(dfb, wdown_ref[cut, :]).astype(BF16)
            gup_ref[:, cut] += dot_tn(n2, dh)
            term = dot_nt(dh, wup_ref[:, cut])
            dn2 = term if dn2 is None else dn2 + term
        d_norm, dnn = norm_bwd(dn2, n2, stat[:, 0:1], gains[1:2])
        ggain_ref[...] += jnp.sum(dnn.reshape(rows // 8, 8, width), 0)
        dm = df + d_norm
        dmb = dm.astype(BF16)
        dm_ref[here, :] = dmb
        gout_ref[...] += dot_tn(early_ref[:, 0:width], dmb)
        do_ref[here, :] = dot_nt(dmb, wout_ref[...]).astype(BF16)

    at(part - 1, lambda: sums.pack_a(gup_ref, gdown_ref, gout_ref))

    @pl.when((step >= part) & (step < 2 * part))
    def _():
        scale = (width // CHAR_HEADS) ** -0.5
        do_now[...] = do_ref[here, :]
        raw = []
        for b in range(blocks):
            sl = slice(128 * b, 128 * b + 128)
            raw.append(dot_nt(head_stack(p_ref[sl, 2 * width : 3 * width], CHAR_HEADS, 1.0), do_now[128 * b : 128 * b + 128, :]))
        for b in range(blocks):
            a = a_ref[size * b : size * b + size, :].astype(F32).reshape(CHAR_HEADS, CHARS, 8, 128)
            dpt = raw[b].reshape(CHAR_HEADS, CHARS, 8, 128)
            delta = jnp.sum(a * dpt, 1, keepdims=True)
            ds_ref[size * b : size * b + size, :] = (a * (dpt - delta)).reshape(size, 128).astype(BF16)
        for b in range(blocks):
            sl = slice(128 * b, 128 * b + 128)
            ds = ds_ref[size * b : size * b + size, :]
            k = head_stack(p_ref[sl, width : 2 * width], CHAR_HEADS, scale)
            dp_now[128 * b : 128 * b + 128, 0:width] = dot_tn(ds, k).astype(BF16)
        for b in range(blocks):
            sl = slice(128 * b, 128 * b + 128)
            cut = lambda h: ds_ref[size * b + 128 * h : size * b + 128 * h + 128, :]
            wide = jnp.concatenate([cut(h) for h in range(CHAR_HEADS)], 1)
            q = head_stack(p_ref[sl, 0:width], CHAR_HEADS, scale)
            dp_now[128 * b : 128 * b + 128, width : 2 * width] = dot_nn(wide, q).astype(BF16)
        for b in range(blocks):
            cut = lambda h: a_ref[size * b + 128 * h : size * b + 128 * h + 128, :]
            wide = jnp.concatenate([cut(h) for h in range(CHAR_HEADS)], 1)
            do = head_stack(do_now[128 * b : 128 * b + 128, :], CHAR_HEADS, 1.0)
            dp_now[128 * b : 128 * b + 128, 2 * width : 3 * width] = dot_nn(wide, do).astype(BF16)
        dp = dp_now[...]
        dp_ref[here, :] = dp
        gqkv_ref[...] += dot_tn(late_ref[:, 0:width], dp)

    def begin_b():
        sums.pack_b(gqkv_ref)
        sums.small[0] = pack_small(ggain_ref, gpool_ref, gqkv_ref, wqkv_ref, gains_ref, wgain_ref)
        sums.tiny_start(0)
    at(2 * part - 1, begin_b)

    @pl.when(step >= 2 * part)
    def _():
        dn1 = dot_nt(dp_ref[here, :], wqkv_ref[...])
        rstd = late_ref[:, width:].astype(F32)[:, 0:1]
        d_norm, _ = norm_bwd(dn1, late_ref[:, 0:width], rstd, gains[0:1])
        dx = dm_ref[here, :].astype(F32) + d_norm
        for b in range(0, blocks, 2):
            for c in range(CHARS):
                pair = [dx[128 * i + 8 * c : 128 * i + 8 * c + 8] for i in (b, b + 1)]
                dx_ref[8 * b : 8 * b + 16, width * c : width * c + width] = jnp.concatenate(pair, 0).astype(BF16)

    def end():
        sums.partb.advance()
        sums.small[1] = sums.tiny_finish(0)
        sums.tiny_start(1)
        for i, (low, high) in enumerate(CHUNKS):
            chunks[i].finish(3)
            sums_ref[low:high, :] = chunks[i].total()
        base = WORD_ROWS
        for i, (low, high) in enumerate(((0, CHAR_CUT), (CHAR_CUT, CHAR_A))):
            sums.parts[i].finish(3)
            sums_ref[base + low : base + high, :] = sums.parts[i].total()
        base += CHAR_A
        sums_ref[base + CHAR_B : base + CHAR_B + 16, :] = sums.tiny_finish(1)
        sums_ref[base : base + CHAR_B, :] = sums.partb.total()
    at(3 * part - 1, end)

    if not fused:
        @pl.when(step == 3 * part - 1)
        def _():
            for out, ref in zip(outs, (gqkv_ref, gout_ref, gup_ref, gdown_ref, ggain_ref, gpool_ref)):
                out[...] = ref[...]


def char_backward(n_dp, dpool, kept, gains, wqkv, wout, wup, wdown, pool, word_sum, wgain):
    words = dpool.shape[0]
    width = wout.shape[0]
    rows = words * CHARS
    step_rows = STEP_WORDS * CHARS
    steps = words // STEP_WORDS
    fused = word_sum is not None
    full = lambda arr: pl.BlockSpec(arr.shape, lambda i: (0,) * arr.ndim)
    fixed = lambda s: pl.BlockSpec(s, lambda i: (0,) * len(s))
    first = lambda n, w: pl.BlockSpec((n, w), lambda i: (lax.min(i, steps - 1), 0))
    second = lambda n, w: pl.BlockSpec((n, w), lambda i: (lax.clamp(0, i - steps, steps - 1), 0))
    third = lambda n, w: pl.BlockSpec((n, w), lambda i: (lax.max(i - 2 * steps, 0), 0))
    twice = lambda n, w: pl.BlockSpec((n, w), lambda i: (lax.rem(lax.max(i - steps, 0), steps), 0))
    grads = [wqkv.shape, wout.shape, wup.shape, wdown.shape, (8, width), (8, width)]
    scratch = [pltpu.VMEM(s, F32) for s in grads] + [
        pltpu.VMEM((rows, width), BF16), pltpu.VMEM((rows, 3 * width), BF16), pltpu.VMEM((rows, width), BF16),
        pltpu.VMEM((step_rows * CHAR_HEADS, 128), BF16), *[pltpu.VMEM(w.shape, BF16) for w in (wqkv, wout, wup, wdown)],
        pltpu.VMEM((step_rows, 3 * width), BF16), pltpu.VMEM((step_rows, width), BF16), pltpu.SemaphoreType.DMA((4,)),
    ]
    any_spec = pl.BlockSpec(memory_space=pl.ANY)
    args = [dpool, gains, pool, wqkv, wout, wup, wdown, *kept]
    in_specs = [first(STEP_WORDS, width), full(gains), full(pool)] + [any_spec] * 4
    in_specs += [f(r.shape[0] // steps, r.shape[1]) for f, r in zip((first, twice, second, second, first), kept)]
    params = dict(vmem_limit_bytes=VMEM_LIMIT)
    if fused:
        outs = [(WORD_ROWS + CHAR_A + CHAR_B + 16, 128)]
        args += [word_sum, wgain]
        in_specs += [pl.BlockSpec(memory_space=pl.ANY), full(wgain)]
        scratch += GradientSums.scratch(n_dp // 2)
        params.update(collective_id=1, has_side_effects=True)
    else:
        outs = grads
    return pl.pallas_call(
        functools.partial(char_bwd_body, n_dp, fused),
        grid=(3 * steps,),
        in_specs=in_specs,
        out_specs=[third(STEP_WORDS, CHARS * width)] + [fixed(s) for s in outs],
        out_shape=[jax.ShapeDtypeStruct((words, CHARS * width), BF16)] + [jax.ShapeDtypeStruct(s, F32) for s in outs],
        scratch_shapes=scratch,
        compiler_params=pltpu.CompilerParams(**params),
        name="char_backward",
    )(*args)


def word_body(
    n_dp, cap, packed,
    pooled_ref, onehot, place, seg_all, cot_ref, gains_ref, wproj_ref, *refs,
):
    slices, wholes, refs = refs[:4], refs[4:7], refs[7:]
    if packed:
        out_ref, dpool_ref, gsum_ref, ggain_ref, gbuf_ref, got_a, got_x, gq_ref, got_q, *refs = refs
    else:
        out_ref, dpool_ref, gqkv_ref, gout_ref, gup_ref, gdown_ref, gproj_ref, ggain_ref, *refs = refs
    (
        wqkv_ref, wout_ref, wup_ref, wdown_ref, vec_send, vec_got, segc_all, pooled_rows, rows_ref, normed_all, rstd_a,
        qkv_all, weights, o_send, o_all, act_ref, dh_ref, dact_ref, dm_ref,
        do_send, do_all, dk_acc, dv_acc, dqkv_send, dqkv_all, back_send, ret,
        ssem, rsem, lsem, wsend, wrecv,
    ) = refs
    dp, mp = lax.axis_index("dp"), lax.axis_index("mp")
    n_mp = 4
    words, narrow = pooled_ref.shape
    width = cot_ref.shape[1]
    slots = n_dp * cap
    pair = 2 * (width // HEADS)
    scale = (width // HEADS) ** -0.5
    to_dp = [(lax.rem(dp + k, n_dp), mp) for k in range(n_dp)]
    from_dp = [(lax.rem(dp + n_dp - k, n_dp), mp) for k in range(n_dp)]
    mates = [(mp // 2 * 2 + (mp + 1) % 2), (mp + 2) % 4, ((mp // 2 * 2 + 2) % 4 + (mp + 1) % 2)]
    barrier = pltpu.get_barrier_semaphore()
    for k in range(1, n_dp):
        pl.semaphore_signal(barrier, inc=1, device_id=to_dp[k], device_id_type=MESH)
    for mate in mates:
        pl.semaphore_signal(barrier, inc=1, device_id=(dp, mate), device_id_type=MESH)
    next_slot = [0]

    def send(src, dst, peer):
        slot = next_slot[0]
        next_slot[0] += 1
        copy = pltpu.make_async_remote_copy(
            src_ref=src, dst_ref=dst, send_sem=ssem.at[slot], recv_sem=rsem.at[slot],
            device_id=peer, device_id_type=MESH,
        )
        copy.start()
        return copy

    z, x, y, core = coordinates()
    loads = []
    for i, held in ((3, wdown_ref), (0, wqkv_ref), (1, wout_ref), (2, wup_ref)):
        loads.append([])
        for j, at in enumerate([mp] if i == 3 else [mp, *mates]):
            src = slices[i] if j == 0 else wholes[i].at[at]
            if i == 0:
                for t in range(3):
                    dst = held.at[at, :, pair * t : pair * t + pair]
                    loads[-1].append(pltpu.make_async_copy(src.at[t], dst, lsem.at[4 + t, j]))
            else:
                loads[-1].append(pltpu.make_async_copy(src, held.at[at], lsem.at[i, j]))
        for load in loads[-1]:
            load.start()
    vec_send[...] = dot_nn(onehot[...], pooled_ref[...]).astype(BF16).reshape(n_dp, cap, narrow)

    pl.semaphore_wait(barrier, n_dp - 1 + 3)
    vec_copies = [send(vec_send.at[k], vec_got.at[k], to_dp[k]) for k in range(1, n_dp)]
    down = WeightGather((slices[3],), (wdown_ref,), (True,), wsend, wrecv)
    down.begin()
    vec_got[0] = vec_send[0]
    gains = gains_ref[...].astype(F32)
    cot = cot_ref[...]
    for j in range(n_mp):
        segc_all[words * j : words * j + words, :] = as_column(seg_all[j, 0:1, :])
    for load in loads[1] + loads[2] + loads[3]:
        load.wait()
    for copy in vec_copies:
        copy.wait()
    pooled_rows[mp] = dot_tn(place[...], vec_got[...].reshape(slots, narrow)).astype(BF16)
    row_copies = [send(pooled_rows.at[mp], pooled_rows.at[mp], (dp, mate)) for mate in reversed(mates)]
    for turn, at in enumerate([mp, *mates]):
        if turn > 0:
            row_copies[3 - turn].wait()
        rows = dot_nn(pooled_rows[at], wproj_ref[...]).astype(BF16).astype(F32)
        n_w, rstd = norm_fwd(rows, gains[0:1])
        normed_all[at] = n_w
        if turn == 0:
            down.pass_on(0)
            rows_ref[...] = rows
            rstd_a[...] = rstd
        qkv_all[at] = dot_nn(n_w, wqkv_ref[mp]).astype(BF16)
    down.pass_last(0)

    low_lane = lax.broadcasted_iota(jnp.int32, (1, pair), 1) < pair // 2
    low_mask = jnp.where(low_lane, 1.0, 0.0).astype(BF16)
    high_mask = jnp.where(low_lane, 0.0, 1.0).astype(BF16)

    def heads(v, factor):
        return jnp.concatenate([v * (low_mask * factor).astype(BF16), v * (high_mask * factor).astype(BF16)], 0)

    o_copies = []
    for i in reversed(range(n_mp)):
        keys = words * (i + 1)
        q = heads(qkv_all[i, :, 0:pair], scale)
        k = qkv_all[0 : i + 1, :, pair : 2 * pair].reshape(keys, pair)
        v = qkv_all[0 : i + 1, :, 2 * pair : 3 * pair].reshape(keys, pair)
        same = segc_all[0:keys, 0:1] == seg_all[i, 0:1, :].astype(F32)
        key_at = lax.broadcasted_iota(jnp.int32, (keys, words), 0)
        query_at = lax.broadcasted_iota(jnp.int32, (keys, words), 1) + words * i
        allowed = same & (key_at <= query_at)
        st = jnp.where(jnp.concatenate([allowed, allowed], 1), dot_nt(k, q), NEGATIVE)
        ex = jnp.exp(st - jnp.max(st, 0, keepdims=True))
        at = (ex * (1.0 / jnp.sum(ex, 0, keepdims=True))).astype(BF16)
        weights[i, 0:keys, :] = at
        both = dot_tn(at, v)
        o_send[i] = jnp.where(low_lane, both[:words], both[words:]).astype(BF16)
    for mate in reversed(mates):
        o_copies.append(send(o_send.at[mate], o_all.at[mp], (dp, mate)))
    o_all[mp] = o_send[mp]
    down.finish()
    for load in loads[0]:
        load.wait()
    for p in range(n_mp):
        dact_ref[p] = dot_nt(cot, wdown_ref[p]).astype(BF16)
    for copy in o_copies:
        copy.wait()
    attended = jnp.concatenate([o_all[p] for p in range(n_mp)], 1)
    mid = rows_ref[...] + dot_nn(attended, wout_ref[...].reshape(width, width))
    n_w2, rstd2 = norm_fwd(mid, gains[1:2])
    out = mid
    dn2 = jnp.zeros((words, width), F32)
    for p in range(n_mp):
        act, slope = gelu_both(dot_nn(n_w2, wup_ref[p]).astype(BF16))
        act_ref[p] = act
        dh = slope * dact_ref[p]
        dh_ref[p] = dh
        out = out + dot_nn(act, wdown_ref[p])
        dn2 = dn2 + dot_nt(dh, wup_ref[p])
    out_ref[...] = out.astype(BF16)
    d_norm, dnn = norm_bwd(dn2, n_w2, rstd2, gains[1:2])
    gain_b = jnp.sum(dnn, 0, keepdims=True) / gains[1:2]
    d_mid = cot.astype(F32) + d_norm
    dm_ref[...] = d_mid
    d_att = d_mid.astype(BF16)
    do_copies = []
    for mate in reversed(mates):
        do_send[mate] = dot_nt(d_att, wout_ref[mate]).astype(BF16)
        do_copies.append(send(do_send.at[mate], do_all.at[mp], (dp, mate)))
    do_all[mp] = dot_nt(d_att, wout_ref[mp]).astype(BF16)

    def pair_sum(i):
        low, high = CHUNKS[i]
        src = gbuf_ref.at[1 - core, :, :, :, low:high]
        return send(src, got_a.at[:, :, :, low:high], device_of(z, x, y, 1 - core))

    def pair_add(i):
        low, high = CHUNKS[i]

        def add(i, carry):
            b, c, d = i // n_dp, (i // (n_dp // 2)) % 2, lax.rem(i, n_dp // 2)
            gsum_ref[b, c, d, low:high] = gbuf_ref[core, b, c, d, low:high] + got_a[b, c, d, low:high]
            return carry
        lax.fori_loop(0, 2 * n_dp, add, 0)

    def x_sum(i):
        low, high = CHUNKS[i]
        return send(gsum_ref.at[:, 1 - x, :, low:high], got_x, device_of(z, 1 - x, y, core))

    def x_add(i):
        low, high = CHUNKS[i]
        for b in range(2):
            for d in range(n_dp // 2):
                gsum_ref[b, x, d, low:high] += got_x[b, d]

    def put(base, p, grad):
        if packed:
            block = grad.shape[0] // n_dp
            for d in range(n_dp):
                for t in range(grad.shape[1] // 128):
                    gbuf_ref[p % 2, p // 2, d % 2, d // 2, base + block * t : base + block * t + block, :] = (
                        grad[block * d : block * d + block, 128 * t : 128 * t + 128].astype(BF16)
                    )
        elif base == ROW_PROJ:
            gproj_ref[:, 128 * p : 128 * p + 128] = grad
        else:
            ref = {ROW_OUT: gout_ref, ROW_UP: gup_ref, ROW_DOWN: gdown_ref}[base]
            ref[p] = grad

    for p in range(n_mp):
        put(ROW_DOWN, p, dot_tn(cot, act_ref[p]))
    if packed:
        pair_three = pair_sum(4)
    for p in range(n_mp):
        put(ROW_UP, p, dot_tn(n_w2, dh_ref[p]))
    if packed:
        pair_two = pair_sum(3)
    for p in range(n_mp):
        put(ROW_OUT, p, dot_tn(d_att, o_all[p]))
    if packed:
        pair_one = pair_sum(2)
        pair_three.wait()
        pair_add(4)
        x_three = x_sum(4)
    dk_acc[...] = jnp.zeros_like(dk_acc)
    dv_acc[...] = jnp.zeros_like(dv_acc)
    for copy in do_copies:
        copy.wait()
    for i in reversed(range(n_mp)):
        keys = words * (i + 1)
        q = qkv_all[i, :, 0:pair]
        k = qkv_all[0 : i + 1, :, pair : 2 * pair].reshape(keys, pair)
        v = qkv_all[0 : i + 1, :, 2 * pair : 3 * pair].reshape(keys, pair)
        do = heads(do_all[i], 1.0)
        at = weights[i, 0:keys, :]
        af = at.astype(F32)
        dpt = dot_nt(v, do)
        ds = (af * (dpt - jnp.sum(af * dpt, 0, keepdims=True))).astype(BF16)
        both = dot_tn(ds, k)
        dq = jnp.where(low_lane, both[:words], both[words:]) * scale
        dk_acc[0:keys, :] += dot_nn(ds, heads(q, scale))
        dv_acc[0:keys, :] += dot_nn(at, do)
        dqkv_send[i, :, 0:pair] = dq.astype(BF16)
        dqkv_send[i, :, pair : 2 * pair] = dk_acc[words * i : keys, :].astype(BF16)
        dqkv_send[i, :, 2 * pair : 3 * pair] = dv_acc[words * i : keys, :].astype(BF16)
    dqkv_copies = []
    for mate in reversed(mates):
        dqkv_copies.append(send(dqkv_send.at[mate], dqkv_all.at[mp], (dp, mate)))
    dqkv_all[mp] = dqkv_send[mp]
    grad_qkv = dot_tn(normed_all[...].reshape(n_mp * words, width), dqkv_send[...].reshape(n_mp * words, 3 * pair))
    if packed:
        block = width // n_dp
        for d in range(n_dp):
            for t in range(3):
                gq_ref[d % 2, d // 2, block * t : block * t + block, :] = (
                    grad_qkv[block * d : block * d + block, 128 * t : 128 * t + 128].astype(BF16)
                )
        q_sum = send(gq_ref.at[1 - x], got_q, device_of(z, 1 - x, y, core))
        pair_two.wait()
        pair_add(3)
        pair_one.wait()
        pair_add(2)
    else:
        gqkv_ref[...] = grad_qkv
    for copy in dqkv_copies:
        copy.wait()
    d_normed = jnp.zeros((words, width), F32)
    for p in range(n_mp):
        d_normed = d_normed + dot_nt(dqkv_all[p], wqkv_ref[p])
    d_first, dnn = norm_bwd(d_normed, normed_all[mp], rstd_a[...], gains[0:1])
    gain_a = jnp.sum(dnn, 0, keepdims=True) / gains[0:1]
    d_rows = (dm_ref[...] + d_first).astype(BF16)
    ggain_ref[0:1, :] = gain_a
    ggain_ref[1:2, :] = gain_b
    d_pooled = dot_nt(d_rows, wproj_ref[...]).astype(BF16)
    back_send[...] = dot_nn(place[...], d_pooled).astype(BF16).reshape(n_dp, cap, narrow)
    back_copies = [send(back_send.at[k], ret.at[k], from_dp[k]) for k in range(1, n_dp)]
    ret[0] = back_send[0]
    grad_proj = dot_tn(pooled_rows[mp], d_rows)
    for p in range(n_mp):
        put(ROW_PROJ, p, grad_proj[:, 128 * p : 128 * p + 128])
    if packed:
        pair_zero = pair_sum(1)
        q_sum.wait()
        low, high = CHUNKS[0]
        gsum_ref[y, x, :, low:high] = gq_ref[x] + got_q[...]
        x_three.wait()
        x_add(4)
        pair_zero.wait()
        pair_add(1)
    for copy in back_copies:
        copy.wait()
    dpool_ref[...] = dot_tn(onehot[...], ret[...].reshape(slots, narrow)).astype(BF16)


def word_layer(n_dp, pooled, onehot, place, segments, cotangent, gains, wproj, slices, wholes):
    words, narrow = pooled.shape
    width = cotangent.shape[1]
    wqkv, wout, wup = wholes
    n_mp = wqkv.shape[0]
    cap = -(-2 * words // n_dp // 16) * 16
    slots = cap * n_dp
    pair = 2 * (width // HEADS)
    packed = n_dp == 8
    outs = [((words, width), BF16), ((words, narrow), BF16)]
    if packed:
        outs.append(((2, 2, n_dp // 2, WORD_ROWS, 128), BF16))
    else:
        outs.append(((width, 3 * pair), F32))
        outs += [((n_mp, width, n), F32) for n in (pair, wup.shape[2], wup.shape[2])]
        outs.append(((narrow, width), F32))
    outs.append(((2, width), F32))
    hid = wup.shape[2]
    n_sem = 2 * (n_dp - 1) + 4 * 3 + 3 + 6
    vm = pl.BlockSpec(memory_space=pltpu.VMEM)
    args = (pooled, onehot, place, segments, cotangent, gains, wproj, *slices, *wholes)
    shapes = [
        ((n_mp, width, 3 * pair), BF16), (wout.shape, BF16), (wup.shape, BF16), ((n_mp, *slices[3].shape), BF16),
        ((n_dp, cap, narrow), BF16), ((n_dp, cap, narrow), BF16), ((n_mp * words, 128), F32), ((n_mp, words, narrow), BF16),
        ((words, width), F32), ((n_mp, words, width), BF16), ((words, 1), F32),
        ((n_mp, words, 3 * pair), BF16), ((n_mp, n_mp * words, 2 * words), BF16),
        ((n_mp, words, pair), BF16), ((n_mp, words, pair), BF16),
        ((n_mp, words, hid), BF16), ((n_mp, words, hid), BF16), ((n_mp, words, hid), BF16), ((words, width), F32),
        ((n_mp, words, pair), BF16), ((n_mp, words, pair), BF16), ((n_mp * words, pair), F32), ((n_mp * words, pair), F32),
        ((n_mp, words, 3 * pair), BF16), ((n_mp, words, 3 * pair), BF16), ((n_dp, cap, narrow), BF16), ((n_dp, cap, narrow), BF16),
    ]
    if packed:
        shapes = [
            ((2, 2, 2, n_dp // 2, WORD_ROWS, 128), BF16), ((2, 2, n_dp // 2, WORD_ROWS, 128), BF16),
            ((2, n_dp // 2, CHUNK_ROWS, 128), BF16),
            ((2, n_dp // 2, CHUNK_ROWS, 128), BF16), ((n_dp // 2, CHUNK_ROWS, 128), BF16), *shapes,
        ]
    return pl.pallas_call(
        functools.partial(word_body, n_dp, cap, packed),
        in_specs=[vm] * (len(args) - 7) + [pl.BlockSpec(memory_space=pl.ANY)] * 7,
        out_specs=[vm] * len(outs),
        out_shape=[jax.ShapeDtypeStruct(s, d) for s, d in outs],
        scratch_shapes=[pltpu.VMEM(s, d) for s, d in shapes]
        + [pltpu.SemaphoreType.DMA((n_sem,)), pltpu.SemaphoreType.DMA((n_sem,)), pltpu.SemaphoreType.DMA((7, 4)), pltpu.SemaphoreType.DMA((5,)), pltpu.SemaphoreType.DMA((5,))],
        compiler_params=pltpu.CompilerParams(collective_id=0, has_side_effects=True, vmem_limit_bytes=VMEM_LIMIT),
        name="word_layer",
    )(*args)


def plain_reduce(char_parts, char_gains, char_qkv, word_parts, word_gains):
    *char_mats, gain_rows, pool_rows = char_parts
    gain_sums = jnp.stack([jnp.sum(char_mats[0] * char_qkv.astype(F32), 1), jnp.sum(gain_rows, 0)]) / char_gains.astype(F32)
    small = lax.psum((gain_sums, jnp.sum(pool_rows, 0), word_gains), ("dp", "mp"))
    mats = []
    for grad in char_mats:
        part = lax.psum_scatter(grad, "dp", scatter_dimension=0, tiled=True)
        part = lax.psum_scatter(part.astype(BF16), "mp", scatter_dimension=1, tiled=True)
        mats.append(part.astype(F32))
    qkv, *rest = word_parts
    words = []
    for grad in rest:
        part = lax.psum_scatter(grad, "dp", scatter_dimension=1, tiled=True)
        words.append(lax.psum_scatter(part, "mp", scatter_dimension=0, tiled=False))
    out, up, down = words
    qkv = lax.psum_scatter(qkv, "dp", scatter_dimension=0, tiled=True)
    qkv = jnp.transpose(qkv.reshape(qkv.shape[0], 3, -1), (1, 0, 2))
    return (*mats, qkv, out.T, up, down.T, *small)


def per_device(
    char_input,
    char_counts,
    word_source,
    segment_ids,
    cotangent,
    char_norm_gains,
    char_qkv,
    char_out,
    char_up,
    char_down,
    pool_vector,
    char_proj,
    word_norm_gains,
    word_qkv,
    word_out,
    word_up,
    word_down,
):
    groups = lax.axis_size("dp")
    char_weights = (char_norm_gains, char_qkv, char_out, char_up, char_down, pool_vector)
    slices = (word_qkv, word_out, word_up, word_down)
    pooled, *kept = char_forward(
        groups, char_input, char_counts.reshape(1, -1), *char_weights,
        word_source.reshape(1, -1), segment_ids.reshape(1, -1), slices[:3],
    )
    char_kept, (onehot, place, segments, *word_weights) = kept[:5], kept[5:]
    output, d_pooled, *word_parts, word_gains = word_layer(
        groups, pooled, onehot, place, segments, cotangent, word_norm_gains, char_proj, slices, word_weights
    )
    fused = groups == 8
    d_chars, *char_parts = char_backward(
        groups, d_pooled, char_kept, *char_weights, word_parts[0] if fused else None, word_gains
    )
    if fused:
        return finish(d_chars, output, char_parts[0])
    *word_parts, grad_proj = word_parts
    char_parts = (*char_parts[:4], grad_proj, *char_parts[4:])
    *mats, grad_char_gains, grad_pool, grad_word_gains = plain_reduce(
        char_parts, char_norm_gains, char_qkv, word_parts, word_gains
    )
    return (output, d_chars.astype(F32), *mats, grad_char_gains, grad_pool, grad_word_gains)


def solution(mesh):
    placed = (
        P(("dp", "mp"), None),
        P(("dp", "mp")),
        P(("dp", "mp")),
        P(("dp", "mp")),
        P(("dp", "mp"), None),
        P(),
        P(),
        P(),
        P(),
        P(),
        P(),
        P(),
        P(),
        P(None, None, "mp"),
        P("mp", None),
        P(None, "mp"),
        P("mp", None),
    )
    return jax.shard_map(
        per_device,
        mesh=mesh,
        in_specs=placed,
        out_specs=(
            P(("dp", "mp"), None),
            P(("dp", "mp"), None),
            P("dp", "mp"),
            P("dp", "mp"),
            P("dp", "mp"),
            P("dp", "mp"),
            P("dp", "mp"),
            P(None, "dp", "mp"),
            P("mp", "dp"),
            P("dp", "mp"),
            P("mp", "dp"),
            P(),
            P(),
            P(),
        ),
        check_vma=False,
    )
```

```python
import functools
import jax
import jax.numpy as jnp
from jax import lax
from jax.experimental import pallas as pl
from jax.experimental.pallas import tpu as pltpu
from jax.sharding import PartitionSpec as P

HEADS = 8
CHARS = 16
CHAR_HEADS = 4
EPSILON = 1e-05
NEGATIVE = -1e30
GELU_A = 0.7978845608028654
GELU_B = 0.044715
F32 = jnp.float32
BF16 = jnp.bfloat16
MESH = pl.DeviceIdType.MESH
VMEM_LIMIT = 62 * 1024 * 1024
STEP_WORDS = 64
HIDDEN_CUT = 256


def dot_nn(left, right):
    return jnp.dot(left, right, preferred_element_type=F32)


def dot_nt(left, right):
    return lax.dot_general(left, right, (((1,), (1,)), ((), ())), preferred_element_type=F32)


def dot_tn(left, right):
    return lax.dot_general(left, right, (((0,), (0,)), ((), ())), preferred_element_type=F32)


def as_column(row):
    return jnp.transpose(jnp.broadcast_to(row.astype(F32), (128, row.shape[1])))


def head_stack(values, heads, factor):
    width = values.shape[1] // heads
    lane = lax.broadcasted_iota(jnp.int32, (1, values.shape[1]), 1) // width
    return jnp.concatenate(
        [values * jnp.where(lane == h, factor, 0.0).astype(values.dtype) for h in range(heads)], 0
    )


def gelu_both(hidden):
    c = lambda value: jnp.asarray(value, hidden.dtype)
    square = hidden * hidden
    tanh = jnp.tanh(hidden * (c(GELU_A) + c(GELU_A * GELU_B) * square))
    half = c(0.5) + c(0.5) * tanh
    slope = half + (c(0.5) * hidden) * (c(1.0) - tanh * tanh) * (c(GELU_A) + c(3.0 * GELU_A * GELU_B) * square)
    return hidden * half, slope


def norm_fwd(values, gain):
    mean = jnp.mean(values, -1, keepdims=True)
    centered = values - mean
    rstd = lax.rsqrt(jnp.mean(centered * centered, -1, keepdims=True) + EPSILON)
    return (centered * rstd * gain).astype(BF16), rstd


def norm_bwd(dn, n, rstd, gain):
    n = n.astype(F32)
    d1 = dn * gain
    dnn = dn * n
    m1 = jnp.mean(d1, -1, keepdims=True)
    m2 = jnp.mean(dnn, -1, keepdims=True)
    return rstd * (d1 - m1 - n * (1.0 / gain) * m2), dnn


def coordinates():
    dp, mp = lax.axis_index("dp"), lax.axis_index("mp")
    return dp // 2, dp % 2, mp // 2, mp % 2


def device_of(z, x, y, core):
    return (z * 2 + x, y * 2 + core)


def remote_copy(src, dst, ssem, rsem, slot, peer):
    return pltpu.make_async_remote_copy(
        src_ref=src, dst_ref=dst, send_sem=ssem.at[slot], recv_sem=rsem.at[slot],
        device_id=peer, device_id_type=MESH,
    )


class WeightGather:
    def __init__(self, slices, wholes, split, ssem, rsem):
        self.slices, self.wholes, self.split, self.ssem, self.rsem = slices, wholes, split, ssem, rsem
        self.z, self.x, self.y, self.core = coordinates()
        self.mp = self.y * 2 + self.core
        self.across = (1 - self.y) * 2 + self.core

    @staticmethod
    def half(ref, axis, which):
        rows = ref.shape[axis] // 2
        return ref.at[(slice(None),) * axis + (pl.ds(pl.multiple_of(which * rows, rows), rows),)]

    def copy(self, i, kind):
        z, x, y, core = self.z, self.x, self.y, self.core
        piece, whole = self.slices[i], self.wholes[i]
        axis = len(piece.shape) - 2
        far = whole.at[self.across]
        if kind == "far":
            src, dst = piece, whole.at[self.mp]
            if self.split[i]:
                src, dst = self.half(src, axis, x), self.half(dst, axis, x)
            peer = device_of(z, x, 1 - y, core)
        elif kind == "near":
            src, dst, peer = piece, whole.at[self.mp], device_of(z, x, y, 1 - core)
        else:
            which = 1 - x if kind == "late" else x
            src = dst = self.half(far, axis, which) if self.split[i] else far
            peer = device_of(z, 1 - x, y, core) if kind == "side" else device_of(z, x, y, 1 - core)
        slot = i * 5 + ("far", "near", "side", "early", "late").index(kind)
        return remote_copy(src, dst, self.ssem, self.rsem, slot, peer)

    def peers(self):
        z, x, y, core = self.z, self.x, self.y, self.core
        return [device_of(z, x, 1 - y, core), device_of(z, x, y, 1 - core), device_of(z, 1 - x, y, core)]

    def begin(self):
        for i in range(len(self.slices)):
            self.copy(i, "far").start()
        for i in range(len(self.slices)):
            self.copy(i, "near").start()

    def pass_on(self, i):
        self.copy(i, "far").wait()
        if self.split[i]:
            self.copy(i, "side").start()
        self.copy(i, "early").start()

    def pass_last(self, i):
        self.copy(i, "side").wait()
        self.copy(i, "late").start()

    def finish(self):
        for i in range(len(self.slices)):
            for kind in ("near", "early", "late")[: 2 + self.split[i]]:
                self.copy(i, kind).wait()


def char_fwd_body(
    n_dp, cap,
    x_ref, cnt_ref, gains_ref, wqkv_ref, wout_ref, wup_ref, wdown_ref, pool_ref,
    src_ref, seg_ref, s_qkv, s_out, s_up,
    pooled_ref, early_ref, late_ref, p_any, a_any, act_any,
    onehot_ref, place_ref, seg_out, g_qkv, g_out, g_up,
    cnt_col, row_send, row_got, seg_all, ssem, rsem, wsend, wrecv, p_buf, a_buf, act_buf, osem,
):
    step, last = pl.program_id(0), pl.num_programs(0) - 1
    dp, mp = lax.axis_index("dp"), lax.axis_index("mp")
    gather = WeightGather((s_qkv, s_out, s_up), (g_qkv, g_out, g_up), (True, True, False), wsend, wrecv)
    mates = [mp // 2 * 2 + (mp + 1) % 2, (mp + 2) % 4, (mp // 2 * 2 + 2) % 4 + (mp + 1) % 2]
    all_words = src_ref.shape[1]
    slots = n_dp * cap
    row_copy = lambda k: remote_copy(row_send.at[k], row_got.at[k], ssem, rsem, k, (lax.rem(dp + k, n_dp), mp))
    seg_copy = lambda j: remote_copy(seg_all.at[mp], seg_all.at[mp], ssem, rsem, n_dp + j, (dp, mates[j]))

    @pl.when(step == 0)
    def _():
        barrier = pltpu.get_barrier_semaphore()
        greeted = [(lax.rem(dp + k, n_dp), mp) for k in range(1, n_dp)] + [(dp, mate) for mate in mates]
        for peer in greeted:
            pl.semaphore_signal(barrier, inc=1, device_id=peer, device_id_type=MESH)
        source = src_ref[...]
        owner = source // (all_words * 4)
        owner_c = as_column(owner)[:, 0:1]
        index_r = lax.broadcasted_iota(jnp.int32, (all_words, all_words), 0)
        index_c = lax.broadcasted_iota(jnp.int32, (all_words, all_words), 1)
        earlier = (owner_c == owner.astype(F32)) & (index_r < index_c)
        rank = jnp.sum(jnp.where(earlier, 1.0, 0.0), 0, keepdims=True).astype(jnp.int32)
        slot_of = lax.rem(owner - dp + n_dp, n_dp) * cap + rank
        at_slot = lax.broadcasted_iota(jnp.int32, (slots, all_words), 0) == slot_of
        onehot_ref[...] = jnp.where(at_slot, 1.0, 0.0).astype(BF16)
        row_mat = as_column(lax.rem(source, all_words) + 1).astype(BF16)
        row_send[...] = dot_nn(onehot_ref[...], row_mat).astype(BF16).reshape(n_dp, cap, 128)
        seg_all[mp] = jnp.broadcast_to(seg_ref[...], (8, all_words))
        cnt_col[...] = as_column(cnt_ref[...])
        pl.semaphore_wait(barrier, len(greeted))
        gather.begin()
        for k in range(1, n_dp):
            row_copy(k).start()
        for j in range(3):
            seg_copy(j).start()
        row_got[0] = row_send[0]

    @pl.when(step == last)
    def _():
        gather.pass_last(0)
        gather.pass_last(1)

    words, wide = x_ref.shape
    width = wide // CHARS
    blocks = words // 8
    gains = gains_ref[...].astype(F32)
    counts_here = cnt_col[pl.ds(pl.multiple_of(step * words, words), words), :].astype(jnp.int32)
    pieces = []
    for g in range(words // 16):
        xt = x_ref[16 * g : 16 * g + 16, :].astype(F32)
        for half in range(2):
            for c in range(CHARS):
                pieces.append(xt[8 * half : 8 * half + 8, width * c : width * c + width])
    x = jnp.concatenate(pieces, 0)
    hid = wup_ref.shape[1]
    rows = words * CHARS
    cuts = range(0, hid, HIDDEN_CUT)
    held = lax.rem(step, 2)
    p_ref, a_ref, act_ref = p_buf.at[held], a_buf.at[held], act_buf.at[held]

    def out_copies(of):
        slot = lax.rem(of, 2)
        at = lambda n: pl.ds(pl.multiple_of(of * n, n), n)
        heads = rows * CHAR_HEADS
        copies = [
            pltpu.make_async_copy(p_buf.at[slot], p_any.at[at(rows)], osem.at[slot, 0]),
            pltpu.make_async_copy(a_buf.at[slot], a_any.at[at(heads)], osem.at[slot, 1]),
        ]
        for i in range(2 * hid // HIDDEN_CUT):
            cut = pl.ds(HIDDEN_CUT * i, HIDDEN_CUT)
            copies.append(pltpu.make_async_copy(act_buf.at[slot, :, cut], act_any.at[at(rows), cut], osem.at[slot, 2 + i]))
        return copies

    leaving = out_copies(step)

    @pl.when(step >= 2)
    def _():
        for copy in out_copies(step - 2):
            copy.wait()

    n1, rs1 = norm_fwd(x, gains[0:1])
    lane = lax.broadcasted_iota(jnp.int32, (rows, 128), 1)
    late_ref[:, 0:width] = n1
    late_ref[:, width:] = jnp.where(lane == 0, rs1, 0.0).astype(BF16)
    p_ref[...] = dot_nn(n1, wqkv_ref[...]).astype(BF16)
    row_w = lax.broadcasted_iota(jnp.int32, (8, 128), 0)
    lane_w = lax.broadcasted_iota(jnp.int32, (8, 128), 1) % 8
    same = row_w == lane_w
    slot = lax.broadcasted_iota(jnp.int32, (CHARS, 8, 128), 0)
    size = CHAR_HEADS * 128
    scale = (width // CHAR_HEADS) ** -0.5
    scores = []
    for b in range(blocks):
        sl = slice(128 * b, 128 * b + 128)
        scores.append(dot_nt(head_stack(p_ref[sl, width : 2 * width], CHAR_HEADS, scale), p_ref[sl, 0:width]))
    for b in range(blocks):
        here = slot < counts_here[8 * b : 8 * b + 8][None]
        st = jnp.where(here[None], scores[b].reshape(CHAR_HEADS, CHARS, 8, 128), NEGATIVE)
        e = jnp.exp(st - jnp.max(st, 1, keepdims=True))
        r = jnp.where(same[None, None], 1.0 / jnp.sum(e, 1, keepdims=True), 0.0)
        a_ref[size * b : size * b + size, :] = (e * r).reshape(size, 128).astype(BF16)
    for b in range(blocks):
        sl = slice(128 * b, 128 * b + 128)
        a = a_ref[size * b : size * b + size, :]
        early_ref[sl, 0:width] = dot_tn(a, head_stack(p_ref[sl, 2 * width : 3 * width], CHAR_HEADS, 1.0)).astype(BF16)
    leaving[0].start()
    leaving[1].start()
    m = x + dot_nn(early_ref[:, 0:width], wout_ref[...])
    n2, rs2 = norm_fwd(m, gains[1:2])
    early_ref[:, width : 2 * width] = n2

    @pl.when(step == 1)
    def _():
        gather.pass_on(0)
        gather.pass_on(1)


    @pl.when(step == last)
    def _():
        gather.pass_on(2)

    f = m
    for i, j in enumerate(cuts):
        cut = slice(j, j + HIDDEN_CUT)
        act, slope = gelu_both(dot_nn(n2, wup_ref[:, cut]).astype(BF16))
        act_ref[:, cut] = act
        act_ref[:, hid + j : hid + j + HIDDEN_CUT] = slope
        leaving[2 + i].start()
        leaving[2 + len(cuts) + i].start()
        f = f + dot_nn(act, wdown_ref[cut, :])
    early_ref[:, 2 * width : 3 * width] = f.astype(BF16)
    t = jnp.sum(f * pool_ref[...].astype(F32).reshape(1, width), -1, keepdims=True).reshape(blocks, CHARS, 8, 1)
    counts = counts_here[:, 0:1].reshape(blocks, 1, 8, 1)
    t = jnp.where(lax.broadcasted_iota(jnp.int32, t.shape, 1) < counts, t, NEGATIVE)
    et = jnp.exp(t - jnp.max(t, 1, keepdims=True))
    aw = et / jnp.sum(et, 1, keepdims=True)
    early_ref[:, 3 * width :] = jnp.where(lane == 0, rs2, aw.reshape(rows, 1)).astype(BF16)
    pooled_ref[...] = jnp.sum(aw * f.reshape(blocks, CHARS, 8, width), 1).reshape(words, width).astype(BF16)

    @pl.when(step == last)
    def _():
        for k in range(1, n_dp):
            row_copy(k).wait()
        for j in range(3):
            seg_copy(j).wait()
        at_row = row_got[...].reshape(slots, 128)[:, 0:1].astype(F32) - 1.0
        lanes = lax.broadcasted_iota(jnp.int32, (slots, all_words), 1).astype(F32)
        place_ref[...] = jnp.where(lanes == at_row, 1.0, 0.0).astype(BF16)
        seg_out[...] = seg_all[...]
        gather.finish()
        for copy in out_copies(step - 1) + leaving:
            copy.wait()


def char_forward(n_dp, x, counts, gains, wqkv, wout, wup, wdown, pool, source, segments, slices):
    words, wide = x.shape
    width = wide // CHARS
    rows = words * CHARS
    step_rows = STEP_WORDS * CHARS
    cap = -(-2 * words // n_dp // 16) * 16
    slots = n_dp * cap
    full = lambda arr: pl.BlockSpec(arr.shape, lambda i: (0,) * arr.ndim)
    blk = lambda n, w: pl.BlockSpec((n, w), lambda i: (i, 0))
    hid = wup.shape[1]
    outs = [
        (words, STEP_WORDS, width), (rows, step_rows, 3 * width + 128), (rows, step_rows, width + 128),
        (rows, None, 3 * width), (rows * CHAR_HEADS, None, 128), (rows, None, 2 * hid),
    ]
    fixed = [((slots, words), BF16), ((slots, words), BF16), ((4, 8, words), jnp.int32)]
    any_spec = pl.BlockSpec(memory_space=pl.ANY)
    return pl.pallas_call(
        functools.partial(char_fwd_body, n_dp, cap),
        grid=(words // STEP_WORDS,),
        in_specs=[blk(STEP_WORDS, wide)]
        + [full(w) for w in (counts, gains, wqkv, wout, wup, wdown, pool, source, segments)]
        + [any_spec] * len(slices),
        out_specs=[blk(b, w) if b else any_spec for _, b, w in outs]
        + [pl.BlockSpec(s, lambda i, n=len(s): (0,) * n) for s, _ in fixed]
        + [any_spec] * len(slices),
        out_shape=[jax.ShapeDtypeStruct((n, w), BF16) for n, _, w in outs]
        + [jax.ShapeDtypeStruct(s, d) for s, d in fixed]
        + [jax.ShapeDtypeStruct((4, *s.shape), s.dtype) for s in slices],
        scratch_shapes=[
            pltpu.VMEM((words, 128), F32),
            pltpu.VMEM((n_dp, cap, 128), BF16), pltpu.VMEM((n_dp, cap, 128), BF16), pltpu.VMEM((4, 8, words), jnp.int32),
            pltpu.SemaphoreType.DMA((n_dp + 3,)), pltpu.SemaphoreType.DMA((n_dp + 3,)),
            pltpu.SemaphoreType.DMA((5 * len(slices),)), pltpu.SemaphoreType.DMA((5 * len(slices),)),
            pltpu.VMEM((2, step_rows, 3 * width), BF16), pltpu.VMEM((2, step_rows * CHAR_HEADS, 128), BF16),
            pltpu.VMEM((2, step_rows, 2 * hid), BF16),
            pltpu.SemaphoreType.DMA((2, 2 + 2 * (hid // HIDDEN_CUT))),
        ],
        compiler_params=pltpu.CompilerParams(collective_id=2, has_side_effects=True, vmem_limit_bytes=VMEM_LIMIT),
        name="char_forward",
    )(x, counts, gains, wqkv, wout, wup, wdown, pool, source, segments, *slices)


CHAR_A = 144
CHAR_CUT = 80
CHAR_B = 48
WORD_ROWS = 800
CHUNK_ROWS = 192
CHUNKS = ((0, 192), (192, 224), (224, 416), (416, 608), (608, 800))
ROW_QKV, ROW_PROJ, ROW_OUT, ROW_UP, ROW_DOWN = 0, 192, 224, 288, 544
SEMS = 8


def fold_half(block):
    half = block.shape[0] // 2
    return jnp.concatenate([block[:half], block[half:]], 1)


def unfold_half(block):
    return jnp.concatenate([block[:, :64], block[:, 64:]], 0)


class Halving:
    def __init__(self, n_z, sent, work, got, ssem, rsem, base, order):
        self.n_z, self.sent, self.work, self.got = n_z, sent, work, got
        self.ssem, self.rsem, self.base, self.order = ssem, rsem, base, order
        self.z, self.x, self.y, self.core = coordinates()

    def copies(self, phase):
        z, x, y, core = self.z, self.x, self.y, self.core
        work = self.work
        step = "c" if phase == 0 else self.order[phase - 1]
        if step == "c":
            pairs = [(self.sent, self.got[0], device_of(z, x, y, 1 - core))]
        elif step == "y":
            src = work.at[1 - y] if phase == 1 else work.at[1 - y, x]
            pairs = [(src, self.got[phase], device_of(z, x, 1 - y, core))]
        elif step == "x":
            src = work.at[:, 1 - x] if phase == 1 else work.at[y, 1 - x]
            pairs = [(src, self.got[phase], device_of(z, 1 - x, y, core))]
        else:
            pairs = []
            for k in range(1, self.n_z):
                other = lax.rem(z + k, self.n_z)
                pairs.append((work.at[y, x, other], self.got[3].at[k - 1], device_of(other, x, y, core)))
        return [
            remote_copy(src, dst, self.ssem, self.rsem, self.base + phase + i, peer)
            for i, (src, dst, peer) in enumerate(pairs)
        ]

    def start(self, phase):
        for copy in self.copies(phase):
            copy.start()

    def finish(self, phase):
        for copy in self.copies(phase):
            copy.wait()
        x, y = self.x, self.y
        work, got = self.work, self.got[phase]
        step = "c" if phase == 0 else self.order[phase - 1]

        def add(mine, other):
            def body(i, carry):
                mine[i] = mine[i] + other[i]
                return carry
            lax.fori_loop(0, self.n_z, body, 0)

        if step == "c":
            for i in range(2):
                for j in range(2):
                    add(work.at[i, j], got.at[i, j])
        elif step == "y" and phase == 1:
            for j in range(2):
                add(work.at[y, j], got.at[j])
        elif step == "x" and phase == 1:
            for i in range(2):
                add(work.at[i, x], got.at[i])
        elif step in "yx":
            add(work.at[y, x], got)

    def advance(self, phase):
        self.finish(phase)
        self.start(phase + 1)

    def total(self):
        value = self.work[self.y, self.x, self.z].astype(F32)
        for k in range(self.n_z - 1):
            value += self.got[3][k].astype(F32)
        return value

    @staticmethod
    def got_shapes(n_z, rows, first=0):
        shapes = [(2, 2, n_z, rows, 128), (2, n_z, rows, 128), (n_z, rows, 128), (n_z - 1, rows, 128)]
        return [pltpu.VMEM(s, BF16) for s in shapes[first:]]


class DirectSum:
    def __init__(self, n_dp, buf, got_mp, held, got_dp, ssem, rsem, base):
        self.n_dp, self.buf, self.got_mp, self.held, self.got_dp = n_dp, buf, got_mp, held, got_dp
        self.ssem, self.rsem, self.base = ssem, rsem, base
        self.dp, self.mp = lax.axis_index("dp"), lax.axis_index("mp")

    def copies(self, phase):
        dp, mp, n_dp = self.dp, self.mp, self.n_dp
        make = lambda src, dst, slot, peer: remote_copy(src, dst, self.ssem, self.rsem, self.base + slot, peer)
        if phase == 0:
            to = [lax.rem(mp + k, 4) for k in range(1, 4)]
            return [make(self.buf.at[p], self.got_mp.at[k], k, (dp, p)) for k, p in enumerate(to)]
        to = [lax.rem(dp + k, n_dp) for k in range(1, n_dp)]
        return [make(self.held.at[d], self.got_dp.at[k], 3 + k, (d, mp)) for k, d in enumerate(to)]

    def start(self, phase):
        for copy in self.copies(phase):
            copy.start()

    def advance(self):
        for copy in self.copies(0):
            copy.wait()
        got, buf, mp = self.got_mp, self.buf, self.mp

        def add(d, carry):
            total = buf[mp, d].astype(F32) + got[0, d].astype(F32)
            total = total + got[1, d].astype(F32) + got[2, d].astype(F32)
            self.held[d] = total.astype(self.held.dtype)
            return carry
        lax.fori_loop(0, self.n_dp, add, 0)
        self.start(1)

    def total(self):
        for copy in self.copies(1):
            copy.wait()
        value = self.held[self.dp].astype(F32)
        for k in range(self.n_dp - 1):
            value += self.got_dp[k].astype(F32)
        return value

    @staticmethod
    def shapes(n_dp, rows, dtype):
        shapes = [(4, n_dp, rows, 128), (3, n_dp, rows, 128), (n_dp, rows, 128), (n_dp - 1, rows, 128)]
        return [pltpu.VMEM(s, dtype) for s in shapes]


class GradientSums:
    def __init__(self, n_z, word_sum, refs):
        self.n_z, self.word_sum = n_z, word_sum
        abuf, wbuf, small, sgot, ssem, rsem, lsem, *got = refs
        self.abuf, self.wbuf, self.small, self.sgot = abuf, wbuf, small, sgot
        self.ssem, self.rsem, self.lsem = ssem, rsem, lsem
        self.z, self.x, self.y, self.core = coordinates()
        self.chunks = []
        for i, order in enumerate(("yxz", "yxz", "yxz", "xyz", "xyz")):
            rows = wbuf.at[:, :, :, CHUNKS[i][0] : CHUNKS[i][1]]
            self.chunks.append(
                Halving(n_z, None, rows, [None, *got[3 * i : 3 * i + 3]], ssem, rsem, SEMS * i, order)
            )
        core = self.core
        self.parts = []
        for i, (low, high, order) in enumerate(((0, CHAR_CUT, "yxz"), (CHAR_CUT, CHAR_A, "xyz"))):
            rows = abuf.at[:, :, :, :, low:high]
            at = 3 * len(CHUNKS) + 4 * i
            self.parts.append(
                Halving(n_z, rows.at[1 - core], rows.at[core], got[at : at + 4], ssem, rsem, (5 + i) * SEMS, order)
            )
        at = 3 * len(CHUNKS) + 8
        self.partb = DirectSum(2 * n_z, *got[at : at + 4], ssem, rsem, 7 * SEMS)
        self.tiny = 9 * SEMS

    @staticmethod
    def scratch(n_z):
        n_sem = 11 * SEMS
        shapes = [
            pltpu.VMEM((2, 2, 2, n_z, CHAR_A, 128), BF16), pltpu.VMEM((2, 2, n_z, WORD_ROWS, 128), BF16),
            pltpu.VMEM((2, 16, 128), F32), pltpu.VMEM((2 + 2 * n_z, 16, 128), F32),
            pltpu.SemaphoreType.DMA((n_sem,)), pltpu.SemaphoreType.DMA((n_sem,)), pltpu.SemaphoreType.DMA,
        ]
        for low, high in CHUNKS:
            shapes += Halving.got_shapes(n_z, high - low, 1)
        for rows in (CHAR_CUT, CHAR_A - CHAR_CUT):
            shapes += Halving.got_shapes(n_z, rows)
        return shapes + DirectSum.shapes(2 * n_z, CHAR_B, BF16)

    def begin(self):
        load = pltpu.make_async_copy(self.word_sum, self.wbuf, self.lsem)
        load.start()
        dp, mp, n_dp = self.partb.dp, self.partb.mp, 2 * self.n_z
        peers = [(lax.rem(dp + k, n_dp), mp) for k in range(1, n_dp)] + [(dp, lax.rem(mp + k, 4)) for k in range(1, 4)]
        barrier = pltpu.get_barrier_semaphore()
        for peer in peers:
            pl.semaphore_signal(barrier, inc=1, device_id=peer, device_id_type=MESH)
        pl.semaphore_wait(barrier, len(peers))
        load.wait()
        for i, phase in enumerate((3, 1, 1, 1, 2)):
            self.chunks[i].start(phase)

    def pack_a(self, gup_ref, gdown_ref, gout_ref):
        for d in range(2 * self.n_z):
            down = gdown_ref[128 * d : 128 * d + 128, :]
            out = gout_ref[32 * d : 32 * d + 32, :]
            for p in range(4):
                block = self.abuf.at[p % 2, p // 2, d % 2, d // 2]
                block[0:32, :] = gup_ref[32 * d : 32 * d + 32, 256 * p : 256 * p + 128].astype(BF16)
                block[32:64, :] = gup_ref[32 * d : 32 * d + 32, 256 * p + 128 : 256 * p + 256].astype(BF16)
                block[64:128, :] = fold_half(down[:, 64 * p : 64 * p + 64]).astype(BF16)
                block[128:144, :] = fold_half(out[:, 64 * p : 64 * p + 64]).astype(BF16)
        for part in self.parts:
            part.start(0)

    def pack_b(self, gqkv_ref):
        for d in range(2 * self.n_z):
            qkv = gqkv_ref[32 * d : 32 * d + 32, :]
            for p in range(4):
                own = qkv[:, 192 * p : 192 * p + 192]
                self.partb.buf[p, d, 0:32, :] = own[:, 0:128].astype(BF16)
                self.partb.buf[p, d, 32:48, :] = fold_half(own[:, 128:192]).astype(BF16)
        self.partb.start(0)

    def tiny_copies(self, phase):
        dp, mp, n_dp = self.partb.dp, self.partb.mp, 2 * self.n_z
        if phase == 0:
            peers = [(dp, lax.rem(mp + k, 4)) for k in range(1, 4)]
        else:
            peers = [(lax.rem(dp + k, n_dp), mp) for k in range(1, n_dp)]
        at = 3 * phase
        return [
            remote_copy(self.small.at[phase], self.sgot.at[at + k], self.ssem, self.rsem, self.tiny + at + k, peer)
            for k, peer in enumerate(peers)
        ]

    def tiny_start(self, phase):
        for copy in self.tiny_copies(phase):
            copy.start()

    def tiny_finish(self, phase):
        copies = self.tiny_copies(phase)
        for copy in copies:
            copy.wait()
        total = self.small[phase]
        for k in range(len(copies)):
            total += self.sgot[3 * phase + k]
        return total


def pack_small(cgain_ref, cpool_ref, gqkv_ref, wqkv_ref, gains_ref, wgain_ref):
    gains = gains_ref[...].astype(F32)
    width = gains.shape[1]
    first = jnp.sum(gqkv_ref[...] * wqkv_ref[...].astype(F32), -1, keepdims=True)
    first = jnp.transpose(jnp.broadcast_to(first, (width, 128)))[0:1, :]
    sums = [
        first / gains[0:1], jnp.sum(cgain_ref[...], 0, keepdims=True) / gains[1:2],
        jnp.sum(cpool_ref[...], 0, keepdims=True), wgain_ref[0:1, :], wgain_ref[1:2, :],
    ]
    rows = [v[:, t : t + 128] for v in sums for t in range(0, v.shape[1], 128)]
    rows.append(jnp.zeros((2, 128), F32))
    return jnp.concatenate(rows, 0)


def finish_body(
    dx_ref, wide_ref, sums_ref,
    odx_ref, owide_ref, oqkv_ref, oout_ref, oup_ref, odown_ref, oproj_ref, owqkv_ref, owout_ref, owup_ref, owdown_ref,
    ocgain_ref, opool_ref, owgain_ref,
):
    odx_ref[...] = dx_ref[...].astype(F32)

    @pl.when(pl.program_id(0) == 0)
    def _():
        base = WORD_ROWS
        owide_ref[...] = wide_ref[...]
        for t in range(3):
            owqkv_ref[t] = sums_ref[64 * t : 64 * t + 64, :]
        oproj_ref[...] = sums_ref[ROW_PROJ : ROW_PROJ + 32, :]
        owout_ref[...] = sums_ref[ROW_OUT : ROW_OUT + 64, :]
        for t in range(4):
            owup_ref[:, 128 * t : 128 * t + 128] = sums_ref[ROW_UP + 64 * t : ROW_UP + 64 * t + 64, :]
            owdown_ref[:, 128 * t : 128 * t + 128] = sums_ref[ROW_DOWN + 64 * t : ROW_DOWN + 64 * t + 64, :]
        oup_ref[:, 0:128] = sums_ref[base : base + 32, :]
        oup_ref[:, 128:256] = sums_ref[base + 32 : base + 64, :]
        odown_ref[...] = unfold_half(sums_ref[base + 64 : base + 128, :]).T
        oout_ref[...] = unfold_half(sums_ref[base + 128 : base + 144, :])
        base = WORD_ROWS + CHAR_A
        oqkv_ref[:, 0:128] = sums_ref[base : base + 32, :]
        oqkv_ref[:, 128:192] = unfold_half(sums_ref[base + 32 : base + 48, :])
        total = sums_ref[base + CHAR_B : base + CHAR_B + 16, :]
        for j in range(2):
            for t in range(2):
                ocgain_ref[j : j + 1, 128 * t : 128 * t + 128] = total[2 * j + t : 2 * j + t + 1]
            for t in range(4):
                owgain_ref[j : j + 1, 128 * t : 128 * t + 128] = total[6 + 4 * j + t : 7 + 4 * j + t]
        for t in range(2):
            opool_ref[:, 128 * t : 128 * t + 128] = total[4 + t : 5 + t]


def finish(d_chars, word_out, sums):
    words, wide = d_chars.shape
    steps = 2
    full = lambda s: pl.BlockSpec(s, lambda i: (0,) * len(s))
    blk = pl.BlockSpec((words // steps, wide), lambda i: (i, 0))
    outs = [
        word_out.shape, (32, 192), (32, 64), (32, 256), (64, 128), (32, 128),
        (3, 64, 128), (64, 128), (64, 512), (64, 512), (2, 256), (1, 256), (2, 512),
    ]
    result = pl.pallas_call(
        finish_body,
        grid=(steps,),
        in_specs=[blk, full(word_out.shape), full(sums.shape)],
        out_specs=[blk] + [full(s) for s in outs],
        out_shape=[jax.ShapeDtypeStruct((words, wide), F32), jax.ShapeDtypeStruct(outs[0], BF16)]
        + [jax.ShapeDtypeStruct(s, F32) for s in outs[1:]],
        compiler_params=pltpu.CompilerParams(vmem_limit_bytes=VMEM_LIMIT),
        name="finish",
    )(d_chars, word_out, sums)
    dx, out, qkv, cout, up, down, proj, wqkv, wout, wup, wdown, cgain, pool, wgain = result
    return (out, dx, qkv, cout, up, down.T, proj, wqkv, wout.T, wup, wdown.T, cgain, pool.reshape(-1), wgain)


def char_bwd_body(
    n_dp, fused,
    dpool_ref, gains_ref, pool_ref, wqkv_any, wout_any, wup_any, wdown_any,
    early_ref, late_ref, p_ref, a_ref, act_ref,
    *refs,
):
    if fused:
        word_sum, wgain_ref, dx_ref, sums_ref, *refs = refs
    else:
        dx_ref, *refs = refs
        outs, refs = refs[:6], refs[6:]
    gqkv_ref, gout_ref, gup_ref, gdown_ref, ggain_ref, gpool_ref, *refs = refs
    dm_ref, dp_ref, do_ref, ds_ref, wqkv_ref, wout_ref, wup_ref, wdown_ref, dp_now, do_now, wsem, *refs = refs
    step = pl.program_id(0)
    part = pl.num_programs(0) // 3
    words = dpool_ref.shape[0]
    width = wout_ref.shape[0]
    hid = wup_ref.shape[1]
    blocks = words // 8
    rows = words * CHARS
    size = CHAR_HEADS * 128
    gains = gains_ref[...].astype(F32)
    here = pl.ds(pl.multiple_of(lax.rem(step, part) * rows, rows), rows)
    sums = GradientSums(n_dp // 2, word_sum, refs) if fused else None
    chunks = sums.chunks if fused else None

    def at(when, act):
        if fused:
            pl.when(step == when)(act)

    @pl.when(step == 0)
    def _():
        pairs = ((wdown_any, wdown_ref), (wup_any, wup_ref), (wout_any, wout_ref), (wqkv_any, wqkv_ref))
        loads = [pltpu.make_async_copy(src, dst, wsem.at[i]) for i, (src, dst) in enumerate(pairs)]
        for load in loads:
            load.start()
        if fused:
            sums.begin()
        for load in loads:
            load.wait()
        for ref in (gqkv_ref, gout_ref, gup_ref, gdown_ref, ggain_ref, gpool_ref):
            ref[...] = jnp.zeros_like(ref)

    def event(when, *moves):
        def act():
            for sum_of, phase in moves:
                if phase < 3:
                    sum_of.advance(phase)
                else:
                    sum_of.finish(3)
        at(when, act)

    if fused:
        first, other = sums.parts
        event(2, (chunks[1], 1), (chunks[3], 1))
        event(3, (chunks[2], 1), (chunks[4], 2))
        event(4, (chunks[1], 2), (chunks[3], 2))
        event(5, (first, 0), (other, 0))
        event(6, (chunks[2], 2))
        event(7, (first, 1), (other, 1))
        event(9, (first, 2), (other, 2))

    @pl.when(step < part)
    def _():
        dpool = dpool_ref[...].astype(F32).reshape(blocks, 1, 8, width)
        f = early_ref[:, 2 * width : 3 * width].astype(F32).reshape(blocks, CHARS, 8, width)
        stat = early_ref[:, 3 * width :].astype(F32)
        aw = stat[:, 1:2].reshape(blocks, CHARS, 8, 1)
        g = jnp.sum(f * dpool, -1, keepdims=True)
        dt = aw * (g - jnp.sum(aw * g, 1, keepdims=True))
        gpool_ref[...] += jnp.sum((dt * f).reshape(rows // 8, 8, width), 0)
        df = (aw * dpool + dt * pool_ref[...].astype(F32).reshape(1, width)).reshape(rows, width)
        dfb = df.astype(BF16)
        n2 = early_ref[:, width : 2 * width]
        dn2 = None
        for j in range(0, wup_ref.shape[1], HIDDEN_CUT):
            cut = slice(j, j + HIDDEN_CUT)
            gdown_ref[cut, :] += dot_tn(act_ref[:, cut], dfb)
            dh = act_ref[:, hid + j : hid + j + HIDDEN_CUT] * dot_nt(dfb, wdown_ref[cut, :]).astype(BF16)
            gup_ref[:, cut] += dot_tn(n2, dh)
            term = dot_nt(dh, wup_ref[:, cut])
            dn2 = term if dn2 is None else dn2 + term
        d_norm, dnn = norm_bwd(dn2, n2, stat[:, 0:1], gains[1:2])
        ggain_ref[...] += jnp.sum(dnn.reshape(rows // 8, 8, width), 0)
        dm = df + d_norm
        dmb = dm.astype(BF16)
        dm_ref[here, :] = dmb
        gout_ref[...] += dot_tn(early_ref[:, 0:width], dmb)
        do_ref[here, :] = dot_nt(dmb, wout_ref[...]).astype(BF16)

    at(part - 1, lambda: sums.pack_a(gup_ref, gdown_ref, gout_ref))

    @pl.when((step >= part) & (step < 2 * part))
    def _():
        scale = (width // CHAR_HEADS) ** -0.5
        do_now[...] = do_ref[here, :]
        raw = []
        for b in range(blocks):
            sl = slice(128 * b, 128 * b + 128)
            raw.append(dot_nt(head_stack(p_ref[sl, 2 * width : 3 * width], CHAR_HEADS, 1.0), do_now[128 * b : 128 * b + 128, :]))
        for b in range(blocks):
            a = a_ref[size * b : size * b + size, :].astype(F32).reshape(CHAR_HEADS, CHARS, 8, 128)
            dpt = raw[b].reshape(CHAR_HEADS, CHARS, 8, 128)
            delta = jnp.sum(a * dpt, 1, keepdims=True)
            ds_ref[size * b : size * b + size, :] = (a * (dpt - delta)).reshape(size, 128).astype(BF16)
        for b in range(blocks):
            sl = slice(128 * b, 128 * b + 128)
            ds = ds_ref[size * b : size * b + size, :]
            k = head_stack(p_ref[sl, width : 2 * width], CHAR_HEADS, scale)
            dp_now[128 * b : 128 * b + 128, 0:width] = dot_tn(ds, k).astype(BF16)
        for b in range(blocks):
            sl = slice(128 * b, 128 * b + 128)
            cut = lambda h: ds_ref[size * b + 128 * h : size * b + 128 * h + 128, :]
            wide = jnp.concatenate([cut(h) for h in range(CHAR_HEADS)], 1)
            q = head_stack(p_ref[sl, 0:width], CHAR_HEADS, scale)
            dp_now[128 * b : 128 * b + 128, width : 2 * width] = dot_nn(wide, q).astype(BF16)
        for b in range(blocks):
            cut = lambda h: a_ref[size * b + 128 * h : size * b + 128 * h + 128, :]
            wide = jnp.concatenate([cut(h) for h in range(CHAR_HEADS)], 1)
            do = head_stack(do_now[128 * b : 128 * b + 128, :], CHAR_HEADS, 1.0)
            dp_now[128 * b : 128 * b + 128, 2 * width : 3 * width] = dot_nn(wide, do).astype(BF16)
        dp = dp_now[...]
        dp_ref[here, :] = dp
        gqkv_ref[...] += dot_tn(late_ref[:, 0:width], dp)

    def begin_b():
        sums.pack_b(gqkv_ref)
        sums.small[0] = pack_small(ggain_ref, gpool_ref, gqkv_ref, wqkv_ref, gains_ref, wgain_ref)
        sums.tiny_start(0)
    at(2 * part - 1, begin_b)

    @pl.when(step >= 2 * part)
    def _():
        dn1 = dot_nt(dp_ref[here, :], wqkv_ref[...])
        rstd = late_ref[:, width:].astype(F32)[:, 0:1]
        d_norm, _ = norm_bwd(dn1, late_ref[:, 0:width], rstd, gains[0:1])
        dx = dm_ref[here, :].astype(F32) + d_norm
        for b in range(0, blocks, 2):
            for c in range(CHARS):
                pair = [dx[128 * i + 8 * c : 128 * i + 8 * c + 8] for i in (b, b + 1)]
                dx_ref[8 * b : 8 * b + 16, width * c : width * c + width] = jnp.concatenate(pair, 0).astype(BF16)

    def end():
        sums.partb.advance()
        sums.small[1] = sums.tiny_finish(0)
        sums.tiny_start(1)
        for i, (low, high) in enumerate(CHUNKS):
            chunks[i].finish(3)
            sums_ref[low:high, :] = chunks[i].total()
        base = WORD_ROWS
        for i, (low, high) in enumerate(((0, CHAR_CUT), (CHAR_CUT, CHAR_A))):
            sums.parts[i].finish(3)
            sums_ref[base + low : base + high, :] = sums.parts[i].total()
        base += CHAR_A
        sums_ref[base + CHAR_B : base + CHAR_B + 16, :] = sums.tiny_finish(1)
        sums_ref[base : base + CHAR_B, :] = sums.partb.total()
    at(3 * part - 1, end)

    if not fused:
        @pl.when(step == 3 * part - 1)
        def _():
            for out, ref in zip(outs, (gqkv_ref, gout_ref, gup_ref, gdown_ref, ggain_ref, gpool_ref)):
                out[...] = ref[...]


def char_backward(n_dp, dpool, kept, gains, wqkv, wout, wup, wdown, pool, word_sum, wgain):
    words = dpool.shape[0]
    width = wout.shape[0]
    rows = words * CHARS
    step_rows = STEP_WORDS * CHARS
    steps = words // STEP_WORDS
    fused = word_sum is not None
    full = lambda arr: pl.BlockSpec(arr.shape, lambda i: (0,) * arr.ndim)
    fixed = lambda s: pl.BlockSpec(s, lambda i: (0,) * len(s))
    first = lambda n, w: pl.BlockSpec((n, w), lambda i: (lax.min(i, steps - 1), 0))
    second = lambda n, w: pl.BlockSpec((n, w), lambda i: (lax.clamp(0, i - steps, steps - 1), 0))
    third = lambda n, w: pl.BlockSpec((n, w), lambda i: (lax.max(i - 2 * steps, 0), 0))
    twice = lambda n, w: pl.BlockSpec((n, w), lambda i: (lax.rem(lax.max(i - steps, 0), steps), 0))
    grads = [wqkv.shape, wout.shape, wup.shape, wdown.shape, (8, width), (8, width)]
    scratch = [pltpu.VMEM(s, F32) for s in grads] + [
        pltpu.VMEM((rows, width), BF16), pltpu.VMEM((rows, 3 * width), BF16), pltpu.VMEM((rows, width), BF16),
        pltpu.VMEM((step_rows * CHAR_HEADS, 128), BF16), *[pltpu.VMEM(w.shape, BF16) for w in (wqkv, wout, wup, wdown)],
        pltpu.VMEM((step_rows, 3 * width), BF16), pltpu.VMEM((step_rows, width), BF16), pltpu.SemaphoreType.DMA((4,)),
    ]
    any_spec = pl.BlockSpec(memory_space=pl.ANY)
    args = [dpool, gains, pool, wqkv, wout, wup, wdown, *kept]
    in_specs = [first(STEP_WORDS, width), full(gains), full(pool)] + [any_spec] * 4
    in_specs += [f(r.shape[0] // steps, r.shape[1]) for f, r in zip((first, twice, second, second, first), kept)]
    params = dict(vmem_limit_bytes=VMEM_LIMIT)
    if fused:
        outs = [(WORD_ROWS + CHAR_A + CHAR_B + 16, 128)]
        args += [word_sum, wgain]
        in_specs += [pl.BlockSpec(memory_space=pl.ANY), full(wgain)]
        scratch += GradientSums.scratch(n_dp // 2)
        params.update(collective_id=1, has_side_effects=True)
    else:
        outs = grads
    return pl.pallas_call(
        functools.partial(char_bwd_body, n_dp, fused),
        grid=(3 * steps,),
        in_specs=in_specs,
        out_specs=[third(STEP_WORDS, CHARS * width)] + [fixed(s) for s in outs],
        out_shape=[jax.ShapeDtypeStruct((words, CHARS * width), BF16)] + [jax.ShapeDtypeStruct(s, F32) for s in outs],
        scratch_shapes=scratch,
        compiler_params=pltpu.CompilerParams(**params),
        name="char_backward",
    )(*args)


def word_body(
    n_dp, cap, packed,
    pooled_ref, onehot, place, seg_all, cot_ref, gains_ref, wproj_ref, *refs,
):
    slices, wholes, refs = refs[:4], refs[4:7], refs[7:]
    if packed:
        out_ref, dpool_ref, gsum_ref, ggain_ref, gbuf_ref, got_a, got_x, gq_ref, got_q, *refs = refs
    else:
        out_ref, dpool_ref, gqkv_ref, gout_ref, gup_ref, gdown_ref, gproj_ref, ggain_ref, *refs = refs
    (
        wqkv_ref, wout_ref, wup_ref, wdown_ref, vec_send, vec_got, segc_all, pooled_rows, rows_ref, normed_all, rstd_a,
        qkv_all, weights, o_send, o_all, act_ref, dh_ref, dact_ref, dm_ref,
        do_send, do_all, dk_acc, dv_acc, dqkv_send, dqkv_all, back_send, ret,
        ssem, rsem, lsem, wsend, wrecv, qsend, qrecv,
    ) = refs
    dp, mp = lax.axis_index("dp"), lax.axis_index("mp")
    n_mp = 4
    words, narrow = pooled_ref.shape
    width = cot_ref.shape[1]
    slots = n_dp * cap
    pair = 2 * (width // HEADS)
    scale = (width // HEADS) ** -0.5
    to_dp = [(lax.rem(dp + k, n_dp), mp) for k in range(n_dp)]
    from_dp = [(lax.rem(dp + n_dp - k, n_dp), mp) for k in range(n_dp)]
    mates = [(mp // 2 * 2 + (mp + 1) % 2), (mp + 2) % 4, ((mp // 2 * 2 + 2) % 4 + (mp + 1) % 2)]
    barrier = pltpu.get_barrier_semaphore()
    for k in range(1, n_dp):
        pl.semaphore_signal(barrier, inc=1, device_id=to_dp[k], device_id_type=MESH)
    for mate in mates:
        pl.semaphore_signal(barrier, inc=1, device_id=(dp, mate), device_id_type=MESH)
    next_slot = [0]

    def send(src, dst, peer):
        slot = next_slot[0]
        next_slot[0] += 1
        copy = pltpu.make_async_remote_copy(
            src_ref=src, dst_ref=dst, send_sem=ssem.at[slot], recv_sem=rsem.at[slot],
            device_id=peer, device_id_type=MESH,
        )
        copy.start()
        return copy

    z, x, y, core = coordinates()
    loads = []
    for i, held in ((3, wdown_ref), (0, wqkv_ref), (1, wout_ref), (2, wup_ref)):
        loads.append([])
        for j, at in enumerate([mp] if i == 3 else [mp, *mates]):
            src = slices[i] if j == 0 else wholes[i].at[at]
            if i == 0:
                for t in range(3):
                    dst = held.at[at, :, pair * t : pair * t + pair]
                    loads[-1].append(pltpu.make_async_copy(src.at[t], dst, lsem.at[4 + t, j]))
            else:
                loads[-1].append(pltpu.make_async_copy(src, held.at[at], lsem.at[i, j]))
        for load in loads[-1]:
            load.start()
    vec_send[...] = dot_nn(onehot[...], pooled_ref[...]).astype(BF16).reshape(n_dp, cap, narrow)

    pl.semaphore_wait(barrier, n_dp - 1 + 3)
    vec_copies = [send(vec_send.at[k], vec_got.at[k], to_dp[k]) for k in range(1, n_dp)]
    down = WeightGather((slices[3],), (wdown_ref,), (True,), wsend, wrecv)
    down.begin()
    vec_got[0] = vec_send[0]
    gains = gains_ref[...].astype(F32)
    cot = cot_ref[...]
    for j in range(n_mp):
        segc_all[words * j : words * j + words, :] = as_column(seg_all[j, 0:1, :])
    for load in loads[1] + loads[2] + loads[3]:
        load.wait()
    for copy in vec_copies:
        copy.wait()
    pooled_rows[mp] = dot_tn(place[...], vec_got[...].reshape(slots, narrow)).astype(BF16)
    row_copies = [send(pooled_rows.at[mp], pooled_rows.at[mp], (dp, mate)) for mate in reversed(mates)]
    for turn, at in enumerate([mp, *mates]):
        if turn > 0:
            row_copies[3 - turn].wait()
        rows = dot_nn(pooled_rows[at], wproj_ref[...]).astype(BF16).astype(F32)
        n_w, rstd = norm_fwd(rows, gains[0:1])
        normed_all[at] = n_w
        if turn == 0:
            down.pass_on(0)
            rows_ref[...] = rows
            rstd_a[...] = rstd
        qkv_all[at] = dot_nn(n_w, wqkv_ref[mp]).astype(BF16)
    down.pass_last(0)

    low_lane = lax.broadcasted_iota(jnp.int32, (1, pair), 1) < pair // 2
    low_mask = jnp.where(low_lane, 1.0, 0.0).astype(BF16)
    high_mask = jnp.where(low_lane, 0.0, 1.0).astype(BF16)

    def heads(v, factor):
        return jnp.concatenate([v * (low_mask * factor).astype(BF16), v * (high_mask * factor).astype(BF16)], 0)

    o_copies = []
    for i in reversed(range(n_mp)):
        keys = words * (i + 1)
        q = heads(qkv_all[i, :, 0:pair], scale)
        k = qkv_all[0 : i + 1, :, pair : 2 * pair].reshape(keys, pair)
        v = qkv_all[0 : i + 1, :, 2 * pair : 3 * pair].reshape(keys, pair)
        same = segc_all[0:keys, 0:1] == seg_all[i, 0:1, :].astype(F32)
        key_at = lax.broadcasted_iota(jnp.int32, (keys, words), 0)
        query_at = lax.broadcasted_iota(jnp.int32, (keys, words), 1) + words * i
        allowed = same & (key_at <= query_at)
        st = jnp.where(jnp.concatenate([allowed, allowed], 1), dot_nt(k, q), NEGATIVE)
        ex = jnp.exp(st - jnp.max(st, 0, keepdims=True))
        at = (ex * (1.0 / jnp.sum(ex, 0, keepdims=True))).astype(BF16)
        weights[i, 0:keys, :] = at
        both = dot_tn(at, v)
        o_send[i] = jnp.where(low_lane, both[:words], both[words:]).astype(BF16)
    for mate in reversed(mates):
        o_copies.append(send(o_send.at[mate], o_all.at[mp], (dp, mate)))
    o_all[mp] = o_send[mp]
    down.finish()
    for load in loads[0]:
        load.wait()
    for p in range(n_mp):
        dact_ref[p] = dot_nt(cot, wdown_ref[p]).astype(BF16)
    for copy in o_copies:
        copy.wait()
    attended = jnp.concatenate([o_all[p] for p in range(n_mp)], 1)
    mid = rows_ref[...] + dot_nn(attended, wout_ref[...].reshape(width, width))
    n_w2, rstd2 = norm_fwd(mid, gains[1:2])
    out = mid
    dn2 = jnp.zeros((words, width), F32)
    for p in range(n_mp):
        act, slope = gelu_both(dot_nn(n_w2, wup_ref[p]).astype(BF16))
        act_ref[p] = act
        dh = slope * dact_ref[p]
        dh_ref[p] = dh
        out = out + dot_nn(act, wdown_ref[p])
        dn2 = dn2 + dot_nt(dh, wup_ref[p])
    out_ref[...] = out.astype(BF16)
    d_norm, dnn = norm_bwd(dn2, n_w2, rstd2, gains[1:2])
    gain_b = jnp.sum(dnn, 0, keepdims=True) / gains[1:2]
    d_mid = cot.astype(F32) + d_norm
    dm_ref[...] = d_mid
    d_att = d_mid.astype(BF16)
    do_copies = []
    for mate in reversed(mates):
        do_send[mate] = dot_nt(d_att, wout_ref[mate]).astype(BF16)
        do_copies.append(send(do_send.at[mate], do_all.at[mp], (dp, mate)))
    do_all[mp] = dot_nt(d_att, wout_ref[mp]).astype(BF16)

    def pair_sum(i):
        low, high = CHUNKS[i]
        src = gbuf_ref.at[1 - core, :, :, :, low:high]
        return send(src, got_a.at[:, :, :, low:high], device_of(z, x, y, 1 - core))

    def pair_add(i):
        low, high = CHUNKS[i]

        def add(i, carry):
            b, c, d = i // n_dp, (i // (n_dp // 2)) % 2, lax.rem(i, n_dp // 2)
            gsum_ref[b, c, d, low:high] = gbuf_ref[core, b, c, d, low:high] + got_a[b, c, d, low:high]
            return carry
        lax.fori_loop(0, 2 * n_dp, add, 0)

    def x_sum(i):
        low, high = CHUNKS[i]
        return send(gsum_ref.at[:, 1 - x, :, low:high], got_x, device_of(z, 1 - x, y, core))

    def x_add(i):
        low, high = CHUNKS[i]
        for b in range(2):
            for d in range(n_dp // 2):
                gsum_ref[b, x, d, low:high] += got_x[b, d]

    def put(base, p, grad):
        if packed:
            block = grad.shape[0] // n_dp
            for d in range(n_dp):
                for t in range(grad.shape[1] // 128):
                    gbuf_ref[p % 2, p // 2, d % 2, d // 2, base + block * t : base + block * t + block, :] = (
                        grad[block * d : block * d + block, 128 * t : 128 * t + 128].astype(BF16)
                    )
        elif base == ROW_PROJ:
            gproj_ref[:, 128 * p : 128 * p + 128] = grad
        else:
            ref = {ROW_OUT: gout_ref, ROW_UP: gup_ref, ROW_DOWN: gdown_ref}[base]
            ref[p] = grad

    for p in range(n_mp):
        put(ROW_DOWN, p, dot_tn(cot, act_ref[p]))
    if packed:
        pair_three = pair_sum(4)
    for p in range(n_mp):
        put(ROW_UP, p, dot_tn(n_w2, dh_ref[p]))
    if packed:
        pair_two = pair_sum(3)
    for p in range(n_mp):
        put(ROW_OUT, p, dot_tn(d_att, o_all[p]))
    if packed:
        pair_one = pair_sum(2)
        pair_three.wait()
        pair_add(4)
        x_three = x_sum(4)
    dk_acc[...] = jnp.zeros_like(dk_acc)
    dv_acc[...] = jnp.zeros_like(dv_acc)
    for copy in do_copies:
        copy.wait()
    parts = (slice(0, pair), slice(pair, 3 * pair))

    def dqkv_copy(part, to, slot):
        cut = parts[part]
        return pltpu.make_async_remote_copy(
            src_ref=dqkv_send.at[to, :, cut], dst_ref=dqkv_all.at[mp, :, cut],
            send_sem=qsend.at[part, slot], recv_sem=qrecv.at[part, slot],
            device_id=(dp, to), device_id_type=MESH,
        )

    def dqkv_start(part, i):
        @pl.when(mp != i)
        def _():
            dqkv_copy(part, i, lax.rem(mp + i, 2) + 2 * lax.rem(mp // 2 + i // 2, 2)).start()

    def keep_sums(i):
        here = slice(words * i, words * i + words)
        dqkv_send[i, :, pair : 2 * pair] = dk_acc[here, :].astype(BF16)
        dqkv_send[i, :, 2 * pair : 3 * pair] = dv_acc[here, :].astype(BF16)

    def attention_back(falling):
        for i in reversed(range(n_mp)) if falling else range(n_mp):
            keys = words * (i + 1)
            q = qkv_all[i, :, 0:pair]
            k = qkv_all[0 : i + 1, :, pair : 2 * pair].reshape(keys, pair)
            v = qkv_all[0 : i + 1, :, 2 * pair : 3 * pair].reshape(keys, pair)
            do = heads(do_all[i], 1.0)
            at = weights[i, 0:keys, :]
            af = at.astype(F32)
            dpt = dot_nt(v, do)
            ds = (af * (dpt - jnp.sum(af * dpt, 0, keepdims=True))).astype(BF16)
            both = dot_tn(ds, k)
            dqkv_send[i, :, 0:pair] = (jnp.where(low_lane, both[:words], both[words:]) * scale).astype(BF16)
            dqkv_start(0, i)
            dk_acc[0:keys, :] += dot_nn(ds, heads(q, scale))
            dv_acc[0:keys, :] += dot_nn(at, do)
            if falling:
                keep_sums(i)
                dqkv_start(1, i)
        if not falling:
            for i in range(n_mp):
                keep_sums(i)
                dqkv_start(1, i)

    @pl.when(mp // 2 == 0)
    def _():
        attention_back(True)

    @pl.when(mp // 2 == 1)
    def _():
        attention_back(False)

    dqkv_copies = [dqkv_copy(part, mate, j + 1) for part in range(2) for j, mate in enumerate(mates)]
    dqkv_all[mp] = dqkv_send[mp]
    grad_qkv = dot_tn(normed_all[...].reshape(n_mp * words, width), dqkv_send[...].reshape(n_mp * words, 3 * pair))
    if packed:
        block = width // n_dp
        for d in range(n_dp):
            for t in range(3):
                gq_ref[d % 2, d // 2, block * t : block * t + block, :] = (
                    grad_qkv[block * d : block * d + block, 128 * t : 128 * t + 128].astype(BF16)
                )
        q_sum = send(gq_ref.at[1 - x], got_q, device_of(z, 1 - x, y, core))
        pair_two.wait()
        pair_add(3)
        pair_one.wait()
        pair_add(2)
    else:
        gqkv_ref[...] = grad_qkv
    for copy in dqkv_copies:
        copy.wait()
    d_normed = jnp.zeros((words, width), F32)
    for p in range(n_mp):
        d_normed = d_normed + dot_nt(dqkv_all[p], wqkv_ref[p])
    d_first, dnn = norm_bwd(d_normed, normed_all[mp], rstd_a[...], gains[0:1])
    gain_a = jnp.sum(dnn, 0, keepdims=True) / gains[0:1]
    d_rows = (dm_ref[...] + d_first).astype(BF16)
    ggain_ref[0:1, :] = gain_a
    ggain_ref[1:2, :] = gain_b
    d_pooled = dot_nt(d_rows, wproj_ref[...]).astype(BF16)
    back_send[...] = dot_nn(place[...], d_pooled).astype(BF16).reshape(n_dp, cap, narrow)
    back_copies = [send(back_send.at[k], ret.at[k], from_dp[k]) for k in range(1, n_dp)]
    ret[0] = back_send[0]
    grad_proj = dot_tn(pooled_rows[mp], d_rows)
    for p in range(n_mp):
        put(ROW_PROJ, p, grad_proj[:, 128 * p : 128 * p + 128])
    if packed:
        pair_zero = pair_sum(1)
        q_sum.wait()
        low, high = CHUNKS[0]
        gsum_ref[y, x, :, low:high] = gq_ref[x] + got_q[...]
        x_three.wait()
        x_add(4)
        pair_zero.wait()
        pair_add(1)
    for copy in back_copies:
        copy.wait()
    dpool_ref[...] = dot_tn(onehot[...], ret[...].reshape(slots, narrow)).astype(BF16)


def word_layer(n_dp, pooled, onehot, place, segments, cotangent, gains, wproj, slices, wholes):
    words, narrow = pooled.shape
    width = cotangent.shape[1]
    wqkv, wout, wup = wholes
    n_mp = wqkv.shape[0]
    cap = -(-2 * words // n_dp // 16) * 16
    slots = cap * n_dp
    pair = 2 * (width // HEADS)
    packed = n_dp == 8
    outs = [((words, width), BF16), ((words, narrow), BF16)]
    if packed:
        outs.append(((2, 2, n_dp // 2, WORD_ROWS, 128), BF16))
    else:
        outs.append(((width, 3 * pair), F32))
        outs += [((n_mp, width, n), F32) for n in (pair, wup.shape[2], wup.shape[2])]
        outs.append(((narrow, width), F32))
    outs.append(((2, width), F32))
    hid = wup.shape[2]
    n_sem = 2 * (n_dp - 1) + 4 * 3 + 3 + 6
    vm = pl.BlockSpec(memory_space=pltpu.VMEM)
    args = (pooled, onehot, place, segments, cotangent, gains, wproj, *slices, *wholes)
    shapes = [
        ((n_mp, width, 3 * pair), BF16), (wout.shape, BF16), (wup.shape, BF16), ((n_mp, *slices[3].shape), BF16),
        ((n_dp, cap, narrow), BF16), ((n_dp, cap, narrow), BF16), ((n_mp * words, 128), F32), ((n_mp, words, narrow), BF16),
        ((words, width), F32), ((n_mp, words, width), BF16), ((words, 1), F32),
        ((n_mp, words, 3 * pair), BF16), ((n_mp, n_mp * words, 2 * words), BF16),
        ((n_mp, words, pair), BF16), ((n_mp, words, pair), BF16),
        ((n_mp, words, hid), BF16), ((n_mp, words, hid), BF16), ((n_mp, words, hid), BF16), ((words, width), F32),
        ((n_mp, words, pair), BF16), ((n_mp, words, pair), BF16), ((n_mp * words, pair), F32), ((n_mp * words, pair), F32),
        ((n_mp, words, 3 * pair), BF16), ((n_mp, words, 3 * pair), BF16), ((n_dp, cap, narrow), BF16), ((n_dp, cap, narrow), BF16),
    ]
    if packed:
        shapes = [
            ((2, 2, 2, n_dp // 2, WORD_ROWS, 128), BF16), ((2, 2, n_dp // 2, WORD_ROWS, 128), BF16),
            ((2, n_dp // 2, CHUNK_ROWS, 128), BF16),
            ((2, n_dp // 2, CHUNK_ROWS, 128), BF16), ((n_dp // 2, CHUNK_ROWS, 128), BF16), *shapes,
        ]
    return pl.pallas_call(
        functools.partial(word_body, n_dp, cap, packed),
        in_specs=[vm] * (len(args) - 7) + [pl.BlockSpec(memory_space=pl.ANY)] * 7,
        out_specs=[vm] * len(outs),
        out_shape=[jax.ShapeDtypeStruct(s, d) for s, d in outs],
        scratch_shapes=[pltpu.VMEM(s, d) for s, d in shapes]
        + [pltpu.SemaphoreType.DMA((n_sem,)), pltpu.SemaphoreType.DMA((n_sem,)), pltpu.SemaphoreType.DMA((7, 4)), pltpu.SemaphoreType.DMA((5,)), pltpu.SemaphoreType.DMA((5,)),
        pltpu.SemaphoreType.DMA((2, 4)), pltpu.SemaphoreType.DMA((2, 4))],
        compiler_params=pltpu.CompilerParams(collective_id=0, has_side_effects=True, vmem_limit_bytes=VMEM_LIMIT),
        name="word_layer",
    )(*args)


def plain_reduce(char_parts, char_gains, char_qkv, word_parts, word_gains):
    *char_mats, gain_rows, pool_rows = char_parts
    gain_sums = jnp.stack([jnp.sum(char_mats[0] * char_qkv.astype(F32), 1), jnp.sum(gain_rows, 0)]) / char_gains.astype(F32)
    small = lax.psum((gain_sums, jnp.sum(pool_rows, 0), word_gains), ("dp", "mp"))
    mats = []
    for grad in char_mats:
        part = lax.psum_scatter(grad, "dp", scatter_dimension=0, tiled=True)
        part = lax.psum_scatter(part.astype(BF16), "mp", scatter_dimension=1, tiled=True)
        mats.append(part.astype(F32))
    qkv, *rest = word_parts
    words = []
    for grad in rest:
        part = lax.psum_scatter(grad, "dp", scatter_dimension=1, tiled=True)
        words.append(lax.psum_scatter(part, "mp", scatter_dimension=0, tiled=False))
    out, up, down = words
    qkv = lax.psum_scatter(qkv, "dp", scatter_dimension=0, tiled=True)
    qkv = jnp.transpose(qkv.reshape(qkv.shape[0], 3, -1), (1, 0, 2))
    return (*mats, qkv, out.T, up, down.T, *small)


def per_device(
    char_input,
    char_counts,
    word_source,
    segment_ids,
    cotangent,
    char_norm_gains,
    char_qkv,
    char_out,
    char_up,
    char_down,
    pool_vector,
    char_proj,
    word_norm_gains,
    word_qkv,
    word_out,
    word_up,
    word_down,
):
    groups = lax.axis_size("dp")
    char_weights = (char_norm_gains, char_qkv, char_out, char_up, char_down, pool_vector)
    slices = (word_qkv, word_out, word_up, word_down)
    pooled, *kept = char_forward(
        groups, char_input, char_counts.reshape(1, -1), *char_weights,
        word_source.reshape(1, -1), segment_ids.reshape(1, -1), slices[:3],
    )
    char_kept, (onehot, place, segments, *word_weights) = kept[:5], kept[5:]
    output, d_pooled, *word_parts, word_gains = word_layer(
        groups, pooled, onehot, place, segments, cotangent, word_norm_gains, char_proj, slices, word_weights
    )
    fused = groups == 8
    d_chars, *char_parts = char_backward(
        groups, d_pooled, char_kept, *char_weights, word_parts[0] if fused else None, word_gains
    )
    if fused:
        return finish(d_chars, output, char_parts[0])
    *word_parts, grad_proj = word_parts
    char_parts = (*char_parts[:4], grad_proj, *char_parts[4:])
    *mats, grad_char_gains, grad_pool, grad_word_gains = plain_reduce(
        char_parts, char_norm_gains, char_qkv, word_parts, word_gains
    )
    return (output, d_chars.astype(F32), *mats, grad_char_gains, grad_pool, grad_word_gains)


def solution(mesh):
    placed = (
        P(("dp", "mp"), None),
        P(("dp", "mp")),
        P(("dp", "mp")),
        P(("dp", "mp")),
        P(("dp", "mp"), None),
        P(),
        P(),
        P(),
        P(),
        P(),
        P(),
        P(),
        P(),
        P(None, None, "mp"),
        P("mp", None),
        P(None, "mp"),
        P("mp", None),
    )
    return jax.shard_map(
        per_device,
        mesh=mesh,
        in_specs=placed,
        out_specs=(
            P(("dp", "mp"), None),
            P(("dp", "mp"), None),
            P("dp", "mp"),
            P("dp", "mp"),
            P("dp", "mp"),
            P("dp", "mp"),
            P("dp", "mp"),
            P(None, "dp", "mp"),
            P("mp", "dp"),
            P("dp", "mp"),
            P("mp", "dp"),
            P(),
            P(),
            P(),
        ),
        check_vma=False,
    )
```

```python
import functools
import jax
import jax.numpy as jnp
from jax import lax
from jax.experimental import pallas as pl
from jax.experimental.pallas import tpu as pltpu
from jax.sharding import PartitionSpec as P

HEADS = 8
CHARS = 16
CHAR_HEADS = 4
EPSILON = 1e-05
NEGATIVE = -1e30
GELU_A = 0.7978845608028654
GELU_B = 0.044715
F32 = jnp.float32
BF16 = jnp.bfloat16
MESH = pl.DeviceIdType.MESH
VMEM_LIMIT = 62 * 1024 * 1024
STEP_WORDS = 64
HIDDEN_CUT = 256


def dot_nn(left, right):
    return jnp.dot(left, right, preferred_element_type=F32)


def dot_nt(left, right):
    return lax.dot_general(left, right, (((1,), (1,)), ((), ())), preferred_element_type=F32)


def dot_tn(left, right):
    return lax.dot_general(left, right, (((0,), (0,)), ((), ())), preferred_element_type=F32)


def as_column(row):
    return jnp.transpose(jnp.broadcast_to(row.astype(F32), (128, row.shape[1])))


def head_stack(values, heads, factor):
    width = values.shape[1] // heads
    lane = lax.broadcasted_iota(jnp.int32, (1, values.shape[1]), 1) // width
    return jnp.concatenate(
        [values * jnp.where(lane == h, factor, 0.0).astype(values.dtype) for h in range(heads)], 0
    )


def gelu_both(hidden):
    c = lambda value: jnp.asarray(value, hidden.dtype)
    square = hidden * hidden
    tanh = jnp.tanh(hidden * (c(GELU_A) + c(GELU_A * GELU_B) * square))
    half = c(0.5) + c(0.5) * tanh
    slope = half + (c(0.5) * hidden) * (c(1.0) - tanh * tanh) * (c(GELU_A) + c(3.0 * GELU_A * GELU_B) * square)
    return hidden * half, slope


def norm_fwd(values, gain):
    mean = jnp.mean(values, -1, keepdims=True)
    centered = values - mean
    rstd = lax.rsqrt(jnp.mean(centered * centered, -1, keepdims=True) + EPSILON)
    return (centered * rstd * gain).astype(BF16), rstd


def norm_bwd(dn, n, rstd, gain):
    n = n.astype(F32)
    d1 = dn * gain
    dnn = dn * n
    m1 = jnp.mean(d1, -1, keepdims=True)
    m2 = jnp.mean(dnn, -1, keepdims=True)
    return rstd * (d1 - m1 - n * (1.0 / gain) * m2), dnn


def coordinates():
    dp, mp = lax.axis_index("dp"), lax.axis_index("mp")
    return dp // 2, dp % 2, mp // 2, mp % 2


def device_of(z, x, y, core):
    return (z * 2 + x, y * 2 + core)


def remote_copy(src, dst, ssem, rsem, slot, peer):
    return pltpu.make_async_remote_copy(
        src_ref=src, dst_ref=dst, send_sem=ssem.at[slot], recv_sem=rsem.at[slot],
        device_id=peer, device_id_type=MESH,
    )


class WeightGather:
    def __init__(self, slices, wholes, split, ssem, rsem):
        self.slices, self.wholes, self.split, self.ssem, self.rsem = slices, wholes, split, ssem, rsem
        self.z, self.x, self.y, self.core = coordinates()
        self.mp = self.y * 2 + self.core
        self.across = (1 - self.y) * 2 + self.core

    @staticmethod
    def half(ref, axis, which):
        rows = ref.shape[axis] // 2
        return ref.at[(slice(None),) * axis + (pl.ds(pl.multiple_of(which * rows, rows), rows),)]

    def copy(self, i, kind):
        z, x, y, core = self.z, self.x, self.y, self.core
        piece, whole = self.slices[i], self.wholes[i]
        axis = len(piece.shape) - 2
        far = whole.at[self.across]
        if kind == "far":
            src, dst = piece, whole.at[self.mp]
            if self.split[i]:
                src, dst = self.half(src, axis, x), self.half(dst, axis, x)
            peer = device_of(z, x, 1 - y, core)
        elif kind == "near":
            src, dst, peer = piece, whole.at[self.mp], device_of(z, x, y, 1 - core)
        else:
            which = 1 - x if kind == "late" else x
            src = dst = self.half(far, axis, which) if self.split[i] else far
            peer = device_of(z, 1 - x, y, core) if kind == "side" else device_of(z, x, y, 1 - core)
        slot = i * 5 + ("far", "near", "side", "early", "late").index(kind)
        return remote_copy(src, dst, self.ssem, self.rsem, slot, peer)

    def peers(self):
        z, x, y, core = self.z, self.x, self.y, self.core
        return [device_of(z, x, 1 - y, core), device_of(z, x, y, 1 - core), device_of(z, 1 - x, y, core)]

    def begin(self):
        for i in range(len(self.slices)):
            self.copy(i, "far").start()
        for i in range(len(self.slices)):
            self.copy(i, "near").start()

    def pass_on(self, i):
        self.copy(i, "far").wait()
        if self.split[i]:
            self.copy(i, "side").start()
        self.copy(i, "early").start()

    def pass_last(self, i):
        self.copy(i, "side").wait()
        self.copy(i, "late").start()

    def finish(self):
        for i in range(len(self.slices)):
            for kind in ("near", "early", "late")[: 2 + self.split[i]]:
                self.copy(i, kind).wait()


def char_fwd_body(
    n_dp, cap,
    x_ref, cnt_ref, gains_ref, wqkv_ref, wout_ref, wup_ref, wdown_ref, pool_ref,
    src_ref, seg_ref, s_qkv, s_out, s_up,
    pooled_ref, early_ref, late_ref, p_any, a_any, act_any,
    onehot_ref, place_ref, seg_out, g_qkv, g_out, g_up,
    cnt_col, row_send, row_got, seg_all, ssem, rsem, wsend, wrecv, p_buf, a_buf, act_buf, osem,
):
    step, last = pl.program_id(0), pl.num_programs(0) - 1
    dp, mp = lax.axis_index("dp"), lax.axis_index("mp")
    gather = WeightGather((s_qkv, s_out, s_up), (g_qkv, g_out, g_up), (True, True, False), wsend, wrecv)
    mates = [mp // 2 * 2 + (mp + 1) % 2, (mp + 2) % 4, (mp // 2 * 2 + 2) % 4 + (mp + 1) % 2]
    all_words = src_ref.shape[1]
    slots = n_dp * cap
    row_copy = lambda k: remote_copy(row_send.at[k], row_got.at[k], ssem, rsem, k, (lax.rem(dp + k, n_dp), mp))
    seg_copy = lambda j: remote_copy(seg_all.at[mp], seg_all.at[mp], ssem, rsem, n_dp + j, (dp, mates[j]))

    @pl.when(step == 0)
    def _():
        barrier = pltpu.get_barrier_semaphore()
        greeted = [(lax.rem(dp + k, n_dp), mp) for k in range(1, n_dp)] + [(dp, mate) for mate in mates]
        for peer in greeted:
            pl.semaphore_signal(barrier, inc=1, device_id=peer, device_id_type=MESH)
        source = src_ref[...]
        owner = source // (all_words * 4)
        owner_c = as_column(owner)[:, 0:1]
        index_r = lax.broadcasted_iota(jnp.int32, (all_words, all_words), 0)
        index_c = lax.broadcasted_iota(jnp.int32, (all_words, all_words), 1)
        earlier = (owner_c == owner.astype(F32)) & (index_r < index_c)
        rank = jnp.sum(jnp.where(earlier, 1.0, 0.0), 0, keepdims=True).astype(jnp.int32)
        slot_of = lax.rem(owner - dp + n_dp, n_dp) * cap + rank
        at_slot = lax.broadcasted_iota(jnp.int32, (slots, all_words), 0) == slot_of
        onehot_ref[...] = jnp.where(at_slot, 1.0, 0.0).astype(BF16)
        row_mat = as_column(lax.rem(source, all_words) + 1).astype(BF16)
        row_send[...] = dot_nn(onehot_ref[...], row_mat).astype(BF16).reshape(n_dp, cap, 128)
        seg_all[mp] = jnp.broadcast_to(seg_ref[...], (8, all_words))
        cnt_col[...] = as_column(cnt_ref[...])
        pl.semaphore_wait(barrier, len(greeted))
        gather.begin()
        for k in range(1, n_dp):
            row_copy(k).start()
        for j in range(3):
            seg_copy(j).start()
        row_got[0] = row_send[0]

    @pl.when(step == last)
    def _():
        gather.pass_last(0)
        gather.pass_last(1)

    words, wide = x_ref.shape
    width = wide // CHARS
    blocks = words // 8
    gains = gains_ref[...].astype(F32)
    counts_here = cnt_col[pl.ds(pl.multiple_of(step * words, words), words), :].astype(jnp.int32)
    pieces = []
    for g in range(words // 16):
        xt = x_ref[16 * g : 16 * g + 16, :].astype(F32)
        for half in range(2):
            for c in range(CHARS):
                pieces.append(xt[8 * half : 8 * half + 8, width * c : width * c + width])
    x = jnp.concatenate(pieces, 0)
    hid = wup_ref.shape[1]
    rows = words * CHARS
    cuts = range(0, hid, HIDDEN_CUT)
    held = lax.rem(step, 2)
    p_ref, a_ref, act_ref = p_buf.at[held], a_buf.at[held], act_buf.at[held]

    def out_copies(of):
        slot = lax.rem(of, 2)
        at = lambda n: pl.ds(pl.multiple_of(of * n, n), n)
        heads = rows * CHAR_HEADS
        copies = [
            pltpu.make_async_copy(p_buf.at[slot], p_any.at[at(rows)], osem.at[slot, 0]),
            pltpu.make_async_copy(a_buf.at[slot], a_any.at[at(heads)], osem.at[slot, 1]),
        ]
        for i in range(2 * hid // HIDDEN_CUT):
            cut = pl.ds(HIDDEN_CUT * i, HIDDEN_CUT)
            copies.append(pltpu.make_async_copy(act_buf.at[slot, :, cut], act_any.at[at(rows), cut], osem.at[slot, 2 + i]))
        return copies

    leaving = out_copies(step)

    @pl.when(step >= 2)
    def _():
        for copy in out_copies(step - 2):
            copy.wait()

    n1, rs1 = norm_fwd(x, gains[0:1])
    lane = lax.broadcasted_iota(jnp.int32, (rows, 128), 1)
    late_ref[:, 0:width] = n1
    late_ref[:, width:] = jnp.where(lane == 0, rs1, 0.0).astype(BF16)
    p_ref[...] = dot_nn(n1, wqkv_ref[...]).astype(BF16)
    row_w = lax.broadcasted_iota(jnp.int32, (8, 128), 0)
    lane_w = lax.broadcasted_iota(jnp.int32, (8, 128), 1) % 8
    same = row_w == lane_w
    slot = lax.broadcasted_iota(jnp.int32, (CHARS, 8, 128), 0)
    size = CHAR_HEADS * 128
    scale = (width // CHAR_HEADS) ** -0.5
    scores = []
    for b in range(blocks):
        sl = slice(128 * b, 128 * b + 128)
        scores.append(dot_nt(head_stack(p_ref[sl, width : 2 * width], CHAR_HEADS, scale), p_ref[sl, 0:width]))
    for b in range(blocks):
        here = slot < counts_here[8 * b : 8 * b + 8][None]
        st = jnp.where(here[None], scores[b].reshape(CHAR_HEADS, CHARS, 8, 128), NEGATIVE)
        e = jnp.exp(st - jnp.max(st, 1, keepdims=True))
        r = jnp.where(same[None, None], 1.0 / jnp.sum(e, 1, keepdims=True), 0.0)
        a_ref[size * b : size * b + size, :] = (e * r).reshape(size, 128).astype(BF16)
    for b in range(blocks):
        sl = slice(128 * b, 128 * b + 128)
        a = a_ref[size * b : size * b + size, :]
        early_ref[sl, 0:width] = dot_tn(a, head_stack(p_ref[sl, 2 * width : 3 * width], CHAR_HEADS, 1.0)).astype(BF16)
    leaving[0].start()
    leaving[1].start()
    m = x + dot_nn(early_ref[:, 0:width], wout_ref[...])
    n2, rs2 = norm_fwd(m, gains[1:2])
    early_ref[:, width : 2 * width] = n2

    @pl.when(step == 1)
    def _():
        gather.pass_on(0)
        gather.pass_on(1)


    @pl.when(step == last)
    def _():
        gather.pass_on(2)

    f = m
    for i, j in enumerate(cuts):
        cut = slice(j, j + HIDDEN_CUT)
        act, slope = gelu_both(dot_nn(n2, wup_ref[:, cut]).astype(BF16))
        act_ref[:, cut] = act
        act_ref[:, hid + j : hid + j + HIDDEN_CUT] = slope
        leaving[2 + i].start()
        leaving[2 + len(cuts) + i].start()
        f = f + dot_nn(act, wdown_ref[cut, :])
    early_ref[:, 2 * width : 3 * width] = f.astype(BF16)
    t = jnp.sum(f * pool_ref[...].astype(F32).reshape(1, width), -1, keepdims=True).reshape(blocks, CHARS, 8, 1)
    counts = counts_here[:, 0:1].reshape(blocks, 1, 8, 1)
    t = jnp.where(lax.broadcasted_iota(jnp.int32, t.shape, 1) < counts, t, NEGATIVE)
    et = jnp.exp(t - jnp.max(t, 1, keepdims=True))
    aw = et / jnp.sum(et, 1, keepdims=True)
    early_ref[:, 3 * width :] = jnp.where(lane == 0, rs2, aw.reshape(rows, 1)).astype(BF16)
    pooled_ref[...] = jnp.sum(aw * f.reshape(blocks, CHARS, 8, width), 1).reshape(words, width).astype(BF16)

    @pl.when(step == last)
    def _():
        for k in range(1, n_dp):
            row_copy(k).wait()
        for j in range(3):
            seg_copy(j).wait()
        at_row = row_got[...].reshape(slots, 128)[:, 0:1].astype(F32) - 1.0
        lanes = lax.broadcasted_iota(jnp.int32, (slots, all_words), 1).astype(F32)
        place_ref[...] = jnp.where(lanes == at_row, 1.0, 0.0).astype(BF16)
        seg_out[...] = seg_all[...]
        gather.finish()
        for copy in out_copies(step - 1) + leaving:
            copy.wait()


def char_forward(n_dp, x, counts, gains, wqkv, wout, wup, wdown, pool, source, segments, slices):
    words, wide = x.shape
    width = wide // CHARS
    rows = words * CHARS
    step_rows = STEP_WORDS * CHARS
    cap = -(-2 * words // n_dp // 16) * 16
    slots = n_dp * cap
    full = lambda arr: pl.BlockSpec(arr.shape, lambda i: (0,) * arr.ndim)
    blk = lambda n, w: pl.BlockSpec((n, w), lambda i: (i, 0))
    hid = wup.shape[1]
    outs = [
        (words, STEP_WORDS, width), (rows, step_rows, 3 * width + 128), (rows, step_rows, width + 128),
        (rows, None, 3 * width), (rows * CHAR_HEADS, None, 128), (rows, None, 2 * hid),
    ]
    fixed = [((slots, words), BF16), ((slots, words), BF16), ((4, 8, words), jnp.int32)]
    any_spec = pl.BlockSpec(memory_space=pl.ANY)
    return pl.pallas_call(
        functools.partial(char_fwd_body, n_dp, cap),
        grid=(words // STEP_WORDS,),
        in_specs=[blk(STEP_WORDS, wide)]
        + [full(w) for w in (counts, gains, wqkv, wout, wup, wdown, pool, source, segments)]
        + [any_spec] * len(slices),
        out_specs=[blk(b, w) if b else any_spec for _, b, w in outs]
        + [pl.BlockSpec(s, lambda i, n=len(s): (0,) * n) for s, _ in fixed]
        + [any_spec] * len(slices),
        out_shape=[jax.ShapeDtypeStruct((n, w), BF16) for n, _, w in outs]
        + [jax.ShapeDtypeStruct(s, d) for s, d in fixed]
        + [jax.ShapeDtypeStruct((4, *s.shape), s.dtype) for s in slices],
        scratch_shapes=[
            pltpu.VMEM((words, 128), F32),
            pltpu.VMEM((n_dp, cap, 128), BF16), pltpu.VMEM((n_dp, cap, 128), BF16), pltpu.VMEM((4, 8, words), jnp.int32),
            pltpu.SemaphoreType.DMA((n_dp + 3,)), pltpu.SemaphoreType.DMA((n_dp + 3,)),
            pltpu.SemaphoreType.DMA((5 * len(slices),)), pltpu.SemaphoreType.DMA((5 * len(slices),)),
            pltpu.VMEM((2, step_rows, 3 * width), BF16), pltpu.VMEM((2, step_rows * CHAR_HEADS, 128), BF16),
            pltpu.VMEM((2, step_rows, 2 * hid), BF16),
            pltpu.SemaphoreType.DMA((2, 2 + 2 * (hid // HIDDEN_CUT))),
        ],
        compiler_params=pltpu.CompilerParams(collective_id=2, has_side_effects=True, vmem_limit_bytes=VMEM_LIMIT),
        name="char_forward",
    )(x, counts, gains, wqkv, wout, wup, wdown, pool, source, segments, *slices)


CHAR_A = 144
CHAR_CUT = 80
CHAR_B = 48
WORD_ROWS = 800
CHUNK_ROWS = 192
CHUNKS = ((0, 192), (192, 224), (224, 416), (416, 608), (608, 800))
ROW_QKV, ROW_PROJ, ROW_OUT, ROW_UP, ROW_DOWN = 0, 192, 224, 288, 544
SEMS = 8


def fold_half(block):
    half = block.shape[0] // 2
    return jnp.concatenate([block[:half], block[half:]], 1)


def unfold_half(block):
    return jnp.concatenate([block[:, :64], block[:, 64:]], 0)


class Halving:
    def __init__(self, n_z, sent, work, got, ssem, rsem, base, order):
        self.n_z, self.sent, self.work, self.got = n_z, sent, work, got
        self.ssem, self.rsem, self.base, self.order = ssem, rsem, base, order
        self.z, self.x, self.y, self.core = coordinates()

    def copies(self, phase):
        z, x, y, core = self.z, self.x, self.y, self.core
        work = self.work
        step = "c" if phase == 0 else self.order[phase - 1]
        if step == "c":
            pairs = [(self.sent, self.got[0], device_of(z, x, y, 1 - core))]
        elif step == "y":
            src = work.at[1 - y] if phase == 1 else work.at[1 - y, x]
            pairs = [(src, self.got[phase], device_of(z, x, 1 - y, core))]
        elif step == "x":
            src = work.at[:, 1 - x] if phase == 1 else work.at[y, 1 - x]
            pairs = [(src, self.got[phase], device_of(z, 1 - x, y, core))]
        else:
            pairs = []
            for k in range(1, self.n_z):
                other = lax.rem(z + k, self.n_z)
                pairs.append((work.at[y, x, other], self.got[3].at[k - 1], device_of(other, x, y, core)))
        return [
            remote_copy(src, dst, self.ssem, self.rsem, self.base + phase + i, peer)
            for i, (src, dst, peer) in enumerate(pairs)
        ]

    def start(self, phase):
        for copy in self.copies(phase):
            copy.start()

    def finish(self, phase):
        for copy in self.copies(phase):
            copy.wait()
        x, y = self.x, self.y
        work, got = self.work, self.got[phase]
        step = "c" if phase == 0 else self.order[phase - 1]

        def add(mine, other):
            def body(i, carry):
                mine[i] = mine[i] + other[i]
                return carry
            lax.fori_loop(0, self.n_z, body, 0)

        if step == "c":
            for i in range(2):
                for j in range(2):
                    add(work.at[i, j], got.at[i, j])
        elif step == "y" and phase == 1:
            for j in range(2):
                add(work.at[y, j], got.at[j])
        elif step == "x" and phase == 1:
            for i in range(2):
                add(work.at[i, x], got.at[i])
        elif step in "yx":
            add(work.at[y, x], got)

    def advance(self, phase):
        self.finish(phase)
        self.start(phase + 1)

    def total(self):
        value = self.work[self.y, self.x, self.z].astype(F32)
        for k in range(self.n_z - 1):
            value += self.got[3][k].astype(F32)
        return value

    @staticmethod
    def got_shapes(n_z, rows, first=0):
        shapes = [(2, 2, n_z, rows, 128), (2, n_z, rows, 128), (n_z, rows, 128), (n_z - 1, rows, 128)]
        return [pltpu.VMEM(s, BF16) for s in shapes[first:]]


class DirectSum:
    def __init__(self, n_dp, buf, got_mp, held, got_dp, ssem, rsem, base):
        self.n_dp, self.buf, self.got_mp, self.held, self.got_dp = n_dp, buf, got_mp, held, got_dp
        self.ssem, self.rsem, self.base = ssem, rsem, base
        self.dp, self.mp = lax.axis_index("dp"), lax.axis_index("mp")

    def copies(self, phase):
        dp, mp, n_dp = self.dp, self.mp, self.n_dp
        make = lambda src, dst, slot, peer: remote_copy(src, dst, self.ssem, self.rsem, self.base + slot, peer)
        if phase == 0:
            to = [lax.rem(mp + k, 4) for k in range(1, 4)]
            return [make(self.buf.at[p], self.got_mp.at[k], k, (dp, p)) for k, p in enumerate(to)]
        to = [lax.rem(dp + k, n_dp) for k in range(1, n_dp)]
        return [make(self.held.at[d], self.got_dp.at[k], 3 + k, (d, mp)) for k, d in enumerate(to)]

    def start(self, phase):
        for copy in self.copies(phase):
            copy.start()

    def advance(self, extra):
        for copy in self.copies(0):
            copy.wait()
        got, buf, mp = self.got_mp, self.buf, self.mp
        rows = buf.shape[2]
        extra = extra.astype(self.held.dtype)

        def add(d, carry):
            total = buf[mp, d].astype(F32) + got[0, d].astype(F32)
            total = total + got[1, d].astype(F32) + got[2, d].astype(F32)
            self.held[d, 0:rows] = total.astype(self.held.dtype)
            self.held[d, rows:] = extra
            return carry
        lax.fori_loop(0, self.n_dp, add, 0)
        self.start(1)

    def total(self):
        for copy in self.copies(1):
            copy.wait()
        value = self.held[self.dp].astype(F32)
        for k in range(self.n_dp - 1):
            value += self.got_dp[k].astype(F32)
        return value

    @staticmethod
    def shapes(n_dp, rows, dtype):
        shapes = [(4, n_dp, rows, 128), (3, n_dp, rows, 128), (n_dp, rows + 16, 128), (n_dp - 1, rows + 16, 128)]
        return [pltpu.VMEM(s, dtype) for s in shapes]


class GradientSums:
    def __init__(self, n_z, word_sum, refs):
        self.n_z, self.word_sum = n_z, word_sum
        abuf, wbuf, small, sgot, ssem, rsem, lsem, *got = refs
        self.abuf, self.wbuf, self.small, self.sgot = abuf, wbuf, small, sgot
        self.ssem, self.rsem, self.lsem = ssem, rsem, lsem
        self.z, self.x, self.y, self.core = coordinates()
        self.chunks = []
        for i, order in enumerate(("yxz", "yxz", "yxz", "xyz", "xyz")):
            rows = wbuf.at[:, :, :, CHUNKS[i][0] : CHUNKS[i][1]]
            self.chunks.append(
                Halving(n_z, None, rows, [None, *got[3 * i : 3 * i + 3]], ssem, rsem, SEMS * i, order)
            )
        core = self.core
        self.parts = []
        for i, (low, high, order) in enumerate(((0, CHAR_CUT, "yxz"), (CHAR_CUT, CHAR_A, "xyz"))):
            rows = abuf.at[:, :, :, :, low:high]
            at = 3 * len(CHUNKS) + 4 * i
            self.parts.append(
                Halving(n_z, rows.at[1 - core], rows.at[core], got[at : at + 4], ssem, rsem, (5 + i) * SEMS, order)
            )
        at = 3 * len(CHUNKS) + 8
        self.partb = DirectSum(2 * n_z, *got[at : at + 4], ssem, rsem, 7 * SEMS)
        self.tiny = 9 * SEMS

    @staticmethod
    def scratch(n_z):
        n_sem = 11 * SEMS
        shapes = [
            pltpu.VMEM((2, 2, 2, n_z, CHAR_A, 128), BF16), pltpu.VMEM((2, 2, n_z, WORD_ROWS, 128), BF16),
            pltpu.VMEM((16, 128), F32), pltpu.VMEM((3, 16, 128), F32),
            pltpu.SemaphoreType.DMA((n_sem,)), pltpu.SemaphoreType.DMA((n_sem,)), pltpu.SemaphoreType.DMA,
        ]
        for low, high in CHUNKS:
            shapes += Halving.got_shapes(n_z, high - low, 1)
        for rows in (CHAR_CUT, CHAR_A - CHAR_CUT):
            shapes += Halving.got_shapes(n_z, rows)
        return shapes + DirectSum.shapes(2 * n_z, CHAR_B, BF16)

    def begin(self):
        load = pltpu.make_async_copy(self.word_sum, self.wbuf, self.lsem)
        load.start()
        dp, mp, n_dp = self.partb.dp, self.partb.mp, 2 * self.n_z
        peers = [(lax.rem(dp + k, n_dp), mp) for k in range(1, n_dp)] + [(dp, lax.rem(mp + k, 4)) for k in range(1, 4)]
        barrier = pltpu.get_barrier_semaphore()
        for peer in peers:
            pl.semaphore_signal(barrier, inc=1, device_id=peer, device_id_type=MESH)
        pl.semaphore_wait(barrier, len(peers))
        load.wait()
        for i, phase in enumerate((3, 1, 1, 1, 2)):
            self.chunks[i].start(phase)

    def pack_a(self, gup_ref, gdown_ref, gout_ref):
        for d in range(2 * self.n_z):
            down = gdown_ref[128 * d : 128 * d + 128, :]
            out = gout_ref[32 * d : 32 * d + 32, :]
            for p in range(4):
                block = self.abuf.at[p % 2, p // 2, d % 2, d // 2]
                block[0:32, :] = gup_ref[32 * d : 32 * d + 32, 256 * p : 256 * p + 128].astype(BF16)
                block[32:64, :] = gup_ref[32 * d : 32 * d + 32, 256 * p + 128 : 256 * p + 256].astype(BF16)
                block[64:128, :] = fold_half(down[:, 64 * p : 64 * p + 64]).astype(BF16)
                block[128:144, :] = fold_half(out[:, 64 * p : 64 * p + 64]).astype(BF16)
        for part in self.parts:
            part.start(0)

    def pack_b(self, gqkv_ref):
        for d in range(2 * self.n_z):
            qkv = gqkv_ref[32 * d : 32 * d + 32, :]
            for p in range(4):
                own = qkv[:, 192 * p : 192 * p + 192]
                self.partb.buf[p, d, 0:32, :] = own[:, 0:128].astype(BF16)
                self.partb.buf[p, d, 32:48, :] = fold_half(own[:, 128:192]).astype(BF16)
        self.partb.start(0)

    def tiny_copies(self):
        dp, mp = self.partb.dp, self.partb.mp
        return [
            remote_copy(self.small, self.sgot.at[k], self.ssem, self.rsem, self.tiny + k, (dp, lax.rem(mp + k + 1, 4)))
            for k in range(3)
        ]

    def tiny_start(self):
        for copy in self.tiny_copies():
            copy.start()

    def tiny_finish(self):
        for copy in self.tiny_copies():
            copy.wait()
        return self.small[...] + self.sgot[0] + self.sgot[1] + self.sgot[2]


def pack_small(cgain_ref, cpool_ref, gqkv_ref, wqkv_ref, gains_ref, wgain_ref):
    gains = gains_ref[...].astype(F32)
    width = gains.shape[1]
    first = jnp.sum(gqkv_ref[...] * wqkv_ref[...].astype(F32), -1, keepdims=True)
    first = jnp.transpose(jnp.broadcast_to(first, (width, 128)))[0:1, :]
    sums = [
        first / gains[0:1], jnp.sum(cgain_ref[...], 0, keepdims=True) / gains[1:2],
        jnp.sum(cpool_ref[...], 0, keepdims=True), wgain_ref[0:1, :], wgain_ref[1:2, :],
    ]
    rows = [v[:, t : t + 128] for v in sums for t in range(0, v.shape[1], 128)]
    rows.append(jnp.zeros((2, 128), F32))
    return jnp.concatenate(rows, 0)


def finish_body(
    dx_ref, wide_ref, sums_ref,
    odx_ref, owide_ref, oqkv_ref, oout_ref, oup_ref, odown_ref, oproj_ref, owqkv_ref, owout_ref, owup_ref, owdown_ref,
    ocgain_ref, opool_ref, owgain_ref,
):
    odx_ref[...] = dx_ref[...].astype(F32)

    @pl.when(pl.program_id(0) == 0)
    def _():
        base = WORD_ROWS
        owide_ref[...] = wide_ref[...]
        for t in range(3):
            owqkv_ref[t] = sums_ref[64 * t : 64 * t + 64, :]
        oproj_ref[...] = sums_ref[ROW_PROJ : ROW_PROJ + 32, :]
        owout_ref[...] = sums_ref[ROW_OUT : ROW_OUT + 64, :]
        for t in range(4):
            owup_ref[:, 128 * t : 128 * t + 128] = sums_ref[ROW_UP + 64 * t : ROW_UP + 64 * t + 64, :]
            owdown_ref[:, 128 * t : 128 * t + 128] = sums_ref[ROW_DOWN + 64 * t : ROW_DOWN + 64 * t + 64, :]
        oup_ref[:, 0:128] = sums_ref[base : base + 32, :]
        oup_ref[:, 128:256] = sums_ref[base + 32 : base + 64, :]
        odown_ref[...] = unfold_half(sums_ref[base + 64 : base + 128, :]).T
        oout_ref[...] = unfold_half(sums_ref[base + 128 : base + 144, :])
        base = WORD_ROWS + CHAR_A
        oqkv_ref[:, 0:128] = sums_ref[base : base + 32, :]
        oqkv_ref[:, 128:192] = unfold_half(sums_ref[base + 32 : base + 48, :])
        total = sums_ref[base + CHAR_B : base + CHAR_B + 16, :]
        for j in range(2):
            for t in range(2):
                ocgain_ref[j : j + 1, 128 * t : 128 * t + 128] = total[2 * j + t : 2 * j + t + 1]
            for t in range(4):
                owgain_ref[j : j + 1, 128 * t : 128 * t + 128] = total[6 + 4 * j + t : 7 + 4 * j + t]
        for t in range(2):
            opool_ref[:, 128 * t : 128 * t + 128] = total[4 + t : 5 + t]


def finish(d_chars, word_out, sums):
    words, wide = d_chars.shape
    steps = 2
    full = lambda s: pl.BlockSpec(s, lambda i: (0,) * len(s))
    blk = pl.BlockSpec((words // steps, wide), lambda i: (i, 0))
    outs = [
        word_out.shape, (32, 192), (32, 64), (32, 256), (64, 128), (32, 128),
        (3, 64, 128), (64, 128), (64, 512), (64, 512), (2, 256), (1, 256), (2, 512),
    ]
    result = pl.pallas_call(
        finish_body,
        grid=(steps,),
        in_specs=[blk, full(word_out.shape), full(sums.shape)],
        out_specs=[blk] + [full(s) for s in outs],
        out_shape=[jax.ShapeDtypeStruct((words, wide), F32), jax.ShapeDtypeStruct(outs[0], BF16)]
        + [jax.ShapeDtypeStruct(s, F32) for s in outs[1:]],
        compiler_params=pltpu.CompilerParams(vmem_limit_bytes=VMEM_LIMIT),
        name="finish",
    )(d_chars, word_out, sums)
    dx, out, qkv, cout, up, down, proj, wqkv, wout, wup, wdown, cgain, pool, wgain = result
    return (out, dx, qkv, cout, up, down.T, proj, wqkv, wout.T, wup, wdown.T, cgain, pool.reshape(-1), wgain)


def char_bwd_body(
    n_dp, fused,
    dpool_ref, gains_ref, pool_ref, wqkv_any, wout_any, wup_any, wdown_any,
    early_ref, late_ref, p_any, a_any, act_any,
    *refs,
):
    if fused:
        word_sum, wgain_ref, dx_ref, sums_ref, *refs = refs
    else:
        dx_ref, *refs = refs
        outs, refs = refs[:6], refs[6:]
    gqkv_ref, gout_ref, gup_ref, gdown_ref, ggain_ref, gpool_ref, *refs = refs
    dm_ref, dp_ref, do_ref, ds_ref, wqkv_ref, wout_ref, wup_ref, wdown_ref, dp_now, do_now, wsem, p_buf, a_buf, pasem, act_buf, actsem, *refs = refs
    step = pl.program_id(0)
    part = pl.num_programs(0) // 3
    words = dpool_ref.shape[0]
    width = wout_ref.shape[0]
    hid = wup_ref.shape[1]
    blocks = words // 8
    rows = words * CHARS
    size = CHAR_HEADS * 128
    gains = gains_ref[...].astype(F32)
    here = pl.ds(pl.multiple_of(lax.rem(step, part) * rows, rows), rows)
    sums = GradientSums(n_dp // 2, word_sum, refs) if fused else None
    chunks = sums.chunks if fused else None

    def at(when, act):
        if fused:
            pl.when(step == when)(act)

    def act_copy(of):
        slot = lax.rem(of, 2)
        return pltpu.make_async_copy(
            act_any.at[pl.ds(pl.multiple_of(of * rows, rows), rows)], act_buf.at[slot], actsem.at[slot]
        )

    @pl.when(step == 0)
    def _():
        act_copy(step).start()

    @pl.when(step + 1 < part)
    def _():
        act_copy(step + 1).start()

    def pa_copies(of):
        slot = lax.rem(of, 2)
        heads = rows * CHAR_HEADS
        return [
            pltpu.make_async_copy(p_any.at[pl.ds(pl.multiple_of(of * rows, rows), rows)], p_buf.at[slot], pasem.at[slot, 0]),
            pltpu.make_async_copy(a_any.at[pl.ds(pl.multiple_of(of * heads, heads), heads)], a_buf.at[slot], pasem.at[slot, 1]),
        ]

    @pl.when((step + 1 >= part) & (step + 1 < 2 * part))
    def _():
        for copy in pa_copies(step + 1 - part):
            copy.start()

    @pl.when(step == 0)
    def _():
        pairs = ((wdown_any, wdown_ref), (wup_any, wup_ref), (wout_any, wout_ref), (wqkv_any, wqkv_ref))
        loads = [pltpu.make_async_copy(src, dst, wsem.at[i]) for i, (src, dst) in enumerate(pairs)]
        for load in loads:
            load.start()
        if fused:
            sums.begin()
        for load in loads:
            load.wait()
        for ref in (gqkv_ref, gout_ref, gup_ref, gdown_ref, ggain_ref, gpool_ref):
            ref[...] = jnp.zeros_like(ref)

    def event(when, *moves):
        def act():
            for sum_of, phase in moves:
                if phase < 3:
                    sum_of.advance(phase)
                else:
                    sum_of.finish(3)
        at(when, act)

    if fused:
        first, other = sums.parts
        event(2, (chunks[1], 1), (chunks[3], 1))
        event(3, (chunks[2], 1), (chunks[4], 2))
        event(4, (chunks[1], 2), (chunks[3], 2))
        event(5, (first, 0), (other, 0))
        event(6, (chunks[2], 2))
        event(7, (first, 1), (other, 1))
        event(9, (first, 2), (other, 2))

    @pl.when(step < part)
    def _():
        dpool = dpool_ref[...].astype(F32).reshape(blocks, 1, 8, width)
        f = early_ref[:, 2 * width : 3 * width].astype(F32).reshape(blocks, CHARS, 8, width)
        stat = early_ref[:, 3 * width :].astype(F32)
        aw = stat[:, 1:2].reshape(blocks, CHARS, 8, 1)
        g = jnp.sum(f * dpool, -1, keepdims=True)
        dt = aw * (g - jnp.sum(aw * g, 1, keepdims=True))
        gpool_ref[...] += jnp.sum((dt * f).reshape(rows // 8, 8, width), 0)
        df = (aw * dpool + dt * pool_ref[...].astype(F32).reshape(1, width)).reshape(rows, width)
        dfb = df.astype(BF16)
        n2 = early_ref[:, width : 2 * width]
        act_copy(step).wait()
        act_ref = act_buf.at[lax.rem(step, 2)]
        dn2 = None
        for j in range(0, wup_ref.shape[1], HIDDEN_CUT):
            cut = slice(j, j + HIDDEN_CUT)
            gdown_ref[cut, :] += dot_tn(act_ref[:, cut], dfb)
            dh = act_ref[:, hid + j : hid + j + HIDDEN_CUT] * dot_nt(dfb, wdown_ref[cut, :]).astype(BF16)
            gup_ref[:, cut] += dot_tn(n2, dh)
            term = dot_nt(dh, wup_ref[:, cut])
            dn2 = term if dn2 is None else dn2 + term
        d_norm, dnn = norm_bwd(dn2, n2, stat[:, 0:1], gains[1:2])
        ggain_ref[...] += jnp.sum(dnn.reshape(rows // 8, 8, width), 0)
        dm = df + d_norm
        dmb = dm.astype(BF16)
        dm_ref[here, :] = dmb
        gout_ref[...] += dot_tn(early_ref[:, 0:width], dmb)
        do_ref[here, :] = dot_nt(dmb, wout_ref[...]).astype(BF16)

    at(part - 1, lambda: sums.pack_a(gup_ref, gdown_ref, gout_ref))

    @pl.when((step >= part) & (step < 2 * part))
    def _():
        scale = (width // CHAR_HEADS) ** -0.5
        for copy in pa_copies(step - part):
            copy.wait()
        p_ref, a_ref = p_buf.at[lax.rem(step - part, 2)], a_buf.at[lax.rem(step - part, 2)]
        do_now[...] = do_ref[here, :]
        raw = []
        for b in range(blocks):
            sl = slice(128 * b, 128 * b + 128)
            raw.append(dot_nt(head_stack(p_ref[sl, 2 * width : 3 * width], CHAR_HEADS, 1.0), do_now[128 * b : 128 * b + 128, :]))
        for b in range(blocks):
            a = a_ref[size * b : size * b + size, :].astype(F32).reshape(CHAR_HEADS, CHARS, 8, 128)
            dpt = raw[b].reshape(CHAR_HEADS, CHARS, 8, 128)
            delta = jnp.sum(a * dpt, 1, keepdims=True)
            ds_ref[size * b : size * b + size, :] = (a * (dpt - delta)).reshape(size, 128).astype(BF16)
        for b in range(blocks):
            sl = slice(128 * b, 128 * b + 128)
            ds = ds_ref[size * b : size * b + size, :]
            k = head_stack(p_ref[sl, width : 2 * width], CHAR_HEADS, scale)
            dp_now[128 * b : 128 * b + 128, 0:width] = dot_tn(ds, k).astype(BF16)
        for b in range(blocks):
            sl = slice(128 * b, 128 * b + 128)
            cut = lambda h: ds_ref[size * b + 128 * h : size * b + 128 * h + 128, :]
            wide = jnp.concatenate([cut(h) for h in range(CHAR_HEADS)], 1)
            q = head_stack(p_ref[sl, 0:width], CHAR_HEADS, scale)
            dp_now[128 * b : 128 * b + 128, width : 2 * width] = dot_nn(wide, q).astype(BF16)
        for b in range(blocks):
            cut = lambda h: a_ref[size * b + 128 * h : size * b + 128 * h + 128, :]
            wide = jnp.concatenate([cut(h) for h in range(CHAR_HEADS)], 1)
            do = head_stack(do_now[128 * b : 128 * b + 128, :], CHAR_HEADS, 1.0)
            dp_now[128 * b : 128 * b + 128, 2 * width : 3 * width] = dot_nn(wide, do).astype(BF16)
        dp = dp_now[...]
        dp_ref[here, :] = dp
        gqkv_ref[...] += dot_tn(late_ref[:, 0:width], dp)

    def begin_b():
        sums.pack_b(gqkv_ref)
        sums.small[...] = pack_small(ggain_ref, gpool_ref, gqkv_ref, wqkv_ref, gains_ref, wgain_ref)
        sums.tiny_start()
    at(2 * part - 1, begin_b)

    @pl.when(step >= 2 * part)
    def _():
        dn1 = dot_nt(dp_ref[here, :], wqkv_ref[...])
        rstd = late_ref[:, width:].astype(F32)[:, 0:1]
        d_norm, _ = norm_bwd(dn1, late_ref[:, 0:width], rstd, gains[0:1])
        dx = dm_ref[here, :].astype(F32) + d_norm
        for b in range(0, blocks, 2):
            for c in range(CHARS):
                pair = [dx[128 * i + 8 * c : 128 * i + 8 * c + 8] for i in (b, b + 1)]
                dx_ref[8 * b : 8 * b + 16, width * c : width * c + width] = jnp.concatenate(pair, 0).astype(BF16)

    def end():
        sums.partb.advance(sums.tiny_finish())
        for i, (low, high) in enumerate(CHUNKS):
            chunks[i].finish(3)
            sums_ref[low:high, :] = chunks[i].total()
        base = WORD_ROWS
        for i, (low, high) in enumerate(((0, CHAR_CUT), (CHAR_CUT, CHAR_A))):
            sums.parts[i].finish(3)
            sums_ref[base + low : base + high, :] = sums.parts[i].total()
        base += CHAR_A
        sums_ref[base : base + CHAR_B + 16, :] = sums.partb.total()
    at(3 * part - 1, end)

    if not fused:
        @pl.when(step == 3 * part - 1)
        def _():
            for out, ref in zip(outs, (gqkv_ref, gout_ref, gup_ref, gdown_ref, ggain_ref, gpool_ref)):
                out[...] = ref[...]


def char_backward(n_dp, dpool, kept, gains, wqkv, wout, wup, wdown, pool, word_sum, wgain):
    words = dpool.shape[0]
    width = wout.shape[0]
    rows = words * CHARS
    step_rows = STEP_WORDS * CHARS
    steps = words // STEP_WORDS
    fused = word_sum is not None
    full = lambda arr: pl.BlockSpec(arr.shape, lambda i: (0,) * arr.ndim)
    fixed = lambda s: pl.BlockSpec(s, lambda i: (0,) * len(s))
    first = lambda n, w: pl.BlockSpec((n, w), lambda i: (lax.min(i, steps - 1), 0))
    second = lambda n, w: pl.BlockSpec((n, w), lambda i: (lax.clamp(0, i - steps, steps - 1), 0))
    third = lambda n, w: pl.BlockSpec((n, w), lambda i: (lax.max(i - 2 * steps, 0), 0))
    twice = lambda n, w: pl.BlockSpec((n, w), lambda i: (lax.rem(lax.max(i - steps, 0), steps), 0))
    grads = [wqkv.shape, wout.shape, wup.shape, wdown.shape, (8, width), (8, width)]
    scratch = [pltpu.VMEM(s, F32) for s in grads] + [
        pltpu.VMEM((rows, width), BF16), pltpu.VMEM((rows, 3 * width), BF16), pltpu.VMEM((rows, width), BF16),
        pltpu.VMEM((step_rows * CHAR_HEADS, 128), BF16), *[pltpu.VMEM(w.shape, BF16) for w in (wqkv, wout, wup, wdown)],
        pltpu.VMEM((step_rows, 3 * width), BF16), pltpu.VMEM((step_rows, width), BF16), pltpu.SemaphoreType.DMA((4,)),
        pltpu.VMEM((2, step_rows, 3 * width), BF16), pltpu.VMEM((2, step_rows * CHAR_HEADS, 128), BF16), pltpu.SemaphoreType.DMA((2, 2)),
        pltpu.VMEM((2, step_rows, kept[4].shape[1]), BF16), pltpu.SemaphoreType.DMA((2,)),
    ]
    any_spec = pl.BlockSpec(memory_space=pl.ANY)
    args = [dpool, gains, pool, wqkv, wout, wup, wdown, *kept]
    in_specs = [first(STEP_WORDS, width), full(gains), full(pool)] + [any_spec] * 4
    in_specs += [f(r.shape[0] // steps, r.shape[1]) for f, r in zip((first, twice), kept)]
    in_specs += [any_spec] * 2
    in_specs.append(any_spec)
    params = dict(vmem_limit_bytes=VMEM_LIMIT)
    if fused:
        outs = [(WORD_ROWS + CHAR_A + CHAR_B + 16, 128)]
        args += [word_sum, wgain]
        in_specs += [pl.BlockSpec(memory_space=pl.ANY), full(wgain)]
        scratch += GradientSums.scratch(n_dp // 2)
        params.update(collective_id=1, has_side_effects=True)
    else:
        outs = grads
    return pl.pallas_call(
        functools.partial(char_bwd_body, n_dp, fused),
        grid=(3 * steps,),
        in_specs=in_specs,
        out_specs=[third(STEP_WORDS, CHARS * width)] + [fixed(s) for s in outs],
        out_shape=[jax.ShapeDtypeStruct((words, CHARS * width), BF16)] + [jax.ShapeDtypeStruct(s, F32) for s in outs],
        scratch_shapes=scratch,
        compiler_params=pltpu.CompilerParams(**params),
        name="char_backward",
    )(*args)


def word_body(
    n_dp, cap, packed,
    pooled_ref, onehot, place, seg_all, cot_ref, gains_ref, wproj_ref, *refs,
):
    slices, wholes, refs = refs[:4], refs[4:7], refs[7:]
    if packed:
        out_ref, dpool_ref, gsum_ref, ggain_ref, gbuf_ref, got_a, got_x, gq_ref, got_q, *refs = refs
    else:
        out_ref, dpool_ref, gqkv_ref, gout_ref, gup_ref, gdown_ref, gproj_ref, ggain_ref, *refs = refs
    (
        wqkv_ref, wout_ref, wup_ref, wdown_ref, vec_send, vec_got, segc_all, pooled_rows, rows_ref, normed_all, rstd_a,
        qkv_all, weights, o_send, o_all, act_ref, dh_ref, dact_ref, dm_ref,
        do_send, do_all, dk_acc, dv_acc, dqkv_send, dqkv_all, back_send, ret,
        ssem, rsem, lsem, wsend, wrecv, qsend, qrecv,
    ) = refs
    dp, mp = lax.axis_index("dp"), lax.axis_index("mp")
    n_mp = 4
    words, narrow = pooled_ref.shape
    width = cot_ref.shape[1]
    slots = n_dp * cap
    pair = 2 * (width // HEADS)
    scale = (width // HEADS) ** -0.5
    to_dp = [(lax.rem(dp + k, n_dp), mp) for k in range(n_dp)]
    from_dp = [(lax.rem(dp + n_dp - k, n_dp), mp) for k in range(n_dp)]
    mates = [(mp // 2 * 2 + (mp + 1) % 2), (mp + 2) % 4, ((mp // 2 * 2 + 2) % 4 + (mp + 1) % 2)]
    barrier = pltpu.get_barrier_semaphore()
    for k in range(1, n_dp):
        pl.semaphore_signal(barrier, inc=1, device_id=to_dp[k], device_id_type=MESH)
    for mate in mates:
        pl.semaphore_signal(barrier, inc=1, device_id=(dp, mate), device_id_type=MESH)
    next_slot = [0]

    def send(src, dst, peer):
        slot = next_slot[0]
        next_slot[0] += 1
        copy = pltpu.make_async_remote_copy(
            src_ref=src, dst_ref=dst, send_sem=ssem.at[slot], recv_sem=rsem.at[slot],
            device_id=peer, device_id_type=MESH,
        )
        copy.start()
        return copy

    z, x, y, core = coordinates()
    loads = []
    for i, held in ((3, wdown_ref), (0, wqkv_ref), (1, wout_ref), (2, wup_ref)):
        loads.append([])
        for j, at in enumerate([mp] if i == 3 else [mp, *mates]):
            src = slices[i] if j == 0 else wholes[i].at[at]
            if i == 0:
                for t in range(3):
                    dst = held.at[at, :, pair * t : pair * t + pair]
                    loads[-1].append(pltpu.make_async_copy(src.at[t], dst, lsem.at[4 + t, j]))
            else:
                loads[-1].append(pltpu.make_async_copy(src, held.at[at], lsem.at[i, j]))
        for load in loads[-1]:
            load.start()
    vec_send[...] = dot_nn(onehot[...], pooled_ref[...]).astype(BF16).reshape(n_dp, cap, narrow)

    pl.semaphore_wait(barrier, n_dp - 1 + 3)
    vec_copies = [send(vec_send.at[k], vec_got.at[k], to_dp[k]) for k in range(1, n_dp)]
    down = WeightGather((slices[3],), (wdown_ref,), (True,), wsend, wrecv)
    down.begin()
    vec_got[0] = vec_send[0]
    gains = gains_ref[...].astype(F32)
    cot = cot_ref[...]
    for j in range(n_mp):
        segc_all[words * j : words * j + words, :] = as_column(seg_all[j, 0:1, :])
    for load in loads[1] + loads[2] + loads[3]:
        load.wait()
    for copy in vec_copies:
        copy.wait()
    pooled_rows[mp] = dot_tn(place[...], vec_got[...].reshape(slots, narrow)).astype(BF16)
    row_copies = [send(pooled_rows.at[mp], pooled_rows.at[mp], (dp, mate)) for mate in reversed(mates)]
    for turn, at in enumerate([mp, *mates]):
        if turn > 0:
            row_copies[3 - turn].wait()
        rows = dot_nn(pooled_rows[at], wproj_ref[...]).astype(BF16).astype(F32)
        n_w, rstd = norm_fwd(rows, gains[0:1])
        normed_all[at] = n_w
        if turn == 0:
            down.pass_on(0)
            rows_ref[...] = rows
            rstd_a[...] = rstd
        qkv_all[at] = dot_nn(n_w, wqkv_ref[mp]).astype(BF16)
    down.pass_last(0)

    low_lane = lax.broadcasted_iota(jnp.int32, (1, pair), 1) < pair // 2
    low_mask = jnp.where(low_lane, 1.0, 0.0).astype(BF16)
    high_mask = jnp.where(low_lane, 0.0, 1.0).astype(BF16)

    def heads(v, factor):
        return jnp.concatenate([v * (low_mask * factor).astype(BF16), v * (high_mask * factor).astype(BF16)], 0)

    o_copies = []
    for i in reversed(range(n_mp)):
        keys = words * (i + 1)
        q = heads(qkv_all[i, :, 0:pair], scale)
        k = qkv_all[0 : i + 1, :, pair : 2 * pair].reshape(keys, pair)
        v = qkv_all[0 : i + 1, :, 2 * pair : 3 * pair].reshape(keys, pair)
        same = segc_all[0:keys, 0:1] == seg_all[i, 0:1, :].astype(F32)
        key_at = lax.broadcasted_iota(jnp.int32, (keys, words), 0)
        query_at = lax.broadcasted_iota(jnp.int32, (keys, words), 1) + words * i
        allowed = same & (key_at <= query_at)
        st = jnp.where(jnp.concatenate([allowed, allowed], 1), dot_nt(k, q), NEGATIVE)
        ex = jnp.exp(st - jnp.max(st, 0, keepdims=True))
        at = (ex * (1.0 / jnp.sum(ex, 0, keepdims=True))).astype(BF16)
        weights[i, 0:keys, :] = at
        both = dot_tn(at, v)
        o_send[i] = jnp.where(low_lane, both[:words], both[words:]).astype(BF16)
    for mate in reversed(mates):
        o_copies.append(send(o_send.at[mate], o_all.at[mp], (dp, mate)))
    o_all[mp] = o_send[mp]
    down.finish()
    for load in loads[0]:
        load.wait()
    for p in range(n_mp):
        dact_ref[p] = dot_nt(cot, wdown_ref[p]).astype(BF16)
    for copy in o_copies:
        copy.wait()
    attended = jnp.concatenate([o_all[p] for p in range(n_mp)], 1)
    mid = rows_ref[...] + dot_nn(attended, wout_ref[...].reshape(width, width))
    n_w2, rstd2 = norm_fwd(mid, gains[1:2])
    out = mid
    dn2 = jnp.zeros((words, width), F32)
    for p in range(n_mp):
        act, slope = gelu_both(dot_nn(n_w2, wup_ref[p]).astype(BF16))
        act_ref[p] = act
        dh = slope * dact_ref[p]
        dh_ref[p] = dh
        out = out + dot_nn(act, wdown_ref[p])
        dn2 = dn2 + dot_nt(dh, wup_ref[p])
    out_ref[...] = out.astype(BF16)
    d_norm, dnn = norm_bwd(dn2, n_w2, rstd2, gains[1:2])
    gain_b = jnp.sum(dnn, 0, keepdims=True) / gains[1:2]
    d_mid = cot.astype(F32) + d_norm
    dm_ref[...] = d_mid
    d_att = d_mid.astype(BF16)
    do_copies = []
    for mate in reversed(mates):
        do_send[mate] = dot_nt(d_att, wout_ref[mate]).astype(BF16)
        do_copies.append(send(do_send.at[mate], do_all.at[mp], (dp, mate)))
    do_all[mp] = dot_nt(d_att, wout_ref[mp]).astype(BF16)

    def pair_sum(i):
        low, high = CHUNKS[i]
        src = gbuf_ref.at[1 - core, :, :, :, low:high]
        return send(src, got_a.at[:, :, :, low:high], device_of(z, x, y, 1 - core))

    def pair_add(i):
        low, high = CHUNKS[i]

        def add(i, carry):
            b, c, d = i // n_dp, (i // (n_dp // 2)) % 2, lax.rem(i, n_dp // 2)
            gsum_ref[b, c, d, low:high] = gbuf_ref[core, b, c, d, low:high] + got_a[b, c, d, low:high]
            return carry
        lax.fori_loop(0, 2 * n_dp, add, 0)

    def x_sum(i):
        low, high = CHUNKS[i]
        return send(gsum_ref.at[:, 1 - x, :, low:high], got_x, device_of(z, 1 - x, y, core))

    def x_add(i):
        low, high = CHUNKS[i]
        for b in range(2):
            for d in range(n_dp // 2):
                gsum_ref[b, x, d, low:high] += got_x[b, d]

    def put(base, p, grad):
        if packed:
            block = grad.shape[0] // n_dp
            for d in range(n_dp):
                for t in range(grad.shape[1] // 128):
                    gbuf_ref[p % 2, p // 2, d % 2, d // 2, base + block * t : base + block * t + block, :] = (
                        grad[block * d : block * d + block, 128 * t : 128 * t + 128].astype(BF16)
                    )
        elif base == ROW_PROJ:
            gproj_ref[:, 128 * p : 128 * p + 128] = grad
        else:
            ref = {ROW_OUT: gout_ref, ROW_UP: gup_ref, ROW_DOWN: gdown_ref}[base]
            ref[p] = grad

    for p in range(n_mp):
        put(ROW_DOWN, p, dot_tn(cot, act_ref[p]))
    if packed:
        pair_three = pair_sum(4)
    for p in range(n_mp):
        put(ROW_UP, p, dot_tn(n_w2, dh_ref[p]))
    if packed:
        pair_two = pair_sum(3)
    for p in range(n_mp):
        put(ROW_OUT, p, dot_tn(d_att, o_all[p]))
    if packed:
        pair_one = pair_sum(2)
        pair_three.wait()
        pair_add(4)
        x_three = x_sum(4)
    dk_acc[...] = jnp.zeros_like(dk_acc)
    dv_acc[...] = jnp.zeros_like(dv_acc)
    for copy in do_copies:
        copy.wait()
    parts = (slice(0, pair), slice(pair, 3 * pair))

    def dqkv_copy(part, to, slot):
        cut = parts[part]
        return pltpu.make_async_remote_copy(
            src_ref=dqkv_send.at[to, :, cut], dst_ref=dqkv_all.at[mp, :, cut],
            send_sem=qsend.at[part, slot], recv_sem=qrecv.at[part, slot],
            device_id=(dp, to), device_id_type=MESH,
        )

    def dqkv_start(part, i):
        @pl.when(mp != i)
        def _():
            dqkv_copy(part, i, lax.rem(mp + i, 2) + 2 * lax.rem(mp // 2 + i // 2, 2)).start()

    def keep_sums(i):
        here = slice(words * i, words * i + words)
        dqkv_send[i, :, pair : 2 * pair] = dk_acc[here, :].astype(BF16)
        dqkv_send[i, :, 2 * pair : 3 * pair] = dv_acc[here, :].astype(BF16)

    def attention_back(falling):
        for i in reversed(range(n_mp)) if falling else range(n_mp):
            keys = words * (i + 1)
            q = qkv_all[i, :, 0:pair]
            k = qkv_all[0 : i + 1, :, pair : 2 * pair].reshape(keys, pair)
            v = qkv_all[0 : i + 1, :, 2 * pair : 3 * pair].reshape(keys, pair)
            do = heads(do_all[i], 1.0)
            at = weights[i, 0:keys, :]
            af = at.astype(F32)
            dpt = dot_nt(v, do)
            ds = (af * (dpt - jnp.sum(af * dpt, 0, keepdims=True))).astype(BF16)
            both = dot_tn(ds, k)
            dqkv_send[i, :, 0:pair] = (jnp.where(low_lane, both[:words], both[words:]) * scale).astype(BF16)
            dqkv_start(0, i)
            dk_acc[0:keys, :] += dot_nn(ds, heads(q, scale))
            dv_acc[0:keys, :] += dot_nn(at, do)
            if falling:
                keep_sums(i)
                dqkv_start(1, i)
        if not falling:
            for i in range(n_mp):
                keep_sums(i)
                dqkv_start(1, i)

    @pl.when(mp // 2 == 0)
    def _():
        attention_back(True)

    @pl.when(mp // 2 == 1)
    def _():
        attention_back(False)

    dqkv_copies = [dqkv_copy(part, mate, j + 1) for part in range(2) for j, mate in enumerate(mates)]
    dqkv_all[mp] = dqkv_send[mp]
    grad_qkv = dot_tn(normed_all[...].reshape(n_mp * words, width), dqkv_send[...].reshape(n_mp * words, 3 * pair))
    if packed:
        block = width // n_dp
        for d in range(n_dp):
            for t in range(3):
                gq_ref[d % 2, d // 2, block * t : block * t + block, :] = (
                    grad_qkv[block * d : block * d + block, 128 * t : 128 * t + 128].astype(BF16)
                )
        q_sum = send(gq_ref.at[1 - x], got_q, device_of(z, 1 - x, y, core))
        pair_two.wait()
        pair_add(3)
        pair_one.wait()
        pair_add(2)
    else:
        gqkv_ref[...] = grad_qkv
    for copy in dqkv_copies:
        copy.wait()
    d_normed = jnp.zeros((words, width), F32)
    for p in range(n_mp):
        d_normed = d_normed + dot_nt(dqkv_all[p], wqkv_ref[p])
    d_first, dnn = norm_bwd(d_normed, normed_all[mp], rstd_a[...], gains[0:1])
    gain_a = jnp.sum(dnn, 0, keepdims=True) / gains[0:1]
    d_rows = (dm_ref[...] + d_first).astype(BF16)
    ggain_ref[0:1, :] = gain_a
    ggain_ref[1:2, :] = gain_b
    d_pooled = dot_nt(d_rows, wproj_ref[...]).astype(BF16)
    back_send[...] = dot_nn(place[...], d_pooled).astype(BF16).reshape(n_dp, cap, narrow)
    back_copies = [send(back_send.at[k], ret.at[k], from_dp[k]) for k in range(1, n_dp)]
    ret[0] = back_send[0]
    grad_proj = dot_tn(pooled_rows[mp], d_rows)
    for p in range(n_mp):
        put(ROW_PROJ, p, grad_proj[:, 128 * p : 128 * p + 128])
    if packed:
        pair_zero = pair_sum(1)
        q_sum.wait()
        low, high = CHUNKS[0]
        gsum_ref[y, x, :, low:high] = gq_ref[x] + got_q[...]
        x_three.wait()
        x_add(4)
        pair_zero.wait()
        pair_add(1)
    for copy in back_copies:
        copy.wait()
    dpool_ref[...] = dot_tn(onehot[...], ret[...].reshape(slots, narrow)).astype(BF16)


def word_layer(n_dp, pooled, onehot, place, segments, cotangent, gains, wproj, slices, wholes):
    words, narrow = pooled.shape
    width = cotangent.shape[1]
    wqkv, wout, wup = wholes
    n_mp = wqkv.shape[0]
    cap = -(-2 * words // n_dp // 16) * 16
    slots = cap * n_dp
    pair = 2 * (width // HEADS)
    packed = n_dp == 8
    outs = [((words, width), BF16), ((words, narrow), BF16)]
    if packed:
        outs.append(((2, 2, n_dp // 2, WORD_ROWS, 128), BF16))
    else:
        outs.append(((width, 3 * pair), F32))
        outs += [((n_mp, width, n), F32) for n in (pair, wup.shape[2], wup.shape[2])]
        outs.append(((narrow, width), F32))
    outs.append(((2, width), F32))
    hid = wup.shape[2]
    n_sem = 2 * (n_dp - 1) + 4 * 3 + 3 + 6
    vm = pl.BlockSpec(memory_space=pltpu.VMEM)
    args = (pooled, onehot, place, segments, cotangent, gains, wproj, *slices, *wholes)
    shapes = [
        ((n_mp, width, 3 * pair), BF16), (wout.shape, BF16), (wup.shape, BF16), ((n_mp, *slices[3].shape), BF16),
        ((n_dp, cap, narrow), BF16), ((n_dp, cap, narrow), BF16), ((n_mp * words, 128), F32), ((n_mp, words, narrow), BF16),
        ((words, width), F32), ((n_mp, words, width), BF16), ((words, 1), F32),
        ((n_mp, words, 3 * pair), BF16), ((n_mp, n_mp * words, 2 * words), BF16),
        ((n_mp, words, pair), BF16), ((n_mp, words, pair), BF16),
        ((n_mp, words, hid), BF16), ((n_mp, words, hid), BF16), ((n_mp, words, hid), BF16), ((words, width), F32),
        ((n_mp, words, pair), BF16), ((n_mp, words, pair), BF16), ((n_mp * words, pair), F32), ((n_mp * words, pair), F32),
        ((n_mp, words, 3 * pair), BF16), ((n_mp, words, 3 * pair), BF16), ((n_dp, cap, narrow), BF16), ((n_dp, cap, narrow), BF16),
    ]
    if packed:
        shapes = [
            ((2, 2, 2, n_dp // 2, WORD_ROWS, 128), BF16), ((2, 2, n_dp // 2, WORD_ROWS, 128), BF16),
            ((2, n_dp // 2, CHUNK_ROWS, 128), BF16),
            ((2, n_dp // 2, CHUNK_ROWS, 128), BF16), ((n_dp // 2, CHUNK_ROWS, 128), BF16), *shapes,
        ]
    return pl.pallas_call(
        functools.partial(word_body, n_dp, cap, packed),
        in_specs=[vm] * (len(args) - 7) + [pl.BlockSpec(memory_space=pl.ANY)] * 7,
        out_specs=[vm] * len(outs),
        out_shape=[jax.ShapeDtypeStruct(s, d) for s, d in outs],
        scratch_shapes=[pltpu.VMEM(s, d) for s, d in shapes]
        + [pltpu.SemaphoreType.DMA((n_sem,)), pltpu.SemaphoreType.DMA((n_sem,)), pltpu.SemaphoreType.DMA((7, 4)), pltpu.SemaphoreType.DMA((5,)), pltpu.SemaphoreType.DMA((5,)),
        pltpu.SemaphoreType.DMA((2, 4)), pltpu.SemaphoreType.DMA((2, 4))],
        compiler_params=pltpu.CompilerParams(collective_id=0, has_side_effects=True, vmem_limit_bytes=VMEM_LIMIT),
        name="word_layer",
    )(*args)


def plain_reduce(char_parts, char_gains, char_qkv, word_parts, word_gains):
    *char_mats, gain_rows, pool_rows = char_parts
    gain_sums = jnp.stack([jnp.sum(char_mats[0] * char_qkv.astype(F32), 1), jnp.sum(gain_rows, 0)]) / char_gains.astype(F32)
    small = lax.psum((gain_sums, jnp.sum(pool_rows, 0), word_gains), ("dp", "mp"))
    mats = []
    for grad in char_mats:
        part = lax.psum_scatter(grad, "dp", scatter_dimension=0, tiled=True)
        part = lax.psum_scatter(part.astype(BF16), "mp", scatter_dimension=1, tiled=True)
        mats.append(part.astype(F32))
    qkv, *rest = word_parts
    words = []
    for grad in rest:
        part = lax.psum_scatter(grad, "dp", scatter_dimension=1, tiled=True)
        words.append(lax.psum_scatter(part, "mp", scatter_dimension=0, tiled=False))
    out, up, down = words
    qkv = lax.psum_scatter(qkv, "dp", scatter_dimension=0, tiled=True)
    qkv = jnp.transpose(qkv.reshape(qkv.shape[0], 3, -1), (1, 0, 2))
    return (*mats, qkv, out.T, up, down.T, *small)


def per_device(
    char_input,
    char_counts,
    word_source,
    segment_ids,
    cotangent,
    char_norm_gains,
    char_qkv,
    char_out,
    char_up,
    char_down,
    pool_vector,
    char_proj,
    word_norm_gains,
    word_qkv,
    word_out,
    word_up,
    word_down,
):
    groups = lax.axis_size("dp")
    char_weights = (char_norm_gains, char_qkv, char_out, char_up, char_down, pool_vector)
    slices = (word_qkv, word_out, word_up, word_down)
    pooled, *kept = char_forward(
        groups, char_input, char_counts.reshape(1, -1), *char_weights,
        word_source.reshape(1, -1), segment_ids.reshape(1, -1), slices[:3],
    )
    char_kept, (onehot, place, segments, *word_weights) = kept[:5], kept[5:]
    output, d_pooled, *word_parts, word_gains = word_layer(
        groups, pooled, onehot, place, segments, cotangent, word_norm_gains, char_proj, slices, word_weights
    )
    fused = groups == 8
    d_chars, *char_parts = char_backward(
        groups, d_pooled, char_kept, *char_weights, word_parts[0] if fused else None, word_gains
    )
    if fused:
        return finish(d_chars, output, char_parts[0])
    *word_parts, grad_proj = word_parts
    char_parts = (*char_parts[:4], grad_proj, *char_parts[4:])
    *mats, grad_char_gains, grad_pool, grad_word_gains = plain_reduce(
        char_parts, char_norm_gains, char_qkv, word_parts, word_gains
    )
    return (output, d_chars.astype(F32), *mats, grad_char_gains, grad_pool, grad_word_gains)


def solution(mesh):
    placed = (
        P(("dp", "mp"), None),
        P(("dp", "mp")),
        P(("dp", "mp")),
        P(("dp", "mp")),
        P(("dp", "mp"), None),
        P(),
        P(),
        P(),
        P(),
        P(),
        P(),
        P(),
        P(),
        P(None, None, "mp"),
        P("mp", None),
        P(None, "mp"),
        P("mp", None),
    )
    return jax.shard_map(
        per_device,
        mesh=mesh,
        in_specs=placed,
        out_specs=(
            P(("dp", "mp"), None),
            P(("dp", "mp"), None),
            P("dp", "mp"),
            P("dp", "mp"),
            P("dp", "mp"),
            P("dp", "mp"),
            P("dp", "mp"),
            P(None, "dp", "mp"),
            P("mp", "dp"),
            P("dp", "mp"),
            P("mp", "dp"),
            P(),
            P(),
            P(),
        ),
        check_vma=False,
    )
```
